128 devices in a mesh: clip: 16 (over y, z), band: 8 (over x, core).
Axes of the slice: x: 4, y: 4, z: 4, core: 2. Of those that a mesh axis runs over, the one named last changes fastest.
Arguments:
- encoded: bfloat16 [4, 4864, 768], P(None, ('clip', 'band')), may hold values from -6 to 6
- visible_pos: int32 [4, 4864], P(None, ('clip', 'band')), may hold values from 0 to 24575, as said below
- clip_len: int32 [4, 16, 3], P(None, 'clip'), may hold values from 0 to 192, as said below
- cotangent: bfloat16 [4, 16, 192, 8, 512], P(None, 'clip', 'band'), may hold values from -6 to 6
- embed_weight: bfloat16 [768, 512], replicated, may hold values from -0.21875 to 0.21875
- embed_bias: bfloat16 [512], replicated, may hold values from -1.75 to 1.75
- mask_token: bfloat16 [512], replicated, may hold values from -3 to 3
- attn_gain: bfloat16 [512], replicated, may hold values from 0.5 to 1.5
- attn_shift: bfloat16 [512], replicated, may hold values from -1.25 to 1.25
- qkv_weight: bfloat16 [512, 1536], replicated, may hold values from -0.25 to 0.25
- query_bias: bfloat16 [512], replicated, may hold values from -1.75 to 1.75
- value_bias: bfloat16 [512], replicated, may hold values from -1.75 to 1.75
- out_weight: bfloat16 [512, 512], replicated, may hold values from -1 to 1
- out_bias: bfloat16 [512], replicated, may hold values from -1.75 to 1.75
- mlp_gain: bfloat16 [512], replicated, may hold values from 0.5 to 1.5
- mlp_shift: bfloat16 [512], replicated, may hold values from -1.25 to 1.25
- up_weight: bfloat16 [512, 2048], replicated, may hold values from -0.25 to 0.25
- up_bias: bfloat16 [2048], replicated, may hold values from -1.75 to 1.75
- down_weight: bfloat16 [2048, 512], replicated, may hold values from -0.125 to 0.125
- down_bias: bfloat16 [512], replicated, may hold values from -1.75 to 1.75
Outputs:
- output: bfloat16 [4, 16, 192, 8, 512], P(None, 'clip', 'band')
- grad_encoded: bfloat16 [4, 4864, 768], P(None, ('clip', 'band'))
- grad_embed_weight: float32 [768, 512], replicated
- grad_embed_bias: float32 [512], replicated
- grad_mask_token: float32 [512], replicated
- grad_attn_gain: float32 [512], replicated
- grad_attn_shift: float32 [512], replicated
- grad_qkv_weight: float32 [512, 1536], replicated
- grad_query_bias: float32 [512], replicated
- grad_value_bias: float32 [512], replicated
- grad_out_weight: float32 [512, 512], replicated
- grad_out_bias: float32 [512], replicated
- grad_mlp_gain: float32 [512], replicated
- grad_mlp_shift: float32 [512], replicated
- grad_up_weight: float32 [512, 2048], replicated
- grad_up_bias: float32 [2048], replicated
- grad_down_weight: float32 [2048, 512], replicated
- grad_down_bias: float32 [512], replicated
The draws below stay inside these ranges and needn't reach their ends.
Inputs may be any that keep to these rules, and one draw needn't show every extreme that they name: `visible_pos`: cells are distinct within a micro-batch. The patches on a device of band index b lie in time rows b * 24 to (b + 1) * 24 - 1 of their slots. Every device receives exactly 38 cells of its own rows; each device holds at most 9 patches for the slots of any one index of clip, and exactly 9 for one of them. `clip_len`: each slot holds one clip of 192 rows, given as (192, 0, 0), or three clips of 64 rows.
All inputs are finite; a program needn't handle non-finite values.
Results may differ from the reference program's by a relative error of at most 0.014.
Values may be sent and summed in bfloat16 or wider, within the bound.
No kernel may reach another device: no remote copies, remote signals or barrier semaphores. Data moves between devices by JAX's collectives and lax.ppermute only.
A program may use at most 192 MiB of HBM per device.

```python
import jax
import jax.numpy as jnp
from jax import lax

D = 512
HEADS = 16
FF = 2048
ENC = 768
FREQ = 8
LONG = 192
SHORT = 64
MICRO = 4
SLOT_DEV = 1
ROWS = 24
SLOTS = 16
VIS_DEV = 38
CAP = 9
VIS = 4864
N_CLIP = 16
N_BAND = 8


def draw_clip_len(key, part):
    key = jax.random.fold_in(key, 11)
    longs = jax.random.randint(key, (MICRO, SLOTS), 0, 2)
    whole = jnp.array([LONG, 0, 0], dtype=jnp.int32)
    thirds = jnp.array([SHORT, SHORT, SHORT], dtype=jnp.int32)
    return jnp.where(longs[..., None] == 1, whole, thirds).astype(jnp.int32)


def band_positions(key, band):
    cells_dev = SLOT_DEV * ROWS * FREQ
    keys = jax.random.split(key, 4)
    chosen = jax.vmap(lambda sub: jax.random.permutation(sub, cells_dev))(jax.random.split(keys[0], N_CLIP))
    chosen = chosen[:, :VIS_DEV]
    hottest = jax.random.randint(keys[1], (), 0, N_CLIP)
    remain = VIS_DEV - CAP
    share = remain // (N_CLIP - 1)
    spare = remain % (N_CLIP - 1)
    ranks = jax.random.permutation(keys[2], N_CLIP - 1)
    others = share + (ranks < spare).astype(jnp.int32)
    offsets = jnp.arange(N_CLIP).astype(jnp.int32)
    other_index = jnp.clip(offsets - (offsets > hottest).astype(jnp.int32), 0, N_CLIP - 2)
    counts = jnp.where(offsets == hottest, CAP, others[other_index]).astype(jnp.int32)
    ends = jnp.cumsum(counts)
    entry = jnp.arange(VIS_DEV).astype(jnp.int32)
    offset_of = jnp.sum((entry[:, None] >= ends[None, :]).astype(jnp.int32), 1)
    receiver = (offsets[:, None] + offset_of[None, :]) % N_CLIP
    cell = chosen[receiver, entry[None, :]]
    slot_local = cell // (ROWS * FREQ)
    within = cell % (ROWS * FREQ)
    position = ((receiver * SLOT_DEV + slot_local) * LONG + band * ROWS + within // FREQ) * FREQ + within % FREQ
    shuffle = jax.vmap(lambda sub: jax.random.permutation(sub, VIS_DEV))(jax.random.split(keys[3], N_CLIP))
    return jnp.take_along_axis(position, shuffle, 1).astype(jnp.int32)


def draw_visible_pos(key, part):
    key = jax.random.fold_in(key, 7)
    batches = []
    for micro in range(MICRO):
        bands = []
        for band in range(N_BAND):
            bands.append(band_positions(jax.random.fold_in(key, micro * N_BAND + band), band))
        batches.append(jnp.stack(bands, 1))
    return jnp.stack(batches, 0).reshape(MICRO, VIS).astype(jnp.int32)


def block_levels(own_key, shape, cuts, least, largest):
    def one(dim, parts):
        draws = jax.random.uniform(jax.random.fold_in(jax.random.fold_in(own_key, 6), dim), (parts,), jnp.float32, least / len(cuts), largest / len(cuts))
        return jnp.repeat(jnp.exp(draws), shape[dim] // parts).reshape((-1,) + (1,) * (len(shape) - dim - 1))

    loudness = one(*cuts[0])
    for cut in cuts[1:]:
        loudness = loudness * one(*cut)
    return loudness


def gaussian(stream_key, shape, scale, most, shards=(), held_as=jnp.bfloat16):
    drawn = jax.random.normal(stream_key, shape, jnp.float32) * scale
    if len(shards) > 0:
        drawn = block_levels(stream_key, shape, shards, -0.22, 0.18) * drawn
    return jnp.clip(drawn, min=-most, max=most).astype(held_as)


def setup_inputs(seed: int = 0) -> dict:
    key_list = jax.random.split(jax.random.key(seed), 21)
    encoded = gaussian(key_list[0], (MICRO, VIS, ENC), 1.0, 6.0, ((1, 128),))
    visible_pos = draw_visible_pos(jax.random.fold_in(key_list[20], 71), 0)
    clip_len = draw_clip_len(jax.random.fold_in(key_list[20], 71), 0)
    cotangent = gaussian(key_list[3], (MICRO, SLOTS, LONG, FREQ, D), 1.0, 6.0, ((1, 16), (2, 8)))
    embed_weight = gaussian(key_list[4], (ENC, D), ENC ** -0.5, 0.21875)
    embed_bias = gaussian(key_list[5], (D,), 0.3, 1.75)
    mask_token = gaussian(key_list[6], (D,), 0.5, 3.0)
    attn_gain = jnp.clip(1.0 + 0.1 * jax.random.normal(key_list[7], (D,), jnp.float32), 0.5, 1.5).astype(jnp.bfloat16)
    attn_shift = gaussian(key_list[8], (D,), 0.2, 1.25)
    qkv_weight = gaussian(key_list[9], (D, 3 * D), D ** -0.5, 0.25)
    query_bias = gaussian(key_list[10], (D,), 0.3, 1.75)
    value_bias = gaussian(key_list[11], (D,), 0.3, 1.75)
    out_weight = gaussian(key_list[12], (D, D), (D // 16) ** -0.5, 1.0)
    out_bias = gaussian(key_list[13], (D,), 0.3, 1.75)
    mlp_gain = jnp.clip(1.0 + 0.1 * jax.random.normal(key_list[14], (D,), jnp.float32), 0.5, 1.5).astype(jnp.bfloat16)
    mlp_shift = gaussian(key_list[15], (D,), 0.2, 1.25)
    up_weight = gaussian(key_list[16], (D, FF), D ** -0.5, 0.25)
    up_bias = gaussian(key_list[17], (FF,), 0.3, 1.75)
    down_weight = gaussian(key_list[18], (FF, D), FF ** -0.5, 0.125)
    down_bias = gaussian(key_list[19], (D,), 0.3, 1.75)
    return dict(encoded=encoded, visible_pos=visible_pos, clip_len=clip_len, cotangent=cotangent, embed_weight=embed_weight, embed_bias=embed_bias, mask_token=mask_token, attn_gain=attn_gain, attn_shift=attn_shift, qkv_weight=qkv_weight, query_bias=query_bias, value_bias=value_bias, out_weight=out_weight, out_bias=out_bias, mlp_gain=mlp_gain, mlp_shift=mlp_shift, up_weight=up_weight, up_bias=up_bias, down_weight=down_weight, down_bias=down_bias)


epsilon = 1e-06

@jax.custom_vjp
def low(v):
    return lax.optimization_barrier(v.astype(jnp.bfloat16)).astype(jnp.float32)

@jax.custom_vjp
def low_back(v):
    return v

def low_keep(v):
    return (low(v), None)

def low_pass(kept, grad):
    return (grad,)

def back_keep(v):
    return (v, None)

def back_low(kept, grad):
    return (low(grad),)
low.defvjp(low_keep, low_pass)
low_back.defvjp(back_keep, back_low)

def matmul(left, right):
    return jnp.dot(left, right, precision=lax.Precision.HIGHEST)

def layer_norm(values, gain, shift):
    center = values - lax.optimization_barrier(jnp.mean(values, -1, keepdims=True))
    spread = lax.optimization_barrier(jnp.mean(center * center, -1, keepdims=True))
    return center * lax.rsqrt(spread + epsilon) * gain + shift

def clip_ident(lengths, rows):
    first = lengths[:, 0:1]
    second = first + lengths[:, 1:2]
    ident = (rows[None, :] >= first).astype(jnp.int32) + (rows[None, :] >= second).astype(jnp.int32)
    start = jnp.where(ident >= 1, first, 0) + jnp.where(ident >= 2, lengths[:, 1:2], 0)
    inside = (rows >= 0) & (rows < LONG)
    return (jnp.where(inside[None, :], ident, -1), rows[None, :] - start)

def position_table(row_in_clip, width):
    quarter = width // 4
    omega = 1.0 / 10000.0 ** (jnp.arange(quarter, dtype=jnp.float32) / quarter)
    row_angle = row_in_clip.astype(jnp.float32)[..., None] * omega
    freq_angle = jnp.arange(FREQ, dtype=jnp.float32)[:, None] * omega
    row_part = jnp.concatenate([jnp.sin(row_angle), jnp.cos(row_angle)], -1)
    freq_part = jnp.concatenate([jnp.sin(freq_angle), jnp.cos(freq_angle)], -1)
    shape = row_in_clip.shape + (FREQ, width // 2)
    return jnp.concatenate([jnp.broadcast_to(row_part[..., None, :], shape), jnp.broadcast_to(freq_part, shape)], -1)

def to_windows(tensor):
    slots, extent, freq, width = tensor.shape
    tensor = jnp.concatenate([tensor[:, :, 2:], tensor[:, :, :2]], 2)
    tensor = tensor.reshape(slots, extent // 4, 4, 2, 4, HEADS, width // HEADS)
    return tensor.transpose(0, 1, 3, 5, 2, 4, 6).reshape(slots, extent // 4, 2, HEADS, 16, width // HEADS)

def from_windows(tensor):
    slots, count, pairs, heads, tokens, size = tensor.shape
    tensor = tensor.reshape(slots, count, 2, heads, 4, 4, size).transpose(0, 1, 4, 2, 5, 3, 6)
    tensor = tensor.reshape(slots, count * 4, FREQ, heads * size)
    return jnp.concatenate([tensor[:, :, -2:], tensor[:, :, :-2]], 2)

def window_mask(ident):
    slots, extent = ident.shape
    tokens = jnp.repeat(ident.reshape(slots, extent // 4, 4), 4, axis=2)
    same = (tokens[..., :, None] == tokens[..., None, :]) & (tokens[..., None, :] >= 0)
    return same[:, :, None, None]

def layer(enc, places, lengths, params):
    embed_weight, embed_bias, mask_token, attn_gain, attn_shift, qkv_weight, query_bias, value_bias, out_weight, out_bias, mlp_gain, mlp_shift, up_weight, up_bias, down_weight, down_bias = params
    width = embed_weight.shape[1]
    cells = SLOTS * LONG * FREQ
    proj = low_back(low(matmul(enc, embed_weight) + embed_bias))
    filled = jnp.zeros((cells, width), enc.dtype).at[places].set(proj)
    seen = jnp.zeros((cells,), jnp.int32).at[places].set(1) > 0
    unused, row_in_clip = clip_ident(lengths, jnp.arange(LONG).astype(jnp.int32))
    table = position_table(row_in_clip, width).reshape(cells, width)
    hidden = jnp.where(seen[:, None], filled, mask_token[None, :]) + table
    normed_one = low(layer_norm(hidden, attn_gain, attn_shift))
    qkv_bias = jnp.concatenate([query_bias, jnp.zeros_like(query_bias), value_bias])
    mixed = low_back(low(matmul(normed_one, qkv_weight) + qkv_bias)).reshape(SLOTS, LONG, FREQ, 3 * width)
    ident_ext, unused_rows = clip_ident(lengths, jnp.arange(LONG + 4).astype(jnp.int32) - 2)
    allowed = window_mask(ident_ext)
    pad_rows = ((0, 0), (2, 2), (0, 0), (0, 0))
    query_win = to_windows(jnp.pad(mixed[..., :width], pad_rows))
    key_win = to_windows(jnp.pad(mixed[..., width:2 * width], pad_rows))
    value_win = to_windows(jnp.pad(mixed[..., 2 * width:], pad_rows))
    scale = (width // HEADS) ** (-0.5)
    raw = jnp.einsum('swghqd,swghkd->swghqk', query_win, key_win, precision=lax.Precision.HIGHEST) * scale
    scores = jnp.where(allowed, low_back(raw), -1e+30)
    probs = jax.nn.softmax(scores, -1)
    attended = low_back(jnp.einsum('swghqk,swghkd->swghqd', low(probs), value_win, precision=lax.Precision.HIGHEST))
    attended = low(from_windows(attended)[:, 2:2 + LONG].reshape(cells, width))
    middle = hidden + low_back(matmul(attended, out_weight) + out_bias)
    normed_two = low(layer_norm(middle, mlp_gain, mlp_shift))
    expand = low_back(matmul(normed_two, up_weight) + up_bias)
    activated = low(jax.nn.gelu(expand, approximate=False))
    result = middle + low_back(matmul(activated, down_weight) + down_bias)
    return result.reshape(SLOTS, LONG, FREQ, width)

def reference(encoded, visible_pos, clip_len, cotangent, embed_weight, embed_bias, mask_token, attn_gain, attn_shift, qkv_weight, query_bias, value_bias, out_weight, out_bias, mlp_gain, mlp_shift, up_weight, up_bias, down_weight, down_bias):
    params = tuple((weight.astype(jnp.float32) for weight in (embed_weight, embed_bias, mask_token, attn_gain, attn_shift, qkv_weight, query_bias, value_bias, out_weight, out_bias, mlp_gain, mlp_shift, up_weight, up_bias, down_weight, down_bias)))

    def micro_step(carry, inputs):
        enc, places, lengths, cot = inputs

        def forward(enc_float, weights):
            return layer(enc_float, places, lengths, weights)
        result, pull = jax.vjp(forward, enc.astype(jnp.float32), params)
        grad_enc, grads = pull(cot.astype(jnp.float32))
        carry = tuple((total + grad for total, grad in zip(carry, grads)))
        return (carry, (result.astype(jnp.bfloat16), grad_enc.astype(jnp.bfloat16)))
    zeros = tuple((jnp.zeros_like(weight) for weight in params))
    totals, (outputs, grads_enc) = lax.scan(micro_step, zeros, (encoded, visible_pos, clip_len, cotangent))
    return (outputs, grads_enc, totals[0], totals[1], totals[2], totals[3], totals[4], totals[5], totals[6], totals[7], totals[8], totals[9], totals[10], totals[11], totals[12], totals[13], totals[14], totals[15])
```

```python
import jax
import jax.numpy as jnp
import numpy as np
from jax import lax
from jax.experimental import pallas as pl
from jax.experimental.pallas import tpu as pltpu
from jax.sharding import PartitionSpec as P

HEADS = 16
FREQ = 8
LONG = 192
MICRO = 4
ROWS = 24
CELLS = ROWS * FREQ
ALL = MICRO * CELLS
EXT = CELLS + 32
TOK = 48
CAP = 9
BLK = 40
SRC = 16
GOT = SRC * BLK
D = 512
FF = 2048
ENC = 768
CHUNK = 128
CHUNKS = MICRO * EXT // CHUNK
EPS = 1e-06
SCALE = (D // HEADS) ** (-0.5)
F32 = jnp.float32
BF16 = jnp.bfloat16

NN = (((1,), (0,)), ((), ()))
NT = (((1,), (1,)), ((), ()))
TN = (((0,), (0,)), ((), ()))


def dot(left, right, dims=NN):
    return lax.dot_general(left, right, dims, preferred_element_type=F32)


def iota(shape, dim):
    return lax.broadcasted_iota(jnp.int32, shape, dim)


def one_hot(hit):
    return jnp.where(hit, 1.0, 0.0).astype(BF16)


def call(kernel, name, out_shape, args, scratch=(), smem=0, flops=0):
    specs = [pl.BlockSpec(memory_space=pltpu.SMEM)] * smem
    specs += [pl.BlockSpec(memory_space=pltpu.VMEM)] * (len(args) - smem)
    outs = [jax.ShapeDtypeStruct(shape, dtype) for shape, dtype in out_shape]
    size = sum(a.size * a.dtype.itemsize for a in args) + sum(
        o.size * o.dtype.itemsize for o in outs
    )
    return pl.pallas_call(
        kernel,
        name=name,
        out_shape=outs,
        in_specs=specs,
        out_specs=[pl.BlockSpec(memory_space=pltpu.VMEM)] * len(outs),
        scratch_shapes=list(scratch),
        compiler_params=pltpu.CompilerParams(vmem_limit_bytes=56 * 2**20),
        cost_estimate=pl.CostEstimate(flops=flops, bytes_accessed=size, transcendentals=0),
    )(*args)


def pack_kernel(row, col, enc, out, dest):
    count = MICRO * TOK
    key_r, key_c = row[1:2, :], col[:, 1:2]
    same = key_c == key_r
    low = iota((count, count), 0)
    high = iota((count, count), 1)
    rank_r = jnp.sum(jnp.where(same & (low < high), 1, 0), axis=0, keepdims=True)
    rank_c = jnp.sum(jnp.where(same & (high < low), 1, 0), axis=1, keepdims=True)
    place_r = row[2:3, :] * CAP + rank_r
    place_c = col[:, 2:3] * CAP + rank_c
    dest_r = row[0:1, :] * BLK + place_r
    dest[...] = col[:, 0:1] * BLK + place_c
    select = one_hot(iota((GOT, count), 0) == dest_r)
    to_dev = jnp.where(
        iota((SRC, count), 0) == row[0:1, :], row[3:4, :].astype(F32), 0.0
    ).astype(BF16)
    to_lane = one_hot(iota((count, ENC), 1) == place_c)
    places = dot(to_dev, to_lane).astype(BF16)
    spread = one_hot(iota((GOT, SRC), 0) == iota((GOT, SRC), 1) * BLK + (BLK - 4))
    out[...] = (dot(select, enc[...]) + dot(spread, places)).astype(BF16)


def norm_parts(values):
    center = values - jnp.mean(values, -1, keepdims=True)
    inverse = lax.rsqrt(jnp.mean(center * center, -1, keepdims=True) + EPS)
    return center * inverse, inverse


def norm_back(grad, normal, inverse, gain):
    scaled = grad * gain
    return inverse * (
        scaled
        - jnp.mean(scaled, -1, keepdims=True)
        - normal * jnp.mean(scaled * normal, -1, keepdims=True)
    )


def enter_kernel(
    idx_r, idx_c, got, table, embed_w, qkv_w, vecs, qkv_b,
    hidden_o, normed_o, mixed_o, filled_o, seen_o, cell_o, low_o, high_o,
):
    hit = one_hot(iota((SRC, GOT), 1) == iota((SRC, GOT), 0) * BLK + (BLK - 4))
    numbers = dot(hit, got[:, :128]).astype(BF16)
    spread_r = dot(numbers, one_hot(iota((SRC, GOT), 0) == idx_r[0:1, :]), TN)
    value_r = jnp.sum(
        jnp.where(iota((128, GOT), 0) == idx_r[1:2, :], spread_r, 0.0), axis=0, keepdims=True
    )
    cell_r = jnp.where(
        value_r > 0.5, idx_r[2:3, :] * CELLS + value_r.astype(jnp.int32) - 1, -1
    )
    spread_c = dot(one_hot(iota((GOT, SRC), 1) == idx_c[:, 0:1]), numbers)
    value_c = jnp.sum(
        jnp.where(iota((GOT, 128), 1) == idx_c[:, 1:2], spread_c, 0.0), axis=1, keepdims=True
    )
    cell_o[...] = jnp.where(
        value_c > 0.5, idx_c[:, 2:3] * CELLS + value_c.astype(jnp.int32) - 1, -1
    )
    for m in range(MICRO):
        rows = slice(m * CELLS, (m + 1) * CELLS)
        match = jnp.where(iota((CELLS, GOT), 0) + m * CELLS == cell_r, 1.0, 0.0)
        seen = jnp.sum(match, axis=1, keepdims=True)
        filled = dot(match.astype(BF16), got[...]).astype(BF16)
        filled_o[rows, :] = filled
        seen_o[rows, :] = seen
        proj = (dot(filled, embed_w[...]) + vecs[0:1, :]).astype(BF16).astype(F32)
        hidden = jnp.where(seen > 0.5, proj, vecs[1:2, :]) + table[rows, :]
        hidden_o[rows, :] = hidden
        normal, unused = norm_parts(hidden)
        normed = (normal * vecs[2:3, :] + vecs[3:4, :]).astype(BF16)
        normed_o[rows, :] = normed
        mixed = (dot(normed, qkv_w[...]) + qkv_b[...]).astype(BF16)
        mixed_o[rows, :] = mixed
        low_o[m] = mixed[:16, D:]
        high_o[m] = mixed[CELLS - 16 :, D:]


def spread_rows(source, column, width, low, high, target):
    for m in range(MICRO):
        base = m * EXT
        if low is None:
            target[base : base + 16, :] = jnp.zeros((16, width), BF16)
            target[base + 16 + CELLS : base + EXT, :] = jnp.zeros((16, width), BF16)
        else:
            target[base : base + 16, :] = low[m, :, column - D : column - D + width]
            target[base + 16 + CELLS : base + EXT, :] = high[m, :, column - D : column - D + width]
        target[base + 16 : base + 16 + CELLS, :] = source[
            m * CELLS : (m + 1) * CELLS, column : column + width
        ]


def expand_lanes(packed, lanes):
    return jnp.concatenate([packed * lanes[w : w + 1, :] for w in range(4)], axis=0)


def compress(full, lanes):
    out = full[0:32, :] * lanes[0:1, :]
    for w in range(1, 4):
        out = out + full[32 * w : 32 * w + 32, :] * lanes[w : w + 1, :]
    return out


def attend_kernel(
    mixed, low, high, mask, lanes, lanes32, head_mask, attended_o, probs_o, q_s, k_s, v_s, a_s
):
    spread_rows(mixed, 0, D, None, None, q_s)
    spread_rows(mixed, D, D, low, high, k_s)
    spread_rows(mixed, 2 * D, D, low, high, v_s)
    lane_low = lanes[...]
    lane_f = lanes32[...]

    def step(c, carry):
        rows = pl.ds(pl.multiple_of(c * CHUNK, CHUNK), CHUNK)
        allowed = mask[c] > 0.5
        allowed = jnp.concatenate([allowed, allowed], axis=1)
        for j in range(2):
            cols = slice(256 * j, 256 * j + 256)
            q = q_s[rows, cols]
            k = k_s[rows, cols]
            v_t = jnp.transpose(v_s[rows, cols])
            parts = []
            for pair in range(4):
                q_m = jnp.concatenate(
                    [q * head_mask[2 * pair + i : 2 * pair + i + 1, :] for i in range(2)], axis=0
                )
                scores = compress(dot(k, q_m, NT), lane_f) * SCALE
                scores = jnp.where(allowed, scores, -1e30)
                grown = jnp.exp(scores - jnp.max(scores, axis=0, keepdims=True))
                probs = grown / jnp.sum(grown, axis=0, keepdims=True)
                start = (8 * j + 2 * pair) * CHUNK
                probs_o[c, :, start : start + 256] = probs
                full = expand_lanes(probs.astype(BF16), lane_low)
                for i in range(2):
                    h = 2 * pair + i
                    parts.append(
                        dot(v_t[32 * h : 32 * h + 32, :], full[:, CHUNK * i : CHUNK * i + CHUNK])
                    )
            out_t = jnp.concatenate(parts, axis=0).astype(BF16)
            a_s[rows, cols] = jnp.transpose(out_t)
        return carry

    lax.fori_loop(0, CHUNKS, step, 0)
    for m in range(MICRO):
        attended_o[m * CELLS : (m + 1) * CELLS, :] = a_s[m * EXT + 16 : m * EXT + 16 + CELLS, :]


def gelu_parts(x):
    size = jnp.abs(x) * (0.5**0.5)
    bell = jnp.exp(-0.5 * x * x)
    t = 1.0 / (1.0 + 0.3275911 * size)
    poly = t * (
        0.254829592
        + t * (-0.284496736 + t * (1.421413741 + t * (-1.453152027 + t * 1.061405429)))
    )
    tail = 0.5 * poly * bell
    share = jnp.where(x >= 0, 1.0 - tail, tail)
    return x * share, share + x * bell * 0.3989422804014327


def mlp_kernel(
    core, hidden, attended, cot, out_w, up_w, down_w, vecs, up_b,
    output_o, gmid_o, gatt_o, grads_o, gout_o, sums_o, act_s, gexp_s, n2_s, gb_s, n2t_s,
):
    tile = 256
    sums_o[...] = jnp.zeros((8, D), F32)

    def forward(i, carry):
        rows = pl.ds(pl.multiple_of(i * tile, tile), tile)
        middle = hidden[rows, :] + dot(attended[rows, :], out_w[...]) + vecs[0:1, :]
        normal, inverse = norm_parts(middle)
        normed = (normal * vecs[1:2, :] + vecs[2:3, :]).astype(BF16)
        n2_s[rows, :] = normed
        g = cot[rows, :]
        result = middle + vecs[3:4, :]
        grad = jnp.zeros((tile, D), F32)
        for f in range(4):
            cols = slice(512 * f, 512 * f + 512)
            expand = dot(normed, up_w[:, cols]) + up_b[0:1, cols]
            value, slope = gelu_parts(expand)
            act = value.astype(BF16)
            act_s[rows, cols] = act
            result = result + dot(act, down_w[cols, :])
            g_exp = (dot(g, down_w[cols, :], NT) * slope).astype(BF16)
            gexp_s[rows, cols] = g_exp
            sums_o[4 + f : 5 + f, :] += jnp.sum(g_exp.astype(F32), axis=0, keepdims=True)
            grad = grad + dot(g_exp, up_w[:, cols], NT)
        output_o[rows, :] = result.astype(BF16)
        g_float = g.astype(F32)
        g_mid = g_float + norm_back(grad, normal, inverse, vecs[1:2, :])
        gmid_o[rows, :] = g_mid
        g_low = g_mid.astype(BF16)
        gb_s[rows, :] = g_low
        gatt_o[rows, :] = dot(g_low, out_w[...], NT).astype(BF16)
        sums_o[0:1, :] += jnp.sum(g_low.astype(F32), axis=0, keepdims=True)
        sums_o[1:2, :] += jnp.sum(grad * normal, axis=0, keepdims=True)
        sums_o[2:3, :] += jnp.sum(grad, axis=0, keepdims=True)
        sums_o[3:4, :] += jnp.sum(g_float, axis=0, keepdims=True)
        return carry

    lax.fori_loop(0, ALL // tile, forward, 0)
    n2t_s[...] = jnp.transpose(n2_s[...])

    def weights(f, carry):
        cols = pl.ds(pl.multiple_of(f * 512, 512), 512)
        half = f // 2
        slot = jnp.where(half == core[0], 0, 1)
        place = pl.multiple_of((f % 2) * 512, 512)
        grads_o[slot, pl.ds(place, 512), :] = dot(act_s[:, cols], cot[...], TN).astype(BF16)
        grads_o[slot, pl.ds(1024 + place, 512), :] = dot(n2t_s[...], gexp_s[:, cols]).astype(BF16)
        return carry

    lax.fori_loop(0, 4, weights, 0)
    gout_o[...] = dot(attended[...], gb_s[...], TN).astype(BF16)


def attend_back_kernel(
    mixed, low, high, probs_i, gatt, lanes, lanes32, head_mask,
    gmixed_o, low_o, high_o, rim_o, q_s, k_s, v_s, g_s, dq_s, dkv_s,
):
    spread_rows(mixed, 0, D, None, None, q_s)
    spread_rows(mixed, D, D, low, high, k_s)
    spread_rows(mixed, 2 * D, D, low, high, v_s)
    spread_rows(gatt, 0, D, None, None, g_s)
    lane_low = lanes[...]
    lane_f = lanes32[...]

    def step(c, carry):
        rows = pl.ds(pl.multiple_of(c * CHUNK, CHUNK), CHUNK)
        for j in range(2):
            cols = slice(256 * j, 256 * j + 256)
            q = q_s[rows, cols]
            g = g_s[rows, cols]
            v = v_s[rows, cols]
            k_t = jnp.transpose(k_s[rows, cols])
            parts = []
            d_key = jnp.zeros((CHUNK, 256), F32)
            d_value = jnp.zeros((CHUNK, 256), F32)
            for pair in range(4):
                masks = [head_mask[2 * pair + i : 2 * pair + i + 1, :] for i in range(2)]
                q_m = jnp.concatenate([q * one for one in masks], axis=0)
                g_m = jnp.concatenate([g * one for one in masks], axis=0)
                start = (8 * j + 2 * pair) * CHUNK
                probs = probs_i[c, :, start : start + 256]
                g_probs = compress(dot(v, g_m, NT), lane_f)
                inner = jnp.sum(probs * g_probs, axis=0, keepdims=True)
                g_scores = (probs * (g_probs - inner)).astype(BF16)
                d_value = d_value + dot(expand_lanes(probs.astype(BF16), lane_low), g_m)
                full = expand_lanes(g_scores, lane_low)
                d_key = d_key + dot(full, q_m)
                for i in range(2):
                    h = 2 * pair + i
                    parts.append(
                        dot(k_t[32 * h : 32 * h + 32, :], full[:, CHUNK * i : CHUNK * i + CHUNK])
                    )
            dq_t = (jnp.concatenate(parts, axis=0) * SCALE).astype(BF16)
            dq_s[rows, cols] = jnp.transpose(dq_t)
            dkv_s[rows, cols] = d_key * SCALE
            dkv_s[rows, slice(D + 256 * j, D + 256 * j + 256)] = d_value
        return carry

    lax.fori_loop(0, CHUNKS, step, 0)
    for m in range(MICRO):
        base = m * EXT
        rows = slice(m * CELLS, (m + 1) * CELLS)
        gmixed_o[rows, :D] = dq_s[base + 16 : base + 16 + CELLS, :]
        gmixed_o[rows, D:] = dkv_s[base + 16 : base + 16 + CELLS, :].astype(BF16)
        low_o[m] = dkv_s[base : base + 16, :].astype(BF16)
        high_o[m] = dkv_s[base + 16 + CELLS : base + EXT, :].astype(BF16)
        rim_o[m, 0] = dkv_s[base + 16 : base + 32, :]
        rim_o[m, 1] = dkv_s[base + CELLS : base + CELLS + 16, :]


def leave_kernel(
    core, gmixed, from_low, from_high, rim, hidden, normed, filled, seen, cell, gmid, qkv_w, vecs,
    gout, sums, grads_o, ret_o, gm_s, gf_s, nt_s, ft_s,
):
    first, second = core[0], 1 - core[0]
    small = jnp.zeros((1, D), F32)
    gain_sum, shift_sum, mask_sum, embed_sum, query_sum, value_sum = [small] * 6
    for m in range(MICRO):
        base = m * CELLS
        rows = slice(base, base + CELLS)
        gm_s[rows, :] = gmixed[rows, :]
        gm_s[base : base + 16, D:] = (rim[m, 0] + from_low[m].astype(F32)).astype(BF16)
        gm_s[base + CELLS - 16 : base + CELLS, D:] = (rim[m, 1] + from_high[m].astype(F32)).astype(
            BF16
        )
        gm = gm_s[rows, :]
        grad = dot(gm, qkv_w[...], NT)
        normal, inverse = norm_parts(hidden[rows, :])
        g_hidden = gmid[rows, :] + norm_back(grad, normal, inverse, vecs[2:3, :])
        there = seen[rows, :] > 0.5
        g_low = g_hidden.astype(BF16)
        gf_s[rows, :] = g_low
        gain_sum += jnp.sum(grad * normal, axis=0, keepdims=True)
        shift_sum += jnp.sum(grad, axis=0, keepdims=True)
        mask_sum += jnp.sum(jnp.where(there, 0.0, g_hidden), axis=0, keepdims=True)
        embed_sum += jnp.sum(jnp.where(there, g_low.astype(F32), 0.0), axis=0, keepdims=True)
        query_sum += jnp.sum(gm[:, :D].astype(F32), axis=0, keepdims=True)
        value_sum += jnp.sum(gm[:, 2 * D :].astype(F32), axis=0, keepdims=True)
    nt_s[...] = jnp.transpose(normed[...])
    ft_s[...] = jnp.transpose(filled[...])
    ret_o[...] = dot(one_hot(iota((GOT, ALL), 1) == cell[...]), gf_s[...]).astype(BF16)

    def weights(b, carry):
        cols = pl.ds(pl.multiple_of(b * 512, 512), 512)
        grads_o[first, cols, :] = dot(nt_s[...], gm_s[:, cols]).astype(BF16)
        return carry

    lax.fori_loop(0, 3, weights, 0)
    grads_o[second, 0:512, :] = gout[...]
    grads_o[second, 512:1280, :] = dot(ft_s[...], gf_s[...]).astype(BF16)
    grads_o[second, 1280:1296, :] = jnp.concatenate(
        [
            embed_sum, mask_sum, gain_sum, shift_sum, query_sum, value_sum,
            small, small, sums[...],
        ],
        axis=0,
    ).astype(BF16)
    grads_o[second, 1296:1536, :] = jnp.zeros((240, D), BF16)


def return_kernel(dest, came, embed_w, out):
    select = one_hot(iota((MICRO * TOK, GOT), 1) == dest[...])
    g_proj = dot(select, came[...]).astype(BF16)
    out[...] = dot(g_proj, embed_w[...], NT).astype(BF16)


def clip_ident(lengths, rows):
    first = lengths[:, 0:1]
    second = first + lengths[:, 1:2]
    ident = (rows[None, :] >= first).astype(jnp.int32) + (rows[None, :] >= second).astype(jnp.int32)
    start = jnp.where(ident >= 1, first, 0) + jnp.where(ident >= 2, lengths[:, 1:2], 0)
    inside = (rows >= 0) & (rows < LONG)
    return (jnp.where(inside[None, :], ident, -1), rows[None, :] - start)


def position_table(row_in_clip, width):
    quarter = width // 4
    omega = 1.0 / 10000.0 ** (jnp.arange(quarter, dtype=jnp.float32) / quarter)
    row_angle = row_in_clip.astype(jnp.float32)[..., None] * omega
    freq_angle = jnp.arange(FREQ, dtype=jnp.float32)[:, None] * omega
    row_part = jnp.concatenate([jnp.sin(row_angle), jnp.cos(row_angle)], -1)
    freq_part = jnp.concatenate([jnp.sin(freq_angle), jnp.cos(freq_angle)], -1)
    shape = row_in_clip.shape + (FREQ, width // 2)
    return jnp.concatenate(
        [jnp.broadcast_to(row_part[..., None, :], shape), jnp.broadcast_to(freq_part, shape)], -1
    )


def window_mask(ident):
    cells = jnp.repeat(ident.reshape(MICRO * 7, 4), FREQ, axis=1)
    freq = np.tile((np.arange(FREQ) + 2) % 8 // 4, 4)
    same = (cells[:, :, None] == cells[:, None, :]) & (cells[:, :, None] >= 0)
    same = same & jnp.asarray(freq[:, None] == freq[None, :])[None]
    return same.astype(F32).reshape(CHUNKS, 4, 32, 32).transpose(0, 2, 1, 3).reshape(CHUNKS, 32, CHUNK)


def on_device(
    encoded, visible_pos, clip_len, cotangent, embed_weight, embed_bias, mask_token, attn_gain,
    attn_shift, qkv_weight, query_bias, value_bias, out_weight, out_bias, mlp_gain, mlp_shift,
    up_weight, up_bias, down_weight, down_bias,
):
    both = ("clip", "band")
    groups = lax.axis_size("clip")
    bands = lax.axis_size("band")
    band = lax.axis_index("band")
    side = band % 2
    core = side.astype(jnp.int32).reshape(1)
    halves = [
        [c * bands + 2 * x + k for c in range(groups) for x in range(bands // 2)] for k in range(2)
    ]
    swap = [(i, i ^ 1) for i in range(bands)]
    forward = [(i, i + 1) for i in range(bands - 1)]
    backward = [(b, a) for a, b in forward]
    chips = groups * bands // 2

    def to_all(block):
        return lax.all_to_all(
            block, both, split_axis=0, concat_axis=0, tiled=True, axis_index_groups=halves
        )

    def chip_sum(grads):
        rows = grads.shape[1] // chips
        other = lax.ppermute(grads[1], "band", swap)
        mine = (grads[0].astype(F32) + other.astype(F32)).astype(BF16)
        return mine.reshape(chips, rows, D)

    def total(parts):
        return jnp.sum(parts.astype(F32), 0).astype(BF16)

    pos = jnp.pad(visible_pos, ((0, 0), (0, TOK - visible_pos.shape[1])), constant_values=-1)
    micro = lax.broadcasted_iota(jnp.int32, pos.shape, 0)
    target = jnp.where(pos < 0, 99, pos // (LONG * FREQ))
    number = pos // FREQ % LONG % ROWS * FREQ + pos % FREQ + 1
    meta = jnp.stack(
        [x.reshape(-1) for x in (target, target * MICRO + micro, micro, number)] * 2
    )
    enc = jnp.pad(encoded, ((0, 0), (0, TOK - encoded.shape[1]), (0, 0))).reshape(MICRO * TOK, ENC)
    packed, dest = call(
        pack_kernel, "pack", [((GOT, ENC), BF16), ((MICRO * TOK, 1), jnp.int32)],
        (meta, meta.T, enc), flops=GOT * MICRO * TOK * ENC * 2,
    )
    got = lax.all_to_all(
        packed.reshape(SRC, BLK, ENC), "clip", split_axis=0, concat_axis=0, tiled=True
    ).reshape(GOT, ENC)

    place = np.arange(GOT)
    within = place % BLK
    index = np.zeros((8, GOT), np.int32)
    index[0], index[1], index[2] = place // BLK, within, np.where(within < 36, within // CAP, 99)
    lane = np.arange(256) % CHUNK // 32
    lanes = np.zeros((8, 256), np.float32)
    for w in range(4):
        lanes[w] = lane == w
    head_mask = (np.arange(256)[None, :] // 32 == np.arange(8)[:, None]).astype(np.float32)
    lanes_f = jnp.asarray(lanes)
    lanes_low = jnp.asarray(lanes, BF16)
    head_mask = jnp.asarray(head_mask, BF16)

    unused, row_in_clip = clip_ident(clip_len[:, 0], band * ROWS + jnp.arange(ROWS))
    table = position_table(row_in_clip, D).reshape(ALL, D)
    ident_ext, unused = clip_ident(clip_len[:, 0], band * ROWS - 2 + jnp.arange(ROWS + 4))
    mask = window_mask(ident_ext)
    zero = jnp.zeros((D,), BF16)
    vecs_one = jnp.stack([embed_bias, mask_token, attn_gain, attn_shift] * 2).astype(F32)
    vecs_two = jnp.stack([out_bias, mlp_gain, mlp_shift, down_bias] * 2).astype(F32)
    qkv_b = jnp.concatenate([query_bias, zero, value_bias]).astype(F32)[None]
    up_b = up_bias.astype(F32)[None]

    hidden, normed, mixed, filled, seen, cell, low, high = call(
        enter_kernel, "enter",
        [
            ((ALL, D), F32), ((ALL, D), BF16), ((ALL, 3 * D), BF16), ((ALL, ENC), BF16),
            ((ALL, 1), F32), ((GOT, 1), jnp.int32),
            ((MICRO, 16, 2 * D), BF16), ((MICRO, 16, 2 * D), BF16),
        ],
        (
            jnp.asarray(index), jnp.asarray(np.ascontiguousarray(index.T)), got, table,
            embed_weight, qkv_weight, vecs_one, qkv_b,
        ),
        flops=2 * ALL * (GOT * ENC + ENC * D + 3 * D * D),
    )
    from_low = lax.ppermute(high, "band", forward)
    from_high = lax.ppermute(low, "band", backward)
    ext = MICRO * EXT
    attended, probs = call(
        attend_kernel, "attend",
        [((ALL, D), BF16), ((CHUNKS, 32, HEADS * CHUNK), F32)],
        (mixed, from_low, from_high, mask, lanes_low, lanes_f, head_mask),
        scratch=[pltpu.VMEM((ext, D), BF16)] * 4,
        flops=ext * HEADS * CHUNK * 256 * 4,
    )
    cot = cotangent.reshape(ALL, D)
    output, gmid, gatt, grads_one, gout, sums = call(
        mlp_kernel, "mlp",
        [
            ((ALL, D), BF16), ((ALL, D), F32), ((ALL, D), BF16), ((2, FF, D), BF16),
            ((D, D), BF16), ((8, D), F32),
        ],
        (core, hidden, attended, cot, out_weight, up_weight, down_weight, vecs_two, up_b),
        scratch=[
            pltpu.VMEM((ALL, FF), BF16), pltpu.VMEM((ALL, FF), BF16), pltpu.VMEM((ALL, D), BF16),
            pltpu.VMEM((ALL, D), BF16), pltpu.VMEM((D, ALL), BF16),
        ],
        smem=1, flops=2 * ALL * (6 * D * FF + 3 * D * D),
    )
    chip_one = chip_sum(grads_one)
    gatt, chip_one = lax.optimization_barrier((gatt, chip_one))
    parts_one = to_all(chip_one)
    gmixed, low, high, rim = call(
        attend_back_kernel, "attend_back",
        [
            ((ALL, 3 * D), BF16), ((MICRO, 16, 2 * D), BF16), ((MICRO, 16, 2 * D), BF16),
            ((MICRO, 2, 16, 2 * D), F32),
        ],
        (mixed, from_low, from_high, probs, gatt, lanes_low, lanes_f, head_mask),
        scratch=[pltpu.VMEM((ext, D), BF16)] * 5 + [pltpu.VMEM((ext, 2 * D), F32)],
        flops=ext * HEADS * CHUNK * 256 * 8,
    )
    from_low = lax.ppermute(high, "band", forward)
    from_high = lax.ppermute(low, "band", backward)
    grads_two, returned = call(
        leave_kernel, "leave",
        [((2, 3 * D, D), BF16), ((GOT, D), BF16)],
        (
            core, gmixed, from_low, from_high, rim, hidden, normed, filled, seen, cell, gmid,
            qkv_weight, vecs_one, gout, sums,
        ),
        scratch=[
            pltpu.VMEM((ALL, 3 * D), BF16), pltpu.VMEM((ALL, D), BF16),
            pltpu.VMEM((D, ALL), BF16), pltpu.VMEM((ENC, ALL), BF16),
        ],
        smem=1, flops=2 * ALL * (6 * D * D + GOT * D + ENC * D),
    )
    parts_one, grads_two = lax.optimization_barrier((parts_one, grads_two))
    total_one = lax.all_gather(total(parts_one), both, axis=0)
    total_one = total_one.reshape(chips, 2, -1, D)
    half_one = [total_one[:, k].reshape(-1, D).astype(F32) for k in range(2)]
    mine = total(to_all(chip_sum(grads_two)))
    mine = to_all(jnp.broadcast_to(mine[None], (chips,) + mine.shape)).reshape(-1, D)
    mine, returned = lax.optimization_barrier((mine, returned))
    other = lax.ppermute(mine, "band", swap)
    half_two = (
        jnp.where(side == 0, mine, other).astype(F32),
        jnp.where(side == 0, other, mine).astype(F32),
    )
    came = lax.all_to_all(
        returned.reshape(SRC, BLK, D), "clip", split_axis=0, concat_axis=0, tiled=True
    ).reshape(GOT, D)
    (grad_enc,) = call(
        return_kernel, "return", [((MICRO * TOK, ENC), BF16)], (dest, came, embed_weight),
        flops=2 * MICRO * TOK * D * (GOT + ENC),
    )
    grad_enc = grad_enc.reshape(MICRO, TOK, ENC)[:, : encoded.shape[1]]

    down = jnp.concatenate([half_one[0][:1024], half_one[1][:1024]], 0)
    up = jnp.concatenate([h[1024 + 512 * b : 1536 + 512 * b] for h in half_one for b in range(2)], 1)
    qkv = jnp.concatenate([half_two[0][512 * b : 512 * b + 512] for b in range(3)], 1)
    rest = half_two[1]
    small = rest[1280:1296]
    return (
        output.reshape(cotangent.shape), grad_enc, rest[512:1280], small[0], small[1], small[2],
        small[3], qkv, small[4], small[5], rest[:512], small[8], small[9], small[10], up,
        small[12:16].reshape(FF), down, small[11],
    )


def solution(mesh):
    whole = P()
    return jax.shard_map(
        on_device,
        mesh=mesh,
        in_specs=(
            P(None, ("clip", "band"), None),
            P(None, ("clip", "band")),
            P(None, "clip", None),
            P(None, "clip", "band", None, None),
        )
        + (whole,) * 16,
        out_specs=(P(None, "clip", "band", None, None), P(None, ("clip", "band"), None))
        + (whole,) * 16,
        check_vma=False,
    )
```

```python
import jax
import jax.numpy as jnp
import numpy as np
from jax import lax
from jax.experimental import pallas as pl
from jax.experimental.pallas import tpu as pltpu
from jax.sharding import PartitionSpec as P

HEADS = 16
FREQ = 8
LONG = 192
MICRO = 4
ROWS = 24
CELLS = ROWS * FREQ
ALL = MICRO * CELLS
CAP = 9
BLK = 40
SRC = 16
GOT = SRC * BLK
D = 512
FF = 2048
ENC = 768
EPS = 1e-06
SCALE = (D // HEADS) ** (-0.5)
F32 = jnp.float32
BF16 = jnp.bfloat16

NN = (((1,), (0,)), ((), ()))
NT = (((1,), (1,)), ((), ()))
TN = (((0,), (0,)), ((), ()))


def dot(left, right, dims=NN):
    return lax.dot_general(left, right, dims, preferred_element_type=F32)


def iota(shape, dim):
    return lax.broadcasted_iota(jnp.int32, shape, dim)


def one_hot(hit):
    return jnp.where(hit, 1.0, 0.0).astype(BF16)


def call(kernel, name, out_shape, args, scratch=(), smem=0, flops=0, vmem=16):
    specs = [pl.BlockSpec(memory_space=pltpu.SMEM)] * smem
    specs += [pl.BlockSpec(memory_space=pltpu.VMEM)] * (len(args) - smem)
    outs = [jax.ShapeDtypeStruct(shape, dtype) for shape, dtype in out_shape]
    size = sum(a.size * a.dtype.itemsize for a in args) + sum(
        o.size * o.dtype.itemsize for o in outs
    )
    return pl.pallas_call(
        kernel,
        name=name,
        out_shape=outs,
        in_specs=specs,
        out_specs=[pl.BlockSpec(memory_space=pltpu.VMEM)] * len(outs),
        scratch_shapes=list(scratch),
        compiler_params=pltpu.CompilerParams(vmem_limit_bytes=vmem * 2**20),
        cost_estimate=pl.CostEstimate(flops=flops, bytes_accessed=size, transcendentals=0),
    )(*args)


def pack_kernel(band, pos, enc, out, dest):
    count = pos.shape[1]
    low = iota((count, count), 0)
    high = iota((count, count), 1)
    packed = jnp.zeros((GOT, ENC), F32)
    places = jnp.zeros((SRC, 128), F32)
    for m in range(MICRO):
        cell_r = pos[m : m + 1, :]
        cell_c = jnp.sum(jnp.where(low == high, cell_r, 0), axis=1, keepdims=True)
        slot = LONG * FREQ
        dev_r = jnp.sum(
            jnp.where(cell_r >= slot * iota((SRC, count), 0) + slot, 1, 0), axis=0, keepdims=True
        )
        dev_c = jnp.sum(
            jnp.where(cell_c >= slot * iota((count, SRC), 1) + slot, 1, 0), axis=1, keepdims=True
        )
        same = dev_c == dev_r
        rank_r = jnp.sum(jnp.where(same & (low < high), 1, 0), axis=0, keepdims=True)
        rank_c = jnp.sum(jnp.where(same & (high < low), 1, 0), axis=1, keepdims=True)
        dest[m] = dev_c * BLK + m * CAP + rank_c
        select = one_hot(iota((GOT, count), 0) == dev_r * BLK + m * CAP + rank_r)
        packed = packed + dot(select, enc[m])
        number = cell_r - dev_r * slot - band[0] * CELLS + 1
        to_dev = jnp.where(iota((SRC, count), 0) == dev_r, number.astype(F32), 0.0).astype(BF16)
        to_lane = one_hot(iota((count, 128), 1) == m * CAP + rank_c)
        places = places + dot(to_dev, to_lane)
    spread = one_hot(iota((GOT, SRC), 0) == iota((GOT, SRC), 1) * BLK + (BLK - 4))
    out[:, :128] = (packed[:, :128] + dot(spread, places.astype(BF16))).astype(BF16)
    out[:, 128:] = packed[:, 128:].astype(BF16)


def norm_parts(values):
    center = values - jnp.mean(values, -1, keepdims=True)
    inverse = lax.rsqrt(jnp.mean(center * center, -1, keepdims=True) + EPS)
    return center * inverse, inverse


def norm_back(grad, normal, inverse, gain):
    scaled = grad * gain
    return inverse * (
        scaled
        - jnp.mean(scaled, -1, keepdims=True)
        - normal * jnp.mean(scaled * normal, -1, keepdims=True)
    )


def enter_kernel(
    idx_r, idx_c, got, table, embed_w, qkv_w, vecs, qkv_b,
    hidden_o, normed_o, mixed_o, filled_o, seen_o, cell_o, low_o, high_o,
):
    hit = one_hot(iota((SRC, GOT), 1) == iota((SRC, GOT), 0) * BLK + (BLK - 4))
    numbers = dot(hit, got[:, :128]).astype(BF16)
    spread_r = dot(numbers, one_hot(iota((SRC, GOT), 0) == idx_r[0:1, :]), TN)
    value_r = jnp.sum(
        jnp.where(iota((128, GOT), 0) == idx_r[1:2, :], spread_r, 0.0), axis=0, keepdims=True
    )
    cell_r = jnp.where(
        value_r > 0.5, idx_r[2:3, :] * CELLS + value_r.astype(jnp.int32) - 1, -1
    )
    spread_c = dot(one_hot(iota((GOT, SRC), 1) == idx_c[:, 0:1]), numbers)
    value_c = jnp.sum(
        jnp.where(iota((GOT, 128), 1) == idx_c[:, 1:2], spread_c, 0.0), axis=1, keepdims=True
    )
    cell_o[...] = jnp.where(
        value_c > 0.5, idx_c[:, 2:3] * CELLS + value_c.astype(jnp.int32) - 1, -1
    )
    for m in range(MICRO):
        rows = slice(m * CELLS, (m + 1) * CELLS)
        match = jnp.where(iota((CELLS, GOT), 0) + m * CELLS == cell_r, 1.0, 0.0)
        seen = jnp.sum(match, axis=1, keepdims=True)
        filled = dot(match.astype(BF16), got[...]).astype(BF16)
        filled_o[rows, :] = filled
        seen_o[rows, :] = seen
        proj = (dot(filled, embed_w[...]) + vecs[0:1, :]).astype(BF16).astype(F32)
        hidden = jnp.where(seen > 0.5, proj, vecs[1:2, :]) + table[rows, :]
        hidden_o[rows, :] = hidden
        normal, unused = norm_parts(hidden)
        normed = (normal * vecs[2:3, :] + vecs[3:4, :]).astype(BF16)
        normed_o[rows, :] = normed
        mixed = (dot(normed, qkv_w[...]) + qkv_b[...]).astype(BF16)
        mixed_o[rows, :] = mixed
        low_o[m] = mixed[:16, D:]
        high_o[m] = mixed[CELLS - 16 :, D:]


def head_rows(block, heads):
    return jnp.concatenate([block * heads[h : h + 1, :] for h in range(4)], axis=0)


def own_head(full, lane_head):
    out = full[0:32, :]
    for h in range(1, 4):
        out = jnp.where(lane_head == h, full[32 * h : 32 * h + 32, :], out)
    return out


def window_loop(edge, inner):
    def inside(p, carry):
        places = []
        for m in range(MICRO):
            base = pl.multiple_of(m * CELLS + 32 * p - 16, 16)
            places.append((m * 7 + p, pl.ds(base, 32)))
        inner(places)
        return carry

    def ends(i, carry):
        places = []
        for j in range(2):
            m = 2 * i + j
            first = pl.multiple_of(m * CELLS, 16)
            last = pl.multiple_of(m * CELLS + CELLS - 16, 16)
            places.append((m, m * 7, pl.ds(first, 16), 0))
            places.append((m, m * 7 + 6, pl.ds(last, 16), 1))
        edge(places)
        return carry

    lax.fori_loop(1, 6, inside, 0)
    lax.fori_loop(0, MICRO // 2, ends, 0)


def with_halo(own, halo, side):
    return jnp.concatenate([own, halo] if side else [halo, own], axis=0)


COLS = [[slice(D * i + 128 * g, D * i + 128 * g + 128) for i in range(3)] for g in range(4)]


def load_inner(mixed, places, grads=None):
    items = []
    for w, rows in places:
        for g in range(4):
            item = [mixed[rows, c] for c in COLS[g]]
            items.append((w, g, *item, None if grads is None else grads[rows, COLS[g][0]]))
    return items


def load_edge(mixed, low, high, places, grads=None):
    zero = jnp.zeros((16, 128), BF16)
    items = []
    for m, w, rows, side in places:
        halo = high if side else low
        for g in range(4):
            cols = COLS[g]
            q = with_halo(mixed[rows, cols[0]], zero, side)
            k = with_halo(mixed[rows, cols[1]], halo[m, :, cols[0]], side)
            v = with_halo(mixed[rows, cols[2]], halo[m, :, cols[1]], side)
            grad = None if grads is None else with_halo(grads[rows, cols[0]], zero, side)
            items.append((w, g, q, k, v, grad))
    return items


def attend_kernel(mixed, low, high, mask, heads_i, attended_o, probs_o):
    heads = heads_i[...]
    lane_head = iota((32, 128), 1) // 32

    def windows(items):
        scores = [dot(k, head_rows(q, heads), NT) * SCALE for w, g, q, k, v, _ in items]
        probs = []
        for (w, g, *_), score in zip(items, scores):
            score = jnp.where(mask[w] > 0.5, score, -1e30)
            grown = jnp.exp(score - jnp.max(score, axis=0, keepdims=True))
            one = grown * (1.0 / jnp.sum(grown, axis=0, keepdims=True))
            probs_o[w, :, 128 * g : 128 * g + 128] = one
            probs.append(one.astype(BF16))
        full = [dot(one, item[4], TN) for item, one in zip(items, probs)]
        return [own_head(one, lane_head).astype(BF16) for one in full]

    def inner(places):
        outs = windows(load_inner(mixed, places))
        for i, (w, rows) in enumerate(places):
            for g in range(4):
                attended_o[rows, COLS[g][0]] = outs[4 * i + g]

    def edge(places):
        outs = windows(load_edge(mixed, low, high, places))
        for i, (m, w, rows, side) in enumerate(places):
            for g in range(4):
                out = outs[4 * i + g]
                attended_o[rows, COLS[g][0]] = out[:16] if side else out[16:]

    window_loop(edge, inner)


def gelu_parts(x):
    size = jnp.abs(x) * (0.5**0.5)
    bell = jnp.exp(-0.5 * x * x)
    t = 1.0 / (1.0 + 0.3275911 * size)
    poly = t * (
        0.254829592
        + t * (-0.284496736 + t * (1.421413741 + t * (-1.453152027 + t * 1.061405429)))
    )
    tail = 0.5 * poly * bell
    share = jnp.where(x >= 0, 1.0 - tail, tail)
    return x * share, share + x * bell * 0.3989422804014327


def before_kernel(cot, down_w, g_act_o):
    for f in range(4):
        cols = slice(512 * f, 512 * f + 512)
        g_act_o[:, cols] = dot(cot[...], down_w[cols, :], NT)


def mlp_kernel(
    core, hidden, attended, cot, g_act, out_w, up_w, vecs, up_b,
    middle_o, act_o, gexp_o, keep_o, send_o, n2_s, n2t_s,
):
    tile = 256
    blocks = [slice(512 * f, 512 * f + 512) for f in range(4)]

    def forward(i, carry):
        rows = pl.ds(pl.multiple_of(i * tile, tile), tile)
        middle = hidden[rows, :] + dot(attended[rows, :], out_w[...]) + vecs[0:1, :]
        middle_o[rows, :] = middle
        normal, unused = norm_parts(middle)
        normed = (normal * vecs[1:2, :] + vecs[2:3, :]).astype(BF16)
        n2_s[rows, :] = normed
        expand = [dot(normed, up_w[:, cols]) for cols in blocks]
        for cols, one in zip(blocks, expand):
            value, slope = gelu_parts(one + up_b[0:1, cols])
            act_o[rows, cols] = value.astype(BF16)
            gexp_o[rows, cols] = (g_act[rows, cols] * slope).astype(BF16)
        return carry

    lax.fori_loop(0, ALL // tile, forward, 0)
    n2t_s[...] = jnp.transpose(n2_s[...])
    for grads_o, half in ((keep_o, core[0]), (send_o, 1 - core[0])):
        for b in range(2):
            cols = pl.ds(pl.multiple_of(half * 1024 + 512 * b, 512), 512)
            rows = slice(512 * b, 512 * b + 512)
            grads_o[rows, :] = dot(act_o[:, cols], cot[...], TN).astype(BF16)
            rows = slice(1024 + 512 * b, 1536 + 512 * b)
            grads_o[rows, :] = dot(n2t_s[...], gexp_o[:, cols]).astype(BF16)


def mlp_back_kernel(
    middle_i, attended, cot, act, gexp, out_w, up_w, down_w, vecs,
    output_o, gmid_o, gatt_o, gout_o, sums_o, gb_s,
):
    tile = 256
    sums_o[...] = jnp.zeros((8, D), F32)

    def step(i, carry):
        rows = pl.ds(pl.multiple_of(i * tile, tile), tile)
        middle = middle_i[rows, :]
        grad = dot(gexp[rows, :], up_w[...], NT)
        output_o[rows, :] = (middle + vecs[3:4, :] + dot(act[rows, :], down_w[...])).astype(BF16)
        normal, inverse = norm_parts(middle)
        g_float = cot[rows, :].astype(F32)
        g_mid = g_float + norm_back(grad, normal, inverse, vecs[1:2, :])
        gmid_o[rows, :] = g_mid
        g_low = g_mid.astype(BF16)
        gb_s[rows, :] = g_low
        gatt_o[rows, :] = dot(g_low, out_w[...], NT).astype(BF16)
        sums_o[0:1, :] += jnp.sum(g_low.astype(F32), axis=0, keepdims=True)
        sums_o[1:2, :] += jnp.sum(grad * normal, axis=0, keepdims=True)
        sums_o[2:3, :] += jnp.sum(grad, axis=0, keepdims=True)
        sums_o[3:4, :] += jnp.sum(g_float, axis=0, keepdims=True)
        for f in range(4):
            part = gexp[rows, 512 * f : 512 * f + 512].astype(F32)
            sums_o[4 + f : 5 + f, :] += jnp.sum(part, axis=0, keepdims=True)
        return carry

    lax.fori_loop(0, ALL // tile, step, 0)
    gout_o[...] = dot(attended[...], gb_s[...], TN).astype(BF16)


def attend_back_kernel(
    mixed, low, high, probs_i, gatt, heads_i, gmixed_o, low_o, high_o, rim_o
):
    heads = heads_i[...]
    lane_head = iota((32, 128), 1) // 32

    def windows(items):
        q_m = [head_rows(q, heads) for w, g, q, k, v, grad in items]
        g_m = [head_rows(grad, heads) for w, g, q, k, v, grad in items]
        g_probs = [dot(item[4], one, NT) for item, one in zip(items, g_m)]
        low_probs, g_scores = [], []
        for (w, g, *_), g_prob in zip(items, g_probs):
            probs = probs_i[w, :, 128 * g : 128 * g + 128]
            inner = jnp.sum(probs * g_prob, axis=0, keepdims=True)
            g_scores.append((probs * (g_prob - inner)).astype(BF16))
            low_probs.append(probs.astype(BF16))
        d_value = [dot(one, grad) for one, grad in zip(low_probs, g_m)]
        d_key = [dot(one, q) * SCALE for one, q in zip(g_scores, q_m)]
        full = [dot(one, item[3], TN) for item, one in zip(items, g_scores)]
        d_query = [(own_head(one, lane_head) * SCALE).astype(BF16) for one in full]
        return list(zip(d_query, d_key, d_value))

    def inner(places):
        outs = windows(load_inner(mixed, places, gatt))
        for i, (w, rows) in enumerate(places):
            for g in range(4):
                for col, value in zip(COLS[g], outs[4 * i + g]):
                    gmixed_o[rows, col] = value.astype(BF16)

    def edge(places):
        outs = windows(load_edge(mixed, low, high, places, gatt))
        for i, (m, w, rows, side) in enumerate(places):
            out = high_o if side else low_o
            own, far = (slice(0, 16), slice(16, 32)) if side else (slice(16, 32), slice(0, 16))
            for g in range(4):
                cols = COLS[g]
                d_query, d_key, d_value = outs[4 * i + g]
                gmixed_o[rows, cols[0]] = d_query[own]
                rim_o[m, side, :, cols[0]] = d_key[own]
                rim_o[m, side, :, cols[1]] = d_value[own]
                out[m, :, cols[0]] = d_key[far].astype(BF16)
                out[m, :, cols[1]] = d_value[far].astype(BF16)

    window_loop(edge, inner)
    for m in range(MICRO):
        for base in (m * CELLS, m * CELLS + CELLS - 16):
            gmixed_o[base : base + 16, D:] = jnp.zeros((16, 2 * D), BF16)


def leave_kernel(
    core, gmixed, from_low, from_high, rim, hidden, normed, filled, seen, cell, gmid, qkv_w, vecs,
    gout, sums, keep_o, send_o, ret_o, gm_s, gf_s, nt_s, ft_s,
):
    small = jnp.zeros((1, D), F32)
    gain_sum, shift_sum, mask_sum, embed_sum, query_sum, value_sum = [small] * 6
    for m in range(MICRO):
        base = m * CELLS
        rows = slice(base, base + CELLS)
        gm_s[rows, :] = gmixed[rows, :]
        gm_s[base : base + 16, D:] = (rim[m, 0] + from_low[m].astype(F32)).astype(BF16)
        gm_s[base + CELLS - 16 : base + CELLS, D:] = (rim[m, 1] + from_high[m].astype(F32)).astype(
            BF16
        )
        gm = gm_s[rows, :]
        grad = dot(gm, qkv_w[...], NT)
        normal, inverse = norm_parts(hidden[rows, :])
        g_hidden = gmid[rows, :] + norm_back(grad, normal, inverse, vecs[2:3, :])
        there = seen[rows, :] > 0.5
        g_low = g_hidden.astype(BF16)
        gf_s[rows, :] = g_low
        gain_sum += jnp.sum(grad * normal, axis=0, keepdims=True)
        shift_sum += jnp.sum(grad, axis=0, keepdims=True)
        mask_sum += jnp.sum(jnp.where(there, 0.0, g_hidden), axis=0, keepdims=True)
        embed_sum += jnp.sum(jnp.where(there, g_low.astype(F32), 0.0), axis=0, keepdims=True)
        query_sum += jnp.sum(gm[:, :D].astype(F32), axis=0, keepdims=True)
        value_sum += jnp.sum(gm[:, 2 * D :].astype(F32), axis=0, keepdims=True)
    nt_s[...] = jnp.transpose(normed[...])
    ft_s[...] = jnp.transpose(filled[...])
    ret_o[...] = dot(one_hot(iota((GOT, ALL), 1) == cell[...]), gf_s[...]).astype(BF16)


    def write(first, second):
        def weights(b, carry):
            cols = pl.ds(pl.multiple_of(b * 512, 512), 512)
            first[cols, :] = dot(nt_s[...], gm_s[:, cols]).astype(BF16)
            return carry

        lax.fori_loop(0, 3, weights, 0)
        second[0:512, :] = gout[...]
        second[512:1280, :] = dot(ft_s[...], gf_s[...]).astype(BF16)
        second[1280:1296, :] = jnp.concatenate(
            [
                embed_sum, mask_sum, gain_sum, shift_sum, query_sum, value_sum,
                small, small, sums[...],
            ],
            axis=0,
        ).astype(BF16)
        second[1296:1536, :] = jnp.zeros((240, D), BF16)

    @pl.when(core[0] == 0)
    def _():
        write(keep_o, send_o)

    @pl.when(core[0] != 0)
    def _():
        write(send_o, keep_o)


def return_kernel(dest, came, embed_w, out):
    for m in range(MICRO):
        select = one_hot(iota((dest.shape[1], GOT), 1) == dest[m])
        g_proj = dot(select, came[...]).astype(BF16)
        out[m] = dot(g_proj, embed_w[...], NT).astype(BF16)


def unpack_one_kernel(down_i, up_i, down_o, up_o):
    down_o[...] = down_i[...].reshape(512, D).astype(F32)
    up_o[...] = up_i[...].reshape(512, D).astype(F32)


def unpack_one(gathered):
    block = (16, 1, 32, D)
    return pl.pallas_call(
        unpack_one_kernel,
        name="unpack_one",
        grid=(4,),
        out_shape=[jax.ShapeDtypeStruct((FF, D), F32), jax.ShapeDtypeStruct((D, FF), F32)],
        in_specs=[
            pl.BlockSpec(block, lambda i: (i % 2, i // 2, 0, 0)),
            pl.BlockSpec(block, lambda i: (2 + i % 2, i // 2, 0, 0)),
        ],
        out_specs=[
            pl.BlockSpec((512, D), lambda i: (i, 0)),
            pl.BlockSpec((512, D), lambda i: (0, i)),
        ],
        compiler_params=pltpu.CompilerParams(vmem_limit_bytes=16 * 2**20),
        cost_estimate=pl.CostEstimate(flops=0, bytes_accessed=12 * 2**20, transcendentals=0),
    )(gathered, gathered)


def unpack_two_kernel(core, mine, other, qkv_o, embed_o, out_o, small_o):
    def write(first, second):
        for b in range(3):
            qkv_o[:, 512 * b : 512 * b + 512] = first[512 * b : 512 * b + 512, :].astype(F32)
        out_o[...] = second[0:512, :].astype(F32)
        embed_o[...] = second[512:1280, :].astype(F32)
        small_o[...] = second[1280:1296, :].astype(F32)

    @pl.when(core[0] == 0)
    def _():
        write(mine, other)

    @pl.when(core[0] != 0)
    def _():
        write(other, mine)


def clip_ident(lengths, rows):
    first = lengths[:, 0:1]
    second = first + lengths[:, 1:2]
    ident = (rows[None, :] >= first).astype(jnp.int32) + (rows[None, :] >= second).astype(jnp.int32)
    start = jnp.where(ident >= 1, first, 0) + jnp.where(ident >= 2, lengths[:, 1:2], 0)
    inside = (rows >= 0) & (rows < LONG)
    return (jnp.where(inside[None, :], ident, -1), rows[None, :] - start)


def position_table(row_in_clip, width):
    quarter = width // 4
    omega = 1.0 / 10000.0 ** (jnp.arange(quarter, dtype=jnp.float32) / quarter)
    row_angle = row_in_clip.astype(jnp.float32)[..., None] * omega
    freq_angle = jnp.arange(FREQ, dtype=jnp.float32)[:, None] * omega
    row_part = jnp.concatenate([jnp.sin(row_angle), jnp.cos(row_angle)], -1)
    freq_part = jnp.concatenate([jnp.sin(freq_angle), jnp.cos(freq_angle)], -1)
    shape = row_in_clip.shape + (FREQ, width // 2)
    return jnp.concatenate(
        [jnp.broadcast_to(row_part[..., None, :], shape), jnp.broadcast_to(freq_part, shape)], -1
    )


def window_mask(ident):
    cells = jnp.repeat(ident.reshape(MICRO * 7, 4), FREQ, axis=1)
    freq = np.tile((np.arange(FREQ) + 2) % 8 // 4, 4)
    same = (cells[:, :, None] == cells[:, None, :]) & (cells[:, :, None] >= 0)
    same = same & jnp.asarray(freq[:, None] == freq[None, :])[None]
    return jnp.tile(same.astype(F32), (1, 1, 4))


def on_device(
    encoded, visible_pos, clip_len, cotangent, embed_weight, embed_bias, mask_token, attn_gain,
    attn_shift, qkv_weight, query_bias, value_bias, out_weight, out_bias, mlp_gain, mlp_shift,
    up_weight, up_bias, down_weight, down_bias,
):
    both = ("clip", "band")
    groups = lax.axis_size("clip")
    bands = lax.axis_size("band")
    band = lax.axis_index("band")
    side = band % 2
    core = side.astype(jnp.int32).reshape(1)
    halves = [
        [c * bands + 2 * x + k for c in range(groups) for x in range(bands // 2)] for k in range(2)
    ]
    swap = [(i, i ^ 1) for i in range(bands)]
    forward = [(i, i + 1) for i in range(bands - 1)]
    backward = [(b, a) for a, b in forward]
    chips = groups * bands // 2

    def to_all(block):
        return lax.all_to_all(
            block, both, split_axis=0, concat_axis=0, tiled=True, axis_index_groups=halves
        )

    def chip_sum(keep, send):
        other = lax.ppermute(send, "band", swap)
        mine = (keep.astype(F32) + other.astype(F32)).astype(BF16)
        return mine.reshape(chips, -1, D)

    def total(parts):
        return jnp.sum(parts.astype(F32), 0).astype(BF16)

    vis = visible_pos.shape[1]
    packed, dest = call(
        pack_kernel, "pack", [((GOT, ENC), BF16), ((MICRO, vis, 1), jnp.int32)],
        (band.astype(jnp.int32).reshape(1), visible_pos, encoded), smem=1,
        flops=GOT * MICRO * vis * ENC * 2,
    )
    cot = cotangent.reshape(ALL, D)
    (g_act,) = call(
        before_kernel, "before", [((ALL, FF), F32)], (cot, down_weight), flops=2 * ALL * D * FF,
    )
    got = lax.all_to_all(
        packed.reshape(SRC, BLK, ENC), "clip", split_axis=0, concat_axis=0, tiled=True
    ).reshape(GOT, ENC)

    place = np.arange(GOT)
    within = place % BLK
    index = np.zeros((8, GOT), np.int32)
    index[0], index[1], index[2] = place // BLK, within, np.where(within < 36, within // CAP, 99)
    heads = jnp.asarray(np.arange(128)[None, :] // 32 == np.arange(16)[:, None] % 4, BF16)

    unused, row_in_clip = clip_ident(clip_len[:, 0], band * ROWS + jnp.arange(ROWS))
    table = position_table(row_in_clip, D).reshape(ALL, D)
    ident_ext, unused = clip_ident(clip_len[:, 0], band * ROWS - 2 + jnp.arange(ROWS + 4))
    mask = window_mask(ident_ext)
    zero = jnp.zeros((D,), BF16)
    vecs_one = jnp.stack([embed_bias, mask_token, attn_gain, attn_shift] * 2).astype(F32)
    vecs_two = jnp.stack([out_bias, mlp_gain, mlp_shift, down_bias] * 2).astype(F32)
    qkv_b = jnp.concatenate([query_bias, zero, value_bias]).astype(F32)[None]
    up_b = up_bias.astype(F32)[None]

    hidden, normed, mixed, filled, seen, cell, low, high = call(
        enter_kernel, "enter",
        [
            ((ALL, D), F32), ((ALL, D), BF16), ((ALL, 3 * D), BF16), ((ALL, ENC), BF16),
            ((ALL, 1), F32), ((GOT, 1), jnp.int32),
            ((MICRO, 16, 2 * D), BF16), ((MICRO, 16, 2 * D), BF16),
        ],
        (
            jnp.asarray(index), jnp.asarray(np.ascontiguousarray(index.T)), got, table,
            embed_weight, qkv_weight, vecs_one, qkv_b,
        ),
        flops=2 * ALL * (GOT * ENC + ENC * D + 3 * D * D),
    )
    from_low = lax.ppermute(high, "band", forward)
    from_high = lax.ppermute(low, "band", backward)
    attended, probs = call(
        attend_kernel, "attend",
        [((ALL, D), BF16), ((MICRO * 7, 32, D), F32)],
        (mixed, from_low, from_high, mask, heads),
        flops=MICRO * 7 * 4 * 2**20,
    )
    middle, act, gexp, keep, send = call(
        mlp_kernel, "mlp",
        [
            ((ALL, D), F32), ((ALL, FF), BF16), ((ALL, FF), BF16), ((FF, D), BF16), ((FF, D), BF16),
        ],
        (core, hidden, attended, cot, g_act, out_weight, up_weight, vecs_two, up_b),
        scratch=[pltpu.VMEM((ALL, D), BF16), pltpu.VMEM((D, ALL), BF16)],
        smem=1, flops=2 * ALL * (3 * D * FF + D * D), vmem=24,
    )
    chip_one = chip_sum(keep, send)
    act, chip_one = lax.optimization_barrier((act, chip_one))
    output, gmid, gatt, gout, sums = call(
        mlp_back_kernel, "mlp_back",
        [
            ((ALL, D), BF16), ((ALL, D), F32), ((ALL, D), BF16), ((D, D), BF16), ((8, D), F32),
        ],
        (middle, attended, cot, act, gexp, out_weight, up_weight, down_weight, vecs_two),
        scratch=[pltpu.VMEM((ALL, D), BF16)],
        flops=2 * ALL * (2 * D * FF + 2 * D * D), vmem=24,
    )
    parts_one = to_all(chip_one)
    gmixed, low, high, rim = call(
        attend_back_kernel, "attend_back",
        [
            ((ALL, 3 * D), BF16), ((MICRO, 16, 2 * D), BF16), ((MICRO, 16, 2 * D), BF16),
            ((MICRO, 2, 16, 2 * D), F32),
        ],
        (mixed, from_low, from_high, probs, gatt, heads),
        flops=MICRO * 7 * 4 * 2**22,
    )
    from_low = lax.ppermute(high, "band", forward)
    from_high = lax.ppermute(low, "band", backward)
    keep, send, returned = call(
        leave_kernel, "leave",
        [((3 * D, D), BF16), ((3 * D, D), BF16), ((GOT, D), BF16)],
        (
            core, gmixed, from_low, from_high, rim, hidden, normed, filled, seen, cell, gmid,
            qkv_weight, vecs_one, gout, sums,
        ),
        scratch=[
            pltpu.VMEM((ALL, 3 * D), BF16), pltpu.VMEM((ALL, D), BF16),
            pltpu.VMEM((D, ALL), BF16), pltpu.VMEM((ENC, ALL), BF16),
        ],
        smem=1, flops=2 * ALL * (6 * D * D + GOT * D + ENC * D),
    )
    parts_one, chip_two = lax.optimization_barrier((parts_one, chip_sum(keep, send)))
    total_one = lax.all_gather(total(parts_one), both, axis=0).reshape(chips, 2, -1, D)
    mine = total(to_all(chip_two))
    mine = to_all(jnp.broadcast_to(mine[None], (chips,) + mine.shape)).reshape(-1, D)
    mine, returned = lax.optimization_barrier((mine, returned))
    other = lax.ppermute(mine, "band", swap)
    qkv, g_embed, g_out, small = call(
        unpack_two_kernel, "unpack_two",
        [((D, 3 * D), F32), ((ENC, D), F32), ((D, D), F32), ((16, D), F32)],
        (core, mine, other), smem=1,
    )
    came = lax.all_to_all(
        returned.reshape(SRC, BLK, D), "clip", split_axis=0, concat_axis=0, tiled=True
    ).reshape(GOT, D)
    (grad_enc,) = call(
        return_kernel, "return", [((MICRO, vis, ENC), BF16)], (dest, came, embed_weight),
        flops=2 * MICRO * vis * D * (GOT + ENC),
    )
    down, up = unpack_one(total_one)
    return (
        output.reshape(cotangent.shape), grad_enc, g_embed, small[0], small[1], small[2],
        small[3], qkv, small[4], small[5], g_out, small[8], small[9], small[10], up,
        small[12:16].reshape(FF), down, small[11],
    )


def solution(mesh):
    whole = P()
    return jax.shard_map(
        on_device,
        mesh=mesh,
        in_specs=(
            P(None, ("clip", "band"), None),
            P(None, ("clip", "band")),
            P(None, "clip", None),
            P(None, "clip", "band", None, None),
        )
        + (whole,) * 16,
        out_specs=(P(None, "clip", "band", None, None), P(None, ("clip", "band"), None))
        + (whole,) * 16,
        check_vma=False,
    )
```

```python
import jax
import jax.numpy as jnp
import numpy as np
from jax import lax
from jax.experimental import pallas as pl
from jax.experimental.pallas import tpu as pltpu
from jax.sharding import PartitionSpec as P

HEADS = 16
FREQ = 8
LONG = 192
MICRO = 4
ROWS = 24
CELLS = ROWS * FREQ
ALL = MICRO * CELLS
CAP = 9
BLK = 40
SRC = 16
GOT = SRC * BLK
D = 512
FF = 2048
ENC = 768
EPS = 1e-06
SCALE = (D // HEADS) ** (-0.5)
F32 = jnp.float32
BF16 = jnp.bfloat16

NN = (((1,), (0,)), ((), ()))
NT = (((1,), (1,)), ((), ()))
TN = (((0,), (0,)), ((), ()))


def dot(left, right, dims=NN):
    return lax.dot_general(left, right, dims, preferred_element_type=F32)


def iota(shape, dim):
    return lax.broadcasted_iota(jnp.int32, shape, dim)


def one_hot(hit):
    return jnp.where(hit, 1.0, 0.0).astype(BF16)


def call(kernel, name, out_shape, args, scratch=(), smem=0, flops=0, vmem=16):
    specs = [pl.BlockSpec(memory_space=pltpu.SMEM)] * smem
    specs += [pl.BlockSpec(memory_space=pltpu.VMEM)] * (len(args) - smem)
    outs = [jax.ShapeDtypeStruct(shape, dtype) for shape, dtype in out_shape]
    size = sum(a.size * a.dtype.itemsize for a in args) + sum(
        o.size * o.dtype.itemsize for o in outs
    )
    return pl.pallas_call(
        kernel,
        name=name,
        out_shape=outs,
        in_specs=specs,
        out_specs=[pl.BlockSpec(memory_space=pltpu.VMEM)] * len(outs),
        scratch_shapes=list(scratch),
        compiler_params=pltpu.CompilerParams(vmem_limit_bytes=vmem * 2**20),
        cost_estimate=pl.CostEstimate(flops=flops, bytes_accessed=size, transcendentals=0),
    )(*args)


def pack_kernel(band, pos, enc, out, dest):
    count = pos.shape[1]
    low = iota((count, count), 0)
    high = iota((count, count), 1)
    packed = jnp.zeros((GOT, ENC), F32)
    places = jnp.zeros((SRC, 128), F32)
    for m in range(MICRO):
        cell_r = pos[m : m + 1, :]
        cell_c = jnp.sum(jnp.where(low == high, cell_r, 0), axis=1, keepdims=True)
        slot = LONG * FREQ
        dev_r = jnp.sum(
            jnp.where(cell_r >= slot * iota((SRC, count), 0) + slot, 1, 0), axis=0, keepdims=True
        )
        dev_c = jnp.sum(
            jnp.where(cell_c >= slot * iota((count, SRC), 1) + slot, 1, 0), axis=1, keepdims=True
        )
        same = dev_c == dev_r
        rank_r = jnp.sum(jnp.where(same & (low < high), 1, 0), axis=0, keepdims=True)
        rank_c = jnp.sum(jnp.where(same & (high < low), 1, 0), axis=1, keepdims=True)
        dest[m] = dev_c * BLK + m * CAP + rank_c
        select = one_hot(iota((GOT, count), 0) == dev_r * BLK + m * CAP + rank_r)
        packed = packed + dot(select, enc[m])
        number = cell_r - dev_r * slot - band[0] * CELLS + 1
        to_dev = jnp.where(iota((SRC, count), 0) == dev_r, number.astype(F32), 0.0).astype(BF16)
        to_lane = one_hot(iota((count, 128), 1) == m * CAP + rank_c)
        places = places + dot(to_dev, to_lane)
    spread = one_hot(iota((GOT, SRC), 0) == iota((GOT, SRC), 1) * BLK + (BLK - 4))
    out[:, :128] = (packed[:, :128] + dot(spread, places.astype(BF16))).astype(BF16)
    out[:, 128:] = packed[:, 128:].astype(BF16)


def norm_parts(values):
    center = values - jnp.mean(values, -1, keepdims=True)
    inverse = lax.rsqrt(jnp.mean(center * center, -1, keepdims=True) + EPS)
    return center * inverse, inverse


def norm_back(grad, normal, inverse, gain):
    scaled = grad * gain
    return inverse * (
        scaled
        - jnp.mean(scaled, -1, keepdims=True)
        - normal * jnp.mean(scaled * normal, -1, keepdims=True)
    )


def enter_kernel(
    idx_r, idx_c, got, table, embed_w, qkv_w, vecs, qkv_b,
    hidden_o, normed_o, mixed_o, filled_o, seen_o, cell_o, low_o, high_o,
):
    hit = one_hot(iota((SRC, GOT), 1) == iota((SRC, GOT), 0) * BLK + (BLK - 4))
    numbers = dot(hit, got[:, :128]).astype(BF16)
    spread_r = dot(numbers, one_hot(iota((SRC, GOT), 0) == idx_r[0:1, :]), TN)
    value_r = jnp.sum(
        jnp.where(iota((128, GOT), 0) == idx_r[1:2, :], spread_r, 0.0), axis=0, keepdims=True
    )
    cell_r = jnp.where(
        value_r > 0.5, idx_r[2:3, :] * CELLS + value_r.astype(jnp.int32) - 1, -1
    )
    spread_c = dot(one_hot(iota((GOT, SRC), 1) == idx_c[:, 0:1]), numbers)
    value_c = jnp.sum(
        jnp.where(iota((GOT, 128), 1) == idx_c[:, 1:2], spread_c, 0.0), axis=1, keepdims=True
    )
    cell_o[...] = jnp.where(
        value_c > 0.5, idx_c[:, 2:3] * CELLS + value_c.astype(jnp.int32) - 1, -1
    )
    for m in range(MICRO):
        rows = slice(m * CELLS, (m + 1) * CELLS)
        match = jnp.where(iota((CELLS, GOT), 0) + m * CELLS == cell_r, 1.0, 0.0)
        seen = jnp.sum(match, axis=1, keepdims=True)
        filled = dot(match.astype(BF16), got[...]).astype(BF16)
        filled_o[rows, :] = filled
        seen_o[rows, :] = seen
        proj = (dot(filled, embed_w[...]) + vecs[0:1, :]).astype(BF16).astype(F32)
        hidden = jnp.where(seen > 0.5, proj, vecs[1:2, :]) + table[rows, :]
        hidden_o[rows, :] = hidden
        normal, unused = norm_parts(hidden)
        normed = (normal * vecs[2:3, :] + vecs[3:4, :]).astype(BF16)
        normed_o[rows, :] = normed
        mixed = (dot(normed, qkv_w[...]) + qkv_b[...]).astype(BF16)
        mixed_o[rows, :] = mixed
        low_o[m] = mixed[:16, D:]
        high_o[m] = mixed[CELLS - 16 :, D:]


def head_rows(block, heads):
    return jnp.concatenate([block * heads[h : h + 1, :] for h in range(4)], axis=0)


def own_head(full, lane_head):
    out = full[0:32, :]
    for h in range(1, 4):
        out = jnp.where(lane_head == h, full[32 * h : 32 * h + 32, :], out)
    return out


def window_loop(edge, inner):
    def inside(p, carry):
        places = []
        for m in range(MICRO):
            base = pl.multiple_of(m * CELLS + 32 * p - 16, 16)
            places.append((m * 7 + p, pl.ds(base, 32)))
        inner(places)
        return carry

    def ends(i, carry):
        places = []
        for j in range(2):
            m = 2 * i + j
            first = pl.multiple_of(m * CELLS, 16)
            last = pl.multiple_of(m * CELLS + CELLS - 16, 16)
            places.append((m, m * 7, pl.ds(first, 16), 0))
            places.append((m, m * 7 + 6, pl.ds(last, 16), 1))
        edge(places)
        return carry

    lax.fori_loop(1, 6, inside, 0)
    lax.fori_loop(0, MICRO // 2, ends, 0)


def with_halo(own, halo, side):
    return jnp.concatenate([own, halo] if side else [halo, own], axis=0)


COLS = [[slice(D * i + 128 * g, D * i + 128 * g + 128) for i in range(3)] for g in range(4)]


def load_inner(mixed, places, grads=None):
    items = []
    for w, rows in places:
        for g in range(4):
            item = [mixed[rows, c] for c in COLS[g]]
            items.append((w, g, *item, None if grads is None else grads[rows, COLS[g][0]]))
    return items


def load_edge(mixed, low, high, places, grads=None):
    zero = jnp.zeros((16, 128), BF16)
    items = []
    for m, w, rows, side in places:
        halo = high if side else low
        for g in range(4):
            cols = COLS[g]
            q = with_halo(mixed[rows, cols[0]], zero, side)
            k = with_halo(mixed[rows, cols[1]], halo[m, :, cols[0]], side)
            v = with_halo(mixed[rows, cols[2]], halo[m, :, cols[1]], side)
            grad = None if grads is None else with_halo(grads[rows, cols[0]], zero, side)
            items.append((w, g, q, k, v, grad))
    return items


def attend_kernel(mixed, low, high, mask, heads_i, attended_o, probs_o):
    heads = heads_i[...]
    lane_head = iota((32, 128), 1) // 32

    def windows(items):
        scores = [dot(k, head_rows(q, heads), NT) * SCALE for w, g, q, k, v, _ in items]
        probs = []
        for (w, g, *_), score in zip(items, scores):
            score = jnp.where(mask[w] > 0.5, score, -1e30)
            grown = jnp.exp(score - jnp.max(score, axis=0, keepdims=True))
            one = grown * (1.0 / jnp.sum(grown, axis=0, keepdims=True))
            probs_o[w, :, 128 * g : 128 * g + 128] = one
            probs.append(one.astype(BF16))
        full = [dot(one, item[4], TN) for item, one in zip(items, probs)]
        return [own_head(one, lane_head).astype(BF16) for one in full]

    def inner(places):
        outs = windows(load_inner(mixed, places))
        for i, (w, rows) in enumerate(places):
            for g in range(4):
                attended_o[rows, COLS[g][0]] = outs[4 * i + g]

    def edge(places):
        outs = windows(load_edge(mixed, low, high, places))
        for i, (m, w, rows, side) in enumerate(places):
            for g in range(4):
                out = outs[4 * i + g]
                attended_o[rows, COLS[g][0]] = out[:16] if side else out[16:]

    window_loop(edge, inner)


def gelu_parts(x):
    size = jnp.abs(x) * (0.5**0.5)
    bell = jnp.exp(-0.5 * x * x)
    t = 1.0 / (1.0 + 0.3275911 * size)
    poly = t * (
        0.254829592
        + t * (-0.284496736 + t * (1.421413741 + t * (-1.453152027 + t * 1.061405429)))
    )
    tail = 0.5 * poly * bell
    share = jnp.where(x >= 0, 1.0 - tail, tail)
    return x * share, share + x * bell * 0.3989422804014327


def before_kernel(cot, down_w, g_act_o):
    for f in range(4):
        cols = slice(512 * f, 512 * f + 512)
        g_act_o[:, cols] = dot(cot[...], down_w[cols, :], NT)


def mlp_kernel(
    core, hidden, attended, cot, g_act, out_w, up_w, vecs, up_b,
    middle_o, act_o, gexp_o, n2t_o, send_o, n2_s,
):
    tile = 256
    blocks = [slice(512 * f, 512 * f + 512) for f in range(4)]

    def forward(i, carry):
        rows = pl.ds(pl.multiple_of(i * tile, tile), tile)
        middle = hidden[rows, :] + dot(attended[rows, :], out_w[...]) + vecs[0:1, :]
        middle_o[rows, :] = middle
        normal, unused = norm_parts(middle)
        normed = (normal * vecs[1:2, :] + vecs[2:3, :]).astype(BF16)
        n2_s[rows, :] = normed
        expand = [dot(normed, up_w[:, cols]) for cols in blocks]
        for cols, one in zip(blocks, expand):
            value, slope = gelu_parts(one + up_b[0:1, cols])
            act_o[rows, cols] = value.astype(BF16)
            gexp_o[rows, cols] = (g_act[rows, cols] * slope).astype(BF16)
        return carry

    lax.fori_loop(0, ALL // tile, forward, 0)
    n2t_o[...] = jnp.transpose(n2_s[...])
    weight_half(1 - core[0], send_o, act_o, gexp_o, n2t_o, cot)


def weight_half(half, out, act, gexp, n2t, cot):
    for b in range(2):
        cols = pl.ds(pl.multiple_of(half * 1024 + 512 * b, 512), 512)
        rows = slice(512 * b, 512 * b + 512)
        out[rows, :] = dot(act[:, cols], cot[...], TN).astype(BF16)
        rows = slice(1024 + 512 * b, 1536 + 512 * b)
        out[rows, :] = dot(n2t[...], gexp[:, cols]).astype(BF16)


def mlp_keep_kernel(core, act, gexp, n2t, cot, keep_o):
    weight_half(core[0], keep_o, act, gexp, n2t, cot)


def mlp_back_kernel(
    middle_i, attended, cot, act, gexp, out_w, up_w, down_w, vecs,
    output_o, gmid_o, gatt_o, gout_o, sums_o, gb_s,
):
    tile = 256
    sums_o[...] = jnp.zeros((8, D), F32)

    def step(i, carry):
        rows = pl.ds(pl.multiple_of(i * tile, tile), tile)
        middle = middle_i[rows, :]
        grad = dot(gexp[rows, :], up_w[...], NT)
        output_o[rows, :] = (middle + vecs[3:4, :] + dot(act[rows, :], down_w[...])).astype(BF16)
        normal, inverse = norm_parts(middle)
        g_float = cot[rows, :].astype(F32)
        g_mid = g_float + norm_back(grad, normal, inverse, vecs[1:2, :])
        gmid_o[rows, :] = g_mid
        g_low = g_mid.astype(BF16)
        gb_s[rows, :] = g_low
        gatt_o[rows, :] = dot(g_low, out_w[...], NT).astype(BF16)
        sums_o[0:1, :] += jnp.sum(g_low.astype(F32), axis=0, keepdims=True)
        sums_o[1:2, :] += jnp.sum(grad * normal, axis=0, keepdims=True)
        sums_o[2:3, :] += jnp.sum(grad, axis=0, keepdims=True)
        sums_o[3:4, :] += jnp.sum(g_float, axis=0, keepdims=True)
        for f in range(4):
            part = gexp[rows, 512 * f : 512 * f + 512].astype(F32)
            sums_o[4 + f : 5 + f, :] += jnp.sum(part, axis=0, keepdims=True)
        return carry

    lax.fori_loop(0, ALL // tile, step, 0)
    gout_o[...] = dot(attended[...], gb_s[...], TN).astype(BF16)


def attend_back_kernel(
    mixed, low, high, probs_i, gatt, heads_i, gmixed_o, low_o, high_o, rim_o
):
    heads = heads_i[...]
    lane_head = iota((32, 128), 1) // 32

    def windows(items):
        q_m = [head_rows(q, heads) for w, g, q, k, v, grad in items]
        g_m = [head_rows(grad, heads) for w, g, q, k, v, grad in items]
        g_probs = [dot(item[4], one, NT) for item, one in zip(items, g_m)]
        low_probs, g_scores = [], []
        for (w, g, *_), g_prob in zip(items, g_probs):
            probs = probs_i[w, :, 128 * g : 128 * g + 128]
            inner = jnp.sum(probs * g_prob, axis=0, keepdims=True)
            g_scores.append((probs * (g_prob - inner)).astype(BF16))
            low_probs.append(probs.astype(BF16))
        d_value = [dot(one, grad) for one, grad in zip(low_probs, g_m)]
        d_key = [dot(one, q) * SCALE for one, q in zip(g_scores, q_m)]
        full = [dot(one, item[3], TN) for item, one in zip(items, g_scores)]
        d_query = [(own_head(one, lane_head) * SCALE).astype(BF16) for one in full]
        return list(zip(d_query, d_key, d_value))

    def inner(places):
        outs = windows(load_inner(mixed, places, gatt))
        for i, (w, rows) in enumerate(places):
            for g in range(4):
                for col, value in zip(COLS[g], outs[4 * i + g]):
                    gmixed_o[rows, col] = value.astype(BF16)

    def edge(places):
        outs = windows(load_edge(mixed, low, high, places, gatt))
        for i, (m, w, rows, side) in enumerate(places):
            out = high_o if side else low_o
            own, far = (slice(0, 16), slice(16, 32)) if side else (slice(16, 32), slice(0, 16))
            for g in range(4):
                cols = COLS[g]
                d_query, d_key, d_value = outs[4 * i + g]
                gmixed_o[rows, cols[0]] = d_query[own]
                rim_o[m, side, :, cols[0]] = d_key[own]
                rim_o[m, side, :, cols[1]] = d_value[own]
                out[m, :, cols[0]] = d_key[far].astype(BF16)
                out[m, :, cols[1]] = d_value[far].astype(BF16)

    window_loop(edge, inner)
    for m in range(MICRO):
        for base in (m * CELLS, m * CELLS + CELLS - 16):
            gmixed_o[base : base + 16, D:] = jnp.zeros((16, 2 * D), BF16)


def leave_kernel(
    core, gmixed, from_low, from_high, rim, hidden, normed, filled, seen, gmid, qkv_w, vecs,
    gout, sums, gm_o, gf_o, small_o, send_o,
):
    small = jnp.zeros((1, D), F32)
    gain_sum, shift_sum, mask_sum, embed_sum, query_sum, value_sum = [small] * 6
    for m in range(MICRO):
        base = m * CELLS
        rows = slice(base, base + CELLS)
        gm_o[rows, :] = gmixed[rows, :]
        gm_o[base : base + 16, D:] = (rim[m, 0] + from_low[m].astype(F32)).astype(BF16)
        gm_o[base + CELLS - 16 : base + CELLS, D:] = (rim[m, 1] + from_high[m].astype(F32)).astype(
            BF16
        )
        gm = gm_o[rows, :]
        grad = dot(gm, qkv_w[...], NT)
        normal, inverse = norm_parts(hidden[rows, :])
        g_hidden = gmid[rows, :] + norm_back(grad, normal, inverse, vecs[2:3, :])
        there = seen[rows, :] > 0.5
        g_low = g_hidden.astype(BF16)
        gf_o[rows, :] = g_low
        gain_sum += jnp.sum(grad * normal, axis=0, keepdims=True)
        shift_sum += jnp.sum(grad, axis=0, keepdims=True)
        mask_sum += jnp.sum(jnp.where(there, 0.0, g_hidden), axis=0, keepdims=True)
        embed_sum += jnp.sum(jnp.where(there, g_low.astype(F32), 0.0), axis=0, keepdims=True)
        query_sum += jnp.sum(gm[:, :D].astype(F32), axis=0, keepdims=True)
        value_sum += jnp.sum(gm[:, 2 * D :].astype(F32), axis=0, keepdims=True)
    small_o[...] = jnp.concatenate(
        [
            embed_sum, mask_sum, gain_sum, shift_sum, query_sum, value_sum,
            small, small, sums[...],
        ],
        axis=0,
    )
    one_half(core[0] != 0, send_o, normed, filled, gm_o, gf_o, gout, small_o)


def one_half(first, out, normed, filled, gm, gf, gout, small):
    @pl.when(first)
    def _():
        turned = jnp.transpose(normed[...])
        for b in range(3):
            cols = slice(512 * b, 512 * b + 512)
            out[cols, :] = dot(turned, gm[:, cols]).astype(BF16)

    @pl.when(jnp.logical_not(first))
    def _():
        out[0:512, :] = gout[...]
        out[512:1280, :] = dot(jnp.transpose(filled[...]), gf[...]).astype(BF16)
        out[1280:1296, :] = small[...].astype(BF16)
        out[1296:1536, :] = jnp.zeros((240, D), BF16)


def leave_keep_kernel(core, gm, gf, small, normed, filled, gout, cell, keep_o, ret_o):
    one_half(core[0] == 0, keep_o, normed, filled, gm, gf, gout, small)
    ret_o[...] = dot(one_hot(iota((GOT, ALL), 1) == cell[...]), gf[...]).astype(BF16)


def return_kernel(dest, came, embed_w, out):
    for m in range(MICRO):
        select = one_hot(iota((dest.shape[1], GOT), 1) == dest[m])
        g_proj = dot(select, came[...]).astype(BF16)
        out[m] = dot(g_proj, embed_w[...], NT).astype(BF16)


def unpack_one_kernel(down_i, up_i, down_o, up_o):
    down_o[...] = down_i[...].reshape(512, D).astype(F32)
    up_o[...] = up_i[...].reshape(512, D).astype(F32)


def unpack_one(gathered):
    block = (16, 1, 32, D)
    return pl.pallas_call(
        unpack_one_kernel,
        name="unpack_one",
        grid=(4,),
        out_shape=[jax.ShapeDtypeStruct((FF, D), F32), jax.ShapeDtypeStruct((D, FF), F32)],
        in_specs=[
            pl.BlockSpec(block, lambda i: (i % 2, i // 2, 0, 0)),
            pl.BlockSpec(block, lambda i: (2 + i % 2, i // 2, 0, 0)),
        ],
        out_specs=[
            pl.BlockSpec((512, D), lambda i: (i, 0)),
            pl.BlockSpec((512, D), lambda i: (0, i)),
        ],
        compiler_params=pltpu.CompilerParams(vmem_limit_bytes=58 * 2**20),
        cost_estimate=pl.CostEstimate(flops=0, bytes_accessed=12 * 2**20, transcendentals=0),
    )(gathered, gathered)


def unpack_two_kernel(core, mine, other, qkv_o, embed_o, out_o, small_o):
    def write(first, second):
        for b in range(3):
            qkv_o[:, 512 * b : 512 * b + 512] = first[512 * b : 512 * b + 512, :].astype(F32)
        out_o[...] = second[0:512, :].astype(F32)
        embed_o[...] = second[512:1280, :].astype(F32)
        small_o[...] = second[1280:1296, :].astype(F32)

    @pl.when(core[0] == 0)
    def _():
        write(mine, other)

    @pl.when(core[0] != 0)
    def _():
        write(other, mine)


def clip_ident(lengths, rows):
    first = lengths[:, 0:1]
    second = first + lengths[:, 1:2]
    ident = (rows[None, :] >= first).astype(jnp.int32) + (rows[None, :] >= second).astype(jnp.int32)
    start = jnp.where(ident >= 1, first, 0) + jnp.where(ident >= 2, lengths[:, 1:2], 0)
    inside = (rows >= 0) & (rows < LONG)
    return (jnp.where(inside[None, :], ident, -1), rows[None, :] - start)


def position_table(row_in_clip, width):
    quarter = width // 4
    omega = 1.0 / 10000.0 ** (jnp.arange(quarter, dtype=jnp.float32) / quarter)
    row_angle = row_in_clip.astype(jnp.float32)[..., None] * omega
    freq_angle = jnp.arange(FREQ, dtype=jnp.float32)[:, None] * omega
    row_part = jnp.concatenate([jnp.sin(row_angle), jnp.cos(row_angle)], -1)
    freq_part = jnp.concatenate([jnp.sin(freq_angle), jnp.cos(freq_angle)], -1)
    shape = row_in_clip.shape + (FREQ, width // 2)
    return jnp.concatenate(
        [jnp.broadcast_to(row_part[..., None, :], shape), jnp.broadcast_to(freq_part, shape)], -1
    )


def window_mask(ident):
    cells = jnp.repeat(ident.reshape(MICRO * 7, 4), FREQ, axis=1)
    freq = np.tile((np.arange(FREQ) + 2) % 8 // 4, 4)
    same = (cells[:, :, None] == cells[:, None, :]) & (cells[:, :, None] >= 0)
    same = same & jnp.asarray(freq[:, None] == freq[None, :])[None]
    return jnp.tile(same.astype(F32), (1, 1, 4))


def on_device(
    encoded, visible_pos, clip_len, cotangent, embed_weight, embed_bias, mask_token, attn_gain,
    attn_shift, qkv_weight, query_bias, value_bias, out_weight, out_bias, mlp_gain, mlp_shift,
    up_weight, up_bias, down_weight, down_bias,
):
    both = ("clip", "band")
    groups = lax.axis_size("clip")
    bands = lax.axis_size("band")
    band = lax.axis_index("band")
    side = band % 2
    core = side.astype(jnp.int32).reshape(1)
    halves = [
        [c * bands + 2 * x + k for c in range(groups) for x in range(bands // 2)] for k in range(2)
    ]
    swap = [(i, i ^ 1) for i in range(bands)]
    forward = [(i, i + 1) for i in range(bands - 1)]
    backward = [(b, a) for a, b in forward]
    chips = groups * bands // 2

    def to_all(block):
        return lax.all_to_all(
            block, both, split_axis=0, concat_axis=0, tiled=True, axis_index_groups=halves
        )

    def chip_sum(keep, other):
        mine = (keep.astype(F32) + other.astype(F32)).astype(BF16)
        return mine.reshape(chips, -1, D)

    def total(parts):
        return jnp.sum(parts.astype(F32), 0).astype(BF16)

    vis = visible_pos.shape[1]
    packed, dest = call(
        pack_kernel, "pack", [((GOT, ENC), BF16), ((MICRO, vis, 1), jnp.int32)],
        (band.astype(jnp.int32).reshape(1), visible_pos, encoded), smem=1,
        flops=GOT * MICRO * vis * ENC * 2,
    )
    cot = cotangent.reshape(ALL, D)
    (g_act,) = call(
        before_kernel, "before", [((ALL, FF), F32)], (cot, down_weight), flops=2 * ALL * D * FF,
    )
    got = lax.all_to_all(
        packed.reshape(SRC, BLK, ENC), "clip", split_axis=0, concat_axis=0, tiled=True
    ).reshape(GOT, ENC)

    place = np.arange(GOT)
    within = place % BLK
    index = np.zeros((8, GOT), np.int32)
    index[0], index[1], index[2] = place // BLK, within, np.where(within < 36, within // CAP, 99)
    heads = jnp.asarray(np.arange(128)[None, :] // 32 == np.arange(16)[:, None] % 4, BF16)

    unused, row_in_clip = clip_ident(clip_len[:, 0], band * ROWS + jnp.arange(ROWS))
    table = position_table(row_in_clip, D).reshape(ALL, D)
    ident_ext, unused = clip_ident(clip_len[:, 0], band * ROWS - 2 + jnp.arange(ROWS + 4))
    mask = window_mask(ident_ext)
    zero = jnp.zeros((D,), BF16)
    vecs_one = jnp.stack([embed_bias, mask_token, attn_gain, attn_shift] * 2).astype(F32)
    vecs_two = jnp.stack([out_bias, mlp_gain, mlp_shift, down_bias] * 2).astype(F32)
    qkv_b = jnp.concatenate([query_bias, zero, value_bias]).astype(F32)[None]
    up_b = up_bias.astype(F32)[None]

    hidden, normed, mixed, filled, seen, cell, low, high = call(
        enter_kernel, "enter",
        [
            ((ALL, D), F32), ((ALL, D), BF16), ((ALL, 3 * D), BF16), ((ALL, ENC), BF16),
            ((ALL, 1), F32), ((GOT, 1), jnp.int32),
            ((MICRO, 16, 2 * D), BF16), ((MICRO, 16, 2 * D), BF16),
        ],
        (
            jnp.asarray(index), jnp.asarray(np.ascontiguousarray(index.T)), got, table,
            embed_weight, qkv_weight, vecs_one, qkv_b,
        ),
        flops=2 * ALL * (GOT * ENC + ENC * D + 3 * D * D),
    )
    from_low = lax.ppermute(high, "band", forward)
    from_high = lax.ppermute(low, "band", backward)
    attended, probs = call(
        attend_kernel, "attend",
        [((ALL, D), BF16), ((MICRO * 7, 32, D), F32)],
        (mixed, from_low, from_high, mask, heads),
        flops=MICRO * 7 * 4 * 2**20,
    )
    middle, act, gexp, n2t, send = call(
        mlp_kernel, "mlp",
        [
            ((ALL, D), F32), ((ALL, FF), BF16), ((ALL, FF), BF16), ((D, ALL), BF16),
            ((FF, D), BF16),
        ],
        (core, hidden, attended, cot, g_act, out_weight, up_weight, vecs_two, up_b),
        scratch=[pltpu.VMEM((ALL, D), BF16)],
        smem=1, flops=2 * ALL * (2 * D * FF + D * D), vmem=24,
    )
    (keep,) = call(
        mlp_keep_kernel, "mlp_keep", [((FF, D), BF16)], (core, act, gexp, n2t, cot),
        smem=1, flops=2 * ALL * D * FF,
    )
    chip_one = chip_sum(keep, lax.ppermute(send, "band", swap))
    act, chip_one = lax.optimization_barrier((act, chip_one))
    output, gmid, gatt, gout, sums = call(
        mlp_back_kernel, "mlp_back",
        [
            ((ALL, D), BF16), ((ALL, D), F32), ((ALL, D), BF16), ((D, D), BF16), ((8, D), F32),
        ],
        (middle, attended, cot, act, gexp, out_weight, up_weight, down_weight, vecs_two),
        scratch=[pltpu.VMEM((ALL, D), BF16)],
        flops=2 * ALL * (2 * D * FF + 2 * D * D), vmem=24,
    )
    parts_one = to_all(chip_one)
    gmixed, low, high, rim = call(
        attend_back_kernel, "attend_back",
        [
            ((ALL, 3 * D), BF16), ((MICRO, 16, 2 * D), BF16), ((MICRO, 16, 2 * D), BF16),
            ((MICRO, 2, 16, 2 * D), F32),
        ],
        (mixed, from_low, from_high, probs, gatt, heads),
        flops=MICRO * 7 * 4 * 2**22,
    )
    from_low = lax.ppermute(high, "band", forward)
    from_high = lax.ppermute(low, "band", backward)
    gm, gf, small, send = call(
        leave_kernel, "leave",
        [((ALL, 3 * D), BF16), ((ALL, D), BF16), ((16, D), F32), ((3 * D, D), BF16)],
        (
            core, gmixed, from_low, from_high, rim, hidden, normed, filled, seen, gmid,
            qkv_weight, vecs_one, gout, sums,
        ),
        smem=1, flops=2 * ALL * 5 * D * D,
    )
    keep, returned = call(
        leave_keep_kernel, "leave_keep", [((3 * D, D), BF16), ((GOT, D), BF16)],
        (core, gm, gf, small, normed, filled, gout, cell),
        smem=1, flops=2 * ALL * (2 * D * D + GOT * D),
    )
    other = lax.ppermute(send, "band", swap)
    parts_one, returned, other = lax.optimization_barrier((parts_one, returned, other))
    chip_two = chip_sum(keep, other)
    total_one = lax.all_gather(total(parts_one), both, axis=0).reshape(chips, 2, -1, D)
    mine = total(to_all(chip_two))
    mine = to_all(jnp.broadcast_to(mine[None], (chips,) + mine.shape)).reshape(-1, D)
    mine, returned = lax.optimization_barrier((mine, returned))
    other = lax.ppermute(mine, "band", swap)
    qkv, g_embed, g_out, small = call(
        unpack_two_kernel, "unpack_two",
        [((D, 3 * D), F32), ((ENC, D), F32), ((D, D), F32), ((16, D), F32)],
        (core, mine, other), smem=1,
    )
    came = lax.all_to_all(
        returned.reshape(SRC, BLK, D), "clip", split_axis=0, concat_axis=0, tiled=True
    ).reshape(GOT, D)
    came, small = lax.optimization_barrier((came, small))
    (grad_enc,) = call(
        return_kernel, "return", [((MICRO, vis, ENC), BF16)], (dest, came, embed_weight),
        flops=2 * MICRO * vis * D * (GOT + ENC),
    )
    down, up = unpack_one(total_one)
    return (
        output.reshape(cotangent.shape), grad_enc, g_embed, small[0], small[1], small[2],
        small[3], qkv, small[4], small[5], g_out, small[8], small[9], small[10], up,
        small[12:16].reshape(FF), down, small[11],
    )


def solution(mesh):
    whole = P()
    return jax.shard_map(
        on_device,
        mesh=mesh,
        in_specs=(
            P(None, ("clip", "band"), None),
            P(None, ("clip", "band")),
            P(None, "clip", None),
            P(None, "clip", "band", None, None),
        )
        + (whole,) * 16,
        out_specs=(P(None, "clip", "band", None, None), P(None, ("clip", "band"), None))
        + (whole,) * 16,
        check_vma=False,
    )
```

```python
import jax
import jax.numpy as jnp
import numpy as np
from jax import lax
from jax.experimental import pallas as pl
from jax.experimental.pallas import tpu as pltpu
from jax.sharding import PartitionSpec as P

HEADS = 16
FREQ = 8
LONG = 192
MICRO = 4
ROWS = 24
CELLS = ROWS * FREQ
ALL = MICRO * CELLS
CAP = 9
BLK = 40
SRC = 16
GOT = SRC * BLK
D = 512
FF = 2048
ENC = 768
EPS = 1e-06
SCALE = (D // HEADS) ** (-0.5)
F32 = jnp.float32
BF16 = jnp.bfloat16

NN = (((1,), (0,)), ((), ()))
NT = (((1,), (1,)), ((), ()))
TN = (((0,), (0,)), ((), ()))


def dot(left, right, dims=NN):
    return lax.dot_general(left, right, dims, preferred_element_type=F32)


def iota(shape, dim):
    return lax.broadcasted_iota(jnp.int32, shape, dim)


def one_hot(hit):
    return jnp.where(hit, 1.0, 0.0).astype(BF16)


def call(kernel, name, out_shape, args, scratch=(), smem=0, flops=0, vmem=16, far=()):
    spaces = [pltpu.SMEM] * smem + [pltpu.VMEM] * (len(args) - smem)
    for i in far:
        spaces[i] = pltpu.HBM
    outs = [jax.ShapeDtypeStruct(shape, dtype) for shape, dtype in out_shape]
    size = sum(a.size * a.dtype.itemsize for a in args) + sum(
        o.size * o.dtype.itemsize for o in outs
    )
    return pl.pallas_call(
        kernel,
        name=name,
        out_shape=outs,
        in_specs=[pl.BlockSpec(memory_space=space) for space in spaces],
        out_specs=[pl.BlockSpec(memory_space=pltpu.VMEM)] * len(outs),
        scratch_shapes=list(scratch),
        compiler_params=pltpu.CompilerParams(vmem_limit_bytes=vmem * 2**20),
        cost_estimate=pl.CostEstimate(flops=flops, bytes_accessed=size, transcendentals=0),
    )(*args)


def pack_kernel(band, pos, enc, out, dest):
    count = pos.shape[1]
    low = iota((count, count), 0)
    high = iota((count, count), 1)
    packed = jnp.zeros((GOT, ENC), F32)
    places = jnp.zeros((SRC, 128), F32)
    for m in range(MICRO):
        cell_r = pos[m : m + 1, :]
        cell_c = jnp.sum(jnp.where(low == high, cell_r, 0), axis=1, keepdims=True)
        slot = LONG * FREQ
        dev_r = jnp.sum(
            jnp.where(cell_r >= slot * iota((SRC, count), 0) + slot, 1, 0), axis=0, keepdims=True
        )
        dev_c = jnp.sum(
            jnp.where(cell_c >= slot * iota((count, SRC), 1) + slot, 1, 0), axis=1, keepdims=True
        )
        same = dev_c == dev_r
        rank_r = jnp.sum(jnp.where(same & (low < high), 1, 0), axis=0, keepdims=True)
        rank_c = jnp.sum(jnp.where(same & (high < low), 1, 0), axis=1, keepdims=True)
        dest[m] = dev_c * BLK + m * CAP + rank_c
        select = one_hot(iota((GOT, count), 0) == dev_r * BLK + m * CAP + rank_r)
        packed = packed + dot(select, enc[m])
        number = cell_r - dev_r * slot - band[0] * CELLS + 1
        to_dev = jnp.where(iota((SRC, count), 0) == dev_r, number.astype(F32), 0.0).astype(BF16)
        to_lane = one_hot(iota((count, 128), 1) == m * CAP + rank_c)
        places = places + dot(to_dev, to_lane)
    spread = one_hot(iota((GOT, SRC), 0) == iota((GOT, SRC), 1) * BLK + (BLK - 4))
    out[:, :128] = (packed[:, :128] + dot(spread, places.astype(BF16))).astype(BF16)
    out[:, 128:] = packed[:, 128:].astype(BF16)


def norm_parts(values):
    center = values - jnp.mean(values, -1, keepdims=True)
    inverse = lax.rsqrt(jnp.mean(center * center, -1, keepdims=True) + EPS)
    return center * inverse, inverse


def norm_back(grad, normal, inverse, gain):
    scaled = grad * gain
    return inverse * (
        scaled
        - jnp.mean(scaled, -1, keepdims=True)
        - normal * jnp.mean(scaled * normal, -1, keepdims=True)
    )


def fetch(pairs, sems):
    copies = [pltpu.make_async_copy(far, near, sems.at[i]) for i, (far, near) in enumerate(pairs)]
    for copy in copies:
        copy.start()
    return copies


def enter_kernel(
    idx_r, idx_c, got_i, row_table, freq_table, embed_i, qkv_i, vecs, qkv_b,
    hidden_o, normed_o, mixed_o, filled_o, seen_o, cell_o, low_o, high_o,
    got, embed_w, qkv_w, sems,
):
    copies = fetch([(got_i, got), (embed_i, embed_w), (qkv_i, qkv_w)], sems)
    copies[0].wait()
    hit = one_hot(iota((SRC, GOT), 1) == iota((SRC, GOT), 0) * BLK + (BLK - 4))
    numbers = dot(hit, got[:, :128]).astype(BF16)
    spread_r = dot(numbers, one_hot(iota((SRC, GOT), 0) == idx_r[0:1, :]), TN)
    value_r = jnp.sum(
        jnp.where(iota((128, GOT), 0) == idx_r[1:2, :], spread_r, 0.0), axis=0, keepdims=True
    )
    cell_r = jnp.where(
        value_r > 0.5, idx_r[2:3, :] * CELLS + value_r.astype(jnp.int32) - 1, -1
    )
    spread_c = dot(one_hot(iota((GOT, SRC), 1) == idx_c[:, 0:1]), numbers)
    value_c = jnp.sum(
        jnp.where(iota((GOT, 128), 1) == idx_c[:, 1:2], spread_c, 0.0), axis=1, keepdims=True
    )
    cell_o[...] = jnp.where(
        value_c > 0.5, idx_c[:, 2:3] * CELLS + value_c.astype(jnp.int32) - 1, -1
    )
    for m in range(MICRO):
        rows = slice(m * CELLS, (m + 1) * CELLS)
        match = jnp.where(iota((CELLS, GOT), 0) + m * CELLS == cell_r, 1.0, 0.0)
        seen = jnp.sum(match, axis=1, keepdims=True)
        filled = dot(match.astype(BF16), got[...]).astype(BF16)
        filled_o[rows, :] = filled
        seen_o[rows, :] = seen
    copies[1].wait()
    copies[2].wait()
    freq = jnp.broadcast_to(freq_table[...][None], (ROWS, FREQ, D // 2)).reshape(CELLS, D // 2)
    for m in range(MICRO):
        rows = slice(m * CELLS, (m + 1) * CELLS)
        seen = seen_o[rows, :]
        proj = (dot(filled_o[rows, :], embed_w[...]) + vecs[0:1, :]).astype(BF16).astype(F32)
        line = row_table[m * ROWS : (m + 1) * ROWS, :]
        line = jnp.broadcast_to(line[:, None, :], (ROWS, FREQ, D // 2)).reshape(CELLS, D // 2)
        table = jnp.concatenate([line, freq], axis=1)
        hidden = jnp.where(seen > 0.5, proj, vecs[1:2, :]) + table
        hidden_o[rows, :] = hidden
        normal, unused = norm_parts(hidden)
        normed = (normal * vecs[2:3, :] + vecs[3:4, :]).astype(BF16)
        normed_o[rows, :] = normed
        mixed = (dot(normed, qkv_w[...]) + qkv_b[...]).astype(BF16)
        mixed_o[rows, :] = mixed
        low_o[m] = mixed[:16, D:]
        high_o[m] = mixed[CELLS - 16 :, D:]


def head_rows(block, heads):
    return jnp.concatenate([block * heads[h : h + 1, :] for h in range(4)], axis=0)


def own_head(full, lane_head):
    out = full[0:32, :]
    for h in range(1, 4):
        out = jnp.where(lane_head == h, full[32 * h : 32 * h + 32, :], out)
    return out


def window_loop(edge, inner):
    def inside(p, carry):
        places = []
        for m in range(MICRO):
            base = pl.multiple_of(m * CELLS + 32 * p - 16, 16)
            places.append((m * 7 + p, pl.ds(base, 32)))
        inner(places)
        return carry

    def ends(i, carry):
        places = []
        for j in range(2):
            m = 2 * i + j
            first = pl.multiple_of(m * CELLS, 16)
            last = pl.multiple_of(m * CELLS + CELLS - 16, 16)
            places.append((m, m * 7, pl.ds(first, 16), 0))
            places.append((m, m * 7 + 6, pl.ds(last, 16), 1))
        edge(places)
        return carry

    lax.fori_loop(1, 6, inside, 0)
    lax.fori_loop(0, MICRO // 2, ends, 0)


def with_halo(own, halo, side):
    return jnp.concatenate([own, halo] if side else [halo, own], axis=0)


COLS = [[slice(D * i + 128 * g, D * i + 128 * g + 128) for i in range(3)] for g in range(4)]


def load_inner(mixed, places, grads=None):
    items = []
    for w, rows in places:
        for g in range(4):
            item = [mixed[rows, c] for c in COLS[g]]
            items.append((w, g, *item, None if grads is None else grads[rows, COLS[g][0]]))
    return items


def load_edge(mixed, low, high, places, grads=None):
    zero = jnp.zeros((16, 128), BF16)
    items = []
    for m, w, rows, side in places:
        halo = high if side else low
        for g in range(4):
            cols = COLS[g]
            q = with_halo(mixed[rows, cols[0]], zero, side)
            k = with_halo(mixed[rows, cols[1]], halo[m, :, cols[0]], side)
            v = with_halo(mixed[rows, cols[2]], halo[m, :, cols[1]], side)
            grad = None if grads is None else with_halo(grads[rows, cols[0]], zero, side)
            items.append((w, g, q, k, v, grad))
    return items


def attend_kernel(mixed, low, high, mask, heads_i, attended_o, probs_o):
    heads = heads_i[...]
    lane_head = iota((32, 128), 1) // 32

    def windows(items):
        scores = [dot(k, head_rows(q, heads), NT) * SCALE for w, g, q, k, v, _ in items]
        probs = []
        for (w, g, *_), score in zip(items, scores):
            score = jnp.where(mask[w] > 0.5, score, -1e30)
            grown = jnp.exp(score - jnp.max(score, axis=0, keepdims=True))
            one = grown * (1.0 / jnp.sum(grown, axis=0, keepdims=True))
            probs_o[w, :, 128 * g : 128 * g + 128] = one
            probs.append(one.astype(BF16))
        full = [dot(one, item[4], TN) for item, one in zip(items, probs)]
        return [own_head(one, lane_head).astype(BF16) for one in full]

    def inner(places):
        outs = windows(load_inner(mixed, places))
        for i, (w, rows) in enumerate(places):
            for g in range(4):
                attended_o[rows, COLS[g][0]] = outs[4 * i + g]

    def edge(places):
        outs = windows(load_edge(mixed, low, high, places))
        for i, (m, w, rows, side) in enumerate(places):
            for g in range(4):
                out = outs[4 * i + g]
                attended_o[rows, COLS[g][0]] = out[:16] if side else out[16:]

    window_loop(edge, inner)


def gelu_parts(x):
    size = jnp.abs(x) * (0.5**0.5)
    bell = jnp.exp(-0.5 * x * x)
    t = 1.0 / (1.0 + 0.3275911 * size)
    poly = t * (
        0.254829592
        + t * (-0.284496736 + t * (1.421413741 + t * (-1.453152027 + t * 1.061405429)))
    )
    tail = 0.5 * poly * bell
    share = jnp.where(x >= 0, 1.0 - tail, tail)
    return x * share, share + x * bell * 0.3989422804014327


def before_kernel(cot, down_w, g_act_o):
    for f in range(4):
        cols = slice(512 * f, 512 * f + 512)
        g_act_o[:, cols] = dot(cot[...], down_w[cols, :], NT)


def mlp_kernel(
    core, hidden, attended, cot, g_act, out_w, up_w, vecs, up_b,
    middle_o, act_o, gexp_o, n2t_o, send_o, n2_s,
):
    tile = 256
    blocks = [slice(512 * f, 512 * f + 512) for f in range(4)]

    def forward(i, carry):
        rows = pl.ds(pl.multiple_of(i * tile, tile), tile)
        middle = hidden[rows, :] + dot(attended[rows, :], out_w[...]) + vecs[0:1, :]
        middle_o[rows, :] = middle
        normal, unused = norm_parts(middle)
        normed = (normal * vecs[1:2, :] + vecs[2:3, :]).astype(BF16)
        n2_s[rows, :] = normed
        expand = [dot(normed, up_w[:, cols]) for cols in blocks]
        for cols, one in zip(blocks, expand):
            value, slope = gelu_parts(one + up_b[0:1, cols])
            act_o[rows, cols] = value.astype(BF16)
            gexp_o[rows, cols] = (g_act[rows, cols] * slope).astype(BF16)
        return carry

    lax.fori_loop(0, ALL // tile, forward, 0)
    n2t_o[...] = jnp.transpose(n2_s[...])
    weight_half(1 - core[0], send_o, act_o, gexp_o, n2t_o, cot)


def weight_half(half, out, act, gexp, n2t, cot):
    for b in range(2):
        cols = pl.ds(pl.multiple_of(half * 1024 + 512 * b, 512), 512)
        rows = slice(512 * b, 512 * b + 512)
        out[rows, :] = dot(act[:, cols], cot[...], TN).astype(BF16)
        rows = slice(1024 + 512 * b, 1536 + 512 * b)
        out[rows, :] = dot(n2t[...], gexp[:, cols]).astype(BF16)


def mlp_keep_kernel(core, act, gexp, n2t, cot, keep_o):
    weight_half(core[0], keep_o, act, gexp, n2t, cot)


def back_kernel(
    middle_i, attended_i, cot_i, act_i, gexp_i, out_i, up_i, down_i, mixed_i, low_i, high_i,
    probs_f, vecs, heads_i,
    output_o, gmid_o, gout_o, sums_o, gmixed_o, low_o, high_o, rim_o,
    middle_s, attended, cot, act, gexp, out_w, up_w, down_w, mixed, low, high, probs_i, gatt, gb_s,
    sems,
):
    copies = fetch(
        [
            (up_i, up_w), (gexp_i, gexp), (down_i, down_w), (act_i, act), (middle_i, middle_s),
            (cot_i, cot), (out_i, out_w), (attended_i, attended), (mixed_i, mixed),
            (low_i, low), (high_i, high), (probs_f, probs_i),
        ],
        sems,
    )
    tile = 256
    sums_o[...] = jnp.zeros((8, D), F32)
    for i in range(ALL // tile):
        rows = slice(i * tile, (i + 1) * tile)
        if i == 0:
            copies[0].wait()
            copies[1].wait()
        grad = dot(gexp[rows, :], up_w[...], NT)
        if i == 0:
            copies[2].wait()
            copies[3].wait()
            copies[4].wait()
        middle = middle_s[rows, :]
        output_o[rows, :] = (middle + vecs[3:4, :] + dot(act[rows, :], down_w[...])).astype(BF16)
        if i == 0:
            copies[5].wait()
            copies[6].wait()
        normal, inverse = norm_parts(middle)
        g_float = cot[rows, :].astype(F32)
        g_mid = g_float + norm_back(grad, normal, inverse, vecs[1:2, :])
        gmid_o[rows, :] = g_mid
        g_low = g_mid.astype(BF16)
        gb_s[rows, :] = g_low
        gatt[rows, :] = dot(g_low, out_w[...], NT).astype(BF16)
        sums_o[0:1, :] += jnp.sum(g_low.astype(F32), axis=0, keepdims=True)
        sums_o[1:2, :] += jnp.sum(grad * normal, axis=0, keepdims=True)
        sums_o[2:3, :] += jnp.sum(grad, axis=0, keepdims=True)
        sums_o[3:4, :] += jnp.sum(g_float, axis=0, keepdims=True)
        for f in range(4):
            part = gexp[rows, 512 * f : 512 * f + 512].astype(F32)
            sums_o[4 + f : 5 + f, :] += jnp.sum(part, axis=0, keepdims=True)
    copies[7].wait()
    gout_o[...] = dot(attended[...], gb_s[...], TN).astype(BF16)
    for copy in copies[8:]:
        copy.wait()
    attend_back(mixed, low, high, probs_i, gatt, heads_i, gmixed_o, low_o, high_o, rim_o)


def attend_back(
    mixed, low, high, probs_i, gatt, heads_i, gmixed_o, low_o, high_o, rim_o
):
    heads = heads_i[...]
    lane_head = iota((32, 128), 1) // 32

    def windows(items):
        q_m = [head_rows(q, heads) for w, g, q, k, v, grad in items]
        g_m = [head_rows(grad, heads) for w, g, q, k, v, grad in items]
        g_probs = [dot(item[4], one, NT) for item, one in zip(items, g_m)]
        low_probs, g_scores = [], []
        for (w, g, *_), g_prob in zip(items, g_probs):
            probs = probs_i[w, :, 128 * g : 128 * g + 128]
            inner = jnp.sum(probs * g_prob, axis=0, keepdims=True)
            g_scores.append((probs * (g_prob - inner)).astype(BF16))
            low_probs.append(probs.astype(BF16))
        d_value = [dot(one, grad) for one, grad in zip(low_probs, g_m)]
        d_key = [dot(one, q) * SCALE for one, q in zip(g_scores, q_m)]
        full = [dot(one, item[3], TN) for item, one in zip(items, g_scores)]
        d_query = [(own_head(one, lane_head) * SCALE).astype(BF16) for one in full]
        return list(zip(d_query, d_key, d_value))

    def inner(places):
        outs = windows(load_inner(mixed, places, gatt))
        for i, (w, rows) in enumerate(places):
            for g in range(4):
                for col, value in zip(COLS[g], outs[4 * i + g]):
                    gmixed_o[rows, col] = value.astype(BF16)

    def edge(places):
        outs = windows(load_edge(mixed, low, high, places, gatt))
        for i, (m, w, rows, side) in enumerate(places):
            out = high_o if side else low_o
            own, far = (slice(0, 16), slice(16, 32)) if side else (slice(16, 32), slice(0, 16))
            for g in range(4):
                cols = COLS[g]
                d_query, d_key, d_value = outs[4 * i + g]
                gmixed_o[rows, cols[0]] = d_query[own]
                rim_o[m, side, :, cols[0]] = d_key[own]
                rim_o[m, side, :, cols[1]] = d_value[own]
                out[m, :, cols[0]] = d_key[far].astype(BF16)
                out[m, :, cols[1]] = d_value[far].astype(BF16)

    window_loop(edge, inner)
    for m in range(MICRO):
        for base in (m * CELLS, m * CELLS + CELLS - 16):
            gmixed_o[base : base + 16, D:] = jnp.zeros((16, 2 * D), BF16)


def leave_kernel(
    core, gmixed, from_low, from_high, rim, hidden, normed, filled, seen, gmid, qkv_w, vecs,
    gout, sums, gm_o, gf_o, small_o, send_o,
):
    small = jnp.zeros((1, D), F32)
    gain_sum, shift_sum, mask_sum, embed_sum, query_sum, value_sum = [small] * 6
    for m in range(MICRO):
        base = m * CELLS
        rows = slice(base, base + CELLS)
        gm_o[rows, :] = gmixed[rows, :]
        gm_o[base : base + 16, D:] = (rim[m, 0] + from_low[m].astype(F32)).astype(BF16)
        gm_o[base + CELLS - 16 : base + CELLS, D:] = (rim[m, 1] + from_high[m].astype(F32)).astype(
            BF16
        )
        gm = gm_o[rows, :]
        grad = dot(gm, qkv_w[...], NT)
        normal, inverse = norm_parts(hidden[rows, :])
        g_hidden = gmid[rows, :] + norm_back(grad, normal, inverse, vecs[2:3, :])
        there = seen[rows, :] > 0.5
        g_low = g_hidden.astype(BF16)
        gf_o[rows, :] = g_low
        gain_sum += jnp.sum(grad * normal, axis=0, keepdims=True)
        shift_sum += jnp.sum(grad, axis=0, keepdims=True)
        mask_sum += jnp.sum(jnp.where(there, 0.0, g_hidden), axis=0, keepdims=True)
        embed_sum += jnp.sum(jnp.where(there, g_low.astype(F32), 0.0), axis=0, keepdims=True)
        query_sum += jnp.sum(gm[:, :D].astype(F32), axis=0, keepdims=True)
        value_sum += jnp.sum(gm[:, 2 * D :].astype(F32), axis=0, keepdims=True)
    small_o[...] = jnp.concatenate(
        [
            embed_sum, mask_sum, gain_sum, shift_sum, query_sum, value_sum,
            small, small, sums[...],
        ],
        axis=0,
    )
    one_half(core[0] != 0, send_o, normed, filled, gm_o, gf_o, gout, small_o)


def one_half(first, out, normed, filled, gm, gf, gout, small):
    @pl.when(first)
    def _():
        turned = jnp.transpose(normed[...])
        for b in range(3):
            cols = slice(512 * b, 512 * b + 512)
            out[cols, :] = dot(turned, gm[:, cols]).astype(BF16)

    @pl.when(jnp.logical_not(first))
    def _():
        out[0:512, :] = gout[...]
        out[512:1280, :] = dot(jnp.transpose(filled[...]), gf[...]).astype(BF16)
        out[1280:1296, :] = small[...].astype(BF16)
        out[1296:1536, :] = jnp.zeros((240, D), BF16)


def leave_keep_kernel(core, gm, gf, small, normed, filled, gout, cell, keep_o, ret_o):
    one_half(core[0] == 0, keep_o, normed, filled, gm, gf, gout, small)
    ret_o[...] = dot(one_hot(iota((GOT, ALL), 1) == cell[...]), gf[...]).astype(BF16)


def return_kernel(dest, came, embed_w, out):
    for m in range(MICRO):
        select = one_hot(iota((dest.shape[1], GOT), 1) == dest[m])
        g_proj = dot(select, came[...]).astype(BF16)
        out[m] = dot(g_proj, embed_w[...], NT).astype(BF16)


def unpack_one_kernel(down_i, up_i, down_o, up_o):
    down_o[...] = down_i[...].reshape(512, D).astype(F32)
    up_o[...] = up_i[...].reshape(512, D).astype(F32)


def unpack_one(gathered):
    block = (16, 1, 32, D)
    return pl.pallas_call(
        unpack_one_kernel,
        name="unpack_one",
        grid=(4,),
        out_shape=[jax.ShapeDtypeStruct((FF, D), F32), jax.ShapeDtypeStruct((D, FF), F32)],
        in_specs=[
            pl.BlockSpec(block, lambda i: (i % 2, i // 2, 0, 0)),
            pl.BlockSpec(block, lambda i: (2 + i % 2, i // 2, 0, 0)),
        ],
        out_specs=[
            pl.BlockSpec((512, D), lambda i: (i, 0)),
            pl.BlockSpec((512, D), lambda i: (0, i)),
        ],
        compiler_params=pltpu.CompilerParams(vmem_limit_bytes=16 * 2**20),
        cost_estimate=pl.CostEstimate(flops=0, bytes_accessed=12 * 2**20, transcendentals=0),
    )(gathered, gathered)


def unpack_two_kernel(core, mine, other, qkv_o, embed_o, out_o, small_o):
    def write(first, second):
        for b in range(3):
            qkv_o[:, 512 * b : 512 * b + 512] = first[512 * b : 512 * b + 512, :].astype(F32)
        out_o[...] = second[0:512, :].astype(F32)
        embed_o[...] = second[512:1280, :].astype(F32)
        small_o[...] = second[1280:1296, :].astype(F32)

    @pl.when(core[0] == 0)
    def _():
        write(mine, other)

    @pl.when(core[0] != 0)
    def _():
        write(other, mine)


def clip_ident(lengths, rows):
    first = lengths[:, 0:1]
    second = first + lengths[:, 1:2]
    ident = (rows[None, :] >= first).astype(jnp.int32) + (rows[None, :] >= second).astype(jnp.int32)
    start = jnp.where(ident >= 1, first, 0) + jnp.where(ident >= 2, lengths[:, 1:2], 0)
    inside = (rows >= 0) & (rows < LONG)
    return (jnp.where(inside[None, :], ident, -1), rows[None, :] - start)


def position_tables(row_in_clip, width):
    quarter = width // 4
    omega = 1.0 / 10000.0 ** (jnp.arange(quarter, dtype=jnp.float32) / quarter)
    row_angle = row_in_clip.astype(jnp.float32)[..., None] * omega
    freq_angle = jnp.arange(FREQ, dtype=jnp.float32)[:, None] * omega
    row_part = jnp.concatenate([jnp.sin(row_angle), jnp.cos(row_angle)], -1)
    freq_part = jnp.concatenate([jnp.sin(freq_angle), jnp.cos(freq_angle)], -1)
    return row_part.reshape(-1, width // 2), freq_part


def window_mask(ident):
    cells = jnp.repeat(ident.reshape(MICRO * 7, 4), FREQ, axis=1)
    freq = np.tile((np.arange(FREQ) + 2) % 8 // 4, 4)
    same = (cells[:, :, None] == cells[:, None, :]) & (cells[:, :, None] >= 0)
    same = same & jnp.asarray(freq[:, None] == freq[None, :])[None]
    return jnp.tile(same.astype(F32), (1, 1, 4))


def on_device(
    encoded, visible_pos, clip_len, cotangent, embed_weight, embed_bias, mask_token, attn_gain,
    attn_shift, qkv_weight, query_bias, value_bias, out_weight, out_bias, mlp_gain, mlp_shift,
    up_weight, up_bias, down_weight, down_bias,
):
    both = ("clip", "band")
    groups = lax.axis_size("clip")
    bands = lax.axis_size("band")
    band = lax.axis_index("band")
    side = band % 2
    core = side.astype(jnp.int32).reshape(1)
    halves = [
        [c * bands + 2 * x + k for c in range(groups) for x in range(bands // 2)] for k in range(2)
    ]
    swap = [(i, i ^ 1) for i in range(bands)]
    forward = [(i, i + 1) for i in range(bands - 1)]
    backward = [(b, a) for a, b in forward]
    chips = groups * bands // 2

    def to_all(block):
        return lax.all_to_all(
            block, both, split_axis=0, concat_axis=0, tiled=True, axis_index_groups=halves
        )

    def chip_sum(keep, other):
        mine = (keep.astype(F32) + other.astype(F32)).astype(BF16)
        return mine.reshape(chips, -1, D)

    def total(parts):
        return jnp.sum(parts.astype(F32), 0).astype(BF16)

    def spread(chunk):
        return jnp.broadcast_to(chunk[None], (chips,) + chunk.shape)

    vis = visible_pos.shape[1]
    packed, dest = call(
        pack_kernel, "pack", [((GOT, ENC), BF16), ((MICRO, vis, 1), jnp.int32)],
        (band.astype(jnp.int32).reshape(1), visible_pos, encoded), smem=1,
        flops=GOT * MICRO * vis * ENC * 2,
    )
    cot = cotangent.reshape(ALL, D)
    (g_act,) = call(
        before_kernel, "before", [((ALL, FF), F32)], (cot, down_weight), flops=2 * ALL * D * FF,
    )
    got = lax.all_to_all(
        packed.reshape(SRC, BLK, ENC), "clip", split_axis=0, concat_axis=0, tiled=True
    ).reshape(GOT, ENC)

    place = np.arange(GOT)
    within = place % BLK
    index = np.zeros((8, GOT), np.int32)
    index[0], index[1], index[2] = place // BLK, within, np.where(within < 36, within // CAP, 99)
    heads = jnp.asarray(np.arange(128)[None, :] // 32 == np.arange(16)[:, None] % 4, BF16)

    unused, row_in_clip = clip_ident(clip_len[:, 0], band * ROWS + jnp.arange(ROWS))
    row_table, freq_table = position_tables(row_in_clip, D)
    ident_ext, unused = clip_ident(clip_len[:, 0], band * ROWS - 2 + jnp.arange(ROWS + 4))
    mask = window_mask(ident_ext)
    zero = jnp.zeros((D,), BF16)
    vecs_one = jnp.stack([embed_bias, mask_token, attn_gain, attn_shift] * 2).astype(F32)
    vecs_two = jnp.stack([out_bias, mlp_gain, mlp_shift, down_bias] * 2).astype(F32)
    qkv_b = jnp.concatenate([query_bias, zero, value_bias]).astype(F32)[None]
    up_b = up_bias.astype(F32)[None]

    hidden, normed, mixed, filled, seen, cell, low, high = call(
        enter_kernel, "enter",
        [
            ((ALL, D), F32), ((ALL, D), BF16), ((ALL, 3 * D), BF16), ((ALL, ENC), BF16),
            ((ALL, 1), F32), ((GOT, 1), jnp.int32),
            ((MICRO, 16, 2 * D), BF16), ((MICRO, 16, 2 * D), BF16),
        ],
        (
            jnp.asarray(index), jnp.asarray(np.ascontiguousarray(index.T)), got, row_table,
            freq_table, embed_weight, qkv_weight, vecs_one, qkv_b,
        ),
        scratch=[
            pltpu.VMEM((GOT, ENC), BF16), pltpu.VMEM((ENC, D), BF16), pltpu.VMEM((D, 3 * D), BF16),
            pltpu.SemaphoreType.DMA((3,)),
        ],
        far=(2, 5, 6),
        flops=2 * ALL * (GOT * ENC + ENC * D + 3 * D * D),
    )
    from_low = lax.ppermute(high, "band", forward)
    from_high = lax.ppermute(low, "band", backward)
    attended, probs = call(
        attend_kernel, "attend",
        [((ALL, D), BF16), ((MICRO * 7, 32, D), F32)],
        (mixed, from_low, from_high, mask, heads),
        flops=MICRO * 7 * 4 * 2**20,
    )
    middle, act, gexp, n2t, send = call(
        mlp_kernel, "mlp",
        [
            ((ALL, D), F32), ((ALL, FF), BF16), ((ALL, FF), BF16), ((D, ALL), BF16),
            ((FF, D), BF16),
        ],
        (core, hidden, attended, cot, g_act, out_weight, up_weight, vecs_two, up_b),
        scratch=[pltpu.VMEM((ALL, D), BF16)],
        smem=1, flops=2 * ALL * (2 * D * FF + D * D), vmem=24,
    )
    (keep,) = call(
        mlp_keep_kernel, "mlp_keep", [((FF, D), BF16)], (core, act, gexp, n2t, cot),
        smem=1, flops=2 * ALL * D * FF,
    )
    chip_one = chip_sum(keep, lax.ppermute(send, "band", swap))
    act, chip_one = lax.optimization_barrier((act, chip_one))
    parts_one = to_all(chip_one)
    inputs = (
        middle, attended, cot, act, gexp, out_weight, up_weight, down_weight, mixed, from_low,
        from_high, probs,
    )
    output, gmid, gout, sums, gmixed, low, high, rim = call(
        back_kernel, "back",
        [
            ((ALL, D), BF16), ((ALL, D), F32), ((D, D), BF16), ((8, D), F32),
            ((ALL, 3 * D), BF16), ((MICRO, 16, 2 * D), BF16), ((MICRO, 16, 2 * D), BF16),
            ((MICRO, 2, 16, 2 * D), F32),
        ],
        inputs + (vecs_two, heads),
        scratch=[pltpu.VMEM(x.shape, x.dtype) for x in inputs]
        + [pltpu.VMEM((ALL, D), BF16)] * 2
        + [pltpu.SemaphoreType.DMA((len(inputs),))],
        flops=2 * ALL * (2 * D * FF + 2 * D * D) + MICRO * 7 * 4 * 2**22,
        far=range(len(inputs)), vmem=44,
    )
    from_low = lax.ppermute(high, "band", forward)
    from_high = lax.ppermute(low, "band", backward)
    gm, gf, small, send = call(
        leave_kernel, "leave",
        [((ALL, 3 * D), BF16), ((ALL, D), BF16), ((16, D), F32), ((3 * D, D), BF16)],
        (
            core, gmixed, from_low, from_high, rim, hidden, normed, filled, seen, gmid,
            qkv_weight, vecs_one, gout, sums,
        ),
        smem=1, flops=2 * ALL * 5 * D * D,
    )
    other = lax.ppermute(send, "band", swap)
    parts_one, gf = lax.optimization_barrier((parts_one, gf))
    total_one = lax.all_gather(total(parts_one), both, axis=0).reshape(chips, 2, -1, D)
    keep, returned = call(
        leave_keep_kernel, "leave_keep", [((3 * D, D), BF16), ((GOT, D), BF16)],
        (core, gm, gf, small, normed, filled, gout, cell),
        smem=1, flops=2 * ALL * (2 * D * D + GOT * D),
    )
    mine = to_all(spread(total(to_all(chip_sum(keep, other))))).reshape(-1, D)
    mine, returned = lax.optimization_barrier((mine, returned))
    qkv, g_embed, g_out, small = call(
        unpack_two_kernel, "unpack_two",
        [((D, 3 * D), F32), ((ENC, D), F32), ((D, D), F32), ((16, D), F32)],
        (core, mine, lax.ppermute(mine, "band", swap)), smem=1,
    )
    came = lax.all_to_all(
        returned.reshape(SRC, BLK, D), "clip", split_axis=0, concat_axis=0, tiled=True
    ).reshape(GOT, D)
    down, up = unpack_one(total_one)
    came, small, down = lax.optimization_barrier((came, small, down))
    (grad_enc,) = call(
        return_kernel, "return", [((MICRO, vis, ENC), BF16)], (dest, came, embed_weight),
        flops=2 * MICRO * vis * D * (GOT + ENC),
    )
    return (
        output.reshape(cotangent.shape), grad_enc, g_embed, small[0], small[1], small[2],
        small[3], qkv, small[4], small[5], g_out, small[8], small[9], small[10], up,
        small[12:16].reshape(FF), down, small[11],
    )


def solution(mesh):
    whole = P()
    return jax.shard_map(
        on_device,
        mesh=mesh,
        in_specs=(
            P(None, ("clip", "band"), None),
            P(None, ("clip", "band")),
            P(None, "clip", None),
            P(None, "clip", "band", None, None),
        )
        + (whole,) * 16,
        out_specs=(P(None, "clip", "band", None, None), P(None, ("clip", "band"), None))
        + (whole,) * 16,
        check_vma=False,
    )
```

```python
import jax
import jax.numpy as jnp
import numpy as np
from jax import lax
from jax.experimental import pallas as pl
from jax.experimental.pallas import tpu as pltpu
from jax.sharding import PartitionSpec as P

HEADS = 16
FREQ = 8
LONG = 192
MICRO = 4
ROWS = 24
CELLS = ROWS * FREQ
ALL = MICRO * CELLS
CAP = 9
BLK = 40
SRC = 16
GOT = SRC * BLK
D = 512
FF = 2048
ENC = 768
EPS = 1e-06
SCALE = (D // HEADS) ** (-0.5)
F32 = jnp.float32
BF16 = jnp.bfloat16

NN = (((1,), (0,)), ((), ()))
NT = (((1,), (1,)), ((), ()))
TN = (((0,), (0,)), ((), ()))


def dot(left, right, dims=NN):
    return lax.dot_general(left, right, dims, preferred_element_type=F32)


def iota(shape, dim):
    return lax.broadcasted_iota(jnp.int32, shape, dim)


def one_hot(hit):
    return jnp.where(hit, 1.0, 0.0).astype(BF16)


def call(kernel, name, out_shape, args, scratch=(), smem=0, flops=0, vmem=16, far=()):
    spaces = [pltpu.SMEM] * smem + [pltpu.VMEM] * (len(args) - smem)
    for i in far:
        spaces[i] = pltpu.HBM
    outs = [jax.ShapeDtypeStruct(shape, dtype) for shape, dtype in out_shape]
    size = sum(a.size * a.dtype.itemsize for a in args) + sum(
        o.size * o.dtype.itemsize for o in outs
    )
    return pl.pallas_call(
        kernel,
        name=name,
        out_shape=outs,
        in_specs=[pl.BlockSpec(memory_space=space) for space in spaces],
        out_specs=[pl.BlockSpec(memory_space=pltpu.VMEM)] * len(outs),
        scratch_shapes=list(scratch),
        compiler_params=pltpu.CompilerParams(vmem_limit_bytes=vmem * 2**20),
        cost_estimate=pl.CostEstimate(flops=flops, bytes_accessed=size, transcendentals=0),
    )(*args)


def pack_kernel(band, pos, enc, out, dest):
    count = pos.shape[1]
    low = iota((count, count), 0)
    high = iota((count, count), 1)
    packed = jnp.zeros((GOT, ENC), F32)
    places = jnp.zeros((SRC, 128), F32)
    for m in range(MICRO):
        cell_r = pos[m : m + 1, :]
        cell_c = jnp.sum(jnp.where(low == high, cell_r, 0), axis=1, keepdims=True)
        slot = LONG * FREQ
        dev_r = jnp.sum(
            jnp.where(cell_r >= slot * iota((SRC, count), 0) + slot, 1, 0), axis=0, keepdims=True
        )
        dev_c = jnp.sum(
            jnp.where(cell_c >= slot * iota((count, SRC), 1) + slot, 1, 0), axis=1, keepdims=True
        )
        same = dev_c == dev_r
        rank_r = jnp.sum(jnp.where(same & (low < high), 1, 0), axis=0, keepdims=True)
        rank_c = jnp.sum(jnp.where(same & (high < low), 1, 0), axis=1, keepdims=True)
        dest[m] = dev_c * BLK + m * CAP + rank_c
        select = one_hot(iota((GOT, count), 0) == dev_r * BLK + m * CAP + rank_r)
        packed = packed + dot(select, enc[m])
        number = cell_r - dev_r * slot - band[0] * CELLS + 1
        to_dev = jnp.where(iota((SRC, count), 0) == dev_r, number.astype(F32), 0.0).astype(BF16)
        to_lane = one_hot(iota((count, 128), 1) == m * CAP + rank_c)
        places = places + dot(to_dev, to_lane)
    spread = one_hot(iota((GOT, SRC), 0) == iota((GOT, SRC), 1) * BLK + (BLK - 4))
    out[:, :128] = (packed[:, :128] + dot(spread, places.astype(BF16))).astype(BF16)
    out[:, 128:] = packed[:, 128:].astype(BF16)


def norm_parts(values):
    center = values - jnp.mean(values, -1, keepdims=True)
    inverse = lax.rsqrt(jnp.mean(center * center, -1, keepdims=True) + EPS)
    return center * inverse, inverse


def norm_back(grad, normal, inverse, gain):
    scaled = grad * gain
    return inverse * (
        scaled
        - jnp.mean(scaled, -1, keepdims=True)
        - normal * jnp.mean(scaled * normal, -1, keepdims=True)
    )


def fetch(pairs, sems):
    copies = [pltpu.make_async_copy(far, near, sems.at[i]) for i, (far, near) in enumerate(pairs)]
    for copy in copies:
        copy.start()
    return copies


def enter_kernel(
    idx_r, idx_c, got_i, row_table, freq_table, embed_i, qkv_i, vecs, qkv_b,
    hidden_o, normed_o, mixed_o, filled_o, seen_o, cell_o, low_o, high_o,
    got, embed_w, qkv_w, sems,
):
    copies = fetch([(got_i, got), (embed_i, embed_w), (qkv_i, qkv_w)], sems)
    copies[0].wait()
    hit = one_hot(iota((SRC, GOT), 1) == iota((SRC, GOT), 0) * BLK + (BLK - 4))
    numbers = dot(hit, got[:, :128]).astype(BF16)
    spread_r = dot(numbers, one_hot(iota((SRC, GOT), 0) == idx_r[0:1, :]), TN)
    value_r = jnp.sum(
        jnp.where(iota((128, GOT), 0) == idx_r[1:2, :], spread_r, 0.0), axis=0, keepdims=True
    )
    cell_r = jnp.where(
        value_r > 0.5, idx_r[2:3, :] * CELLS + value_r.astype(jnp.int32) - 1, -1
    )
    spread_c = dot(one_hot(iota((GOT, SRC), 1) == idx_c[:, 0:1]), numbers)
    value_c = jnp.sum(
        jnp.where(iota((GOT, 128), 1) == idx_c[:, 1:2], spread_c, 0.0), axis=1, keepdims=True
    )
    cell_o[...] = jnp.where(
        value_c > 0.5, idx_c[:, 2:3] * CELLS + value_c.astype(jnp.int32) - 1, -1
    )
    for m in range(MICRO):
        rows = slice(m * CELLS, (m + 1) * CELLS)
        match = jnp.where(iota((CELLS, GOT), 0) + m * CELLS == cell_r, 1.0, 0.0)
        seen = jnp.sum(match, axis=1, keepdims=True)
        filled = dot(match.astype(BF16), got[...]).astype(BF16)
        filled_o[rows, :] = filled
        seen_o[rows, :] = seen
    copies[1].wait()
    copies[2].wait()
    freq = jnp.broadcast_to(freq_table[...][None], (ROWS, FREQ, D // 2)).reshape(CELLS, D // 2)
    for m in range(MICRO):
        rows = slice(m * CELLS, (m + 1) * CELLS)
        seen = seen_o[rows, :]
        proj = (dot(filled_o[rows, :], embed_w[...]) + vecs[0:1, :]).astype(BF16).astype(F32)
        line = row_table[m * ROWS : (m + 1) * ROWS, :]
        line = jnp.broadcast_to(line[:, None, :], (ROWS, FREQ, D // 2)).reshape(CELLS, D // 2)
        table = jnp.concatenate([line, freq], axis=1)
        hidden = jnp.where(seen > 0.5, proj, vecs[1:2, :]) + table
        hidden_o[rows, :] = hidden
        normal, unused = norm_parts(hidden)
        normed = (normal * vecs[2:3, :] + vecs[3:4, :]).astype(BF16)
        normed_o[rows, :] = normed
        mixed = (dot(normed, qkv_w[...]) + qkv_b[...]).astype(BF16)
        mixed_o[rows, :] = mixed
        low_o[m] = mixed[:16, D:]
        high_o[m] = mixed[CELLS - 16 :, D:]


def head_rows(block, heads):
    return jnp.concatenate([block * heads[h : h + 1, :] for h in range(4)], axis=0)


def own_head(full, lane_head):
    out = full[0:32, :]
    for h in range(1, 4):
        out = jnp.where(lane_head == h, full[32 * h : 32 * h + 32, :], out)
    return out


def window_loop(edge, inner):
    def inside(p, carry):
        places = []
        for m in range(MICRO):
            base = pl.multiple_of(m * CELLS + 32 * p - 16, 16)
            places.append((m * 7 + p, pl.ds(base, 32)))
        inner(places)
        return carry

    def ends(i, carry):
        places = []
        for j in range(2):
            m = 2 * i + j
            first = pl.multiple_of(m * CELLS, 16)
            last = pl.multiple_of(m * CELLS + CELLS - 16, 16)
            places.append((m, m * 7, pl.ds(first, 16), 0))
            places.append((m, m * 7 + 6, pl.ds(last, 16), 1))
        edge(places)
        return carry

    lax.fori_loop(1, 6, inside, 0)
    lax.fori_loop(0, MICRO // 2, ends, 0)


def with_halo(own, halo, side):
    return jnp.concatenate([own, halo] if side else [halo, own], axis=0)


COLS = [[slice(D * i + 128 * g, D * i + 128 * g + 128) for i in range(3)] for g in range(4)]


def load_inner(mixed, places, grads=None):
    items = []
    for w, rows in places:
        for g in range(4):
            item = [mixed[rows, c] for c in COLS[g]]
            items.append((w, g, *item, None if grads is None else grads[rows, COLS[g][0]]))
    return items


def load_edge(mixed, low, high, places, grads=None):
    zero = jnp.zeros((16, 128), BF16)
    items = []
    for m, w, rows, side in places:
        halo = high if side else low
        for g in range(4):
            cols = COLS[g]
            q = with_halo(mixed[rows, cols[0]], zero, side)
            k = with_halo(mixed[rows, cols[1]], halo[m, :, cols[0]], side)
            v = with_halo(mixed[rows, cols[2]], halo[m, :, cols[1]], side)
            grad = None if grads is None else with_halo(grads[rows, cols[0]], zero, side)
            items.append((w, g, q, k, v, grad))
    return items


def attend_kernel(mixed, low, high, mask, heads_i, attended_o, probs_o):
    heads = heads_i[...]
    lane_head = iota((32, 128), 1) // 32

    def windows(items):
        scores = [dot(k, head_rows(q, heads), NT) * SCALE for w, g, q, k, v, _ in items]
        probs = []
        for (w, g, *_), score in zip(items, scores):
            score = jnp.where(mask[w] > 0.5, score, -1e30)
            grown = jnp.exp(score - jnp.max(score, axis=0, keepdims=True))
            one = grown * (1.0 / jnp.sum(grown, axis=0, keepdims=True))
            probs_o[w, :, 128 * g : 128 * g + 128] = one
            probs.append(one.astype(BF16))
        full = [dot(one, item[4], TN) for item, one in zip(items, probs)]
        return [own_head(one, lane_head).astype(BF16) for one in full]

    def inner(places):
        outs = windows(load_inner(mixed, places))
        for i, (w, rows) in enumerate(places):
            for g in range(4):
                attended_o[rows, COLS[g][0]] = outs[4 * i + g]

    def edge(places):
        outs = windows(load_edge(mixed, low, high, places))
        for i, (m, w, rows, side) in enumerate(places):
            for g in range(4):
                out = outs[4 * i + g]
                attended_o[rows, COLS[g][0]] = out[:16] if side else out[16:]

    window_loop(edge, inner)


def gelu_parts(x):
    size = jnp.abs(x) * (0.5**0.5)
    bell = jnp.exp(-0.5 * x * x)
    t = 1.0 / (1.0 + 0.3275911 * size)
    poly = t * (
        0.254829592
        + t * (-0.284496736 + t * (1.421413741 + t * (-1.453152027 + t * 1.061405429)))
    )
    tail = 0.5 * poly * bell
    share = jnp.where(x >= 0, 1.0 - tail, tail)
    return x * share, share + x * bell * 0.3989422804014327


def before_kernel(cot, down_w, g_act_o):
    for f in range(4):
        cols = slice(512 * f, 512 * f + 512)
        g_act_o[:, cols] = dot(cot[...], down_w[cols, :], NT)


def mlp_kernel(
    core, hidden, attended, cot, g_act, out_w, up_w, vecs, up_b,
    middle_o, act_o, gexp_o, n2t_o, send_o, n2_s,
):
    tile = 256
    blocks = [slice(512 * f, 512 * f + 512) for f in range(4)]

    def forward(i, carry):
        rows = pl.ds(pl.multiple_of(i * tile, tile), tile)
        middle = hidden[rows, :] + dot(attended[rows, :], out_w[...]) + vecs[0:1, :]
        middle_o[rows, :] = middle
        normal, unused = norm_parts(middle)
        normed = (normal * vecs[1:2, :] + vecs[2:3, :]).astype(BF16)
        n2_s[rows, :] = normed
        expand = [dot(normed, up_w[:, cols]) for cols in blocks]
        for cols, one in zip(blocks, expand):
            value, slope = gelu_parts(one + up_b[0:1, cols])
            act_o[rows, cols] = value.astype(BF16)
            gexp_o[rows, cols] = (g_act[rows, cols] * slope).astype(BF16)
        return carry

    lax.fori_loop(0, ALL // tile, forward, 0)
    n2t_o[...] = jnp.transpose(n2_s[...])
    weight_half(1 - core[0], send_o, act_o, gexp_o, n2t_o, cot)


def weight_half(half, out, act, gexp, n2t, cot):
    for b in range(2):
        cols = pl.ds(pl.multiple_of(half * 1024 + 512 * b, 512), 512)
        rows = slice(512 * b, 512 * b + 512)
        out[rows, :] = dot(act[:, cols], cot[...], TN).astype(BF16)
        rows = slice(1024 + 512 * b, 1536 + 512 * b)
        out[rows, :] = dot(n2t[...], gexp[:, cols]).astype(BF16)


def mlp_keep_kernel(core, act, gexp, n2t, cot, keep_o):
    weight_half(core[0], keep_o, act, gexp, n2t, cot)


def mlp_back_kernel(
    middle_i, attended, cot, act, gexp, out_w, up_w, down_w, vecs,
    output_o, gmid_o, gatt_o, gout_o, sums_o, gb_s,
):
    tile = 256
    sums_o[...] = jnp.zeros((8, D), F32)

    def step(i, carry):
        rows = pl.ds(pl.multiple_of(i * tile, tile), tile)
        middle = middle_i[rows, :]
        grad = dot(gexp[rows, :], up_w[...], NT)
        output_o[rows, :] = (middle + vecs[3:4, :] + dot(act[rows, :], down_w[...])).astype(BF16)
        normal, inverse = norm_parts(middle)
        g_float = cot[rows, :].astype(F32)
        g_mid = g_float + norm_back(grad, normal, inverse, vecs[1:2, :])
        gmid_o[rows, :] = g_mid
        g_low = g_mid.astype(BF16)
        gb_s[rows, :] = g_low
        gatt_o[rows, :] = dot(g_low, out_w[...], NT).astype(BF16)
        sums_o[0:1, :] += jnp.sum(g_low.astype(F32), axis=0, keepdims=True)
        sums_o[1:2, :] += jnp.sum(grad * normal, axis=0, keepdims=True)
        sums_o[2:3, :] += jnp.sum(grad, axis=0, keepdims=True)
        sums_o[3:4, :] += jnp.sum(g_float, axis=0, keepdims=True)
        for f in range(4):
            part = gexp[rows, 512 * f : 512 * f + 512].astype(F32)
            sums_o[4 + f : 5 + f, :] += jnp.sum(part, axis=0, keepdims=True)
        return carry

    lax.fori_loop(0, ALL // tile, step, 0)
    gout_o[...] = dot(attended[...], gb_s[...], TN).astype(BF16)


def attend_back_kernel(
    mixed, low, high, probs_i, gatt, heads_i, gmixed_o, low_o, high_o, rim_o
):
    heads = heads_i[...]
    lane_head = iota((32, 128), 1) // 32

    def windows(items):
        q_m = [head_rows(q, heads) for w, g, q, k, v, grad in items]
        g_m = [head_rows(grad, heads) for w, g, q, k, v, grad in items]
        g_probs = [dot(item[4], one, NT) for item, one in zip(items, g_m)]
        low_probs, g_scores = [], []
        for (w, g, *_), g_prob in zip(items, g_probs):
            probs = probs_i[w, :, 128 * g : 128 * g + 128]
            inner = jnp.sum(probs * g_prob, axis=0, keepdims=True)
            g_scores.append((probs * (g_prob - inner)).astype(BF16))
            low_probs.append(probs.astype(BF16))
        d_value = [dot(one, grad) for one, grad in zip(low_probs, g_m)]
        d_key = [dot(one, q) * SCALE for one, q in zip(g_scores, q_m)]
        full = [dot(one, item[3], TN) for item, one in zip(items, g_scores)]
        d_query = [(own_head(one, lane_head) * SCALE).astype(BF16) for one in full]
        return list(zip(d_query, d_key, d_value))

    def inner(places):
        outs = windows(load_inner(mixed, places, gatt))
        for i, (w, rows) in enumerate(places):
            for g in range(4):
                for col, value in zip(COLS[g], outs[4 * i + g]):
                    gmixed_o[rows, col] = value.astype(BF16)

    def edge(places):
        outs = windows(load_edge(mixed, low, high, places, gatt))
        for i, (m, w, rows, side) in enumerate(places):
            out = high_o if side else low_o
            own, far = (slice(0, 16), slice(16, 32)) if side else (slice(16, 32), slice(0, 16))
            for g in range(4):
                cols = COLS[g]
                d_query, d_key, d_value = outs[4 * i + g]
                gmixed_o[rows, cols[0]] = d_query[own]
                rim_o[m, side, :, cols[0]] = d_key[own]
                rim_o[m, side, :, cols[1]] = d_value[own]
                out[m, :, cols[0]] = d_key[far].astype(BF16)
                out[m, :, cols[1]] = d_value[far].astype(BF16)

    window_loop(edge, inner)
    for m in range(MICRO):
        for base in (m * CELLS, m * CELLS + CELLS - 16):
            gmixed_o[base : base + 16, D:] = jnp.zeros((16, 2 * D), BF16)


def leave_kernel(
    core, gmixed, from_low, from_high, rim, hidden, normed, filled, seen, gmid, qkv_w, vecs,
    gout, sums, gm_o, gf_o, small_o, send_o,
):
    small = jnp.zeros((1, D), F32)
    gain_sum, shift_sum, mask_sum, embed_sum, query_sum, value_sum = [small] * 6
    for m in range(MICRO):
        base = m * CELLS
        rows = slice(base, base + CELLS)
        gm_o[rows, :] = gmixed[rows, :]
        gm_o[base : base + 16, D:] = (rim[m, 0] + from_low[m].astype(F32)).astype(BF16)
        gm_o[base + CELLS - 16 : base + CELLS, D:] = (rim[m, 1] + from_high[m].astype(F32)).astype(
            BF16
        )
        gm = gm_o[rows, :]
        grad = dot(gm, qkv_w[...], NT)
        normal, inverse = norm_parts(hidden[rows, :])
        g_hidden = gmid[rows, :] + norm_back(grad, normal, inverse, vecs[2:3, :])
        there = seen[rows, :] > 0.5
        g_low = g_hidden.astype(BF16)
        gf_o[rows, :] = g_low
        gain_sum += jnp.sum(grad * normal, axis=0, keepdims=True)
        shift_sum += jnp.sum(grad, axis=0, keepdims=True)
        mask_sum += jnp.sum(jnp.where(there, 0.0, g_hidden), axis=0, keepdims=True)
        embed_sum += jnp.sum(jnp.where(there, g_low.astype(F32), 0.0), axis=0, keepdims=True)
        query_sum += jnp.sum(gm[:, :D].astype(F32), axis=0, keepdims=True)
        value_sum += jnp.sum(gm[:, 2 * D :].astype(F32), axis=0, keepdims=True)
    small_o[...] = jnp.concatenate(
        [
            embed_sum, mask_sum, gain_sum, shift_sum, query_sum, value_sum,
            small, small, sums[...],
        ],
        axis=0,
    )
    one_half(core[0] != 0, send_o, normed, filled, gm_o, gf_o, gout, small_o)


def one_half(first, out, normed, filled, gm, gf, gout, small):
    @pl.when(first)
    def _():
        turned = jnp.transpose(normed[...])
        for b in range(3):
            cols = slice(512 * b, 512 * b + 512)
            out[cols, :] = dot(turned, gm[:, cols]).astype(BF16)

    @pl.when(jnp.logical_not(first))
    def _():
        out[0:512, :] = gout[...]
        out[512:1280, :] = dot(jnp.transpose(filled[...]), gf[...]).astype(BF16)
        out[1280:1296, :] = small[...].astype(BF16)
        out[1296:1536, :] = jnp.zeros((240, D), BF16)


def leave_keep_kernel(core, gm, gf, small, normed, filled, gout, cell, keep_o, ret_o):
    one_half(core[0] == 0, keep_o, normed, filled, gm, gf, gout, small)
    ret_o[...] = dot(one_hot(iota((GOT, ALL), 1) == cell[...]), gf[...]).astype(BF16)


def return_kernel(dest, came, embed_w, out):
    for m in range(MICRO):
        select = one_hot(iota((dest.shape[1], GOT), 1) == dest[m])
        g_proj = dot(select, came[...]).astype(BF16)
        out[m] = dot(g_proj, embed_w[...], NT).astype(BF16)


def unpack_one_kernel(core, mine, other, down_o, up_o):
    for half, source in ((core[0], mine), (1 - core[0], other)):
        start = pl.multiple_of(half * 1024, 1024)
        down_o[pl.ds(start, 1024), :] = source[0:1024, :].astype(F32)
        for b in range(2):
            up_o[:, pl.ds(start + 512 * b, 512)] = source[
                1024 + 512 * b : 1536 + 512 * b, :
            ].astype(F32)


def unpack_two_kernel(core, mine, other, qkv_o, embed_o, out_o, small_o):
    def write(first, second):
        for b in range(3):
            qkv_o[:, 512 * b : 512 * b + 512] = first[512 * b : 512 * b + 512, :].astype(F32)
        out_o[...] = second[0:512, :].astype(F32)
        embed_o[...] = second[512:1280, :].astype(F32)
        small_o[...] = second[1280:1296, :].astype(F32)

    @pl.when(core[0] == 0)
    def _():
        write(mine, other)

    @pl.when(core[0] != 0)
    def _():
        write(other, mine)


def clip_ident(lengths, rows):
    first = lengths[:, 0:1]
    second = first + lengths[:, 1:2]
    ident = (rows[None, :] >= first).astype(jnp.int32) + (rows[None, :] >= second).astype(jnp.int32)
    start = jnp.where(ident >= 1, first, 0) + jnp.where(ident >= 2, lengths[:, 1:2], 0)
    inside = (rows >= 0) & (rows < LONG)
    return (jnp.where(inside[None, :], ident, -1), rows[None, :] - start)


def position_tables(row_in_clip, width):
    quarter = width // 4
    omega = 1.0 / 10000.0 ** (jnp.arange(quarter, dtype=jnp.float32) / quarter)
    row_angle = row_in_clip.astype(jnp.float32)[..., None] * omega
    freq_angle = jnp.arange(FREQ, dtype=jnp.float32)[:, None] * omega
    row_part = jnp.concatenate([jnp.sin(row_angle), jnp.cos(row_angle)], -1)
    freq_part = jnp.concatenate([jnp.sin(freq_angle), jnp.cos(freq_angle)], -1)
    return row_part.reshape(-1, width // 2), freq_part


def window_mask(ident):
    cells = jnp.repeat(ident.reshape(MICRO * 7, 4), FREQ, axis=1)
    freq = np.tile((np.arange(FREQ) + 2) % 8 // 4, 4)
    same = (cells[:, :, None] == cells[:, None, :]) & (cells[:, :, None] >= 0)
    same = same & jnp.asarray(freq[:, None] == freq[None, :])[None]
    return jnp.tile(same.astype(F32), (1, 1, 4))


def on_device(
    encoded, visible_pos, clip_len, cotangent, embed_weight, embed_bias, mask_token, attn_gain,
    attn_shift, qkv_weight, query_bias, value_bias, out_weight, out_bias, mlp_gain, mlp_shift,
    up_weight, up_bias, down_weight, down_bias,
):
    both = ("clip", "band")
    groups = lax.axis_size("clip")
    bands = lax.axis_size("band")
    band = lax.axis_index("band")
    side = band % 2
    core = side.astype(jnp.int32).reshape(1)
    halves = [
        [c * bands + 2 * x + k for c in range(groups) for x in range(bands // 2)] for k in range(2)
    ]
    swap = [(i, i ^ 1) for i in range(bands)]
    forward = [(i, i + 1) for i in range(bands - 1)]
    backward = [(b, a) for a, b in forward]
    chips = groups * bands // 2

    def to_all(block):
        return lax.all_to_all(
            block, both, split_axis=0, concat_axis=0, tiled=True, axis_index_groups=halves
        )

    def chip_sum(keep, other):
        mine = (keep.astype(F32) + other.astype(F32)).astype(BF16)
        return mine.reshape(chips, -1, D)

    def total(parts):
        return jnp.sum(parts.astype(F32), 0).astype(BF16)

    def spread(chunk):
        return jnp.broadcast_to(chunk[None], (chips,) + chunk.shape)

    vis = visible_pos.shape[1]
    packed, dest = call(
        pack_kernel, "pack", [((GOT, ENC), BF16), ((MICRO, vis, 1), jnp.int32)],
        (band.astype(jnp.int32).reshape(1), visible_pos, encoded), smem=1,
        flops=GOT * MICRO * vis * ENC * 2,
    )
    cot = cotangent.reshape(ALL, D)
    (g_act,) = call(
        before_kernel, "before", [((ALL, FF), F32)], (cot, down_weight), flops=2 * ALL * D * FF,
    )
    got = lax.all_to_all(
        packed.reshape(SRC, BLK, ENC), "clip", split_axis=0, concat_axis=0, tiled=True
    ).reshape(GOT, ENC)

    place = np.arange(GOT)
    within = place % BLK
    index = np.zeros((8, GOT), np.int32)
    index[0], index[1], index[2] = place // BLK, within, np.where(within < 36, within // CAP, 99)
    heads = jnp.asarray(np.arange(128)[None, :] // 32 == np.arange(16)[:, None] % 4, BF16)

    unused, row_in_clip = clip_ident(clip_len[:, 0], band * ROWS + jnp.arange(ROWS))
    row_table, freq_table = position_tables(row_in_clip, D)
    ident_ext, unused = clip_ident(clip_len[:, 0], band * ROWS - 2 + jnp.arange(ROWS + 4))
    mask = window_mask(ident_ext)
    zero = jnp.zeros((D,), BF16)
    vecs_one = jnp.stack([embed_bias, mask_token, attn_gain, attn_shift] * 2).astype(F32)
    vecs_two = jnp.stack([out_bias, mlp_gain, mlp_shift, down_bias] * 2).astype(F32)
    qkv_b = jnp.concatenate([query_bias, zero, value_bias]).astype(F32)[None]
    up_b = up_bias.astype(F32)[None]

    hidden, normed, mixed, filled, seen, cell, low, high = call(
        enter_kernel, "enter",
        [
            ((ALL, D), F32), ((ALL, D), BF16), ((ALL, 3 * D), BF16), ((ALL, ENC), BF16),
            ((ALL, 1), F32), ((GOT, 1), jnp.int32),
            ((MICRO, 16, 2 * D), BF16), ((MICRO, 16, 2 * D), BF16),
        ],
        (
            jnp.asarray(index), jnp.asarray(np.ascontiguousarray(index.T)), got, row_table,
            freq_table, embed_weight, qkv_weight, vecs_one, qkv_b,
        ),
        scratch=[
            pltpu.VMEM((GOT, ENC), BF16), pltpu.VMEM((ENC, D), BF16), pltpu.VMEM((D, 3 * D), BF16),
            pltpu.SemaphoreType.DMA((3,)),
        ],
        far=(2, 5, 6),
        flops=2 * ALL * (GOT * ENC + ENC * D + 3 * D * D),
    )
    from_low = lax.ppermute(high, "band", forward)
    from_high = lax.ppermute(low, "band", backward)
    attended, probs = call(
        attend_kernel, "attend",
        [((ALL, D), BF16), ((MICRO * 7, 32, D), F32)],
        (mixed, from_low, from_high, mask, heads),
        flops=MICRO * 7 * 4 * 2**20,
    )
    middle, act, gexp, n2t, send = call(
        mlp_kernel, "mlp",
        [
            ((ALL, D), F32), ((ALL, FF), BF16), ((ALL, FF), BF16), ((D, ALL), BF16),
            ((FF, D), BF16),
        ],
        (core, hidden, attended, cot, g_act, out_weight, up_weight, vecs_two, up_b),
        scratch=[pltpu.VMEM((ALL, D), BF16)],
        smem=1, flops=2 * ALL * (2 * D * FF + D * D), vmem=24,
    )
    (keep,) = call(
        mlp_keep_kernel, "mlp_keep", [((FF, D), BF16)], (core, act, gexp, n2t, cot),
        smem=1, flops=2 * ALL * D * FF,
    )
    chip_one = chip_sum(keep, lax.ppermute(send, "band", swap))
    output, gmid, gatt, gout, sums = call(
        mlp_back_kernel, "mlp_back",
        [
            ((ALL, D), BF16), ((ALL, D), F32), ((ALL, D), BF16), ((D, D), BF16), ((8, D), F32),
        ],
        (middle, attended, cot, act, gexp, out_weight, up_weight, down_weight, vecs_two),
        scratch=[pltpu.VMEM((ALL, D), BF16)],
        flops=2 * ALL * (2 * D * FF + 2 * D * D), vmem=24,
    )
    gmixed, low, high, rim = call(
        attend_back_kernel, "attend_back",
        [
            ((ALL, 3 * D), BF16), ((MICRO, 16, 2 * D), BF16), ((MICRO, 16, 2 * D), BF16),
            ((MICRO, 2, 16, 2 * D), F32),
        ],
        (mixed, from_low, from_high, probs, gatt, heads),
        flops=MICRO * 7 * 4 * 2**22,
    )
    chip_one, low, high = lax.optimization_barrier((chip_one, low, high))
    from_low = lax.ppermute(high, "band", forward)
    from_high = lax.ppermute(low, "band", backward)
    total_one = total(to_all(chip_one))
    total_one, from_low, from_high = lax.optimization_barrier((total_one, from_low, from_high))
    mine_one = lax.all_gather(total_one, both, axis=0, axis_index_groups=halves).reshape(-1, D)
    gm, gf, small, send = call(
        leave_kernel, "leave",
        [((ALL, 3 * D), BF16), ((ALL, D), BF16), ((16, D), F32), ((3 * D, D), BF16)],
        (
            core, gmixed, from_low, from_high, rim, hidden, normed, filled, seen, gmid,
            qkv_weight, vecs_one, gout, sums,
        ),
        smem=1, flops=2 * ALL * 5 * D * D,
    )
    other = lax.ppermute(send, "band", swap)
    keep, returned = call(
        leave_keep_kernel, "leave_keep", [((3 * D, D), BF16), ((GOT, D), BF16)],
        (core, gm, gf, small, normed, filled, gout, cell),
        smem=1, flops=2 * ALL * (2 * D * D + GOT * D),
    )
    mine = to_all(spread(total(to_all(chip_sum(keep, other))))).reshape(-1, D)
    mine, returned = lax.optimization_barrier((mine, returned))
    came = lax.all_to_all(
        returned.reshape(SRC, BLK, D), "clip", split_axis=0, concat_axis=0, tiled=True
    ).reshape(GOT, D)
    qkv, g_embed, g_out, small = call(
        unpack_two_kernel, "unpack_two",
        [((D, 3 * D), F32), ((ENC, D), F32), ((D, D), F32), ((16, D), F32)],
        (core, mine, lax.ppermute(mine, "band", swap)), smem=1,
    )
    came, small = lax.optimization_barrier((came, small))
    mine_one, came = lax.optimization_barrier((mine_one, came))
    down, up = call(
        unpack_one_kernel, "unpack_one", [((FF, D), F32), ((D, FF), F32)],
        (core, mine_one, lax.ppermute(mine_one, "band", swap)), smem=1,
    )
    (grad_enc,) = call(
        return_kernel, "return", [((MICRO, vis, ENC), BF16)], (dest, came, embed_weight),
        flops=2 * MICRO * vis * D * (GOT + ENC),
    )
    return (
        output.reshape(cotangent.shape), grad_enc, g_embed, small[0], small[1], small[2],
        small[3], qkv, small[4], small[5], g_out, small[8], small[9], small[10], up,
        small[12:16].reshape(FF), down, small[11],
    )


def solution(mesh):
    whole = P()
    return jax.shard_map(
        on_device,
        mesh=mesh,
        in_specs=(
            P(None, ("clip", "band"), None),
            P(None, ("clip", "band")),
            P(None, "clip", None),
            P(None, "clip", "band", None, None),
        )
        + (whole,) * 16,
        out_specs=(P(None, "clip", "band", None, None), P(None, ("clip", "band"), None))
        + (whole,) * 16,
        check_vma=False,
    )
```

```python
import jax
import jax.numpy as jnp
import numpy as np
from jax import lax
from jax.experimental import pallas as pl
from jax.experimental.pallas import tpu as pltpu
from jax.sharding import PartitionSpec as P

HEADS = 16
FREQ = 8
LONG = 192
MICRO = 4
ROWS = 24
CELLS = ROWS * FREQ
ALL = MICRO * CELLS
CAP = 9
BLK = 40
SRC = 16
GOT = SRC * BLK
D = 512
FF = 2048
ENC = 768
EPS = 1e-06
SCALE = (D // HEADS) ** (-0.5)
F32 = jnp.float32
BF16 = jnp.bfloat16

NN = (((1,), (0,)), ((), ()))
NT = (((1,), (1,)), ((), ()))
TN = (((0,), (0,)), ((), ()))


def dot(left, right, dims=NN):
    return lax.dot_general(left, right, dims, preferred_element_type=F32)


def iota(shape, dim):
    return lax.broadcasted_iota(jnp.int32, shape, dim)


def one_hot(hit):
    return jnp.where(hit, 1.0, 0.0).astype(BF16)


def call(kernel, name, out_shape, args, scratch=(), smem=0, flops=0, vmem=16, far=()):
    spaces = [pltpu.SMEM] * smem + [pltpu.VMEM] * (len(args) - smem)
    for i in far:
        spaces[i] = pltpu.HBM
    outs = [jax.ShapeDtypeStruct(shape, dtype) for shape, dtype in out_shape]
    size = sum(a.size * a.dtype.itemsize for a in args) + sum(
        o.size * o.dtype.itemsize for o in outs
    )
    return pl.pallas_call(
        kernel,
        name=name,
        out_shape=outs,
        in_specs=[pl.BlockSpec(memory_space=space) for space in spaces],
        out_specs=[pl.BlockSpec(memory_space=pltpu.VMEM)] * len(outs),
        scratch_shapes=list(scratch),
        compiler_params=pltpu.CompilerParams(vmem_limit_bytes=vmem * 2**20),
        cost_estimate=pl.CostEstimate(flops=flops, bytes_accessed=size, transcendentals=0),
    )(*args)


def pack_kernel(band, pos, enc, out, dest):
    count = pos.shape[1]
    low = iota((count, count), 0)
    high = iota((count, count), 1)
    packed = jnp.zeros((GOT, ENC), F32)
    places = jnp.zeros((SRC, 128), F32)
    for m in range(MICRO):
        cell_r = pos[m : m + 1, :]
        cell_c = jnp.sum(jnp.where(low == high, cell_r, 0), axis=1, keepdims=True)
        slot = LONG * FREQ
        dev_r = jnp.sum(
            jnp.where(cell_r >= slot * iota((SRC, count), 0) + slot, 1, 0), axis=0, keepdims=True
        )
        dev_c = jnp.sum(
            jnp.where(cell_c >= slot * iota((count, SRC), 1) + slot, 1, 0), axis=1, keepdims=True
        )
        same = dev_c == dev_r
        rank_r = jnp.sum(jnp.where(same & (low < high), 1, 0), axis=0, keepdims=True)
        rank_c = jnp.sum(jnp.where(same & (high < low), 1, 0), axis=1, keepdims=True)
        dest[m] = dev_c * BLK + m * CAP + rank_c
        select = one_hot(iota((GOT, count), 0) == dev_r * BLK + m * CAP + rank_r)
        packed = packed + dot(select, enc[m])
        number = cell_r - dev_r * slot - band[0] * CELLS + 1
        to_dev = jnp.where(iota((SRC, count), 0) == dev_r, number.astype(F32), 0.0).astype(BF16)
        to_lane = one_hot(iota((count, 128), 1) == m * CAP + rank_c)
        places = places + dot(to_dev, to_lane)
    spread = one_hot(iota((GOT, SRC), 0) == iota((GOT, SRC), 1) * BLK + (BLK - 4))
    out[:, :128] = (packed[:, :128] + dot(spread, places.astype(BF16))).astype(BF16)
    out[:, 128:] = packed[:, 128:].astype(BF16)


def norm_parts(values):
    center = values - jnp.mean(values, -1, keepdims=True)
    inverse = lax.rsqrt(jnp.mean(center * center, -1, keepdims=True) + EPS)
    return center * inverse, inverse


def norm_back(grad, normal, inverse, gain):
    scaled = grad * gain
    return inverse * (
        scaled
        - jnp.mean(scaled, -1, keepdims=True)
        - normal * jnp.mean(scaled * normal, -1, keepdims=True)
    )


def fetch(pairs, sems):
    copies = [pltpu.make_async_copy(far, near, sems.at[i]) for i, (far, near) in enumerate(pairs)]
    for copy in copies:
        copy.start()
    return copies


def enter_kernel(
    idx_r, idx_c, got_i, row_table, freq_table, embed_i, qkv_i, vecs, qkv_b,
    hidden_o, normed_o, mixed_o, filled_o, seen_o, cell_o, low_o, high_o,
    got, embed_w, qkv_w, sems,
):
    copies = fetch([(got_i, got), (embed_i, embed_w), (qkv_i, qkv_w)], sems)
    copies[0].wait()
    hit = one_hot(iota((SRC, GOT), 1) == iota((SRC, GOT), 0) * BLK + (BLK - 4))
    numbers = dot(hit, got[:, :128]).astype(BF16)
    spread_r = dot(numbers, one_hot(iota((SRC, GOT), 0) == idx_r[0:1, :]), TN)
    value_r = jnp.sum(
        jnp.where(iota((128, GOT), 0) == idx_r[1:2, :], spread_r, 0.0), axis=0, keepdims=True
    )
    cell_r = jnp.where(
        value_r > 0.5, idx_r[2:3, :] * CELLS + value_r.astype(jnp.int32) - 1, -1
    )
    spread_c = dot(one_hot(iota((GOT, SRC), 1) == idx_c[:, 0:1]), numbers)
    value_c = jnp.sum(
        jnp.where(iota((GOT, 128), 1) == idx_c[:, 1:2], spread_c, 0.0), axis=1, keepdims=True
    )
    cell_o[...] = jnp.where(
        value_c > 0.5, idx_c[:, 2:3] * CELLS + value_c.astype(jnp.int32) - 1, -1
    )
    for m in range(MICRO):
        rows = slice(m * CELLS, (m + 1) * CELLS)
        match = jnp.where(iota((CELLS, GOT), 0) + m * CELLS == cell_r, 1.0, 0.0)
        seen = jnp.sum(match, axis=1, keepdims=True)
        filled = dot(match.astype(BF16), got[...]).astype(BF16)
        filled_o[rows, :] = filled
        seen_o[rows, :] = seen
    copies[1].wait()
    copies[2].wait()
    freq = jnp.broadcast_to(freq_table[...][None], (ROWS, FREQ, D // 2)).reshape(CELLS, D // 2)
    for m in range(MICRO):
        rows = slice(m * CELLS, (m + 1) * CELLS)
        seen = seen_o[rows, :]
        proj = (dot(filled_o[rows, :], embed_w[...]) + vecs[0:1, :]).astype(BF16).astype(F32)
        line = row_table[m * ROWS : (m + 1) * ROWS, :]
        line = jnp.broadcast_to(line[:, None, :], (ROWS, FREQ, D // 2)).reshape(CELLS, D // 2)
        table = jnp.concatenate([line, freq], axis=1)
        hidden = jnp.where(seen > 0.5, proj, vecs[1:2, :]) + table
        hidden_o[rows, :] = hidden
        normal, unused = norm_parts(hidden)
        normed = (normal * vecs[2:3, :] + vecs[3:4, :]).astype(BF16)
        normed_o[rows, :] = normed
        mixed = (dot(normed, qkv_w[...]) + qkv_b[...]).astype(BF16)
        mixed_o[rows, :] = mixed
        low_o[m] = mixed[:16, D:]
        high_o[m] = mixed[CELLS - 16 :, D:]


def head_rows(block, heads):
    return jnp.concatenate([block * heads[h : h + 1, :] for h in range(4)], axis=0)


def own_head(full, lane_head):
    out = full[0:32, :]
    for h in range(1, 4):
        out = jnp.where(lane_head == h, full[32 * h : 32 * h + 32, :], out)
    return out


def window_loop(edge, inner):
    def inside(p, carry):
        places = []
        for m in range(MICRO):
            base = pl.multiple_of(m * CELLS + 32 * p - 16, 16)
            places.append((m * 7 + p, pl.ds(base, 32)))
        inner(places)
        return carry

    def ends(i, carry):
        places = []
        for j in range(2):
            m = 2 * i + j
            first = pl.multiple_of(m * CELLS, 16)
            last = pl.multiple_of(m * CELLS + CELLS - 16, 16)
            places.append((m, m * 7, pl.ds(first, 16), 0))
            places.append((m, m * 7 + 6, pl.ds(last, 16), 1))
        edge(places)
        return carry

    lax.fori_loop(1, 6, inside, 0)
    lax.fori_loop(0, MICRO // 2, ends, 0)


def with_halo(own, halo, side):
    return jnp.concatenate([own, halo] if side else [halo, own], axis=0)


COLS = [[slice(D * i + 128 * g, D * i + 128 * g + 128) for i in range(3)] for g in range(4)]


def load_inner(mixed, places, grads=None):
    items = []
    for w, rows in places:
        for g in range(4):
            item = [mixed[rows, c] for c in COLS[g]]
            items.append((w, g, *item, None if grads is None else grads[rows, COLS[g][0]]))
    return items


def load_edge(mixed, low, high, places, grads=None):
    zero = jnp.zeros((16, 128), BF16)
    items = []
    for m, w, rows, side in places:
        halo = high if side else low
        for g in range(4):
            cols = COLS[g]
            q = with_halo(mixed[rows, cols[0]], zero, side)
            k = with_halo(mixed[rows, cols[1]], halo[m, :, cols[0]], side)
            v = with_halo(mixed[rows, cols[2]], halo[m, :, cols[1]], side)
            grad = None if grads is None else with_halo(grads[rows, cols[0]], zero, side)
            items.append((w, g, q, k, v, grad))
    return items


def attend_kernel(mixed, low, high, mask, heads_i, attended_o, probs_o):
    heads = heads_i[...]
    lane_head = iota((32, 128), 1) // 32

    def windows(items):
        scores = [dot(k, head_rows(q, heads), NT) * SCALE for w, g, q, k, v, _ in items]
        probs = []
        for (w, g, *_), score in zip(items, scores):
            score = jnp.where(mask[w] > 0.5, score, -1e30)
            grown = jnp.exp(score - jnp.max(score, axis=0, keepdims=True))
            one = grown * (1.0 / jnp.sum(grown, axis=0, keepdims=True))
            probs_o[w, :, 128 * g : 128 * g + 128] = one
            probs.append(one.astype(BF16))
        full = [dot(one, item[4], TN) for item, one in zip(items, probs)]
        return [own_head(one, lane_head).astype(BF16) for one in full]

    def inner(places):
        outs = windows(load_inner(mixed, places))
        for i, (w, rows) in enumerate(places):
            for g in range(4):
                attended_o[rows, COLS[g][0]] = outs[4 * i + g]

    def edge(places):
        outs = windows(load_edge(mixed, low, high, places))
        for i, (m, w, rows, side) in enumerate(places):
            for g in range(4):
                out = outs[4 * i + g]
                attended_o[rows, COLS[g][0]] = out[:16] if side else out[16:]

    window_loop(edge, inner)


def gelu_parts(x):
    size = jnp.abs(x) * (0.5**0.5)
    bell = jnp.exp(-0.5 * x * x)
    t = 1.0 / (1.0 + 0.3275911 * size)
    poly = t * (
        0.254829592
        + t * (-0.284496736 + t * (1.421413741 + t * (-1.453152027 + t * 1.061405429)))
    )
    tail = 0.5 * poly * bell
    share = jnp.where(x >= 0, 1.0 - tail, tail)
    return x * share, share + x * bell * 0.3989422804014327


def before_kernel(cot, down_w, g_act_o):
    for f in range(4):
        cols = slice(512 * f, 512 * f + 512)
        g_act_o[:, cols] = dot(cot[...], down_w[cols, :], NT)


def mlp_kernel(
    core, hidden, attended, cot, g_act, out_w, up_w, vecs, up_b,
    middle_o, act_o, gexp_o, n2t_o, send_o, n2_s,
):
    tile = 256
    blocks = [slice(512 * f, 512 * f + 512) for f in range(4)]

    def forward(i, carry):
        rows = pl.ds(pl.multiple_of(i * tile, tile), tile)
        middle = hidden[rows, :] + dot(attended[rows, :], out_w[...]) + vecs[0:1, :]
        middle_o[rows, :] = middle
        normal, unused = norm_parts(middle)
        normed = (normal * vecs[1:2, :] + vecs[2:3, :]).astype(BF16)
        n2_s[rows, :] = normed
        expand = [dot(normed, up_w[:, cols]) for cols in blocks]
        for cols, one in zip(blocks, expand):
            value, slope = gelu_parts(one + up_b[0:1, cols])
            act_o[rows, cols] = value.astype(BF16)
            gexp_o[rows, cols] = (g_act[rows, cols] * slope).astype(BF16)
        return carry

    lax.fori_loop(0, ALL // tile, forward, 0)
    n2t_o[...] = jnp.transpose(n2_s[...])
    weight_half(1 - core[0], send_o, act_o, gexp_o, n2t_o, cot)


def weight_half(half, out, act, gexp, n2t, cot):
    for b in range(2):
        cols = pl.ds(pl.multiple_of(half * 1024 + 512 * b, 512), 512)
        rows = slice(512 * b, 512 * b + 512)
        out[rows, :] = dot(act[:, cols], cot[...], TN).astype(BF16)
        rows = slice(1024 + 512 * b, 1536 + 512 * b)
        out[rows, :] = dot(n2t[...], gexp[:, cols]).astype(BF16)


def mlp_keep_kernel(core, act, gexp, n2t, cot, keep_o):
    weight_half(core[0], keep_o, act, gexp, n2t, cot)


def mlp_back_kernel(
    middle_i, attended, cot, act, gexp, out_w, up_w, down_w, vecs,
    output_o, gmid_o, gatt_o, gout_o, sums_o, gb_s,
):
    tile = 256
    sums_o[...] = jnp.zeros((8, D), F32)

    def step(i, carry):
        rows = pl.ds(pl.multiple_of(i * tile, tile), tile)
        middle = middle_i[rows, :]
        grad = dot(gexp[rows, :], up_w[...], NT)
        output_o[rows, :] = (middle + vecs[3:4, :] + dot(act[rows, :], down_w[...])).astype(BF16)
        normal, inverse = norm_parts(middle)
        g_float = cot[rows, :].astype(F32)
        g_mid = g_float + norm_back(grad, normal, inverse, vecs[1:2, :])
        gmid_o[rows, :] = g_mid
        g_low = g_mid.astype(BF16)
        gb_s[rows, :] = g_low
        gatt_o[rows, :] = dot(g_low, out_w[...], NT).astype(BF16)
        sums_o[0:1, :] += jnp.sum(g_low.astype(F32), axis=0, keepdims=True)
        sums_o[1:2, :] += jnp.sum(grad * normal, axis=0, keepdims=True)
        sums_o[2:3, :] += jnp.sum(grad, axis=0, keepdims=True)
        sums_o[3:4, :] += jnp.sum(g_float, axis=0, keepdims=True)
        for f in range(4):
            part = gexp[rows, 512 * f : 512 * f + 512].astype(F32)
            sums_o[4 + f : 5 + f, :] += jnp.sum(part, axis=0, keepdims=True)
        return carry

    lax.fori_loop(0, ALL // tile, step, 0)
    gout_o[...] = dot(attended[...], gb_s[...], TN).astype(BF16)


def attend_back_kernel(
    mixed, low, high, probs_i, gatt, heads_i, gmixed_o, low_o, high_o, rim_o
):
    heads = heads_i[...]
    lane_head = iota((32, 128), 1) // 32

    def windows(items):
        q_m = [head_rows(q, heads) for w, g, q, k, v, grad in items]
        g_m = [head_rows(grad, heads) for w, g, q, k, v, grad in items]
        g_probs = [dot(item[4], one, NT) for item, one in zip(items, g_m)]
        low_probs, g_scores = [], []
        for (w, g, *_), g_prob in zip(items, g_probs):
            probs = probs_i[w, :, 128 * g : 128 * g + 128]
            inner = jnp.sum(probs * g_prob, axis=0, keepdims=True)
            g_scores.append((probs * (g_prob - inner)).astype(BF16))
            low_probs.append(probs.astype(BF16))
        d_value = [dot(one, grad) for one, grad in zip(low_probs, g_m)]
        d_key = [dot(one, q) * SCALE for one, q in zip(g_scores, q_m)]
        full = [dot(one, item[3], TN) for item, one in zip(items, g_scores)]
        d_query = [(own_head(one, lane_head) * SCALE).astype(BF16) for one in full]
        return list(zip(d_query, d_key, d_value))

    def inner(places):
        outs = windows(load_inner(mixed, places, gatt))
        for i, (w, rows) in enumerate(places):
            for g in range(4):
                for col, value in zip(COLS[g], outs[4 * i + g]):
                    gmixed_o[rows, col] = value.astype(BF16)

    def edge(places):
        outs = windows(load_edge(mixed, low, high, places, gatt))
        for i, (m, w, rows, side) in enumerate(places):
            out = high_o if side else low_o
            own, far = (slice(0, 16), slice(16, 32)) if side else (slice(16, 32), slice(0, 16))
            for g in range(4):
                cols = COLS[g]
                d_query, d_key, d_value = outs[4 * i + g]
                gmixed_o[rows, cols[0]] = d_query[own]
                rim_o[m, side, :, cols[0]] = d_key[own]
                rim_o[m, side, :, cols[1]] = d_value[own]
                out[m, :, cols[0]] = d_key[far].astype(BF16)
                out[m, :, cols[1]] = d_value[far].astype(BF16)

    window_loop(edge, inner)
    for m in range(MICRO):
        for base in (m * CELLS, m * CELLS + CELLS - 16):
            gmixed_o[base : base + 16, D:] = jnp.zeros((16, 2 * D), BF16)


def leave_kernel(
    core, gmixed, from_low, from_high, rim, hidden, normed, filled, seen, gmid, qkv_w, vecs,
    gout, sums, gm_o, gf_o, small_o, send_o,
):
    small = jnp.zeros((1, D), F32)
    gain_sum, shift_sum, mask_sum, embed_sum, query_sum, value_sum = [small] * 6
    for m in range(MICRO):
        base = m * CELLS
        rows = slice(base, base + CELLS)
        gm_o[rows, :] = gmixed[rows, :]
        gm_o[base : base + 16, D:] = (rim[m, 0] + from_low[m].astype(F32)).astype(BF16)
        gm_o[base + CELLS - 16 : base + CELLS, D:] = (rim[m, 1] + from_high[m].astype(F32)).astype(
            BF16
        )
        gm = gm_o[rows, :]
        grad = dot(gm, qkv_w[...], NT)
        normal, inverse = norm_parts(hidden[rows, :])
        g_hidden = gmid[rows, :] + norm_back(grad, normal, inverse, vecs[2:3, :])
        there = seen[rows, :] > 0.5
        g_low = g_hidden.astype(BF16)
        gf_o[rows, :] = g_low
        gain_sum += jnp.sum(grad * normal, axis=0, keepdims=True)
        shift_sum += jnp.sum(grad, axis=0, keepdims=True)
        mask_sum += jnp.sum(jnp.where(there, 0.0, g_hidden), axis=0, keepdims=True)
        embed_sum += jnp.sum(jnp.where(there, g_low.astype(F32), 0.0), axis=0, keepdims=True)
        query_sum += jnp.sum(gm[:, :D].astype(F32), axis=0, keepdims=True)
        value_sum += jnp.sum(gm[:, 2 * D :].astype(F32), axis=0, keepdims=True)
    small_o[...] = jnp.concatenate(
        [
            embed_sum, mask_sum, gain_sum, shift_sum, query_sum, value_sum,
            small, small, sums[...],
        ],
        axis=0,
    )
    one_half(core[0] != 0, send_o, normed, filled, gm_o, gf_o, gout, small_o)


def one_half(first, out, normed, filled, gm, gf, gout, small):
    @pl.when(first)
    def _():
        turned = jnp.transpose(normed[...])
        for b in range(3):
            cols = slice(512 * b, 512 * b + 512)
            out[cols, :] = dot(turned, gm[:, cols]).astype(BF16)

    @pl.when(jnp.logical_not(first))
    def _():
        out[0:512, :] = gout[...]
        out[512:1280, :] = dot(jnp.transpose(filled[...]), gf[...]).astype(BF16)
        out[1280:1296, :] = small[...].astype(BF16)
        out[1296:1536, :] = jnp.zeros((240, D), BF16)


def leave_keep_kernel(core, gm, gf, small, normed, filled, gout, cell, keep_o, ret_o):
    one_half(core[0] == 0, keep_o, normed, filled, gm, gf, gout, small)
    ret_o[...] = dot(one_hot(iota((GOT, ALL), 1) == cell[...]), gf[...]).astype(BF16)


def return_kernel(dest, came, embed_w, out):
    for m in range(MICRO):
        select = one_hot(iota((dest.shape[1], GOT), 1) == dest[m])
        g_proj = dot(select, came[...]).astype(BF16)
        out[m] = dot(g_proj, embed_w[...], NT).astype(BF16)


def unpack_one_kernel(core, mine, other, down_o, up_o):
    for half, source in ((core[0], mine), (1 - core[0], other)):
        start = pl.multiple_of(half * 1024, 1024)
        down_o[pl.ds(start, 1024), :] = source[0:1024, :].astype(F32)
        for b in range(2):
            up_o[:, pl.ds(start + 512 * b, 512)] = source[
                1024 + 512 * b : 1536 + 512 * b, :
            ].astype(F32)


def unpack_two_kernel(core, mine, other, qkv_o, embed_o, out_o, small_o):
    def write(first, second):
        for b in range(3):
            qkv_o[:, 512 * b : 512 * b + 512] = first[512 * b : 512 * b + 512, :].astype(F32)
        out_o[...] = second[0:512, :].astype(F32)
        embed_o[...] = second[512:1280, :].astype(F32)
        small_o[...] = second[1280:1296, :].astype(F32)

    @pl.when(core[0] == 0)
    def _():
        write(mine, other)

    @pl.when(core[0] != 0)
    def _():
        write(other, mine)


def clip_ident(lengths, rows):
    first = lengths[:, 0:1]
    second = first + lengths[:, 1:2]
    ident = (rows[None, :] >= first).astype(jnp.int32) + (rows[None, :] >= second).astype(jnp.int32)
    start = jnp.where(ident >= 1, first, 0) + jnp.where(ident >= 2, lengths[:, 1:2], 0)
    inside = (rows >= 0) & (rows < LONG)
    return (jnp.where(inside[None, :], ident, -1), rows[None, :] - start)


def position_tables(row_in_clip, width):
    quarter = width // 4
    omega = 1.0 / 10000.0 ** (jnp.arange(quarter, dtype=jnp.float32) / quarter)
    row_angle = row_in_clip.astype(jnp.float32)[..., None] * omega
    freq_angle = jnp.arange(FREQ, dtype=jnp.float32)[:, None] * omega
    row_part = jnp.concatenate([jnp.sin(row_angle), jnp.cos(row_angle)], -1)
    freq_part = jnp.concatenate([jnp.sin(freq_angle), jnp.cos(freq_angle)], -1)
    return row_part.reshape(-1, width // 2), freq_part


def window_mask(ident):
    cells = jnp.repeat(ident.reshape(MICRO * 7, 4), FREQ, axis=1)
    freq = np.tile((np.arange(FREQ) + 2) % 8 // 4, 4)
    same = (cells[:, :, None] == cells[:, None, :]) & (cells[:, :, None] >= 0)
    same = same & jnp.asarray(freq[:, None] == freq[None, :])[None]
    return jnp.tile(same.astype(F32), (1, 1, 4))


def on_device(
    encoded, visible_pos, clip_len, cotangent, embed_weight, embed_bias, mask_token, attn_gain,
    attn_shift, qkv_weight, query_bias, value_bias, out_weight, out_bias, mlp_gain, mlp_shift,
    up_weight, up_bias, down_weight, down_bias,
):
    both = ("clip", "band")
    groups = lax.axis_size("clip")
    bands = lax.axis_size("band")
    band = lax.axis_index("band")
    side = band % 2
    core = side.astype(jnp.int32).reshape(1)
    halves = [
        [c * bands + 2 * x + k for c in range(groups) for x in range(bands // 2)] for k in range(2)
    ]
    swap = [(i, i ^ 1) for i in range(bands)]
    forward = [(i, i + 1) for i in range(bands - 1)]
    backward = [(b, a) for a, b in forward]
    chips = groups * bands // 2

    def to_all(block):
        return lax.all_to_all(
            block, both, split_axis=0, concat_axis=0, tiled=True, axis_index_groups=halves
        )

    def chip_sum(keep, other):
        mine = (keep.astype(F32) + other.astype(F32)).astype(BF16)
        return mine.reshape(chips, -1, D)

    def total(parts):
        return jnp.sum(parts.astype(F32), 0).astype(BF16)

    def spread(chunk):
        return jnp.broadcast_to(chunk[None], (chips,) + chunk.shape)

    vis = visible_pos.shape[1]
    packed, dest = call(
        pack_kernel, "pack", [((GOT, ENC), BF16), ((MICRO, vis, 1), jnp.int32)],
        (band.astype(jnp.int32).reshape(1), visible_pos, encoded), smem=1,
        flops=GOT * MICRO * vis * ENC * 2,
    )
    cot = cotangent.reshape(ALL, D)
    (g_act,) = call(
        before_kernel, "before", [((ALL, FF), F32)], (cot, down_weight), flops=2 * ALL * D * FF,
    )
    got = lax.all_to_all(
        packed.reshape(SRC, BLK, ENC), "clip", split_axis=0, concat_axis=0, tiled=True
    ).reshape(GOT, ENC)

    place = np.arange(GOT)
    within = place % BLK
    index = np.zeros((8, GOT), np.int32)
    index[0], index[1], index[2] = place // BLK, within, np.where(within < 36, within // CAP, 99)
    heads = jnp.asarray(np.arange(128)[None, :] // 32 == np.arange(16)[:, None] % 4, BF16)

    unused, row_in_clip = clip_ident(clip_len[:, 0], band * ROWS + jnp.arange(ROWS))
    row_table, freq_table = position_tables(row_in_clip, D)
    ident_ext, unused = clip_ident(clip_len[:, 0], band * ROWS - 2 + jnp.arange(ROWS + 4))
    mask = window_mask(ident_ext)
    zero = jnp.zeros((D,), BF16)
    vecs_one = jnp.stack([embed_bias, mask_token, attn_gain, attn_shift] * 2).astype(F32)
    vecs_two = jnp.stack([out_bias, mlp_gain, mlp_shift, down_bias] * 2).astype(F32)
    qkv_b = jnp.concatenate([query_bias, zero, value_bias]).astype(F32)[None]
    up_b = up_bias.astype(F32)[None]

    hidden, normed, mixed, filled, seen, cell, low, high = call(
        enter_kernel, "enter",
        [
            ((ALL, D), F32), ((ALL, D), BF16), ((ALL, 3 * D), BF16), ((ALL, ENC), BF16),
            ((ALL, 1), F32), ((GOT, 1), jnp.int32),
            ((MICRO, 16, 2 * D), BF16), ((MICRO, 16, 2 * D), BF16),
        ],
        (
            jnp.asarray(index), jnp.asarray(np.ascontiguousarray(index.T)), got, row_table,
            freq_table, embed_weight, qkv_weight, vecs_one, qkv_b,
        ),
        scratch=[
            pltpu.VMEM((GOT, ENC), BF16), pltpu.VMEM((ENC, D), BF16), pltpu.VMEM((D, 3 * D), BF16),
            pltpu.SemaphoreType.DMA((3,)),
        ],
        far=(2, 5, 6),
        flops=2 * ALL * (GOT * ENC + ENC * D + 3 * D * D),
    )
    from_low = lax.ppermute(high, "band", forward)
    from_high = lax.ppermute(low, "band", backward)
    attended, probs = call(
        attend_kernel, "attend",
        [((ALL, D), BF16), ((MICRO * 7, 32, D), F32)],
        (mixed, from_low, from_high, mask, heads),
        flops=MICRO * 7 * 4 * 2**20,
    )
    middle, act, gexp, n2t, send = call(
        mlp_kernel, "mlp",
        [
            ((ALL, D), F32), ((ALL, FF), BF16), ((ALL, FF), BF16), ((D, ALL), BF16),
            ((FF, D), BF16),
        ],
        (core, hidden, attended, cot, g_act, out_weight, up_weight, vecs_two, up_b),
        scratch=[pltpu.VMEM((ALL, D), BF16)],
        smem=1, flops=2 * ALL * (2 * D * FF + D * D), vmem=24,
    )
    (keep,) = call(
        mlp_keep_kernel, "mlp_keep", [((FF, D), BF16)], (core, act, gexp, n2t, cot),
        smem=1, flops=2 * ALL * D * FF,
    )
    chip_one = chip_sum(keep, lax.ppermute(send, "band", swap))
    output, gmid, gatt, gout, sums = call(
        mlp_back_kernel, "mlp_back",
        [
            ((ALL, D), BF16), ((ALL, D), F32), ((ALL, D), BF16), ((D, D), BF16), ((8, D), F32),
        ],
        (middle, attended, cot, act, gexp, out_weight, up_weight, down_weight, vecs_two),
        scratch=[pltpu.VMEM((ALL, D), BF16)],
        flops=2 * ALL * (2 * D * FF + 2 * D * D), vmem=24,
    )
    gmixed, low, high, rim = call(
        attend_back_kernel, "attend_back",
        [
            ((ALL, 3 * D), BF16), ((MICRO, 16, 2 * D), BF16), ((MICRO, 16, 2 * D), BF16),
            ((MICRO, 2, 16, 2 * D), F32),
        ],
        (mixed, from_low, from_high, probs, gatt, heads),
        flops=MICRO * 7 * 4 * 2**22,
    )
    chip_one, low, high = lax.optimization_barrier((chip_one, low, high))
    from_low = lax.ppermute(high, "band", forward)
    from_high = lax.ppermute(low, "band", backward)
    parts_one = to_all(chip_one)
    gm, gf, small, send = call(
        leave_kernel, "leave",
        [((ALL, 3 * D), BF16), ((ALL, D), BF16), ((16, D), F32), ((3 * D, D), BF16)],
        (
            core, gmixed, from_low, from_high, rim, hidden, normed, filled, seen, gmid,
            qkv_weight, vecs_one, gout, sums,
        ),
        smem=1, flops=2 * ALL * 5 * D * D,
    )
    other = lax.ppermute(send, "band", swap)
    keep, returned = call(
        leave_keep_kernel, "leave_keep", [((3 * D, D), BF16), ((GOT, D), BF16)],
        (core, gm, gf, small, normed, filled, gout, cell),
        smem=1, flops=2 * ALL * (2 * D * D + GOT * D),
    )
    parts_one, returned, other = lax.optimization_barrier((parts_one, returned, other))
    mine_one = lax.all_gather(total(parts_one), both, axis=0, axis_index_groups=halves)
    mine_one = mine_one.reshape(-1, D)
    mine = to_all(spread(total(to_all(chip_sum(keep, other))))).reshape(-1, D)
    mine, returned = lax.optimization_barrier((mine, returned))
    came = lax.all_to_all(
        returned.reshape(SRC, BLK, D), "clip", split_axis=0, concat_axis=0, tiled=True
    ).reshape(GOT, D)
    qkv, g_embed, g_out, small = call(
        unpack_two_kernel, "unpack_two",
        [((D, 3 * D), F32), ((ENC, D), F32), ((D, D), F32), ((16, D), F32)],
        (core, mine, lax.ppermute(mine, "band", swap)), smem=1,
    )
    came, small = lax.optimization_barrier((came, small))
    mine_one, came = lax.optimization_barrier((mine_one, came))
    down, up = call(
        unpack_one_kernel, "unpack_one", [((FF, D), F32), ((D, FF), F32)],
        (core, mine_one, lax.ppermute(mine_one, "band", swap)), smem=1,
    )
    (grad_enc,) = call(
        return_kernel, "return", [((MICRO, vis, ENC), BF16)], (dest, came, embed_weight),
        flops=2 * MICRO * vis * D * (GOT + ENC),
    )
    return (
        output.reshape(cotangent.shape), grad_enc, g_embed, small[0], small[1], small[2],
        small[3], qkv, small[4], small[5], g_out, small[8], small[9], small[10], up,
        small[12:16].reshape(FF), down, small[11],
    )


def solution(mesh):
    whole = P()
    return jax.shard_map(
        on_device,
        mesh=mesh,
        in_specs=(
            P(None, ("clip", "band"), None),
            P(None, ("clip", "band")),
            P(None, "clip", None),
            P(None, "clip", "band", None, None),
        )
        + (whole,) * 16,
        out_specs=(P(None, "clip", "band", None, None), P(None, ("clip", "band"), None))
        + (whole,) * 16,
        check_vma=False,
    )
```

```python
import jax
import jax.numpy as jnp
import numpy as np
from jax import lax
from jax.experimental import pallas as pl
from jax.experimental.pallas import tpu as pltpu
from jax.sharding import PartitionSpec as P

HEADS = 16
FREQ = 8
LONG = 192
MICRO = 4
ROWS = 24
CELLS = ROWS * FREQ
ALL = MICRO * CELLS
CAP = 9
BLK = 40
SRC = 16
GOT = SRC * BLK
D = 512
FF = 2048
ENC = 768
EPS = 1e-06
SCALE = (D // HEADS) ** (-0.5)
F32 = jnp.float32
BF16 = jnp.bfloat16

NN = (((1,), (0,)), ((), ()))
NT = (((1,), (1,)), ((), ()))
TN = (((0,), (0,)), ((), ()))


def dot(left, right, dims=NN):
    return lax.dot_general(left, right, dims, preferred_element_type=F32)


def iota(shape, dim):
    return lax.broadcasted_iota(jnp.int32, shape, dim)


def one_hot(hit):
    return jnp.where(hit, 1.0, 0.0).astype(BF16)


def call(kernel, name, out_shape, args, scratch=(), smem=0, flops=0, vmem=16, far=()):
    spaces = [pltpu.SMEM] * smem + [pltpu.VMEM] * (len(args) - smem)
    for i in far:
        spaces[i] = pltpu.HBM
    outs = [jax.ShapeDtypeStruct(shape, dtype) for shape, dtype in out_shape]
    size = sum(a.size * a.dtype.itemsize for a in args) + sum(
        o.size * o.dtype.itemsize for o in outs
    )
    return pl.pallas_call(
        kernel,
        name=name,
        out_shape=outs,
        in_specs=[pl.BlockSpec(memory_space=space) for space in spaces],
        out_specs=[pl.BlockSpec(memory_space=pltpu.VMEM)] * len(outs),
        scratch_shapes=list(scratch),
        compiler_params=pltpu.CompilerParams(vmem_limit_bytes=vmem * 2**20),
        cost_estimate=pl.CostEstimate(flops=flops, bytes_accessed=size, transcendentals=0),
    )(*args)


def pack_kernel(band, pos, enc, out, dest):
    count = pos.shape[1]
    low = iota((count, count), 0)
    high = iota((count, count), 1)
    packed = jnp.zeros((GOT, ENC), F32)
    places = jnp.zeros((SRC, 128), F32)
    for m in range(MICRO):
        cell_r = pos[m : m + 1, :]
        cell_c = jnp.sum(jnp.where(low == high, cell_r, 0), axis=1, keepdims=True)
        slot = LONG * FREQ
        dev_r = jnp.sum(
            jnp.where(cell_r >= slot * iota((SRC, count), 0) + slot, 1, 0), axis=0, keepdims=True
        )
        dev_c = jnp.sum(
            jnp.where(cell_c >= slot * iota((count, SRC), 1) + slot, 1, 0), axis=1, keepdims=True
        )
        same = dev_c == dev_r
        rank_r = jnp.sum(jnp.where(same & (low < high), 1, 0), axis=0, keepdims=True)
        rank_c = jnp.sum(jnp.where(same & (high < low), 1, 0), axis=1, keepdims=True)
        dest[m] = dev_c * BLK + m * CAP + rank_c
        select = one_hot(iota((GOT, count), 0) == dev_r * BLK + m * CAP + rank_r)
        packed = packed + dot(select, enc[m])
        number = cell_r - dev_r * slot - band[0] * CELLS + 1
        to_dev = jnp.where(iota((SRC, count), 0) == dev_r, number.astype(F32), 0.0).astype(BF16)
        to_lane = one_hot(iota((count, 128), 1) == m * CAP + rank_c)
        places = places + dot(to_dev, to_lane)
    spread = one_hot(iota((GOT, SRC), 0) == iota((GOT, SRC), 1) * BLK + (BLK - 4))
    out[:, :128] = (packed[:, :128] + dot(spread, places.astype(BF16))).astype(BF16)
    out[:, 128:] = packed[:, 128:].astype(BF16)


def norm_parts(values):
    center = values - jnp.mean(values, -1, keepdims=True)
    inverse = lax.rsqrt(jnp.mean(center * center, -1, keepdims=True) + EPS)
    return center * inverse, inverse


def norm_back(grad, normal, inverse, gain):
    scaled = grad * gain
    return inverse * (
        scaled
        - jnp.mean(scaled, -1, keepdims=True)
        - normal * jnp.mean(scaled * normal, -1, keepdims=True)
    )


def fetch(pairs, sems):
    copies = [pltpu.make_async_copy(far, near, sems.at[i]) for i, (far, near) in enumerate(pairs)]
    for copy in copies:
        copy.start()
    return copies


def enter_kernel(
    idx_r, idx_c, got_i, row_table, freq_table, embed_i, qkv_i, vecs, qkv_b,
    hidden_o, normed_o, mixed_o, filled_o, seen_o, cell_o, low_o, high_o,
    got, embed_w, qkv_w, sems,
):
    copies = fetch([(got_i, got), (embed_i, embed_w), (qkv_i, qkv_w)], sems)
    copies[0].wait()
    hit = one_hot(iota((SRC, GOT), 1) == iota((SRC, GOT), 0) * BLK + (BLK - 4))
    numbers = dot(hit, got[:, :128]).astype(BF16)
    spread_r = dot(numbers, one_hot(iota((SRC, GOT), 0) == idx_r[0:1, :]), TN)
    value_r = jnp.sum(
        jnp.where(iota((128, GOT), 0) == idx_r[1:2, :], spread_r, 0.0), axis=0, keepdims=True
    )
    cell_r = jnp.where(
        value_r > 0.5, idx_r[2:3, :] * CELLS + value_r.astype(jnp.int32) - 1, -1
    )
    spread_c = dot(one_hot(iota((GOT, SRC), 1) == idx_c[:, 0:1]), numbers)
    value_c = jnp.sum(
        jnp.where(iota((GOT, 128), 1) == idx_c[:, 1:2], spread_c, 0.0), axis=1, keepdims=True
    )
    cell_o[...] = jnp.where(
        value_c > 0.5, idx_c[:, 2:3] * CELLS + value_c.astype(jnp.int32) - 1, -1
    )
    for m in range(MICRO):
        rows = slice(m * CELLS, (m + 1) * CELLS)
        match = jnp.where(iota((CELLS, GOT), 0) + m * CELLS == cell_r, 1.0, 0.0)
        seen = jnp.sum(match, axis=1, keepdims=True)
        filled = dot(match.astype(BF16), got[...]).astype(BF16)
        filled_o[rows, :] = filled
        seen_o[rows, :] = seen
    copies[1].wait()
    copies[2].wait()
    freq = jnp.broadcast_to(freq_table[...][None], (ROWS, FREQ, D // 2)).reshape(CELLS, D // 2)
    for m in range(MICRO):
        rows = slice(m * CELLS, (m + 1) * CELLS)
        seen = seen_o[rows, :]
        proj = (dot(filled_o[rows, :], embed_w[...]) + vecs[0:1, :]).astype(BF16).astype(F32)
        line = row_table[m * ROWS : (m + 1) * ROWS, :]
        line = jnp.broadcast_to(line[:, None, :], (ROWS, FREQ, D // 2)).reshape(CELLS, D // 2)
        table = jnp.concatenate([line, freq], axis=1)
        hidden = jnp.where(seen > 0.5, proj, vecs[1:2, :]) + table
        hidden_o[rows, :] = hidden
        normal, unused = norm_parts(hidden)
        normed = (normal * vecs[2:3, :] + vecs[3:4, :]).astype(BF16)
        normed_o[rows, :] = normed
        mixed = (dot(normed, qkv_w[...]) + qkv_b[...]).astype(BF16)
        mixed_o[rows, :] = mixed
        low_o[m] = mixed[:16, D:]
        high_o[m] = mixed[CELLS - 16 :, D:]


def head_rows(block, heads):
    return jnp.concatenate([block * heads[h : h + 1, :] for h in range(4)], axis=0)


def own_head(full, lane_head):
    out = full[0:32, :]
    for h in range(1, 4):
        out = jnp.where(lane_head == h, full[32 * h : 32 * h + 32, :], out)
    return out


def window_loop(edge, inner):
    def inside(p, carry):
        places = []
        for m in range(MICRO):
            base = pl.multiple_of(m * CELLS + 32 * p - 16, 16)
            places.append((m * 7 + p, pl.ds(base, 32)))
        inner(places)
        return carry

    def ends(i, carry):
        places = []
        for j in range(2):
            m = 2 * i + j
            first = pl.multiple_of(m * CELLS, 16)
            last = pl.multiple_of(m * CELLS + CELLS - 16, 16)
            places.append((m, m * 7, pl.ds(first, 16), 0))
            places.append((m, m * 7 + 6, pl.ds(last, 16), 1))
        edge(places)
        return carry

    lax.fori_loop(1, 6, inside, 0)
    lax.fori_loop(0, MICRO // 2, ends, 0)


def with_halo(own, halo, side):
    return jnp.concatenate([own, halo] if side else [halo, own], axis=0)


COLS = [[slice(D * i + 128 * g, D * i + 128 * g + 128) for i in range(3)] for g in range(4)]


def load_inner(mixed, places, grads=None):
    items = []
    for w, rows in places:
        for g in range(4):
            item = [mixed[rows, c] for c in COLS[g]]
            items.append((w, g, *item, None if grads is None else grads[rows, COLS[g][0]]))
    return items


def load_edge(mixed, low, high, places, grads=None):
    zero = jnp.zeros((16, 128), BF16)
    items = []
    for m, w, rows, side in places:
        halo = high if side else low
        for g in range(4):
            cols = COLS[g]
            q = with_halo(mixed[rows, cols[0]], zero, side)
            k = with_halo(mixed[rows, cols[1]], halo[m, :, cols[0]], side)
            v = with_halo(mixed[rows, cols[2]], halo[m, :, cols[1]], side)
            grad = None if grads is None else with_halo(grads[rows, cols[0]], zero, side)
            items.append((w, g, q, k, v, grad))
    return items


def attend_kernel(mixed, low, high, mask, heads_i, attended_o, probs_o):
    heads = heads_i[...]
    lane_head = iota((32, 128), 1) // 32

    def windows(items):
        scores = [dot(k, head_rows(q, heads), NT) * SCALE for w, g, q, k, v, _ in items]
        probs = []
        for (w, g, *_), score in zip(items, scores):
            score = jnp.where(mask[w] > 0.5, score, -1e30)
            grown = jnp.exp(score - jnp.max(score, axis=0, keepdims=True))
            one = grown * (1.0 / jnp.sum(grown, axis=0, keepdims=True))
            probs_o[w, :, 128 * g : 128 * g + 128] = one
            probs.append(one.astype(BF16))
        full = [dot(one, item[4], TN) for item, one in zip(items, probs)]
        return [own_head(one, lane_head).astype(BF16) for one in full]

    def inner(places):
        outs = windows(load_inner(mixed, places))
        for i, (w, rows) in enumerate(places):
            for g in range(4):
                attended_o[rows, COLS[g][0]] = outs[4 * i + g]

    def edge(places):
        outs = windows(load_edge(mixed, low, high, places))
        for i, (m, w, rows, side) in enumerate(places):
            for g in range(4):
                out = outs[4 * i + g]
                attended_o[rows, COLS[g][0]] = out[:16] if side else out[16:]

    window_loop(edge, inner)


def gelu_parts(x):
    size = jnp.abs(x) * (0.5**0.5)
    bell = jnp.exp(-0.5 * x * x)
    t = 1.0 / (1.0 + 0.3275911 * size)
    poly = t * (
        0.254829592
        + t * (-0.284496736 + t * (1.421413741 + t * (-1.453152027 + t * 1.061405429)))
    )
    tail = 0.5 * poly * bell
    share = jnp.where(x >= 0, 1.0 - tail, tail)
    return x * share, share + x * bell * 0.3989422804014327


def before_kernel(cot, down_w, g_act_o):
    for f in range(4):
        cols = slice(512 * f, 512 * f + 512)
        g_act_o[:, cols] = dot(cot[...], down_w[cols, :], NT)


def mlp_kernel(
    core, hidden, attended, cot, g_act, out_w, up_w, vecs, up_b,
    middle_o, act_o, gexp_o, n2t_o, send_o, n2_s,
):
    tile = 256
    blocks = [slice(512 * f, 512 * f + 512) for f in range(4)]

    def forward(i, carry):
        rows = pl.ds(pl.multiple_of(i * tile, tile), tile)
        middle = hidden[rows, :] + dot(attended[rows, :], out_w[...]) + vecs[0:1, :]
        middle_o[rows, :] = middle
        normal, unused = norm_parts(middle)
        normed = (normal * vecs[1:2, :] + vecs[2:3, :]).astype(BF16)
        n2_s[rows, :] = normed
        expand = [dot(normed, up_w[:, cols]) for cols in blocks]
        for cols, one in zip(blocks, expand):
            value, slope = gelu_parts(one + up_b[0:1, cols])
            act_o[rows, cols] = value.astype(BF16)
            gexp_o[rows, cols] = (g_act[rows, cols] * slope).astype(BF16)
        return carry

    lax.fori_loop(0, ALL // tile, forward, 0)
    n2t_o[...] = jnp.transpose(n2_s[...])
    weight_half(1 - core[0], send_o, act_o, gexp_o, n2t_o, cot)


def weight_half(half, out, act, gexp, n2t, cot):
    for b in range(2):
        cols = pl.ds(pl.multiple_of(half * 1024 + 512 * b, 512), 512)
        rows = slice(512 * b, 512 * b + 512)
        out[rows, :] = dot(act[:, cols], cot[...], TN).astype(BF16)
        rows = slice(1024 + 512 * b, 1536 + 512 * b)
        out[rows, :] = dot(n2t[...], gexp[:, cols]).astype(BF16)


def mlp_keep_kernel(core, act, gexp, n2t, cot, keep_o):
    weight_half(core[0], keep_o, act, gexp, n2t, cot)


def back_kernel(
    middle_i, attended_i, cot_i, act_i, gexp_i, out_i, up_i, down_i, mixed_i, low_i, high_i,
    probs_f, vecs, heads_i,
    output_o, gmid_o, gout_o, sums_o, gmixed_o, low_o, high_o, rim_o,
    middle_s, attended, cot, act, gexp, out_w, up_w, down_w, mixed, low, high, probs_i, gatt, gb_s,
    sems,
):
    copies = fetch(
        [
            (up_i, up_w), (gexp_i, gexp), (down_i, down_w), (act_i, act), (middle_i, middle_s),
            (cot_i, cot), (out_i, out_w), (attended_i, attended), (mixed_i, mixed),
            (low_i, low), (high_i, high), (probs_f, probs_i),
        ],
        sems,
    )
    tile = 256
    sums_o[...] = jnp.zeros((8, D), F32)
    for i in range(ALL // tile):
        rows = slice(i * tile, (i + 1) * tile)
        if i == 0:
            copies[0].wait()
            copies[1].wait()
        grad = dot(gexp[rows, :], up_w[...], NT)
        if i == 0:
            copies[2].wait()
            copies[3].wait()
            copies[4].wait()
        middle = middle_s[rows, :]
        output_o[rows, :] = (middle + vecs[3:4, :] + dot(act[rows, :], down_w[...])).astype(BF16)
        if i == 0:
            copies[5].wait()
            copies[6].wait()
        normal, inverse = norm_parts(middle)
        g_float = cot[rows, :].astype(F32)
        g_mid = g_float + norm_back(grad, normal, inverse, vecs[1:2, :])
        gmid_o[rows, :] = g_mid
        g_low = g_mid.astype(BF16)
        gb_s[rows, :] = g_low
        gatt[rows, :] = dot(g_low, out_w[...], NT).astype(BF16)
        sums_o[0:1, :] += jnp.sum(g_low.astype(F32), axis=0, keepdims=True)
        sums_o[1:2, :] += jnp.sum(grad * normal, axis=0, keepdims=True)
        sums_o[2:3, :] += jnp.sum(grad, axis=0, keepdims=True)
        sums_o[3:4, :] += jnp.sum(g_float, axis=0, keepdims=True)
        for f in range(4):
            part = gexp[rows, 512 * f : 512 * f + 512].astype(F32)
            sums_o[4 + f : 5 + f, :] += jnp.sum(part, axis=0, keepdims=True)
    copies[7].wait()
    gout_o[...] = dot(attended[...], gb_s[...], TN).astype(BF16)
    for copy in copies[8:]:
        copy.wait()
    attend_back(mixed, low, high, probs_i, gatt, heads_i, gmixed_o, low_o, high_o, rim_o)


def attend_back(
    mixed, low, high, probs_i, gatt, heads_i, gmixed_o, low_o, high_o, rim_o
):
    heads = heads_i[...]
    lane_head = iota((32, 128), 1) // 32

    def windows(items):
        q_m = [head_rows(q, heads) for w, g, q, k, v, grad in items]
        g_m = [head_rows(grad, heads) for w, g, q, k, v, grad in items]
        g_probs = [dot(item[4], one, NT) for item, one in zip(items, g_m)]
        low_probs, g_scores = [], []
        for (w, g, *_), g_prob in zip(items, g_probs):
            probs = probs_i[w, :, 128 * g : 128 * g + 128]
            inner = jnp.sum(probs * g_prob, axis=0, keepdims=True)
            g_scores.append((probs * (g_prob - inner)).astype(BF16))
            low_probs.append(probs.astype(BF16))
        d_value = [dot(one, grad) for one, grad in zip(low_probs, g_m)]
        d_key = [dot(one, q) * SCALE for one, q in zip(g_scores, q_m)]
        full = [dot(one, item[3], TN) for item, one in zip(items, g_scores)]
        d_query = [(own_head(one, lane_head) * SCALE).astype(BF16) for one in full]
        return list(zip(d_query, d_key, d_value))

    def inner(places):
        outs = windows(load_inner(mixed, places, gatt))
        for i, (w, rows) in enumerate(places):
            for g in range(4):
                for col, value in zip(COLS[g], outs[4 * i + g]):
                    gmixed_o[rows, col] = value.astype(BF16)

    def edge(places):
        outs = windows(load_edge(mixed, low, high, places, gatt))
        for i, (m, w, rows, side) in enumerate(places):
            out = high_o if side else low_o
            own, far = (slice(0, 16), slice(16, 32)) if side else (slice(16, 32), slice(0, 16))
            for g in range(4):
                cols = COLS[g]
                d_query, d_key, d_value = outs[4 * i + g]
                gmixed_o[rows, cols[0]] = d_query[own]
                rim_o[m, side, :, cols[0]] = d_key[own]
                rim_o[m, side, :, cols[1]] = d_value[own]
                out[m, :, cols[0]] = d_key[far].astype(BF16)
                out[m, :, cols[1]] = d_value[far].astype(BF16)

    window_loop(edge, inner)
    for m in range(MICRO):
        for base in (m * CELLS, m * CELLS + CELLS - 16):
            gmixed_o[base : base + 16, D:] = jnp.zeros((16, 2 * D), BF16)


def leave_kernel(
    core, gmixed, from_low, from_high, rim, hidden, normed, filled, seen, gmid, qkv_w, vecs,
    gout, sums, gm_o, gf_o, small_o, send_o,
):
    small = jnp.zeros((1, D), F32)
    gain_sum, shift_sum, mask_sum, embed_sum, query_sum, value_sum = [small] * 6
    for m in range(MICRO):
        base = m * CELLS
        rows = slice(base, base + CELLS)
        gm_o[rows, :] = gmixed[rows, :]
        gm_o[base : base + 16, D:] = (rim[m, 0] + from_low[m].astype(F32)).astype(BF16)
        gm_o[base + CELLS - 16 : base + CELLS, D:] = (rim[m, 1] + from_high[m].astype(F32)).astype(
            BF16
        )
        gm = gm_o[rows, :]
        grad = dot(gm, qkv_w[...], NT)
        normal, inverse = norm_parts(hidden[rows, :])
        g_hidden = gmid[rows, :] + norm_back(grad, normal, inverse, vecs[2:3, :])
        there = seen[rows, :] > 0.5
        g_low = g_hidden.astype(BF16)
        gf_o[rows, :] = g_low
        gain_sum += jnp.sum(grad * normal, axis=0, keepdims=True)
        shift_sum += jnp.sum(grad, axis=0, keepdims=True)
        mask_sum += jnp.sum(jnp.where(there, 0.0, g_hidden), axis=0, keepdims=True)
        embed_sum += jnp.sum(jnp.where(there, g_low.astype(F32), 0.0), axis=0, keepdims=True)
        query_sum += jnp.sum(gm[:, :D].astype(F32), axis=0, keepdims=True)
        value_sum += jnp.sum(gm[:, 2 * D :].astype(F32), axis=0, keepdims=True)
    small_o[...] = jnp.concatenate(
        [
            embed_sum, mask_sum, gain_sum, shift_sum, query_sum, value_sum,
            small, small, sums[...],
        ],
        axis=0,
    )
    one_half(core[0] != 0, send_o, normed, filled, gm_o, gf_o, gout, small_o)


def one_half(first, out, normed, filled, gm, gf, gout, small):
    @pl.when(first)
    def _():
        turned = jnp.transpose(normed[...])
        for b in range(3):
            cols = slice(512 * b, 512 * b + 512)
            out[cols, :] = dot(turned, gm[:, cols]).astype(BF16)

    @pl.when(jnp.logical_not(first))
    def _():
        out[0:512, :] = gout[...]
        out[512:1280, :] = dot(jnp.transpose(filled[...]), gf[...]).astype(BF16)
        out[1280:1296, :] = small[...].astype(BF16)
        out[1296:1536, :] = jnp.zeros((240, D), BF16)


def leave_keep_kernel(core, gm, gf, small, normed, filled, gout, cell, keep_o, ret_o):
    one_half(core[0] == 0, keep_o, normed, filled, gm, gf, gout, small)
    ret_o[...] = dot(one_hot(iota((GOT, ALL), 1) == cell[...]), gf[...]).astype(BF16)


def return_kernel(dest, came, embed_w, out):
    for m in range(MICRO):
        select = one_hot(iota((dest.shape[1], GOT), 1) == dest[m])
        g_proj = dot(select, came[...]).astype(BF16)
        out[m] = dot(g_proj, embed_w[...], NT).astype(BF16)


def unpack_one_kernel(down_i, up_i, down_o, up_o):
    down_o[...] = down_i[...].reshape(512, D).astype(F32)
    up_o[...] = up_i[...].reshape(512, D).astype(F32)


def unpack_one(gathered):
    block = (16, 1, 32, D)
    return pl.pallas_call(
        unpack_one_kernel,
        name="unpack_one",
        grid=(4,),
        out_shape=[jax.ShapeDtypeStruct((FF, D), F32), jax.ShapeDtypeStruct((D, FF), F32)],
        in_specs=[
            pl.BlockSpec(block, lambda i: (i % 2, i // 2, 0, 0)),
            pl.BlockSpec(block, lambda i: (2 + i % 2, i // 2, 0, 0)),
        ],
        out_specs=[
            pl.BlockSpec((512, D), lambda i: (i, 0)),
            pl.BlockSpec((512, D), lambda i: (0, i)),
        ],
        compiler_params=pltpu.CompilerParams(vmem_limit_bytes=16 * 2**20),
        cost_estimate=pl.CostEstimate(flops=0, bytes_accessed=12 * 2**20, transcendentals=0),
    )(gathered, gathered)


def unpack_two_kernel(core, mine, other, qkv_o, embed_o, out_o, small_o):
    def write(first, second):
        for b in range(3):
            qkv_o[:, 512 * b : 512 * b + 512] = first[512 * b : 512 * b + 512, :].astype(F32)
        out_o[...] = second[0:512, :].astype(F32)
        embed_o[...] = second[512:1280, :].astype(F32)
        small_o[...] = second[1280:1296, :].astype(F32)

    @pl.when(core[0] == 0)
    def _():
        write(mine, other)

    @pl.when(core[0] != 0)
    def _():
        write(other, mine)


def clip_ident(lengths, rows):
    first = lengths[:, 0:1]
    second = first + lengths[:, 1:2]
    ident = (rows[None, :] >= first).astype(jnp.int32) + (rows[None, :] >= second).astype(jnp.int32)
    start = jnp.where(ident >= 1, first, 0) + jnp.where(ident >= 2, lengths[:, 1:2], 0)
    inside = (rows >= 0) & (rows < LONG)
    return (jnp.where(inside[None, :], ident, -1), rows[None, :] - start)


def position_tables(row_in_clip, width):
    quarter = width // 4
    omega = 1.0 / 10000.0 ** (jnp.arange(quarter, dtype=jnp.float32) / quarter)
    row_angle = row_in_clip.astype(jnp.float32)[..., None] * omega
    freq_angle = jnp.arange(FREQ, dtype=jnp.float32)[:, None] * omega
    row_part = jnp.concatenate([jnp.sin(row_angle), jnp.cos(row_angle)], -1)
    freq_part = jnp.concatenate([jnp.sin(freq_angle), jnp.cos(freq_angle)], -1)
    return row_part.reshape(-1, width // 2), freq_part


def window_mask(ident):
    cells = jnp.repeat(ident.reshape(MICRO * 7, 4), FREQ, axis=1)
    freq = np.tile((np.arange(FREQ) + 2) % 8 // 4, 4)
    same = (cells[:, :, None] == cells[:, None, :]) & (cells[:, :, None] >= 0)
    same = same & jnp.asarray(freq[:, None] == freq[None, :])[None]
    return jnp.tile(same.astype(F32), (1, 1, 4))


def on_device(
    encoded, visible_pos, clip_len, cotangent, embed_weight, embed_bias, mask_token, attn_gain,
    attn_shift, qkv_weight, query_bias, value_bias, out_weight, out_bias, mlp_gain, mlp_shift,
    up_weight, up_bias, down_weight, down_bias,
):
    both = ("clip", "band")
    groups = lax.axis_size("clip")
    bands = lax.axis_size("band")
    band = lax.axis_index("band")
    side = band % 2
    core = side.astype(jnp.int32).reshape(1)
    halves = [
        [c * bands + 2 * x + k for c in range(groups) for x in range(bands // 2)] for k in range(2)
    ]
    swap = [(i, i ^ 1) for i in range(bands)]
    forward = [(i, i + 1) for i in range(bands - 1)]
    backward = [(b, a) for a, b in forward]
    chips = groups * bands // 2

    def to_all(block):
        return lax.all_to_all(
            block, both, split_axis=0, concat_axis=0, tiled=True, axis_index_groups=halves
        )

    def chip_sum(keep, other):
        mine = (keep.astype(F32) + other.astype(F32)).astype(BF16)
        return mine.reshape(chips, -1, D)

    def total(parts):
        return jnp.sum(parts.astype(F32), 0).astype(BF16)

    def spread(chunk):
        return jnp.broadcast_to(chunk[None], (chips,) + chunk.shape)

    vis = visible_pos.shape[1]
    packed, dest = call(
        pack_kernel, "pack", [((GOT, ENC), BF16), ((MICRO, vis, 1), jnp.int32)],
        (band.astype(jnp.int32).reshape(1), visible_pos, encoded), smem=1,
        flops=GOT * MICRO * vis * ENC * 2,
    )
    cot = cotangent.reshape(ALL, D)
    (g_act,) = call(
        before_kernel, "before", [((ALL, FF), F32)], (cot, down_weight), flops=2 * ALL * D * FF,
    )
    got = lax.all_to_all(
        packed.reshape(SRC, BLK, ENC), "clip", split_axis=0, concat_axis=0, tiled=True
    ).reshape(GOT, ENC)

    place = np.arange(GOT)
    within = place % BLK
    index = np.zeros((8, GOT), np.int32)
    index[0], index[1], index[2] = place // BLK, within, np.where(within < 36, within // CAP, 99)
    heads = jnp.asarray(np.arange(128)[None, :] // 32 == np.arange(16)[:, None] % 4, BF16)

    unused, row_in_clip = clip_ident(clip_len[:, 0], band * ROWS + jnp.arange(ROWS))
    row_table, freq_table = position_tables(row_in_clip, D)
    ident_ext, unused = clip_ident(clip_len[:, 0], band * ROWS - 2 + jnp.arange(ROWS + 4))
    mask = window_mask(ident_ext)
    zero = jnp.zeros((D,), BF16)
    vecs_one = jnp.stack([embed_bias, mask_token, attn_gain, attn_shift] * 2).astype(F32)
    vecs_two = jnp.stack([out_bias, mlp_gain, mlp_shift, down_bias] * 2).astype(F32)
    qkv_b = jnp.concatenate([query_bias, zero, value_bias]).astype(F32)[None]
    up_b = up_bias.astype(F32)[None]

    hidden, normed, mixed, filled, seen, cell, low, high = call(
        enter_kernel, "enter",
        [
            ((ALL, D), F32), ((ALL, D), BF16), ((ALL, 3 * D), BF16), ((ALL, ENC), BF16),
            ((ALL, 1), F32), ((GOT, 1), jnp.int32),
            ((MICRO, 16, 2 * D), BF16), ((MICRO, 16, 2 * D), BF16),
        ],
        (
            jnp.asarray(index), jnp.asarray(np.ascontiguousarray(index.T)), got, row_table,
            freq_table, embed_weight, qkv_weight, vecs_one, qkv_b,
        ),
        scratch=[
            pltpu.VMEM((GOT, ENC), BF16), pltpu.VMEM((ENC, D), BF16), pltpu.VMEM((D, 3 * D), BF16),
            pltpu.SemaphoreType.DMA((3,)),
        ],
        far=(2, 5, 6),
        flops=2 * ALL * (GOT * ENC + ENC * D + 3 * D * D),
    )
    from_low = lax.ppermute(high, "band", forward)
    from_high = lax.ppermute(low, "band", backward)
    attended, probs = call(
        attend_kernel, "attend",
        [((ALL, D), BF16), ((MICRO * 7, 32, D), F32)],
        (mixed, from_low, from_high, mask, heads),
        flops=MICRO * 7 * 4 * 2**20,
    )
    middle, act, gexp, n2t, send = call(
        mlp_kernel, "mlp",
        [
            ((ALL, D), F32), ((ALL, FF), BF16), ((ALL, FF), BF16), ((D, ALL), BF16),
            ((FF, D), BF16),
        ],
        (core, hidden, attended, cot, g_act, out_weight, up_weight, vecs_two, up_b),
        scratch=[pltpu.VMEM((ALL, D), BF16)],
        smem=1, flops=2 * ALL * (2 * D * FF + D * D), vmem=24,
    )
    (keep,) = call(
        mlp_keep_kernel, "mlp_keep", [((FF, D), BF16)], (core, act, gexp, n2t, cot),
        smem=1, flops=2 * ALL * D * FF,
    )
    chip_one = chip_sum(keep, lax.ppermute(send, "band", swap))
    act, chip_one = lax.optimization_barrier((act, chip_one))
    parts_one = to_all(chip_one)
    inputs = (
        middle, attended, cot, act, gexp, out_weight, up_weight, down_weight, mixed, from_low,
        from_high, probs,
    )
    output, gmid, gout, sums, gmixed, low, high, rim = call(
        back_kernel, "back",
        [
            ((ALL, D), BF16), ((ALL, D), F32), ((D, D), BF16), ((8, D), F32),
            ((ALL, 3 * D), BF16), ((MICRO, 16, 2 * D), BF16), ((MICRO, 16, 2 * D), BF16),
            ((MICRO, 2, 16, 2 * D), F32),
        ],
        inputs + (vecs_two, heads),
        scratch=[pltpu.VMEM(x.shape, x.dtype) for x in inputs]
        + [pltpu.VMEM((ALL, D), BF16)] * 2
        + [pltpu.SemaphoreType.DMA((len(inputs),))],
        flops=2 * ALL * (2 * D * FF + 2 * D * D) + MICRO * 7 * 4 * 2**22,
        far=range(len(inputs)), vmem=44,
    )
    from_low = lax.ppermute(high, "band", forward)
    from_high = lax.ppermute(low, "band", backward)
    total_one = total(parts_one)
    total_one, from_low, from_high = lax.optimization_barrier((total_one, from_low, from_high))
    gm, gf, small, send = call(
        leave_kernel, "leave",
        [((ALL, 3 * D), BF16), ((ALL, D), BF16), ((16, D), F32), ((3 * D, D), BF16)],
        (
            core, gmixed, from_low, from_high, rim, hidden, normed, filled, seen, gmid,
            qkv_weight, vecs_one, gout, sums,
        ),
        smem=1, flops=2 * ALL * 5 * D * D,
    )
    other = lax.ppermute(send, "band", swap)
    total_one = lax.all_gather(total_one, both, axis=0).reshape(chips, 2, -1, D)
    keep, returned = call(
        leave_keep_kernel, "leave_keep", [((3 * D, D), BF16), ((GOT, D), BF16)],
        (core, gm, gf, small, normed, filled, gout, cell),
        smem=1, flops=2 * ALL * (2 * D * D + GOT * D),
    )
    mine = to_all(spread(total(to_all(chip_sum(keep, other))))).reshape(-1, D)
    mine, returned = lax.optimization_barrier((mine, returned))
    qkv, g_embed, g_out, small = call(
        unpack_two_kernel, "unpack_two",
        [((D, 3 * D), F32), ((ENC, D), F32), ((D, D), F32), ((16, D), F32)],
        (core, mine, lax.ppermute(mine, "band", swap)), smem=1,
    )
    came = lax.all_to_all(
        returned.reshape(SRC, BLK, D), "clip", split_axis=0, concat_axis=0, tiled=True
    ).reshape(GOT, D)
    down, up = unpack_one(total_one)
    came, small, down = lax.optimization_barrier((came, small, down))
    (grad_enc,) = call(
        return_kernel, "return", [((MICRO, vis, ENC), BF16)], (dest, came, embed_weight),
        flops=2 * MICRO * vis * D * (GOT + ENC),
    )
    return (
        output.reshape(cotangent.shape), grad_enc, g_embed, small[0], small[1], small[2],
        small[3], qkv, small[4], small[5], g_out, small[8], small[9], small[10], up,
        small[12:16].reshape(FF), down, small[11],
    )


def solution(mesh):
    whole = P()
    return jax.shard_map(
        on_device,
        mesh=mesh,
        in_specs=(
            P(None, ("clip", "band"), None),
            P(None, ("clip", "band")),
            P(None, "clip", None),
            P(None, "clip", "band", None, None),
        )
        + (whole,) * 16,
        out_specs=(P(None, "clip", "band", None, None), P(None, ("clip", "band"), None))
        + (whole,) * 16,
        check_vma=False,
    )
```

```python
import jax
import jax.numpy as jnp
import numpy as np
from jax import lax
from jax.experimental import pallas as pl
from jax.experimental.pallas import tpu as pltpu
from jax.sharding import PartitionSpec as P

HEADS = 16
FREQ = 8
LONG = 192
MICRO = 4
ROWS = 24
CELLS = ROWS * FREQ
ALL = MICRO * CELLS
CAP = 9
BLK = 40
SRC = 16
GOT = SRC * BLK
D = 512
FF = 2048
ENC = 768
EPS = 1e-06
SCALE = (D // HEADS) ** (-0.5)
F32 = jnp.float32
BF16 = jnp.bfloat16

NN = (((1,), (0,)), ((), ()))
NT = (((1,), (1,)), ((), ()))
TN = (((0,), (0,)), ((), ()))


def dot(left, right, dims=NN):
    return lax.dot_general(left, right, dims, preferred_element_type=F32)


def iota(shape, dim):
    return lax.broadcasted_iota(jnp.int32, shape, dim)


def one_hot(hit):
    return jnp.where(hit, 1.0, 0.0).astype(BF16)


def call(kernel, name, out_shape, args, scratch=(), smem=0, flops=0, vmem=16, far=()):
    spaces = [pltpu.SMEM] * smem + [pltpu.VMEM] * (len(args) - smem)
    for i in far:
        spaces[i] = pltpu.HBM
    outs = [jax.ShapeDtypeStruct(shape, dtype) for shape, dtype in out_shape]
    size = sum(a.size * a.dtype.itemsize for a in args) + sum(
        o.size * o.dtype.itemsize for o in outs
    )
    return pl.pallas_call(
        kernel,
        name=name,
        out_shape=outs,
        in_specs=[pl.BlockSpec(memory_space=space) for space in spaces],
        out_specs=[pl.BlockSpec(memory_space=pltpu.VMEM)] * len(outs),
        scratch_shapes=list(scratch),
        compiler_params=pltpu.CompilerParams(vmem_limit_bytes=vmem * 2**20),
        cost_estimate=pl.CostEstimate(flops=flops, bytes_accessed=size, transcendentals=0),
    )(*args)


def pack_kernel(band, pos, enc, out, dest):
    count = pos.shape[1]
    low = iota((count, count), 0)
    high = iota((count, count), 1)
    packed = jnp.zeros((GOT, ENC), F32)
    places = jnp.zeros((SRC, 128), F32)
    for m in range(MICRO):
        cell_r = pos[m : m + 1, :]
        cell_c = jnp.sum(jnp.where(low == high, cell_r, 0), axis=1, keepdims=True)
        slot = LONG * FREQ
        dev_r = jnp.sum(
            jnp.where(cell_r >= slot * iota((SRC, count), 0) + slot, 1, 0), axis=0, keepdims=True
        )
        dev_c = jnp.sum(
            jnp.where(cell_c >= slot * iota((count, SRC), 1) + slot, 1, 0), axis=1, keepdims=True
        )
        same = dev_c == dev_r
        rank_r = jnp.sum(jnp.where(same & (low < high), 1, 0), axis=0, keepdims=True)
        rank_c = jnp.sum(jnp.where(same & (high < low), 1, 0), axis=1, keepdims=True)
        dest[m] = dev_c * BLK + m * CAP + rank_c
        select = one_hot(iota((GOT, count), 0) == dev_r * BLK + m * CAP + rank_r)
        packed = packed + dot(select, enc[m])
        number = cell_r - dev_r * slot - band[0] * CELLS + 1
        to_dev = jnp.where(iota((SRC, count), 0) == dev_r, number.astype(F32), 0.0).astype(BF16)
        to_lane = one_hot(iota((count, 128), 1) == m * CAP + rank_c)
        places = places + dot(to_dev, to_lane)
    spread = one_hot(iota((GOT, SRC), 0) == iota((GOT, SRC), 1) * BLK + (BLK - 4))
    out[:, :128] = (packed[:, :128] + dot(spread, places.astype(BF16))).astype(BF16)
    out[:, 128:] = packed[:, 128:].astype(BF16)


def norm_parts(values):
    center = values - jnp.mean(values, -1, keepdims=True)
    inverse = lax.rsqrt(jnp.mean(center * center, -1, keepdims=True) + EPS)
    return center * inverse, inverse


def norm_back(grad, normal, inverse, gain):
    scaled = grad * gain
    return inverse * (
        scaled
        - jnp.mean(scaled, -1, keepdims=True)
        - normal * jnp.mean(scaled * normal, -1, keepdims=True)
    )


def fetch(pairs, sems):
    copies = [pltpu.make_async_copy(far, near, sems.at[i]) for i, (far, near) in enumerate(pairs)]
    for copy in copies:
        copy.start()
    return copies


def enter_kernel(
    idx_r, idx_c, got_i, row_table, freq_table, embed_i, qkv_i, vecs, qkv_b,
    hidden_o, normed_o, mixed_o, filled_o, seen_o, cell_o, low_o, high_o,
    got, embed_w, qkv_w, sems,
):
    copies = fetch([(got_i, got), (embed_i, embed_w), (qkv_i, qkv_w)], sems)
    copies[0].wait()
    hit = one_hot(iota((SRC, GOT), 1) == iota((SRC, GOT), 0) * BLK + (BLK - 4))
    numbers = dot(hit, got[:, :128]).astype(BF16)
    spread_r = dot(numbers, one_hot(iota((SRC, GOT), 0) == idx_r[0:1, :]), TN)
    value_r = jnp.sum(
        jnp.where(iota((128, GOT), 0) == idx_r[1:2, :], spread_r, 0.0), axis=0, keepdims=True
    )
    cell_r = jnp.where(
        value_r > 0.5, idx_r[2:3, :] * CELLS + value_r.astype(jnp.int32) - 1, -1
    )
    spread_c = dot(one_hot(iota((GOT, SRC), 1) == idx_c[:, 0:1]), numbers)
    value_c = jnp.sum(
        jnp.where(iota((GOT, 128), 1) == idx_c[:, 1:2], spread_c, 0.0), axis=1, keepdims=True
    )
    cell_o[...] = jnp.where(
        value_c > 0.5, idx_c[:, 2:3] * CELLS + value_c.astype(jnp.int32) - 1, -1
    )
    for m in range(MICRO):
        rows = slice(m * CELLS, (m + 1) * CELLS)
        match = jnp.where(iota((CELLS, GOT), 0) + m * CELLS == cell_r, 1.0, 0.0)
        seen = jnp.sum(match, axis=1, keepdims=True)
        filled = dot(match.astype(BF16), got[...]).astype(BF16)
        filled_o[rows, :] = filled
        seen_o[rows, :] = seen
    copies[1].wait()
    copies[2].wait()
    freq = jnp.broadcast_to(freq_table[...][None], (ROWS, FREQ, D // 2)).reshape(CELLS, D // 2)
    for m in range(MICRO):
        rows = slice(m * CELLS, (m + 1) * CELLS)
        seen = seen_o[rows, :]
        proj = (dot(filled_o[rows, :], embed_w[...]) + vecs[0:1, :]).astype(BF16).astype(F32)
        line = row_table[m * ROWS : (m + 1) * ROWS, :]
        line = jnp.broadcast_to(line[:, None, :], (ROWS, FREQ, D // 2)).reshape(CELLS, D // 2)
        table = jnp.concatenate([line, freq], axis=1)
        hidden = jnp.where(seen > 0.5, proj, vecs[1:2, :]) + table
        hidden_o[rows, :] = hidden
        normal, unused = norm_parts(hidden)
        normed = (normal * vecs[2:3, :] + vecs[3:4, :]).astype(BF16)
        normed_o[rows, :] = normed
        mixed = (dot(normed, qkv_w[...]) + qkv_b[...]).astype(BF16)
        mixed_o[rows, :] = mixed
        low_o[m] = mixed[:16, D:]
        high_o[m] = mixed[CELLS - 16 :, D:]


def head_rows(block, heads):
    return jnp.concatenate([block * heads[h : h + 1, :] for h in range(4)], axis=0)


def own_head(full, lane_head):
    out = full[0:32, :]
    for h in range(1, 4):
        out = jnp.where(lane_head == h, full[32 * h : 32 * h + 32, :], out)
    return out


def window_loop(edge, inner):
    def inside(p, carry):
        places = []
        for m in range(MICRO):
            base = pl.multiple_of(m * CELLS + 32 * p - 16, 16)
            places.append((m * 7 + p, pl.ds(base, 32)))
        inner(places)
        return carry

    def ends(i, carry):
        places = []
        for j in range(2):
            m = 2 * i + j
            first = pl.multiple_of(m * CELLS, 16)
            last = pl.multiple_of(m * CELLS + CELLS - 16, 16)
            places.append((m, m * 7, pl.ds(first, 16), 0))
            places.append((m, m * 7 + 6, pl.ds(last, 16), 1))
        edge(places)
        return carry

    lax.fori_loop(1, 6, inside, 0)
    lax.fori_loop(0, MICRO // 2, ends, 0)


def with_halo(own, halo, side):
    return jnp.concatenate([own, halo] if side else [halo, own], axis=0)


COLS = [[slice(D * i + 128 * g, D * i + 128 * g + 128) for i in range(3)] for g in range(4)]


def load_inner(mixed, places, grads=None):
    items = []
    for w, rows in places:
        for g in range(4):
            item = [mixed[rows, c] for c in COLS[g]]
            items.append((w, g, *item, None if grads is None else grads[rows, COLS[g][0]]))
    return items


def load_edge(mixed, low, high, places, grads=None):
    zero = jnp.zeros((16, 128), BF16)
    items = []
    for m, w, rows, side in places:
        halo = high if side else low
        for g in range(4):
            cols = COLS[g]
            q = with_halo(mixed[rows, cols[0]], zero, side)
            k = with_halo(mixed[rows, cols[1]], halo[m, :, cols[0]], side)
            v = with_halo(mixed[rows, cols[2]], halo[m, :, cols[1]], side)
            grad = None if grads is None else with_halo(grads[rows, cols[0]], zero, side)
            items.append((w, g, q, k, v, grad))
    return items


def attend_kernel(mixed, low, high, mask, heads_i, attended_o, probs_o):
    heads = heads_i[...]
    lane_head = iota((32, 128), 1) // 32

    def windows(items):
        scores = [dot(k, head_rows(q, heads), NT) * SCALE for w, g, q, k, v, _ in items]
        probs = []
        for (w, g, *_), score in zip(items, scores):
            score = jnp.where(mask[w] > 0.5, score, -1e30)
            grown = jnp.exp(score - jnp.max(score, axis=0, keepdims=True))
            one = grown * (1.0 / jnp.sum(grown, axis=0, keepdims=True))
            probs_o[w, :, 128 * g : 128 * g + 128] = one
            probs.append(one.astype(BF16))
        full = [dot(one, item[4], TN) for item, one in zip(items, probs)]
        return [own_head(one, lane_head).astype(BF16) for one in full]

    def inner(places):
        outs = windows(load_inner(mixed, places))
        for i, (w, rows) in enumerate(places):
            for g in range(4):
                attended_o[rows, COLS[g][0]] = outs[4 * i + g]

    def edge(places):
        outs = windows(load_edge(mixed, low, high, places))
        for i, (m, w, rows, side) in enumerate(places):
            for g in range(4):
                out = outs[4 * i + g]
                attended_o[rows, COLS[g][0]] = out[:16] if side else out[16:]

    window_loop(edge, inner)


def gelu_parts(x):
    size = jnp.abs(x) * (0.5**0.5)
    bell = jnp.exp(-0.5 * x * x)
    t = 1.0 / (1.0 + 0.3275911 * size)
    poly = t * (
        0.254829592
        + t * (-0.284496736 + t * (1.421413741 + t * (-1.453152027 + t * 1.061405429)))
    )
    tail = 0.5 * poly * bell
    share = jnp.where(x >= 0, 1.0 - tail, tail)
    return x * share, share + x * bell * 0.3989422804014327


def before_kernel(cot, down_w, g_act_o):
    for f in range(4):
        cols = slice(512 * f, 512 * f + 512)
        g_act_o[:, cols] = dot(cot[...], down_w[cols, :], NT)


def mlp_kernel(
    core, hidden, attended, cot, g_act, out_w, up_w, vecs, up_b,
    middle_o, act_o, gexp_o, n2t_o, send_o, n2_s,
):
    tile = 256
    blocks = [slice(512 * f, 512 * f + 512) for f in range(4)]

    def forward(i, carry):
        rows = pl.ds(pl.multiple_of(i * tile, tile), tile)
        middle = hidden[rows, :] + dot(attended[rows, :], out_w[...]) + vecs[0:1, :]
        middle_o[rows, :] = middle
        normal, unused = norm_parts(middle)
        normed = (normal * vecs[1:2, :] + vecs[2:3, :]).astype(BF16)
        n2_s[rows, :] = normed
        expand = [dot(normed, up_w[:, cols]) for cols in blocks]
        for cols, one in zip(blocks, expand):
            value, slope = gelu_parts(one + up_b[0:1, cols])
            act_o[rows, cols] = value.astype(BF16)
            gexp_o[rows, cols] = (g_act[rows, cols] * slope).astype(BF16)
        return carry

    lax.fori_loop(0, ALL // tile, forward, 0)
    n2t_o[...] = jnp.transpose(n2_s[...])
    weight_half(1 - core[0], send_o, act_o, gexp_o, n2t_o, cot)


def weight_half(half, out, act, gexp, n2t, cot):
    for b in range(2):
        cols = pl.ds(pl.multiple_of(half * 1024 + 512 * b, 512), 512)
        rows = slice(512 * b, 512 * b + 512)
        out[rows, :] = dot(act[:, cols], cot[...], TN).astype(BF16)
        rows = slice(1024 + 512 * b, 1536 + 512 * b)
        out[rows, :] = dot(n2t[...], gexp[:, cols]).astype(BF16)


def mlp_keep_kernel(core, act, gexp, n2t, cot, keep_o):
    weight_half(core[0], keep_o, act, gexp, n2t, cot)


def back_kernel(
    middle_i, attended_i, cot_i, act_i, gexp_i, out_i, up_i, down_i, mixed_i, low_i, high_i,
    probs_f, vecs, heads_i,
    output_o, gmid_o, gout_o, sums_o, gmixed_o, low_o, high_o, rim_o,
    middle_s, attended, cot, act, gexp, out_w, up_w, down_w, mixed, low, high, probs_i, gatt, gb_s,
    sems,
):
    copies = fetch(
        [
            (up_i, up_w), (gexp_i, gexp), (down_i, down_w), (act_i, act), (middle_i, middle_s),
            (cot_i, cot), (out_i, out_w), (attended_i, attended), (mixed_i, mixed),
            (low_i, low), (high_i, high), (probs_f, probs_i),
        ],
        sems,
    )
    tile = 256
    sums_o[...] = jnp.zeros((8, D), F32)
    for i in range(ALL // tile):
        rows = slice(i * tile, (i + 1) * tile)
        if i == 0:
            copies[0].wait()
            copies[1].wait()
        grad = dot(gexp[rows, :], up_w[...], NT)
        if i == 0:
            copies[2].wait()
            copies[3].wait()
            copies[4].wait()
        middle = middle_s[rows, :]
        output_o[rows, :] = (middle + vecs[3:4, :] + dot(act[rows, :], down_w[...])).astype(BF16)
        if i == 0:
            copies[5].wait()
            copies[6].wait()
        normal, inverse = norm_parts(middle)
        g_float = cot[rows, :].astype(F32)
        g_mid = g_float + norm_back(grad, normal, inverse, vecs[1:2, :])
        gmid_o[rows, :] = g_mid
        g_low = g_mid.astype(BF16)
        gb_s[rows, :] = g_low
        gatt[rows, :] = dot(g_low, out_w[...], NT).astype(BF16)
        sums_o[0:1, :] += jnp.sum(g_low.astype(F32), axis=0, keepdims=True)
        sums_o[1:2, :] += jnp.sum(grad * normal, axis=0, keepdims=True)
        sums_o[2:3, :] += jnp.sum(grad, axis=0, keepdims=True)
        sums_o[3:4, :] += jnp.sum(g_float, axis=0, keepdims=True)
        for f in range(4):
            part = gexp[rows, 512 * f : 512 * f + 512].astype(F32)
            sums_o[4 + f : 5 + f, :] += jnp.sum(part, axis=0, keepdims=True)
    copies[7].wait()
    gout_o[...] = dot(attended[...], gb_s[...], TN).astype(BF16)
    for copy in copies[8:]:
        copy.wait()
    attend_back(mixed, low, high, probs_i, gatt, heads_i, gmixed_o, low_o, high_o, rim_o)


def attend_back(
    mixed, low, high, probs_i, gatt, heads_i, gmixed_o, low_o, high_o, rim_o
):
    heads = heads_i[...]
    lane_head = iota((32, 128), 1) // 32

    def windows(items):
        q_m = [head_rows(q, heads) for w, g, q, k, v, grad in items]
        g_m = [head_rows(grad, heads) for w, g, q, k, v, grad in items]
        g_probs = [dot(item[4], one, NT) for item, one in zip(items, g_m)]
        low_probs, g_scores = [], []
        for (w, g, *_), g_prob in zip(items, g_probs):
            probs = probs_i[w, :, 128 * g : 128 * g + 128]
            inner = jnp.sum(probs * g_prob, axis=0, keepdims=True)
            g_scores.append((probs * (g_prob - inner)).astype(BF16))
            low_probs.append(probs.astype(BF16))
        d_value = [dot(one, grad) for one, grad in zip(low_probs, g_m)]
        d_key = [dot(one, q) * SCALE for one, q in zip(g_scores, q_m)]
        full = [dot(one, item[3], TN) for item, one in zip(items, g_scores)]
        d_query = [(own_head(one, lane_head) * SCALE).astype(BF16) for one in full]
        return list(zip(d_query, d_key, d_value))

    def inner(places):
        outs = windows(load_inner(mixed, places, gatt))
        for i, (w, rows) in enumerate(places):
            for g in range(4):
                for col, value in zip(COLS[g], outs[4 * i + g]):
                    gmixed_o[rows, col] = value.astype(BF16)

    def edge(places):
        outs = windows(load_edge(mixed, low, high, places, gatt))
        for i, (m, w, rows, side) in enumerate(places):
            out = high_o if side else low_o
            own, far = (slice(0, 16), slice(16, 32)) if side else (slice(16, 32), slice(0, 16))
            for g in range(4):
                cols = COLS[g]
                d_query, d_key, d_value = outs[4 * i + g]
                gmixed_o[rows, cols[0]] = d_query[own]
                rim_o[m, side, :, cols[0]] = d_key[own]
                rim_o[m, side, :, cols[1]] = d_value[own]
                out[m, :, cols[0]] = d_key[far].astype(BF16)
                out[m, :, cols[1]] = d_value[far].astype(BF16)

    window_loop(edge, inner)
    for m in range(MICRO):
        for base in (m * CELLS, m * CELLS + CELLS - 16):
            gmixed_o[base : base + 16, D:] = jnp.zeros((16, 2 * D), BF16)


def leave_kernel(
    core, gmixed_i, low_i, high_i, rim_i, hidden_i, normed_i, filled_i, gmid_i, qkv_i, gout_i,
    seen, vecs, sums, gm_o, gf_o, small_o, send_o,
    from_low, from_high, rim, hidden, normed, filled, gmid, qkv_w, gout, sems,
):
    pairs = [(qkv_i, qkv_w), (low_i, from_low), (high_i, from_high), (rim_i, rim)]
    for m in range(MICRO):
        rows = pl.ds(m * CELLS, CELLS)
        pairs += [(gmixed_i.at[rows], gm_o.at[rows]), (hidden_i.at[rows], hidden.at[rows])]
        pairs.append((gmid_i.at[rows], gmid.at[rows]))
    pairs += [(normed_i, normed), (filled_i, filled), (gout_i, gout)]
    copies = fetch(pairs, sems)
    small = jnp.zeros((1, D), F32)
    gain_sum, shift_sum, mask_sum, embed_sum, query_sum, value_sum = [small] * 6
    for m in range(MICRO):
        base = m * CELLS
        rows = slice(base, base + CELLS)
        for copy in copies[0 if m == 0 else 3 * m + 4 : 3 * m + 7]:
            copy.wait()
        gm_o[base : base + 16, D:] = (rim[m, 0] + from_low[m].astype(F32)).astype(BF16)
        gm_o[base + CELLS - 16 : base + CELLS, D:] = (rim[m, 1] + from_high[m].astype(F32)).astype(
            BF16
        )
        gm = gm_o[rows, :]
        grad = dot(gm, qkv_w[...], NT)
        normal, inverse = norm_parts(hidden[rows, :])
        g_hidden = gmid[rows, :] + norm_back(grad, normal, inverse, vecs[2:3, :])
        there = seen[rows, :] > 0.5
        g_low = g_hidden.astype(BF16)
        gf_o[rows, :] = g_low
        gain_sum += jnp.sum(grad * normal, axis=0, keepdims=True)
        shift_sum += jnp.sum(grad, axis=0, keepdims=True)
        mask_sum += jnp.sum(jnp.where(there, 0.0, g_hidden), axis=0, keepdims=True)
        embed_sum += jnp.sum(jnp.where(there, g_low.astype(F32), 0.0), axis=0, keepdims=True)
        query_sum += jnp.sum(gm[:, :D].astype(F32), axis=0, keepdims=True)
        value_sum += jnp.sum(gm[:, 2 * D :].astype(F32), axis=0, keepdims=True)
    small_o[...] = jnp.concatenate(
        [
            embed_sum, mask_sum, gain_sum, shift_sum, query_sum, value_sum,
            small, small, sums[...],
        ],
        axis=0,
    )
    for copy in copies[3 * MICRO + 4 :]:
        copy.wait()
    one_half(core[0] != 0, send_o, normed, filled, gm_o, gf_o, gout, small_o)


def one_half(first, out, normed, filled, gm, gf, gout, small):
    @pl.when(first)
    def _():
        turned = jnp.transpose(normed[...])
        for b in range(3):
            cols = slice(512 * b, 512 * b + 512)
            out[cols, :] = dot(turned, gm[:, cols]).astype(BF16)

    @pl.when(jnp.logical_not(first))
    def _():
        out[0:512, :] = gout[...]
        out[512:1280, :] = dot(jnp.transpose(filled[...]), gf[...]).astype(BF16)
        out[1280:1296, :] = small[...].astype(BF16)
        out[1296:1536, :] = jnp.zeros((240, D), BF16)


def leave_keep_kernel(core, gm, gf, small, normed, filled, gout, cell, keep_o, ret_o):
    one_half(core[0] == 0, keep_o, normed, filled, gm, gf, gout, small)
    ret_o[...] = dot(one_hot(iota((GOT, ALL), 1) == cell[...]), gf[...]).astype(BF16)


def return_kernel(dest, came, embed_w, out):
    for m in range(MICRO):
        select = one_hot(iota((dest.shape[1], GOT), 1) == dest[m])
        g_proj = dot(select, came[...]).astype(BF16)
        out[m] = dot(g_proj, embed_w[...], NT).astype(BF16)


def unpack_one_kernel(down_i, up_i, down_o, up_o):
    down_o[...] = down_i[...].reshape(512, D).astype(F32)
    up_o[...] = up_i[...].reshape(512, D).astype(F32)


def unpack_one(gathered):
    block = (16, 1, 32, D)
    return pl.pallas_call(
        unpack_one_kernel,
        name="unpack_one",
        grid=(4,),
        out_shape=[jax.ShapeDtypeStruct((FF, D), F32), jax.ShapeDtypeStruct((D, FF), F32)],
        in_specs=[
            pl.BlockSpec(block, lambda i: (i % 2, i // 2, 0, 0)),
            pl.BlockSpec(block, lambda i: (2 + i % 2, i // 2, 0, 0)),
        ],
        out_specs=[
            pl.BlockSpec((512, D), lambda i: (i, 0)),
            pl.BlockSpec((512, D), lambda i: (0, i)),
        ],
        compiler_params=pltpu.CompilerParams(vmem_limit_bytes=16 * 2**20),
        cost_estimate=pl.CostEstimate(flops=0, bytes_accessed=12 * 2**20, transcendentals=0),
    )(gathered, gathered)


def unpack_two_kernel(core, mine, other, qkv_o, embed_o, out_o, small_o):
    def write(first, second):
        for b in range(3):
            qkv_o[:, 512 * b : 512 * b + 512] = first[512 * b : 512 * b + 512, :].astype(F32)
        out_o[...] = second[0:512, :].astype(F32)
        embed_o[...] = second[512:1280, :].astype(F32)
        small_o[...] = second[1280:1296, :].astype(F32)

    @pl.when(core[0] == 0)
    def _():
        write(mine, other)

    @pl.when(core[0] != 0)
    def _():
        write(other, mine)


def clip_ident(lengths, rows):
    first = lengths[:, 0:1]
    second = first + lengths[:, 1:2]
    ident = (rows[None, :] >= first).astype(jnp.int32) + (rows[None, :] >= second).astype(jnp.int32)
    start = jnp.where(ident >= 1, first, 0) + jnp.where(ident >= 2, lengths[:, 1:2], 0)
    inside = (rows >= 0) & (rows < LONG)
    return (jnp.where(inside[None, :], ident, -1), rows[None, :] - start)


def position_tables(row_in_clip, width):
    quarter = width // 4
    omega = 1.0 / 10000.0 ** (jnp.arange(quarter, dtype=jnp.float32) / quarter)
    row_angle = row_in_clip.astype(jnp.float32)[..., None] * omega
    freq_angle = jnp.arange(FREQ, dtype=jnp.float32)[:, None] * omega
    row_part = jnp.concatenate([jnp.sin(row_angle), jnp.cos(row_angle)], -1)
    freq_part = jnp.concatenate([jnp.sin(freq_angle), jnp.cos(freq_angle)], -1)
    return row_part.reshape(-1, width // 2), freq_part


def window_mask(ident):
    cells = jnp.repeat(ident.reshape(MICRO * 7, 4), FREQ, axis=1)
    freq = np.tile((np.arange(FREQ) + 2) % 8 // 4, 4)
    same = (cells[:, :, None] == cells[:, None, :]) & (cells[:, :, None] >= 0)
    same = same & jnp.asarray(freq[:, None] == freq[None, :])[None]
    return jnp.tile(same.astype(F32), (1, 1, 4))


def on_device(
    encoded, visible_pos, clip_len, cotangent, embed_weight, embed_bias, mask_token, attn_gain,
    attn_shift, qkv_weight, query_bias, value_bias, out_weight, out_bias, mlp_gain, mlp_shift,
    up_weight, up_bias, down_weight, down_bias,
):
    both = ("clip", "band")
    groups = lax.axis_size("clip")
    bands = lax.axis_size("band")
    band = lax.axis_index("band")
    side = band % 2
    core = side.astype(jnp.int32).reshape(1)
    halves = [
        [c * bands + 2 * x + k for c in range(groups) for x in range(bands // 2)] for k in range(2)
    ]
    swap = [(i, i ^ 1) for i in range(bands)]
    forward = [(i, i + 1) for i in range(bands - 1)]
    backward = [(b, a) for a, b in forward]
    chips = groups * bands // 2

    def to_all(block):
        return lax.all_to_all(
            block, both, split_axis=0, concat_axis=0, tiled=True, axis_index_groups=halves
        )

    def chip_sum(keep, other):
        mine = (keep.astype(F32) + other.astype(F32)).astype(BF16)
        return mine.reshape(chips, -1, D)

    def total(parts):
        return jnp.sum(parts.astype(F32), 0).astype(BF16)

    def spread(chunk):
        return jnp.broadcast_to(chunk[None], (chips,) + chunk.shape)

    vis = visible_pos.shape[1]
    packed, dest = call(
        pack_kernel, "pack", [((GOT, ENC), BF16), ((MICRO, vis, 1), jnp.int32)],
        (band.astype(jnp.int32).reshape(1), visible_pos, encoded), smem=1,
        flops=GOT * MICRO * vis * ENC * 2,
    )
    cot = cotangent.reshape(ALL, D)
    (g_act,) = call(
        before_kernel, "before", [((ALL, FF), F32)], (cot, down_weight), flops=2 * ALL * D * FF,
    )
    got = lax.all_to_all(
        packed.reshape(SRC, BLK, ENC), "clip", split_axis=0, concat_axis=0, tiled=True
    ).reshape(GOT, ENC)

    place = np.arange(GOT)
    within = place % BLK
    index = np.zeros((8, GOT), np.int32)
    index[0], index[1], index[2] = place // BLK, within, np.where(within < 36, within // CAP, 99)
    heads = jnp.asarray(np.arange(128)[None, :] // 32 == np.arange(16)[:, None] % 4, BF16)

    unused, row_in_clip = clip_ident(clip_len[:, 0], band * ROWS + jnp.arange(ROWS))
    row_table, freq_table = position_tables(row_in_clip, D)
    ident_ext, unused = clip_ident(clip_len[:, 0], band * ROWS - 2 + jnp.arange(ROWS + 4))
    mask = window_mask(ident_ext)
    zero = jnp.zeros((D,), BF16)
    vecs_one = jnp.stack([embed_bias, mask_token, attn_gain, attn_shift] * 2).astype(F32)
    vecs_two = jnp.stack([out_bias, mlp_gain, mlp_shift, down_bias] * 2).astype(F32)
    qkv_b = jnp.concatenate([query_bias, zero, value_bias]).astype(F32)[None]
    up_b = up_bias.astype(F32)[None]

    hidden, normed, mixed, filled, seen, cell, low, high = call(
        enter_kernel, "enter",
        [
            ((ALL, D), F32), ((ALL, D), BF16), ((ALL, 3 * D), BF16), ((ALL, ENC), BF16),
            ((ALL, 1), F32), ((GOT, 1), jnp.int32),
            ((MICRO, 16, 2 * D), BF16), ((MICRO, 16, 2 * D), BF16),
        ],
        (
            jnp.asarray(index), jnp.asarray(np.ascontiguousarray(index.T)), got, row_table,
            freq_table, embed_weight, qkv_weight, vecs_one, qkv_b,
        ),
        scratch=[
            pltpu.VMEM((GOT, ENC), BF16), pltpu.VMEM((ENC, D), BF16), pltpu.VMEM((D, 3 * D), BF16),
            pltpu.SemaphoreType.DMA((3,)),
        ],
        far=(2, 5, 6),
        flops=2 * ALL * (GOT * ENC + ENC * D + 3 * D * D),
    )
    from_low = lax.ppermute(high, "band", forward)
    from_high = lax.ppermute(low, "band", backward)
    attended, probs = call(
        attend_kernel, "attend",
        [((ALL, D), BF16), ((MICRO * 7, 32, D), F32)],
        (mixed, from_low, from_high, mask, heads),
        flops=MICRO * 7 * 4 * 2**20,
    )
    middle, act, gexp, n2t, send = call(
        mlp_kernel, "mlp",
        [
            ((ALL, D), F32), ((ALL, FF), BF16), ((ALL, FF), BF16), ((D, ALL), BF16),
            ((FF, D), BF16),
        ],
        (core, hidden, attended, cot, g_act, out_weight, up_weight, vecs_two, up_b),
        scratch=[pltpu.VMEM((ALL, D), BF16)],
        smem=1, flops=2 * ALL * (2 * D * FF + D * D), vmem=24,
    )
    (keep,) = call(
        mlp_keep_kernel, "mlp_keep", [((FF, D), BF16)], (core, act, gexp, n2t, cot),
        smem=1, flops=2 * ALL * D * FF,
    )
    chip_one = chip_sum(keep, lax.ppermute(send, "band", swap))
    act, chip_one = lax.optimization_barrier((act, chip_one))
    parts_one = to_all(chip_one)
    inputs = (
        middle, attended, cot, act, gexp, out_weight, up_weight, down_weight, mixed, from_low,
        from_high, probs,
    )
    output, gmid, gout, sums, gmixed, low, high, rim = call(
        back_kernel, "back",
        [
            ((ALL, D), BF16), ((ALL, D), F32), ((D, D), BF16), ((8, D), F32),
            ((ALL, 3 * D), BF16), ((MICRO, 16, 2 * D), BF16), ((MICRO, 16, 2 * D), BF16),
            ((MICRO, 2, 16, 2 * D), F32),
        ],
        inputs + (vecs_two, heads),
        scratch=[pltpu.VMEM(x.shape, x.dtype) for x in inputs]
        + [pltpu.VMEM((ALL, D), BF16)] * 2
        + [pltpu.SemaphoreType.DMA((len(inputs),))],
        flops=2 * ALL * (2 * D * FF + 2 * D * D) + MICRO * 7 * 4 * 2**22,
        far=range(len(inputs)), vmem=44,
    )
    from_low = lax.ppermute(high, "band", forward)
    from_high = lax.ppermute(low, "band", backward)
    total_one = total(parts_one)
    total_one, from_low, from_high = lax.optimization_barrier((total_one, from_low, from_high))
    kept = (from_low, from_high, rim, hidden, normed, filled, gmid, qkv_weight, gout)
    fetched = (gmixed,) + kept
    gm, gf, small, send = call(
        leave_kernel, "leave",
        [((ALL, 3 * D), BF16), ((ALL, D), BF16), ((16, D), F32), ((3 * D, D), BF16)],
        (core,) + fetched + (seen, vecs_one, sums),
        scratch=[pltpu.VMEM(x.shape, x.dtype) for x in kept]
        + [pltpu.SemaphoreType.DMA((3 * MICRO + 7,))],
        smem=1, flops=2 * ALL * 5 * D * D, far=range(1, 1 + len(fetched)), vmem=50,
    )
    other = lax.ppermute(send, "band", swap)
    total_one = lax.all_gather(total_one, both, axis=0).reshape(chips, 2, -1, D)
    keep, returned = call(
        leave_keep_kernel, "leave_keep", [((3 * D, D), BF16), ((GOT, D), BF16)],
        (core, gm, gf, small, normed, filled, gout, cell),
        smem=1, flops=2 * ALL * (2 * D * D + GOT * D),
    )
    mine = to_all(spread(total(to_all(chip_sum(keep, other))))).reshape(-1, D)
    mine, returned = lax.optimization_barrier((mine, returned))
    qkv, g_embed, g_out, small = call(
        unpack_two_kernel, "unpack_two",
        [((D, 3 * D), F32), ((ENC, D), F32), ((D, D), F32), ((16, D), F32)],
        (core, mine, lax.ppermute(mine, "band", swap)), smem=1,
    )
    came = lax.all_to_all(
        returned.reshape(SRC, BLK, D), "clip", split_axis=0, concat_axis=0, tiled=True
    ).reshape(GOT, D)
    down, up = unpack_one(total_one)
    came, small, down = lax.optimization_barrier((came, small, down))
    (grad_enc,) = call(
        return_kernel, "return", [((MICRO, vis, ENC), BF16)], (dest, came, embed_weight),
        flops=2 * MICRO * vis * D * (GOT + ENC),
    )
    return (
        output.reshape(cotangent.shape), grad_enc, g_embed, small[0], small[1], small[2],
        small[3], qkv, small[4], small[5], g_out, small[8], small[9], small[10], up,
        small[12:16].reshape(FF), down, small[11],
    )


def solution(mesh):
    whole = P()
    return jax.shard_map(
        on_device,
        mesh=mesh,
        in_specs=(
            P(None, ("clip", "band"), None),
            P(None, ("clip", "band")),
            P(None, "clip", None),
            P(None, "clip", "band", None, None),
        )
        + (whole,) * 16,
        out_specs=(P(None, "clip", "band", None, None), P(None, ("clip", "band"), None))
        + (whole,) * 16,
        check_vma=False,
    )
```

```python
import jax
import jax.numpy as jnp
import numpy as np
from jax import lax
from jax.experimental import pallas as pl
from jax.experimental.pallas import tpu as pltpu
from jax.sharding import PartitionSpec as P

HEADS = 16
FREQ = 8
LONG = 192
MICRO = 4
ROWS = 24
CELLS = ROWS * FREQ
ALL = MICRO * CELLS
CAP = 9
BLK = 40
SRC = 16
GOT = SRC * BLK
D = 512
FF = 2048
ENC = 768
EPS = 1e-06
SCALE = (D // HEADS) ** (-0.5)
F32 = jnp.float32
BF16 = jnp.bfloat16

NN = (((1,), (0,)), ((), ()))
NT = (((1,), (1,)), ((), ()))
TN = (((0,), (0,)), ((), ()))


def dot(left, right, dims=NN):
    return lax.dot_general(left, right, dims, preferred_element_type=F32)


def iota(shape, dim):
    return lax.broadcasted_iota(jnp.int32, shape, dim)


def one_hot(hit):
    return jnp.where(hit, 1.0, 0.0).astype(BF16)


def call(kernel, name, out_shape, args, scratch=(), smem=0, flops=0, vmem=16, far=()):
    spaces = [pltpu.SMEM] * smem + [pltpu.VMEM] * (len(args) - smem)
    for i in far:
        spaces[i] = pltpu.HBM
    outs = [jax.ShapeDtypeStruct(shape, dtype) for shape, dtype in out_shape]
    size = sum(a.size * a.dtype.itemsize for a in args) + sum(
        o.size * o.dtype.itemsize for o in outs
    )
    return pl.pallas_call(
        kernel,
        name=name,
        out_shape=outs,
        in_specs=[pl.BlockSpec(memory_space=space) for space in spaces],
        out_specs=[pl.BlockSpec(memory_space=pltpu.VMEM)] * len(outs),
        scratch_shapes=list(scratch),
        compiler_params=pltpu.CompilerParams(vmem_limit_bytes=vmem * 2**20),
        cost_estimate=pl.CostEstimate(flops=flops, bytes_accessed=size, transcendentals=0),
    )(*args)


def pack_kernel(band, pos, enc, out, dest):
    count = pos.shape[1]
    low = iota((count, count), 0)
    high = iota((count, count), 1)
    packed = jnp.zeros((GOT, ENC), F32)
    places = jnp.zeros((SRC, 128), F32)
    for m in range(MICRO):
        cell_r = pos[m : m + 1, :]
        cell_c = jnp.sum(jnp.where(low == high, cell_r, 0), axis=1, keepdims=True)
        slot = LONG * FREQ
        dev_r = jnp.sum(
            jnp.where(cell_r >= slot * iota((SRC, count), 0) + slot, 1, 0), axis=0, keepdims=True
        )
        dev_c = jnp.sum(
            jnp.where(cell_c >= slot * iota((count, SRC), 1) + slot, 1, 0), axis=1, keepdims=True
        )
        same = dev_c == dev_r
        rank_r = jnp.sum(jnp.where(same & (low < high), 1, 0), axis=0, keepdims=True)
        rank_c = jnp.sum(jnp.where(same & (high < low), 1, 0), axis=1, keepdims=True)
        dest[m] = dev_c * BLK + m * CAP + rank_c
        select = one_hot(iota((GOT, count), 0) == dev_r * BLK + m * CAP + rank_r)
        packed = packed + dot(select, enc[m])
        number = cell_r - dev_r * slot - band[0] * CELLS + 1
        to_dev = jnp.where(iota((SRC, count), 0) == dev_r, number.astype(F32), 0.0).astype(BF16)
        to_lane = one_hot(iota((count, 128), 1) == m * CAP + rank_c)
        places = places + dot(to_dev, to_lane)
    spread = one_hot(iota((GOT, SRC), 0) == iota((GOT, SRC), 1) * BLK + (BLK - 4))
    out[:, :128] = (packed[:, :128] + dot(spread, places.astype(BF16))).astype(BF16)
    out[:, 128:] = packed[:, 128:].astype(BF16)


def norm_parts(values):
    center = values - jnp.mean(values, -1, keepdims=True)
    inverse = lax.rsqrt(jnp.mean(center * center, -1, keepdims=True) + EPS)
    return center * inverse, inverse


def norm_back(grad, normal, inverse, gain):
    scaled = grad * gain
    return inverse * (
        scaled
        - jnp.mean(scaled, -1, keepdims=True)
        - normal * jnp.mean(scaled * normal, -1, keepdims=True)
    )


def fetch(pairs, sems):
    copies = [pltpu.make_async_copy(far, near, sems.at[i]) for i, (far, near) in enumerate(pairs)]
    for copy in copies:
        copy.start()
    return copies


def enter_kernel(
    idx_r, idx_c, got_i, row_table, freq_table, embed_i, qkv_i, vecs, qkv_b,
    hidden_o, normed_o, mixed_o, filled_o, seen_o, cell_o, low_o, high_o,
    got, embed_w, qkv_w, sems,
):
    copies = fetch([(got_i, got), (embed_i, embed_w), (qkv_i, qkv_w)], sems)
    copies[0].wait()
    hit = one_hot(iota((SRC, GOT), 1) == iota((SRC, GOT), 0) * BLK + (BLK - 4))
    numbers = dot(hit, got[:, :128]).astype(BF16)
    spread_r = dot(numbers, one_hot(iota((SRC, GOT), 0) == idx_r[0:1, :]), TN)
    value_r = jnp.sum(
        jnp.where(iota((128, GOT), 0) == idx_r[1:2, :], spread_r, 0.0), axis=0, keepdims=True
    )
    cell_r = jnp.where(
        value_r > 0.5, idx_r[2:3, :] * CELLS + value_r.astype(jnp.int32) - 1, -1
    )
    spread_c = dot(one_hot(iota((GOT, SRC), 1) == idx_c[:, 0:1]), numbers)
    value_c = jnp.sum(
        jnp.where(iota((GOT, 128), 1) == idx_c[:, 1:2], spread_c, 0.0), axis=1, keepdims=True
    )
    cell_o[...] = jnp.where(
        value_c > 0.5, idx_c[:, 2:3] * CELLS + value_c.astype(jnp.int32) - 1, -1
    )
    for m in range(MICRO):
        rows = slice(m * CELLS, (m + 1) * CELLS)
        match = jnp.where(iota((CELLS, GOT), 0) + m * CELLS == cell_r, 1.0, 0.0)
        seen = jnp.sum(match, axis=1, keepdims=True)
        filled = dot(match.astype(BF16), got[...]).astype(BF16)
        filled_o[rows, :] = filled
        seen_o[rows, :] = seen
    copies[1].wait()
    copies[2].wait()
    freq = jnp.broadcast_to(freq_table[...][None], (ROWS, FREQ, D // 2)).reshape(CELLS, D // 2)
    for m in range(MICRO):
        rows = slice(m * CELLS, (m + 1) * CELLS)
        seen = seen_o[rows, :]
        proj = (dot(filled_o[rows, :], embed_w[...]) + vecs[0:1, :]).astype(BF16).astype(F32)
        line = row_table[m * ROWS : (m + 1) * ROWS, :]
        line = jnp.broadcast_to(line[:, None, :], (ROWS, FREQ, D // 2)).reshape(CELLS, D // 2)
        table = jnp.concatenate([line, freq], axis=1)
        hidden = jnp.where(seen > 0.5, proj, vecs[1:2, :]) + table
        hidden_o[rows, :] = hidden
        normal, unused = norm_parts(hidden)
        normed = (normal * vecs[2:3, :] + vecs[3:4, :]).astype(BF16)
        normed_o[rows, :] = normed
        mixed = (dot(normed, qkv_w[...]) + qkv_b[...]).astype(BF16)
        mixed_o[rows, :] = mixed
        low_o[m] = mixed[:16, D:]
        high_o[m] = mixed[CELLS - 16 :, D:]


def head_rows(block, heads):
    return jnp.concatenate([block * heads[h : h + 1, :] for h in range(4)], axis=0)


def own_head(full, lane_head):
    out = full[0:32, :]
    for h in range(1, 4):
        out = jnp.where(lane_head == h, full[32 * h : 32 * h + 32, :], out)
    return out


def window_loop(edge, inner):
    def inside(p, carry):
        places = []
        for m in range(MICRO):
            base = pl.multiple_of(m * CELLS + 32 * p - 16, 16)
            places.append((m * 7 + p, pl.ds(base, 32)))
        inner(places)
        return carry

    def ends(i, carry):
        places = []
        for j in range(2):
            m = 2 * i + j
            first = pl.multiple_of(m * CELLS, 16)
            last = pl.multiple_of(m * CELLS + CELLS - 16, 16)
            places.append((m, m * 7, pl.ds(first, 16), 0))
            places.append((m, m * 7 + 6, pl.ds(last, 16), 1))
        edge(places)
        return carry

    lax.fori_loop(1, 6, inside, 0)
    lax.fori_loop(0, MICRO // 2, ends, 0)


def with_halo(own, halo, side):
    return jnp.concatenate([own, halo] if side else [halo, own], axis=0)


COLS = [[slice(D * i + 128 * g, D * i + 128 * g + 128) for i in range(3)] for g in range(4)]


def load_inner(mixed, places, grads=None):
    items = []
    for w, rows in places:
        for g in range(4):
            item = [mixed[rows, c] for c in COLS[g]]
            items.append((w, g, *item, None if grads is None else grads[rows, COLS[g][0]]))
    return items


def load_edge(mixed, low, high, places, grads=None):
    zero = jnp.zeros((16, 128), BF16)
    items = []
    for m, w, rows, side in places:
        halo = high if side else low
        for g in range(4):
            cols = COLS[g]
            q = with_halo(mixed[rows, cols[0]], zero, side)
            k = with_halo(mixed[rows, cols[1]], halo[m, :, cols[0]], side)
            v = with_halo(mixed[rows, cols[2]], halo[m, :, cols[1]], side)
            grad = None if grads is None else with_halo(grads[rows, cols[0]], zero, side)
            items.append((w, g, q, k, v, grad))
    return items


def attend_kernel(mixed, low, high, mask, heads_i, attended_o, probs_o):
    heads = heads_i[...]
    lane_head = iota((32, 128), 1) // 32

    def windows(items):
        scores = [dot(k, head_rows(q, heads), NT) * SCALE for w, g, q, k, v, _ in items]
        probs = []
        for (w, g, *_), score in zip(items, scores):
            score = jnp.where(mask[w] > 0.5, score, -1e30)
            grown = jnp.exp(score - jnp.max(score, axis=0, keepdims=True))
            one = grown * (1.0 / jnp.sum(grown, axis=0, keepdims=True))
            probs_o[w, :, 128 * g : 128 * g + 128] = one
            probs.append(one.astype(BF16))
        full = [dot(one, item[4], TN) for item, one in zip(items, probs)]
        return [own_head(one, lane_head).astype(BF16) for one in full]

    def inner(places):
        outs = windows(load_inner(mixed, places))
        for i, (w, rows) in enumerate(places):
            for g in range(4):
                attended_o[rows, COLS[g][0]] = outs[4 * i + g]

    def edge(places):
        outs = windows(load_edge(mixed, low, high, places))
        for i, (m, w, rows, side) in enumerate(places):
            for g in range(4):
                out = outs[4 * i + g]
                attended_o[rows, COLS[g][0]] = out[:16] if side else out[16:]

    window_loop(edge, inner)


def gelu_parts(x):
    bell = jnp.exp(-0.5 * x * x)
    t = 1.0 / (1.0 + 0.3275911 * 0.5**0.5 * jnp.abs(x))
    poly = 0.127414796 + t * (
        -0.142248368 + t * (0.7107068705 + t * (-0.7265760135 + t * 0.5307027145))
    )
    tail = t * poly * bell
    share = jnp.where(x >= 0, 1.0 - tail, tail)
    return x * share, share + x * bell * 0.3989422804014327


def before_kernel(cot, down_w, g_act_o):
    for f in range(4):
        cols = slice(512 * f, 512 * f + 512)
        g_act_o[:, cols] = dot(cot[...], down_w[cols, :], NT)


def mlp_kernel(
    core, hidden, attended, cot, g_act, out_w, up_w, vecs, up_b,
    middle_o, act_o, gexp_o, n2t_o, send_o, n2_s,
):
    tile = 256
    blocks = [slice(512 * f, 512 * f + 512) for f in range(4)]

    lines = [slice(i * tile, (i + 1) * tile) for i in range(ALL // tile)]
    for rows in lines:
        middle = hidden[rows, :] + dot(attended[rows, :], out_w[...]) + vecs[0:1, :]
        middle_o[rows, :] = middle
        normal, unused = norm_parts(middle)
        n2_s[rows, :] = (normal * vecs[1:2, :] + vecs[2:3, :]).astype(BF16)
    places = [(rows, cols) for rows in lines for cols in blocks]
    ahead = dot(n2_s[lines[0], :], up_w[:, blocks[0]])
    for i, (rows, cols) in enumerate(places):
        expand = ahead + up_b[0:1, cols]
        if i + 1 < len(places):
            ahead = dot(n2_s[places[i + 1][0], :], up_w[:, places[i + 1][1]])
        value, slope = gelu_parts(expand)
        act_o[rows, cols] = value.astype(BF16)
        gexp_o[rows, cols] = (g_act[rows, cols] * slope).astype(BF16)
    n2t_o[...] = jnp.transpose(n2_s[...])
    weight_half(1 - core[0], send_o, act_o, gexp_o, n2t_o, cot)


def weight_half(half, out, act, gexp, n2t, cot):
    for b in range(2):
        cols = pl.ds(pl.multiple_of(half * 1024 + 512 * b, 512), 512)
        rows = slice(512 * b, 512 * b + 512)
        out[rows, :] = dot(act[:, cols], cot[...], TN).astype(BF16)
        rows = slice(1024 + 512 * b, 1536 + 512 * b)
        out[rows, :] = dot(n2t[...], gexp[:, cols]).astype(BF16)


def mlp_keep_kernel(core, act, gexp, n2t, cot, keep_o):
    weight_half(core[0], keep_o, act, gexp, n2t, cot)


def back_kernel(
    middle_i, attended_i, cot_i, act_i, gexp_i, out_i, up_i, down_i, mixed_i, low_i, high_i,
    probs_f, vecs, heads_i,
    output_o, gmid_o, gout_o, sums_o, gmixed_o, low_o, high_o, rim_o,
    middle_s, attended, cot, act, gexp, out_w, up_w, down_w, mixed, low, high, probs_i, gatt, gb_s,
    sems,
):
    copies = fetch(
        [
            (up_i, up_w), (gexp_i, gexp), (down_i, down_w), (act_i, act), (middle_i, middle_s),
            (cot_i, cot), (out_i, out_w), (attended_i, attended), (mixed_i, mixed),
            (low_i, low), (high_i, high), (probs_f, probs_i),
        ],
        sems,
    )
    tile = 256
    sums_o[...] = jnp.zeros((8, D), F32)
    for i in range(ALL // tile):
        rows = slice(i * tile, (i + 1) * tile)
        if i == 0:
            copies[0].wait()
            copies[1].wait()
        grad = dot(gexp[rows, :], up_w[...], NT)
        if i == 0:
            copies[2].wait()
            copies[3].wait()
            copies[4].wait()
        middle = middle_s[rows, :]
        output_o[rows, :] = (middle + vecs[3:4, :] + dot(act[rows, :], down_w[...])).astype(BF16)
        if i == 0:
            copies[5].wait()
            copies[6].wait()
        normal, inverse = norm_parts(middle)
        g_float = cot[rows, :].astype(F32)
        g_mid = g_float + norm_back(grad, normal, inverse, vecs[1:2, :])
        gmid_o[rows, :] = g_mid
        g_low = g_mid.astype(BF16)
        gb_s[rows, :] = g_low
        gatt[rows, :] = dot(g_low, out_w[...], NT).astype(BF16)
        sums_o[0:1, :] += jnp.sum(g_low.astype(F32), axis=0, keepdims=True)
        sums_o[1:2, :] += jnp.sum(grad * normal, axis=0, keepdims=True)
        sums_o[2:3, :] += jnp.sum(grad, axis=0, keepdims=True)
        sums_o[3:4, :] += jnp.sum(g_float, axis=0, keepdims=True)
        for f in range(4):
            part = gexp[rows, 512 * f : 512 * f + 512].astype(F32)
            sums_o[4 + f : 5 + f, :] += jnp.sum(part, axis=0, keepdims=True)
    copies[7].wait()
    gout_o[...] = dot(attended[...], gb_s[...], TN).astype(BF16)
    for copy in copies[8:]:
        copy.wait()
    attend_back(mixed, low, high, probs_i, gatt, heads_i, gmixed_o, low_o, high_o, rim_o)


def attend_back(
    mixed, low, high, probs_i, gatt, heads_i, gmixed_o, low_o, high_o, rim_o
):
    heads = heads_i[...]
    lane_head = iota((32, 128), 1) // 32

    def windows(items):
        q_m = [head_rows(q, heads) for w, g, q, k, v, grad in items]
        g_m = [head_rows(grad, heads) for w, g, q, k, v, grad in items]
        g_probs = [dot(item[4], one, NT) for item, one in zip(items, g_m)]
        low_probs, g_scores = [], []
        for (w, g, *_), g_prob in zip(items, g_probs):
            probs = probs_i[w, :, 128 * g : 128 * g + 128]
            inner = jnp.sum(probs * g_prob, axis=0, keepdims=True)
            g_scores.append((probs * (g_prob - inner)).astype(BF16))
            low_probs.append(probs.astype(BF16))
        d_value = [dot(one, grad) for one, grad in zip(low_probs, g_m)]
        d_key = [dot(one, q) * SCALE for one, q in zip(g_scores, q_m)]
        full = [dot(one, item[3], TN) for item, one in zip(items, g_scores)]
        d_query = [(own_head(one, lane_head) * SCALE).astype(BF16) for one in full]
        return list(zip(d_query, d_key, d_value))

    def inner(places):
        outs = windows(load_inner(mixed, places, gatt))
        for i, (w, rows) in enumerate(places):
            for g in range(4):
                for col, value in zip(COLS[g], outs[4 * i + g]):
                    gmixed_o[rows, col] = value.astype(BF16)

    def edge(places):
        outs = windows(load_edge(mixed, low, high, places, gatt))
        for i, (m, w, rows, side) in enumerate(places):
            out = high_o if side else low_o
            own, far = (slice(0, 16), slice(16, 32)) if side else (slice(16, 32), slice(0, 16))
            for g in range(4):
                cols = COLS[g]
                d_query, d_key, d_value = outs[4 * i + g]
                gmixed_o[rows, cols[0]] = d_query[own]
                rim_o[m, side, :, cols[0]] = d_key[own]
                rim_o[m, side, :, cols[1]] = d_value[own]
                out[m, :, cols[0]] = d_key[far].astype(BF16)
                out[m, :, cols[1]] = d_value[far].astype(BF16)

    window_loop(edge, inner)
    for m in range(MICRO):
        for base in (m * CELLS, m * CELLS + CELLS - 16):
            gmixed_o[base : base + 16, D:] = jnp.zeros((16, 2 * D), BF16)


def leave_kernel(
    core, gmixed_i, low_i, high_i, rim_i, hidden_i, normed_i, filled_i, gmid_i, qkv_i, gout_i,
    seen, vecs, sums, gm_o, gf_o, small_o, send_o,
    from_low, from_high, rim, hidden, normed, filled, gmid, qkv_w, gout, sems,
):
    pairs = [(qkv_i, qkv_w), (low_i, from_low), (high_i, from_high), (rim_i, rim)]
    for m in range(MICRO):
        rows = pl.ds(m * CELLS, CELLS)
        pairs += [(gmixed_i.at[rows], gm_o.at[rows]), (hidden_i.at[rows], hidden.at[rows])]
        pairs.append((gmid_i.at[rows], gmid.at[rows]))
    pairs += [(normed_i, normed), (filled_i, filled), (gout_i, gout)]
    copies = fetch(pairs, sems)
    small = jnp.zeros((1, D), F32)
    gain_sum, shift_sum, mask_sum, embed_sum, query_sum, value_sum = [small] * 6
    for m in range(MICRO):
        base = m * CELLS
        rows = slice(base, base + CELLS)
        for copy in copies[0 if m == 0 else 3 * m + 4 : 3 * m + 7]:
            copy.wait()
        gm_o[base : base + 16, D:] = (rim[m, 0] + from_low[m].astype(F32)).astype(BF16)
        gm_o[base + CELLS - 16 : base + CELLS, D:] = (rim[m, 1] + from_high[m].astype(F32)).astype(
            BF16
        )
        gm = gm_o[rows, :]
        grad = dot(gm, qkv_w[...], NT)
        normal, inverse = norm_parts(hidden[rows, :])
        g_hidden = gmid[rows, :] + norm_back(grad, normal, inverse, vecs[2:3, :])
        there = seen[rows, :] > 0.5
        g_low = g_hidden.astype(BF16)
        gf_o[rows, :] = g_low
        gain_sum += jnp.sum(grad * normal, axis=0, keepdims=True)
        shift_sum += jnp.sum(grad, axis=0, keepdims=True)
        mask_sum += jnp.sum(jnp.where(there, 0.0, g_hidden), axis=0, keepdims=True)
        embed_sum += jnp.sum(jnp.where(there, g_low.astype(F32), 0.0), axis=0, keepdims=True)
        query_sum += jnp.sum(gm[:, :D].astype(F32), axis=0, keepdims=True)
        value_sum += jnp.sum(gm[:, 2 * D :].astype(F32), axis=0, keepdims=True)
    small_o[...] = jnp.concatenate(
        [
            embed_sum, mask_sum, gain_sum, shift_sum, query_sum, value_sum,
            small, small, sums[...],
        ],
        axis=0,
    )
    for copy in copies[3 * MICRO + 4 :]:
        copy.wait()
    one_half(core[0] != 0, send_o, normed, filled, gm_o, gf_o, gout, small_o)


def one_half(first, out, normed, filled, gm, gf, gout, small):
    @pl.when(first)
    def _():
        turned = jnp.transpose(normed[...])
        for b in range(3):
            cols = slice(512 * b, 512 * b + 512)
            out[cols, :] = dot(turned, gm[:, cols]).astype(BF16)

    @pl.when(jnp.logical_not(first))
    def _():
        out[0:512, :] = gout[...]
        out[512:1280, :] = dot(jnp.transpose(filled[...]), gf[...]).astype(BF16)
        out[1280:1296, :] = small[...].astype(BF16)
        out[1296:1536, :] = jnp.zeros((240, D), BF16)


def leave_keep_kernel(core, gm, gf, small, normed, filled, gout, cell, keep_o, ret_o):
    one_half(core[0] == 0, keep_o, normed, filled, gm, gf, gout, small)
    ret_o[...] = dot(one_hot(iota((GOT, ALL), 1) == cell[...]), gf[...]).astype(BF16)


def return_kernel(dest, came, embed_w, out):
    for m in range(MICRO):
        select = one_hot(iota((dest.shape[1], GOT), 1) == dest[m])
        g_proj = dot(select, came[...]).astype(BF16)
        out[m] = dot(g_proj, embed_w[...], NT).astype(BF16)


def unpack_one_kernel(down_i, up_i, down_o, up_o):
    down_o[...] = down_i[...].reshape(512, D).astype(F32)
    up_o[...] = up_i[...].reshape(512, D).astype(F32)


def unpack_one(gathered):
    block = (16, 1, 32, D)
    return pl.pallas_call(
        unpack_one_kernel,
        name="unpack_one",
        grid=(4,),
        out_shape=[jax.ShapeDtypeStruct((FF, D), F32), jax.ShapeDtypeStruct((D, FF), F32)],
        in_specs=[
            pl.BlockSpec(block, lambda i: (i % 2, i // 2, 0, 0)),
            pl.BlockSpec(block, lambda i: (2 + i % 2, i // 2, 0, 0)),
        ],
        out_specs=[
            pl.BlockSpec((512, D), lambda i: (i, 0)),
            pl.BlockSpec((512, D), lambda i: (0, i)),
        ],
        compiler_params=pltpu.CompilerParams(vmem_limit_bytes=16 * 2**20),
        cost_estimate=pl.CostEstimate(flops=0, bytes_accessed=12 * 2**20, transcendentals=0),
    )(gathered, gathered)


def unpack_two_kernel(core, mine, other, qkv_o, embed_o, out_o, small_o):
    def write(first, second):
        for b in range(3):
            qkv_o[:, 512 * b : 512 * b + 512] = first[512 * b : 512 * b + 512, :].astype(F32)
        out_o[...] = second[0:512, :].astype(F32)
        embed_o[...] = second[512:1280, :].astype(F32)
        small_o[...] = second[1280:1296, :].astype(F32)

    @pl.when(core[0] == 0)
    def _():
        write(mine, other)

    @pl.when(core[0] != 0)
    def _():
        write(other, mine)


def sum_kernel(parts_i, out, parts, sems):
    step = parts_i.shape[0] // 4
    blocks = [pl.ds(i * step, step) for i in range(4)]
    copies = fetch([(parts_i.at[block], parts.at[block]) for block in blocks], sems)
    full = jnp.zeros(out.shape, F32)
    for block, copy in zip(blocks, copies):
        copy.wait()
        full = full + jnp.sum(parts[block].astype(F32), axis=0)
    out[...] = full.astype(BF16)


def clip_ident(lengths, rows):
    first = lengths[:, 0:1]
    second = first + lengths[:, 1:2]
    ident = (rows[None, :] >= first).astype(jnp.int32) + (rows[None, :] >= second).astype(jnp.int32)
    start = jnp.where(ident >= 1, first, 0) + jnp.where(ident >= 2, lengths[:, 1:2], 0)
    inside = (rows >= 0) & (rows < LONG)
    return (jnp.where(inside[None, :], ident, -1), rows[None, :] - start)


def position_tables(row_in_clip, width):
    quarter = width // 4
    omega = 1.0 / 10000.0 ** (jnp.arange(quarter, dtype=jnp.float32) / quarter)
    row_angle = row_in_clip.astype(jnp.float32)[..., None] * omega
    freq_angle = jnp.arange(FREQ, dtype=jnp.float32)[:, None] * omega
    row_part = jnp.concatenate([jnp.sin(row_angle), jnp.cos(row_angle)], -1)
    freq_part = jnp.concatenate([jnp.sin(freq_angle), jnp.cos(freq_angle)], -1)
    return row_part.reshape(-1, width // 2), freq_part


def window_mask(ident):
    cells = jnp.repeat(ident.reshape(MICRO * 7, 4), FREQ, axis=1)
    freq = np.tile((np.arange(FREQ) + 2) % 8 // 4, 4)
    same = (cells[:, :, None] == cells[:, None, :]) & (cells[:, :, None] >= 0)
    same = same & jnp.asarray(freq[:, None] == freq[None, :])[None]
    return jnp.tile(same.astype(F32), (1, 1, 4))


def on_device(
    encoded, visible_pos, clip_len, cotangent, embed_weight, embed_bias, mask_token, attn_gain,
    attn_shift, qkv_weight, query_bias, value_bias, out_weight, out_bias, mlp_gain, mlp_shift,
    up_weight, up_bias, down_weight, down_bias,
):
    both = ("clip", "band")
    groups = lax.axis_size("clip")
    bands = lax.axis_size("band")
    band = lax.axis_index("band")
    side = band % 2
    core = side.astype(jnp.int32).reshape(1)
    halves = [
        [c * bands + 2 * x + k for c in range(groups) for x in range(bands // 2)] for k in range(2)
    ]
    swap = [(i, i ^ 1) for i in range(bands)]
    forward = [(i, i + 1) for i in range(bands - 1)]
    backward = [(b, a) for a, b in forward]
    chips = groups * bands // 2

    def to_all(block):
        return lax.all_to_all(
            block, both, split_axis=0, concat_axis=0, tiled=True, axis_index_groups=halves
        )

    def chip_sum(keep, other):
        mine = (keep.astype(F32) + other.astype(F32)).astype(BF16)
        return mine.reshape(chips, -1, D)

    def total(parts):
        return jnp.sum(parts.astype(F32), 0).astype(BF16)

    def spread(chunk):
        return jnp.broadcast_to(chunk[None], (chips,) + chunk.shape)

    vis = visible_pos.shape[1]
    packed, dest = call(
        pack_kernel, "pack", [((GOT, ENC), BF16), ((MICRO, vis, 1), jnp.int32)],
        (band.astype(jnp.int32).reshape(1), visible_pos, encoded), smem=1,
        flops=GOT * MICRO * vis * ENC * 2,
    )
    cot = cotangent.reshape(ALL, D)
    (g_act,) = call(
        before_kernel, "before", [((ALL, FF), F32)], (cot, down_weight), flops=2 * ALL * D * FF,
    )
    got = lax.all_to_all(
        packed.reshape(SRC, BLK, ENC), "clip", split_axis=0, concat_axis=0, tiled=True
    ).reshape(GOT, ENC)

    place = np.arange(GOT)
    within = place % BLK
    index = np.zeros((8, GOT), np.int32)
    index[0], index[1], index[2] = place // BLK, within, np.where(within < 36, within // CAP, 99)
    heads = jnp.asarray(np.arange(128)[None, :] // 32 == np.arange(16)[:, None] % 4, BF16)

    unused, row_in_clip = clip_ident(clip_len[:, 0], band * ROWS + jnp.arange(ROWS))
    row_table, freq_table = position_tables(row_in_clip, D)
    ident_ext, unused = clip_ident(clip_len[:, 0], band * ROWS - 2 + jnp.arange(ROWS + 4))
    mask = window_mask(ident_ext)
    zero = jnp.zeros((D,), BF16)
    vecs_one = jnp.stack([embed_bias, mask_token, attn_gain, attn_shift] * 2).astype(F32)
    vecs_two = jnp.stack([out_bias, mlp_gain, mlp_shift, down_bias] * 2).astype(F32)
    qkv_b = jnp.concatenate([query_bias, zero, value_bias]).astype(F32)[None]
    up_b = up_bias.astype(F32)[None]

    hidden, normed, mixed, filled, seen, cell, low, high = call(
        enter_kernel, "enter",
        [
            ((ALL, D), F32), ((ALL, D), BF16), ((ALL, 3 * D), BF16), ((ALL, ENC), BF16),
            ((ALL, 1), F32), ((GOT, 1), jnp.int32),
            ((MICRO, 16, 2 * D), BF16), ((MICRO, 16, 2 * D), BF16),
        ],
        (
            jnp.asarray(index), jnp.asarray(np.ascontiguousarray(index.T)), got, row_table,
            freq_table, embed_weight, qkv_weight, vecs_one, qkv_b,
        ),
        scratch=[
            pltpu.VMEM((GOT, ENC), BF16), pltpu.VMEM((ENC, D), BF16), pltpu.VMEM((D, 3 * D), BF16),
            pltpu.SemaphoreType.DMA((3,)),
        ],
        far=(2, 5, 6),
        flops=2 * ALL * (GOT * ENC + ENC * D + 3 * D * D),
    )
    from_low = lax.ppermute(high, "band", forward)
    from_high = lax.ppermute(low, "band", backward)
    attended, probs = call(
        attend_kernel, "attend",
        [((ALL, D), BF16), ((MICRO * 7, 32, D), F32)],
        (mixed, from_low, from_high, mask, heads),
        flops=MICRO * 7 * 4 * 2**20,
    )
    middle, act, gexp, n2t, send = call(
        mlp_kernel, "mlp",
        [
            ((ALL, D), F32), ((ALL, FF), BF16), ((ALL, FF), BF16), ((D, ALL), BF16),
            ((FF, D), BF16),
        ],
        (core, hidden, attended, cot, g_act, out_weight, up_weight, vecs_two, up_b),
        scratch=[pltpu.VMEM((ALL, D), BF16)],
        smem=1, flops=2 * ALL * (2 * D * FF + D * D), vmem=24,
    )
    (keep,) = call(
        mlp_keep_kernel, "mlp_keep", [((FF, D), BF16)], (core, act, gexp, n2t, cot),
        smem=1, flops=2 * ALL * D * FF,
    )
    chip_one = chip_sum(keep, lax.ppermute(send, "band", swap))
    act, chip_one = lax.optimization_barrier((act, chip_one))
    parts_one = to_all(chip_one)
    inputs = (
        middle, attended, cot, act, gexp, out_weight, up_weight, down_weight, mixed, from_low,
        from_high, probs,
    )
    output, gmid, gout, sums, gmixed, low, high, rim = call(
        back_kernel, "back",
        [
            ((ALL, D), BF16), ((ALL, D), F32), ((D, D), BF16), ((8, D), F32),
            ((ALL, 3 * D), BF16), ((MICRO, 16, 2 * D), BF16), ((MICRO, 16, 2 * D), BF16),
            ((MICRO, 2, 16, 2 * D), F32),
        ],
        inputs + (vecs_two, heads),
        scratch=[pltpu.VMEM(x.shape, x.dtype) for x in inputs]
        + [pltpu.VMEM((ALL, D), BF16)] * 2
        + [pltpu.SemaphoreType.DMA((len(inputs),))],
        flops=2 * ALL * (2 * D * FF + 2 * D * D) + MICRO * 7 * 4 * 2**22,
        far=range(len(inputs)), vmem=44,
    )
    from_low = lax.ppermute(high, "band", forward)
    from_high = lax.ppermute(low, "band", backward)
    (total_one,) = call(
        sum_kernel, "sum", [(parts_one.shape[1:], BF16)], (parts_one,),
        scratch=[pltpu.VMEM(parts_one.shape, BF16), pltpu.SemaphoreType.DMA((4,))],
        far=(0,),
    )
    total_one, from_low, from_high = lax.optimization_barrier((total_one, from_low, from_high))
    kept = (from_low, from_high, rim, hidden, normed, filled, gmid, qkv_weight, gout)
    fetched = (gmixed,) + kept
    gm, gf, small, send = call(
        leave_kernel, "leave",
        [((ALL, 3 * D), BF16), ((ALL, D), BF16), ((16, D), F32), ((3 * D, D), BF16)],
        (core,) + fetched + (seen, vecs_one, sums),
        scratch=[pltpu.VMEM(x.shape, x.dtype) for x in kept]
        + [pltpu.SemaphoreType.DMA((3 * MICRO + 7,))],
        smem=1, flops=2 * ALL * 5 * D * D, far=range(1, 1 + len(fetched)), vmem=50,
    )
    other = lax.ppermute(send, "band", swap)
    total_one = lax.all_gather(total_one, both, axis=0).reshape(chips, 2, -1, D)
    keep, returned = call(
        leave_keep_kernel, "leave_keep", [((3 * D, D), BF16), ((GOT, D), BF16)],
        (core, gm, gf, small, normed, filled, gout, cell),
        smem=1, flops=2 * ALL * (2 * D * D + GOT * D),
    )
    mine = to_all(spread(total(to_all(chip_sum(keep, other))))).reshape(-1, D)
    mine, returned = lax.optimization_barrier((mine, returned))
    qkv, g_embed, g_out, small = call(
        unpack_two_kernel, "unpack_two",
        [((D, 3 * D), F32), ((ENC, D), F32), ((D, D), F32), ((16, D), F32)],
        (core, mine, lax.ppermute(mine, "band", swap)), smem=1,
    )
    came = lax.all_to_all(
        returned.reshape(SRC, BLK, D), "clip", split_axis=0, concat_axis=0, tiled=True
    ).reshape(GOT, D)
    down, up = unpack_one(total_one)
    lines = tuple(small[i] for i in (0, 1, 2, 3, 4, 5, 8, 9, 10, 11))
    lines += (small[12:16].reshape(FF),)
    came, down, lines = lax.optimization_barrier((came, down, lines))
    (grad_enc,) = call(
        return_kernel, "return", [((MICRO, vis, ENC), BF16)], (dest, came, embed_weight),
        flops=2 * MICRO * vis * D * (GOT + ENC),
    )
    return (
        output.reshape(cotangent.shape), grad_enc, g_embed, *lines[:4], qkv, *lines[4:6], g_out,
        *lines[6:9], up, lines[10], down, lines[9],
    )


def solution(mesh):
    whole = P()
    return jax.shard_map(
        on_device,
        mesh=mesh,
        in_specs=(
            P(None, ("clip", "band"), None),
            P(None, ("clip", "band")),
            P(None, "clip", None),
            P(None, "clip", "band", None, None),
        )
        + (whole,) * 16,
        out_specs=(P(None, "clip", "band", None, None), P(None, ("clip", "band"), None))
        + (whole,) * 16,
        check_vma=False,
    )
```

```python
import jax
import jax.numpy as jnp
import numpy as np
from jax import lax
from jax.experimental import pallas as pl
from jax.experimental.pallas import tpu as pltpu
from jax.sharding import PartitionSpec as P

HEADS = 16
FREQ = 8
LONG = 192
MICRO = 4
ROWS = 24
CELLS = ROWS * FREQ
ALL = MICRO * CELLS
CAP = 9
BLK = 40
SRC = 16
GOT = SRC * BLK
D = 512
FF = 2048
ENC = 768
EPS = 1e-06
SCALE = (D // HEADS) ** (-0.5)
F32 = jnp.float32
BF16 = jnp.bfloat16

NN = (((1,), (0,)), ((), ()))
NT = (((1,), (1,)), ((), ()))
TN = (((0,), (0,)), ((), ()))


def dot(left, right, dims=NN):
    return lax.dot_general(left, right, dims, preferred_element_type=F32)


def iota(shape, dim):
    return lax.broadcasted_iota(jnp.int32, shape, dim)


def one_hot(hit):
    return jnp.where(hit, 1.0, 0.0).astype(BF16)


def call(kernel, name, out_shape, args, scratch=(), smem=0, flops=0, vmem=16, far=()):
    spaces = [pltpu.SMEM] * smem + [pltpu.VMEM] * (len(args) - smem)
    for i in far:
        spaces[i] = pltpu.HBM
    outs = [jax.ShapeDtypeStruct(shape, dtype) for shape, dtype in out_shape]
    size = sum(a.size * a.dtype.itemsize for a in args) + sum(
        o.size * o.dtype.itemsize for o in outs
    )
    return pl.pallas_call(
        kernel,
        name=name,
        out_shape=outs,
        in_specs=[pl.BlockSpec(memory_space=space) for space in spaces],
        out_specs=[pl.BlockSpec(memory_space=pltpu.VMEM)] * len(outs),
        scratch_shapes=list(scratch),
        compiler_params=pltpu.CompilerParams(vmem_limit_bytes=vmem * 2**20),
        cost_estimate=pl.CostEstimate(flops=flops, bytes_accessed=size, transcendentals=0),
    )(*args)


def pack_kernel(band, pos, enc, out, dest):
    count = pos.shape[1]
    low = iota((count, count), 0)
    high = iota((count, count), 1)
    packed = jnp.zeros((GOT, ENC), F32)
    places = jnp.zeros((SRC, 128), F32)
    for m in range(MICRO):
        cell_r = pos[m : m + 1, :]
        cell_c = jnp.sum(jnp.where(low == high, cell_r, 0), axis=1, keepdims=True)
        slot = LONG * FREQ
        dev_r = jnp.sum(
            jnp.where(cell_r >= slot * iota((SRC, count), 0) + slot, 1, 0), axis=0, keepdims=True
        )
        dev_c = jnp.sum(
            jnp.where(cell_c >= slot * iota((count, SRC), 1) + slot, 1, 0), axis=1, keepdims=True
        )
        same = dev_c == dev_r
        rank_r = jnp.sum(jnp.where(same & (low < high), 1, 0), axis=0, keepdims=True)
        rank_c = jnp.sum(jnp.where(same & (high < low), 1, 0), axis=1, keepdims=True)
        dest[m] = dev_c * BLK + m * CAP + rank_c
        select = one_hot(iota((GOT, count), 0) == dev_r * BLK + m * CAP + rank_r)
        packed = packed + dot(select, enc[m])
        number = cell_r - dev_r * slot - band[0] * CELLS + 1
        to_dev = jnp.where(iota((SRC, count), 0) == dev_r, number.astype(F32), 0.0).astype(BF16)
        to_lane = one_hot(iota((count, 128), 1) == m * CAP + rank_c)
        places = places + dot(to_dev, to_lane)
    spread = one_hot(iota((GOT, SRC), 0) == iota((GOT, SRC), 1) * BLK + (BLK - 4))
    out[:, :128] = (packed[:, :128] + dot(spread, places.astype(BF16))).astype(BF16)
    out[:, 128:] = packed[:, 128:].astype(BF16)


def norm_parts(values):
    center = values - jnp.mean(values, -1, keepdims=True)
    inverse = lax.rsqrt(jnp.mean(center * center, -1, keepdims=True) + EPS)
    return center * inverse, inverse


def norm_back(grad, normal, inverse, gain):
    scaled = grad * gain
    return inverse * (
        scaled
        - jnp.mean(scaled, -1, keepdims=True)
        - normal * jnp.mean(scaled * normal, -1, keepdims=True)
    )


def fetch(pairs, sems):
    copies = [pltpu.make_async_copy(far, near, sems.at[i]) for i, (far, near) in enumerate(pairs)]
    for copy in copies:
        copy.start()
    return copies


def enter_kernel(
    idx_r, idx_c, got_i, row_table, freq_table, embed_i, qkv_i, vecs, qkv_b,
    hidden_o, normed_o, mixed_o, filled_o, seen_o, cell_o, low_o, high_o,
    got, embed_w, qkv_w, sems,
):
    copies = fetch([(got_i, got), (embed_i, embed_w), (qkv_i, qkv_w)], sems)
    copies[0].wait()
    hit = one_hot(iota((SRC, GOT), 1) == iota((SRC, GOT), 0) * BLK + (BLK - 4))
    numbers = dot(hit, got[:, :128]).astype(BF16)
    spread_r = dot(numbers, one_hot(iota((SRC, GOT), 0) == idx_r[0:1, :]), TN)
    value_r = jnp.sum(
        jnp.where(iota((128, GOT), 0) == idx_r[1:2, :], spread_r, 0.0), axis=0, keepdims=True
    )
    cell_r = jnp.where(
        value_r > 0.5, idx_r[2:3, :] * CELLS + value_r.astype(jnp.int32) - 1, -1
    )
    spread_c = dot(one_hot(iota((GOT, SRC), 1) == idx_c[:, 0:1]), numbers)
    value_c = jnp.sum(
        jnp.where(iota((GOT, 128), 1) == idx_c[:, 1:2], spread_c, 0.0), axis=1, keepdims=True
    )
    cell_o[...] = jnp.where(
        value_c > 0.5, idx_c[:, 2:3] * CELLS + value_c.astype(jnp.int32) - 1, -1
    )
    for m in range(MICRO):
        rows = slice(m * CELLS, (m + 1) * CELLS)
        match = jnp.where(iota((CELLS, GOT), 0) + m * CELLS == cell_r, 1.0, 0.0)
        seen = jnp.sum(match, axis=1, keepdims=True)
        filled = dot(match.astype(BF16), got[...]).astype(BF16)
        filled_o[rows, :] = filled
        seen_o[rows, :] = seen
    copies[1].wait()
    copies[2].wait()
    freq = jnp.broadcast_to(freq_table[...][None], (ROWS, FREQ, D // 2)).reshape(CELLS, D // 2)
    for m in range(MICRO):
        rows = slice(m * CELLS, (m + 1) * CELLS)
        seen = seen_o[rows, :]
        proj = (dot(filled_o[rows, :], embed_w[...]) + vecs[0:1, :]).astype(BF16).astype(F32)
        line = row_table[m * ROWS : (m + 1) * ROWS, :]
        line = jnp.broadcast_to(line[:, None, :], (ROWS, FREQ, D // 2)).reshape(CELLS, D // 2)
        table = jnp.concatenate([line, freq], axis=1)
        hidden = jnp.where(seen > 0.5, proj, vecs[1:2, :]) + table
        hidden_o[rows, :] = hidden
        normal, unused = norm_parts(hidden)
        normed = (normal * vecs[2:3, :] + vecs[3:4, :]).astype(BF16)
        normed_o[rows, :] = normed
        mixed = (dot(normed, qkv_w[...]) + qkv_b[...]).astype(BF16)
        mixed_o[rows, :] = mixed
        low_o[m] = mixed[:16, D:]
        high_o[m] = mixed[CELLS - 16 :, D:]


def head_rows(block, heads):
    return jnp.concatenate([block * heads[h : h + 1, :] for h in range(4)], axis=0)


def own_head(full, lane_head):
    out = full[0:32, :]
    for h in range(1, 4):
        out = jnp.where(lane_head == h, full[32 * h : 32 * h + 32, :], out)
    return out


def window_loop(edge, inner):
    def inside(p, carry):
        places = []
        for m in range(MICRO):
            base = pl.multiple_of(m * CELLS + 32 * p - 16, 16)
            places.append((m * 7 + p, pl.ds(base, 32)))
        inner(places)
        return carry

    def ends(i, carry):
        places = []
        for j in range(2):
            m = 2 * i + j
            first = pl.multiple_of(m * CELLS, 16)
            last = pl.multiple_of(m * CELLS + CELLS - 16, 16)
            places.append((m, m * 7, pl.ds(first, 16), 0))
            places.append((m, m * 7 + 6, pl.ds(last, 16), 1))
        edge(places)
        return carry

    lax.fori_loop(1, 6, inside, 0)
    lax.fori_loop(0, MICRO // 2, ends, 0)


def with_halo(own, halo, side):
    return jnp.concatenate([own, halo] if side else [halo, own], axis=0)


COLS = [[slice(D * i + 128 * g, D * i + 128 * g + 128) for i in range(3)] for g in range(4)]


def load_inner(mixed, places, grads=None):
    items = []
    for w, rows in places:
        for g in range(4):
            item = [mixed[rows, c] for c in COLS[g]]
            items.append((w, g, *item, None if grads is None else grads[rows, COLS[g][0]]))
    return items


def load_edge(mixed, low, high, places, grads=None):
    zero = jnp.zeros((16, 128), BF16)
    items = []
    for m, w, rows, side in places:
        halo = high if side else low
        for g in range(4):
            cols = COLS[g]
            q = with_halo(mixed[rows, cols[0]], zero, side)
            k = with_halo(mixed[rows, cols[1]], halo[m, :, cols[0]], side)
            v = with_halo(mixed[rows, cols[2]], halo[m, :, cols[1]], side)
            grad = None if grads is None else with_halo(grads[rows, cols[0]], zero, side)
            items.append((w, g, q, k, v, grad))
    return items


def attend_kernel(mixed, low, high, mask, heads_i, attended_o, probs_o):
    heads = heads_i[...]
    lane_head = iota((32, 128), 1) // 32

    def windows(items):
        scores = [dot(k, head_rows(q, heads), NT) * SCALE for w, g, q, k, v, _ in items]
        probs = []
        for (w, g, *_), score in zip(items, scores):
            score = jnp.where(mask[w] > 0.5, score, -1e30)
            grown = jnp.exp(score - jnp.max(score, axis=0, keepdims=True))
            one = grown * (1.0 / jnp.sum(grown, axis=0, keepdims=True))
            probs_o[w, :, 128 * g : 128 * g + 128] = one
            probs.append(one.astype(BF16))
        full = [dot(one, item[4], TN) for item, one in zip(items, probs)]
        return [own_head(one, lane_head).astype(BF16) for one in full]

    def inner(places):
        outs = windows(load_inner(mixed, places))
        for i, (w, rows) in enumerate(places):
            for g in range(4):
                attended_o[rows, COLS[g][0]] = outs[4 * i + g]

    def edge(places):
        outs = windows(load_edge(mixed, low, high, places))
        for i, (m, w, rows, side) in enumerate(places):
            for g in range(4):
                out = outs[4 * i + g]
                attended_o[rows, COLS[g][0]] = out[:16] if side else out[16:]

    window_loop(edge, inner)


def gelu_parts(x):
    bell = jnp.exp(-0.5 * x * x)
    t = 1.0 / (1.0 + 0.3275911 * 0.5**0.5 * jnp.abs(x))
    poly = 0.127414796 + t * (
        -0.142248368 + t * (0.7107068705 + t * (-0.7265760135 + t * 0.5307027145))
    )
    tail = t * poly * bell
    share = jnp.where(x >= 0, 1.0 - tail, tail)
    return x * share, share + x * bell * 0.3989422804014327


def before_kernel(cot, down_w, g_act_o):
    for f in range(4):
        cols = slice(512 * f, 512 * f + 512)
        g_act_o[:, cols] = dot(cot[...], down_w[cols, :], NT)


def mlp_kernel(
    core, hidden, attended, cot, g_act, out_w, up_w, vecs, up_b,
    middle_o, act_o, gexp_o, n2t_o, send_o, n2_s,
):
    tile = 256
    blocks = [slice(512 * f, 512 * f + 512) for f in range(4)]

    lines = [slice(i * tile, (i + 1) * tile) for i in range(ALL // tile)]
    for rows in lines:
        middle = hidden[rows, :] + dot(attended[rows, :], out_w[...]) + vecs[0:1, :]
        middle_o[rows, :] = middle
        normal, unused = norm_parts(middle)
        n2_s[rows, :] = (normal * vecs[1:2, :] + vecs[2:3, :]).astype(BF16)
    places = [(rows, cols) for rows in lines for cols in blocks]
    ahead = dot(n2_s[lines[0], :], up_w[:, blocks[0]])
    for i, (rows, cols) in enumerate(places):
        expand = ahead + up_b[0:1, cols]
        if i + 1 < len(places):
            ahead = dot(n2_s[places[i + 1][0], :], up_w[:, places[i + 1][1]])
        value, slope = gelu_parts(expand)
        act_o[rows, cols] = value.astype(BF16)
        gexp_o[rows, cols] = (g_act[rows, cols] * slope).astype(BF16)
    n2t_o[...] = jnp.transpose(n2_s[...])
    weight_half(1 - core[0], send_o, act_o, gexp_o, n2t_o, cot)


def weight_half(half, out, act, gexp, n2t, cot):
    for b in range(2):
        cols = pl.ds(pl.multiple_of(half * 1024 + 512 * b, 512), 512)
        rows = slice(512 * b, 512 * b + 512)
        out[rows, :] = dot(act[:, cols], cot[...], TN).astype(BF16)
        rows = slice(1024 + 512 * b, 1536 + 512 * b)
        out[rows, :] = dot(n2t[...], gexp[:, cols]).astype(BF16)


def mlp_keep_kernel(core, act, gexp, n2t, cot, keep_o):
    weight_half(core[0], keep_o, act, gexp, n2t, cot)


def back_kernel(
    middle_i, attended_i, cot_i, act_i, gexp_i, out_i, up_i, down_i, mixed_i, low_i, high_i,
    probs_f, vecs, heads_i,
    output_o, gmid_o, gout_o, sums_o, gmixed_o, low_o, high_o, rim_o,
    middle_s, attended, cot, act, gexp, out_w, up_w, down_w, mixed, low, high, probs_i, gatt, gb_s,
    sems,
):
    copies = fetch(
        [
            (up_i, up_w), (gexp_i, gexp), (down_i, down_w), (act_i, act), (middle_i, middle_s),
            (cot_i, cot), (out_i, out_w), (attended_i, attended), (mixed_i, mixed),
            (low_i, low), (high_i, high), (probs_f, probs_i),
        ],
        sems,
    )
    tile = 256
    sums_o[...] = jnp.zeros((8, D), F32)
    for i in range(ALL // tile):
        rows = slice(i * tile, (i + 1) * tile)
        if i == 0:
            copies[0].wait()
            copies[1].wait()
        grad = dot(gexp[rows, :], up_w[...], NT)
        if i == 0:
            copies[2].wait()
            copies[3].wait()
            copies[4].wait()
        middle = middle_s[rows, :]
        output_o[rows, :] = (middle + vecs[3:4, :] + dot(act[rows, :], down_w[...])).astype(BF16)
        if i == 0:
            copies[5].wait()
            copies[6].wait()
        normal, inverse = norm_parts(middle)
        g_float = cot[rows, :].astype(F32)
        g_mid = g_float + norm_back(grad, normal, inverse, vecs[1:2, :])
        gmid_o[rows, :] = g_mid
        g_low = g_mid.astype(BF16)
        gb_s[rows, :] = g_low
        gatt[rows, :] = dot(g_low, out_w[...], NT).astype(BF16)
        sums_o[0:1, :] += jnp.sum(g_low.astype(F32), axis=0, keepdims=True)
        sums_o[1:2, :] += jnp.sum(grad * normal, axis=0, keepdims=True)
        sums_o[2:3, :] += jnp.sum(grad, axis=0, keepdims=True)
        sums_o[3:4, :] += jnp.sum(g_float, axis=0, keepdims=True)
        for f in range(4):
            part = gexp[rows, 512 * f : 512 * f + 512].astype(F32)
            sums_o[4 + f : 5 + f, :] += jnp.sum(part, axis=0, keepdims=True)
    copies[7].wait()
    gout_o[...] = dot(attended[...], gb_s[...], TN).astype(BF16)
    for copy in copies[8:]:
        copy.wait()
    attend_back(mixed, low, high, probs_i, gatt, heads_i, gmixed_o, low_o, high_o, rim_o)


def attend_back(
    mixed, low, high, probs_i, gatt, heads_i, gmixed_o, low_o, high_o, rim_o
):
    heads = heads_i[...]
    lane_head = iota((32, 128), 1) // 32

    def windows(items):
        q_m = [head_rows(q, heads) for w, g, q, k, v, grad in items]
        g_m = [head_rows(grad, heads) for w, g, q, k, v, grad in items]
        g_probs = [dot(item[4], one, NT) for item, one in zip(items, g_m)]
        low_probs, g_scores = [], []
        for (w, g, *_), g_prob in zip(items, g_probs):
            probs = probs_i[w, :, 128 * g : 128 * g + 128]
            inner = jnp.sum(probs * g_prob, axis=0, keepdims=True)
            g_scores.append((probs * (g_prob - inner)).astype(BF16))
            low_probs.append(probs.astype(BF16))
        d_value = [dot(one, grad) for one, grad in zip(low_probs, g_m)]
        d_key = [dot(one, q) * SCALE for one, q in zip(g_scores, q_m)]
        full = [dot(one, item[3], TN) for item, one in zip(items, g_scores)]
        d_query = [(own_head(one, lane_head) * SCALE).astype(BF16) for one in full]
        return list(zip(d_query, d_key, d_value))

    def inner(places):
        outs = windows(load_inner(mixed, places, gatt))
        for i, (w, rows) in enumerate(places):
            for g in range(4):
                for col, value in zip(COLS[g], outs[4 * i + g]):
                    gmixed_o[rows, col] = value.astype(BF16)

    def edge(places):
        outs = windows(load_edge(mixed, low, high, places, gatt))
        for i, (m, w, rows, side) in enumerate(places):
            out = high_o if side else low_o
            own, far = (slice(0, 16), slice(16, 32)) if side else (slice(16, 32), slice(0, 16))
            for g in range(4):
                cols = COLS[g]
                d_query, d_key, d_value = outs[4 * i + g]
                gmixed_o[rows, cols[0]] = d_query[own]
                rim_o[m, side, :, cols[0]] = d_key[own]
                rim_o[m, side, :, cols[1]] = d_value[own]
                out[m, :, cols[0]] = d_key[far].astype(BF16)
                out[m, :, cols[1]] = d_value[far].astype(BF16)

    window_loop(edge, inner)
    for m in range(MICRO):
        for base in (m * CELLS, m * CELLS + CELLS - 16):
            gmixed_o[base : base + 16, D:] = jnp.zeros((16, 2 * D), BF16)


def leave_kernel(
    core, gmixed_i, low_i, high_i, rim_i, hidden_i, normed_i, filled_i, gmid_i, qkv_i, gout_i,
    seen, vecs, sums, gm_o, gf_o, small_o, send_o,
    from_low, from_high, rim, hidden, normed, filled, gmid, qkv_w, gout, sems,
):
    pairs = [(qkv_i, qkv_w), (low_i, from_low), (high_i, from_high), (rim_i, rim)]
    for m in range(MICRO):
        rows = pl.ds(m * CELLS, CELLS)
        pairs += [(gmixed_i.at[rows], gm_o.at[rows]), (hidden_i.at[rows], hidden.at[rows])]
        pairs.append((gmid_i.at[rows], gmid.at[rows]))
    pairs += [(normed_i, normed), (filled_i, filled), (gout_i, gout)]
    copies = fetch(pairs, sems)
    small = jnp.zeros((1, D), F32)
    gain_sum, shift_sum, mask_sum, embed_sum, query_sum, value_sum = [small] * 6
    for m in range(MICRO):
        base = m * CELLS
        rows = slice(base, base + CELLS)
        for copy in copies[0 if m == 0 else 3 * m + 4 : 3 * m + 7]:
            copy.wait()
        gm_o[base : base + 16, D:] = (rim[m, 0] + from_low[m].astype(F32)).astype(BF16)
        gm_o[base + CELLS - 16 : base + CELLS, D:] = (rim[m, 1] + from_high[m].astype(F32)).astype(
            BF16
        )
        gm = gm_o[rows, :]
        grad = dot(gm, qkv_w[...], NT)
        normal, inverse = norm_parts(hidden[rows, :])
        g_hidden = gmid[rows, :] + norm_back(grad, normal, inverse, vecs[2:3, :])
        there = seen[rows, :] > 0.5
        g_low = g_hidden.astype(BF16)
        gf_o[rows, :] = g_low
        gain_sum += jnp.sum(grad * normal, axis=0, keepdims=True)
        shift_sum += jnp.sum(grad, axis=0, keepdims=True)
        mask_sum += jnp.sum(jnp.where(there, 0.0, g_hidden), axis=0, keepdims=True)
        embed_sum += jnp.sum(jnp.where(there, g_low.astype(F32), 0.0), axis=0, keepdims=True)
        query_sum += jnp.sum(gm[:, :D].astype(F32), axis=0, keepdims=True)
        value_sum += jnp.sum(gm[:, 2 * D :].astype(F32), axis=0, keepdims=True)
    small_o[...] = jnp.concatenate(
        [
            embed_sum, mask_sum, gain_sum, shift_sum, query_sum, value_sum,
            small, small, sums[...],
        ],
        axis=0,
    )
    for copy in copies[3 * MICRO + 4 :]:
        copy.wait()
    one_half(core[0] != 0, send_o, normed, filled, gm_o, gf_o, gout, small_o)


def one_half(first, out, normed, filled, gm, gf, gout, small):
    @pl.when(first)
    def _():
        turned = jnp.transpose(normed[...])
        for b in range(3):
            cols = slice(512 * b, 512 * b + 512)
            out[cols, :] = dot(turned, gm[:, cols]).astype(BF16)

    @pl.when(jnp.logical_not(first))
    def _():
        out[0:512, :] = gout[...]
        out[512:1280, :] = dot(jnp.transpose(filled[...]), gf[...]).astype(BF16)
        out[1280:1296, :] = small[...].astype(BF16)
        out[1296:1536, :] = jnp.zeros((240, D), BF16)


def leave_keep_kernel(core, gm, gf, small, normed, filled, gout, cell, keep_o, ret_o):
    one_half(core[0] == 0, keep_o, normed, filled, gm, gf, gout, small)
    ret_o[...] = dot(one_hot(iota((GOT, ALL), 1) == cell[...]), gf[...]).astype(BF16)


def return_kernel(dest, came, embed_w, out):
    for m in range(MICRO):
        select = one_hot(iota((dest.shape[1], GOT), 1) == dest[m])
        g_proj = dot(select, came[...]).astype(BF16)
        out[m] = dot(g_proj, embed_w[...], NT).astype(BF16)


def unpack_one_kernel(down_i, up_i, down_o, up_o):
    down_o[...] = down_i[...].reshape(512, D).astype(F32)
    up_o[...] = up_i[...].reshape(512, D).astype(F32)


def unpack_one(gathered):
    block = (16, 1, 32, D)
    return pl.pallas_call(
        unpack_one_kernel,
        name="unpack_one",
        grid=(4,),
        out_shape=[jax.ShapeDtypeStruct((FF, D), F32), jax.ShapeDtypeStruct((D, FF), F32)],
        in_specs=[
            pl.BlockSpec(block, lambda i: (i % 2, i // 2, 0, 0)),
            pl.BlockSpec(block, lambda i: (2 + i % 2, i // 2, 0, 0)),
        ],
        out_specs=[
            pl.BlockSpec((512, D), lambda i: (i, 0)),
            pl.BlockSpec((512, D), lambda i: (0, i)),
        ],
        compiler_params=pltpu.CompilerParams(vmem_limit_bytes=16 * 2**20),
        cost_estimate=pl.CostEstimate(flops=0, bytes_accessed=12 * 2**20, transcendentals=0),
    )(gathered, gathered)


def unpack_two_kernel(core, mine, other, qkv_o, embed_o, out_o, small_o):
    def write(first, second):
        for b in range(3):
            qkv_o[:, 512 * b : 512 * b + 512] = first[512 * b : 512 * b + 512, :].astype(F32)
        out_o[...] = second[0:512, :].astype(F32)
        embed_o[...] = second[512:1280, :].astype(F32)
        small_o[...] = second[1280:1296, :].astype(F32)

    @pl.when(core[0] == 0)
    def _():
        write(mine, other)

    @pl.when(core[0] != 0)
    def _():
        write(other, mine)


def clip_ident(lengths, rows):
    first = lengths[:, 0:1]
    second = first + lengths[:, 1:2]
    ident = (rows[None, :] >= first).astype(jnp.int32) + (rows[None, :] >= second).astype(jnp.int32)
    start = jnp.where(ident >= 1, first, 0) + jnp.where(ident >= 2, lengths[:, 1:2], 0)
    inside = (rows >= 0) & (rows < LONG)
    return (jnp.where(inside[None, :], ident, -1), rows[None, :] - start)


def position_tables(row_in_clip, width):
    quarter = width // 4
    omega = 1.0 / 10000.0 ** (jnp.arange(quarter, dtype=jnp.float32) / quarter)
    row_angle = row_in_clip.astype(jnp.float32)[..., None] * omega
    freq_angle = jnp.arange(FREQ, dtype=jnp.float32)[:, None] * omega
    row_part = jnp.concatenate([jnp.sin(row_angle), jnp.cos(row_angle)], -1)
    freq_part = jnp.concatenate([jnp.sin(freq_angle), jnp.cos(freq_angle)], -1)
    return row_part.reshape(-1, width // 2), freq_part


def window_mask(ident):
    cells = jnp.repeat(ident.reshape(MICRO * 7, 4), FREQ, axis=1)
    freq = np.tile((np.arange(FREQ) + 2) % 8 // 4, 4)
    same = (cells[:, :, None] == cells[:, None, :]) & (cells[:, :, None] >= 0)
    same = same & jnp.asarray(freq[:, None] == freq[None, :])[None]
    return jnp.tile(same.astype(F32), (1, 1, 4))


def on_device(
    encoded, visible_pos, clip_len, cotangent, embed_weight, embed_bias, mask_token, attn_gain,
    attn_shift, qkv_weight, query_bias, value_bias, out_weight, out_bias, mlp_gain, mlp_shift,
    up_weight, up_bias, down_weight, down_bias,
):
    both = ("clip", "band")
    groups = lax.axis_size("clip")
    bands = lax.axis_size("band")
    band = lax.axis_index("band")
    side = band % 2
    core = side.astype(jnp.int32).reshape(1)
    halves = [
        [c * bands + 2 * x + k for c in range(groups) for x in range(bands // 2)] for k in range(2)
    ]
    swap = [(i, i ^ 1) for i in range(bands)]
    forward = [(i, i + 1) for i in range(bands - 1)]
    backward = [(b, a) for a, b in forward]
    chips = groups * bands // 2

    def to_all(block):
        return lax.all_to_all(
            block, both, split_axis=0, concat_axis=0, tiled=True, axis_index_groups=halves
        )

    def chip_sum(keep, other):
        mine = (keep.astype(F32) + other.astype(F32)).astype(BF16)
        return mine.reshape(chips, -1, D)

    def total(parts):
        return jnp.sum(parts.astype(F32), 0).astype(BF16)

    def spread(chunk):
        return jnp.broadcast_to(chunk[None], (chips,) + chunk.shape)

    vis = visible_pos.shape[1]
    packed, dest = call(
        pack_kernel, "pack", [((GOT, ENC), BF16), ((MICRO, vis, 1), jnp.int32)],
        (band.astype(jnp.int32).reshape(1), visible_pos, encoded), smem=1,
        flops=GOT * MICRO * vis * ENC * 2,
    )
    cot = cotangent.reshape(ALL, D)
    (g_act,) = call(
        before_kernel, "before", [((ALL, FF), F32)], (cot, down_weight), flops=2 * ALL * D * FF,
    )
    got = lax.all_to_all(
        packed.reshape(SRC, BLK, ENC), "clip", split_axis=0, concat_axis=0, tiled=True
    ).reshape(GOT, ENC)

    place = np.arange(GOT)
    within = place % BLK
    index = np.zeros((8, GOT), np.int32)
    index[0], index[1], index[2] = place // BLK, within, np.where(within < 36, within // CAP, 99)
    heads = jnp.asarray(np.arange(128)[None, :] // 32 == np.arange(16)[:, None] % 4, BF16)

    unused, row_in_clip = clip_ident(clip_len[:, 0], band * ROWS + jnp.arange(ROWS))
    row_table, freq_table = position_tables(row_in_clip, D)
    ident_ext, unused = clip_ident(clip_len[:, 0], band * ROWS - 2 + jnp.arange(ROWS + 4))
    mask = window_mask(ident_ext)
    zero = jnp.zeros((D,), BF16)
    vecs_one = jnp.stack([embed_bias, mask_token, attn_gain, attn_shift] * 2).astype(F32)
    vecs_two = jnp.stack([out_bias, mlp_gain, mlp_shift, down_bias] * 2).astype(F32)
    qkv_b = jnp.concatenate([query_bias, zero, value_bias]).astype(F32)[None]
    up_b = up_bias.astype(F32)[None]

    hidden, normed, mixed, filled, seen, cell, low, high = call(
        enter_kernel, "enter",
        [
            ((ALL, D), F32), ((ALL, D), BF16), ((ALL, 3 * D), BF16), ((ALL, ENC), BF16),
            ((ALL, 1), F32), ((GOT, 1), jnp.int32),
            ((MICRO, 16, 2 * D), BF16), ((MICRO, 16, 2 * D), BF16),
        ],
        (
            jnp.asarray(index), jnp.asarray(np.ascontiguousarray(index.T)), got, row_table,
            freq_table, embed_weight, qkv_weight, vecs_one, qkv_b,
        ),
        scratch=[
            pltpu.VMEM((GOT, ENC), BF16), pltpu.VMEM((ENC, D), BF16), pltpu.VMEM((D, 3 * D), BF16),
            pltpu.SemaphoreType.DMA((3,)),
        ],
        far=(2, 5, 6),
        flops=2 * ALL * (GOT * ENC + ENC * D + 3 * D * D),
    )
    from_low = lax.ppermute(high, "band", forward)
    from_high = lax.ppermute(low, "band", backward)
    attended, probs = call(
        attend_kernel, "attend",
        [((ALL, D), BF16), ((MICRO * 7, 32, D), F32)],
        (mixed, from_low, from_high, mask, heads),
        flops=MICRO * 7 * 4 * 2**20,
    )
    middle, act, gexp, n2t, send = call(
        mlp_kernel, "mlp",
        [
            ((ALL, D), F32), ((ALL, FF), BF16), ((ALL, FF), BF16), ((D, ALL), BF16),
            ((FF, D), BF16),
        ],
        (core, hidden, attended, cot, g_act, out_weight, up_weight, vecs_two, up_b),
        scratch=[pltpu.VMEM((ALL, D), BF16)],
        smem=1, flops=2 * ALL * (2 * D * FF + D * D), vmem=24,
    )
    (keep,) = call(
        mlp_keep_kernel, "mlp_keep", [((FF, D), BF16)], (core, act, gexp, n2t, cot),
        smem=1, flops=2 * ALL * D * FF,
    )
    chip_one = chip_sum(keep, lax.ppermute(send, "band", swap))
    act, chip_one = lax.optimization_barrier((act, chip_one))
    parts_one = to_all(chip_one)
    inputs = (
        middle, attended, cot, act, gexp, out_weight, up_weight, down_weight, mixed, from_low,
        from_high, probs,
    )
    output, gmid, gout, sums, gmixed, low, high, rim = call(
        back_kernel, "back",
        [
            ((ALL, D), BF16), ((ALL, D), F32), ((D, D), BF16), ((8, D), F32),
            ((ALL, 3 * D), BF16), ((MICRO, 16, 2 * D), BF16), ((MICRO, 16, 2 * D), BF16),
            ((MICRO, 2, 16, 2 * D), F32),
        ],
        inputs + (vecs_two, heads),
        scratch=[pltpu.VMEM(x.shape, x.dtype) for x in inputs]
        + [pltpu.VMEM((ALL, D), BF16)] * 2
        + [pltpu.SemaphoreType.DMA((len(inputs),))],
        flops=2 * ALL * (2 * D * FF + 2 * D * D) + MICRO * 7 * 4 * 2**22,
        far=range(len(inputs)), vmem=44,
    )
    from_low = lax.ppermute(high, "band", forward)
    from_high = lax.ppermute(low, "band", backward)
    total_one = total(parts_one)
    total_one, from_low, from_high = lax.optimization_barrier((total_one, from_low, from_high))
    kept = (from_low, from_high, rim, hidden, normed, filled, gmid, qkv_weight, gout)
    fetched = (gmixed,) + kept
    gm, gf, small, send = call(
        leave_kernel, "leave",
        [((ALL, 3 * D), BF16), ((ALL, D), BF16), ((16, D), F32), ((3 * D, D), BF16)],
        (core,) + fetched + (seen, vecs_one, sums),
        scratch=[pltpu.VMEM(x.shape, x.dtype) for x in kept]
        + [pltpu.SemaphoreType.DMA((3 * MICRO + 7,))],
        smem=1, flops=2 * ALL * 5 * D * D, far=range(1, 1 + len(fetched)), vmem=50,
    )
    other = lax.ppermute(send, "band", swap)
    total_one = lax.all_gather(total_one, both, axis=0).reshape(chips, 2, -1, D)
    keep, returned = call(
        leave_keep_kernel, "leave_keep", [((3 * D, D), BF16), ((GOT, D), BF16)],
        (core, gm, gf, small, normed, filled, gout, cell),
        smem=1, flops=2 * ALL * (2 * D * D + GOT * D),
    )
    mine = to_all(spread(total(to_all(chip_sum(keep, other))))).reshape(-1, D)
    mine, returned = lax.optimization_barrier((mine, returned))
    qkv, g_embed, g_out, small = call(
        unpack_two_kernel, "unpack_two",
        [((D, 3 * D), F32), ((ENC, D), F32), ((D, D), F32), ((16, D), F32)],
        (core, mine, lax.ppermute(mine, "band", swap)), smem=1,
    )
    came = lax.all_to_all(
        returned.reshape(SRC, BLK, D), "clip", split_axis=0, concat_axis=0, tiled=True
    ).reshape(GOT, D)
    down, up = unpack_one(total_one)
    lines = tuple(small[i] for i in (0, 1, 2, 3, 4, 5, 8, 9, 10, 11))
    lines += (small[12:16].reshape(FF),)
    came, down, lines = lax.optimization_barrier((came, down, lines))
    (grad_enc,) = call(
        return_kernel, "return", [((MICRO, vis, ENC), BF16)], (dest, came, embed_weight),
        flops=2 * MICRO * vis * D * (GOT + ENC),
    )
    return (
        output.reshape(cotangent.shape), grad_enc, g_embed, *lines[:4], qkv, *lines[4:6], g_out,
        *lines[6:9], up, lines[10], down, lines[9],
    )


def solution(mesh):
    whole = P()
    return jax.shard_map(
        on_device,
        mesh=mesh,
        in_specs=(
            P(None, ("clip", "band"), None),
            P(None, ("clip", "band")),
            P(None, "clip", None),
            P(None, "clip", "band", None, None),
        )
        + (whole,) * 16,
        out_specs=(P(None, "clip", "band", None, None), P(None, ("clip", "band"), None))
        + (whole,) * 16,
        check_vma=False,
    )
```

```python
import jax
import jax.numpy as jnp
import numpy as np
from jax import lax
from jax.experimental import pallas as pl
from jax.experimental.pallas import tpu as pltpu
from jax.sharding import PartitionSpec as P

HEADS = 16
FREQ = 8
LONG = 192
MICRO = 4
ROWS = 24
CELLS = ROWS * FREQ
ALL = MICRO * CELLS
CAP = 9
BLK = 40
SRC = 16
GOT = SRC * BLK
D = 512
FF = 2048
ENC = 768
EPS = 1e-06
SCALE = (D // HEADS) ** (-0.5)
F32 = jnp.float32
BF16 = jnp.bfloat16

NN = (((1,), (0,)), ((), ()))
NT = (((1,), (1,)), ((), ()))
TN = (((0,), (0,)), ((), ()))


def dot(left, right, dims=NN):
    return lax.dot_general(left, right, dims, preferred_element_type=F32)


def iota(shape, dim):
    return lax.broadcasted_iota(jnp.int32, shape, dim)


def one_hot(hit):
    return jnp.where(hit, 1.0, 0.0).astype(BF16)


def call(kernel, name, out_shape, args, scratch=(), smem=0, flops=0, vmem=16, far=()):
    spaces = [pltpu.SMEM] * smem + [pltpu.VMEM] * (len(args) - smem)
    for i in far:
        spaces[i] = pltpu.HBM
    outs = [jax.ShapeDtypeStruct(shape, dtype) for shape, dtype in out_shape]
    size = sum(a.size * a.dtype.itemsize for a in args) + sum(
        o.size * o.dtype.itemsize for o in outs
    )
    return pl.pallas_call(
        kernel,
        name=name,
        out_shape=outs,
        in_specs=[pl.BlockSpec(memory_space=space) for space in spaces],
        out_specs=[pl.BlockSpec(memory_space=pltpu.VMEM)] * len(outs),
        scratch_shapes=list(scratch),
        compiler_params=pltpu.CompilerParams(vmem_limit_bytes=vmem * 2**20),
        cost_estimate=pl.CostEstimate(flops=flops, bytes_accessed=size, transcendentals=0),
    )(*args)


def pack_kernel(band, pos, enc, out, dest):
    count = pos.shape[1]
    low = iota((count, count), 0)
    high = iota((count, count), 1)
    packed = jnp.zeros((GOT, ENC), F32)
    places = jnp.zeros((SRC, 128), F32)
    for m in range(MICRO):
        cell_r = pos[m : m + 1, :]
        cell_c = jnp.sum(jnp.where(low == high, cell_r, 0), axis=1, keepdims=True)
        slot = LONG * FREQ
        dev_r = jnp.sum(
            jnp.where(cell_r >= slot * iota((SRC, count), 0) + slot, 1, 0), axis=0, keepdims=True
        )
        dev_c = jnp.sum(
            jnp.where(cell_c >= slot * iota((count, SRC), 1) + slot, 1, 0), axis=1, keepdims=True
        )
        same = dev_c == dev_r
        rank_r = jnp.sum(jnp.where(same & (low < high), 1, 0), axis=0, keepdims=True)
        rank_c = jnp.sum(jnp.where(same & (high < low), 1, 0), axis=1, keepdims=True)
        dest[m] = dev_c * BLK + m * CAP + rank_c
        select = one_hot(iota((GOT, count), 0) == dev_r * BLK + m * CAP + rank_r)
        packed = packed + dot(select, enc[m])
        number = cell_r - dev_r * slot - band[0] * CELLS + 1
        to_dev = jnp.where(iota((SRC, count), 0) == dev_r, number.astype(F32), 0.0).astype(BF16)
        to_lane = one_hot(iota((count, 128), 1) == m * CAP + rank_c)
        places = places + dot(to_dev, to_lane)
    spread = one_hot(iota((GOT, SRC), 0) == iota((GOT, SRC), 1) * BLK + (BLK - 4))
    out[:, :128] = (packed[:, :128] + dot(spread, places.astype(BF16))).astype(BF16)
    out[:, 128:] = packed[:, 128:].astype(BF16)


def norm_parts(values):
    center = values - jnp.mean(values, -1, keepdims=True)
    inverse = lax.rsqrt(jnp.mean(center * center, -1, keepdims=True) + EPS)
    return center * inverse, inverse


def norm_back(grad, normal, inverse, gain):
    scaled = grad * gain
    return inverse * (
        scaled
        - jnp.mean(scaled, -1, keepdims=True)
        - normal * jnp.mean(scaled * normal, -1, keepdims=True)
    )


def fetch(pairs, sems):
    copies = [pltpu.make_async_copy(far, near, sems.at[i]) for i, (far, near) in enumerate(pairs)]
    for copy in copies:
        copy.start()
    return copies


def enter_kernel(
    idx_r, idx_c, got_i, row_table, freq_table, embed_i, qkv_i, vecs, qkv_b,
    hidden_o, normed_o, mixed_o, filled_o, seen_o, cell_o, low_o, high_o,
    got, embed_w, qkv_w, sems,
):
    copies = fetch([(got_i, got), (embed_i, embed_w), (qkv_i, qkv_w)], sems)
    copies[0].wait()
    hit = one_hot(iota((SRC, GOT), 1) == iota((SRC, GOT), 0) * BLK + (BLK - 4))
    numbers = dot(hit, got[:, :128]).astype(BF16)
    spread_r = dot(numbers, one_hot(iota((SRC, GOT), 0) == idx_r[0:1, :]), TN)
    value_r = jnp.sum(
        jnp.where(iota((128, GOT), 0) == idx_r[1:2, :], spread_r, 0.0), axis=0, keepdims=True
    )
    cell_r = jnp.where(
        value_r > 0.5, idx_r[2:3, :] * CELLS + value_r.astype(jnp.int32) - 1, -1
    )
    spread_c = dot(one_hot(iota((GOT, SRC), 1) == idx_c[:, 0:1]), numbers)
    value_c = jnp.sum(
        jnp.where(iota((GOT, 128), 1) == idx_c[:, 1:2], spread_c, 0.0), axis=1, keepdims=True
    )
    cell_o[...] = jnp.where(
        value_c > 0.5, idx_c[:, 2:3] * CELLS + value_c.astype(jnp.int32) - 1, -1
    )
    for m in range(MICRO):
        rows = slice(m * CELLS, (m + 1) * CELLS)
        match = jnp.where(iota((CELLS, GOT), 0) + m * CELLS == cell_r, 1.0, 0.0)
        seen = jnp.sum(match, axis=1, keepdims=True)
        filled = dot(match.astype(BF16), got[...]).astype(BF16)
        filled_o[rows, :] = filled
        seen_o[rows, :] = seen
    copies[1].wait()
    copies[2].wait()
    freq = jnp.broadcast_to(freq_table[...][None], (ROWS, FREQ, D // 2)).reshape(CELLS, D // 2)
    for m in range(MICRO):
        rows = slice(m * CELLS, (m + 1) * CELLS)
        seen = seen_o[rows, :]
        proj = (dot(filled_o[rows, :], embed_w[...]) + vecs[0:1, :]).astype(BF16).astype(F32)
        line = row_table[m * ROWS : (m + 1) * ROWS, :]
        line = jnp.broadcast_to(line[:, None, :], (ROWS, FREQ, D // 2)).reshape(CELLS, D // 2)
        table = jnp.concatenate([line, freq], axis=1)
        hidden = jnp.where(seen > 0.5, proj, vecs[1:2, :]) + table
        hidden_o[rows, :] = hidden
        normal, unused = norm_parts(hidden)
        normed = (normal * vecs[2:3, :] + vecs[3:4, :]).astype(BF16)
        normed_o[rows, :] = normed
        mixed = (dot(normed, qkv_w[...]) + qkv_b[...]).astype(BF16)
        mixed_o[rows, :] = mixed
        low_o[m] = mixed[:16, D:]
        high_o[m] = mixed[CELLS - 16 :, D:]


def head_rows(block, heads):
    return jnp.concatenate([block * heads[h : h + 1, :] for h in range(4)], axis=0)


def own_head(full, lane_head):
    out = full[0:32, :]
    for h in range(1, 4):
        out = jnp.where(lane_head == h, full[32 * h : 32 * h + 32, :], out)
    return out


def window_loop(edge, inner):
    def inside(p, carry):
        places = []
        for m in range(MICRO):
            base = pl.multiple_of(m * CELLS + 32 * p - 16, 16)
            places.append((m * 7 + p, pl.ds(base, 32)))
        inner(places)
        return carry

    def ends(i, carry):
        places = []
        for j in range(2):
            m = 2 * i + j
            first = pl.multiple_of(m * CELLS, 16)
            last = pl.multiple_of(m * CELLS + CELLS - 16, 16)
            places.append((m, m * 7, pl.ds(first, 16), 0))
            places.append((m, m * 7 + 6, pl.ds(last, 16), 1))
        edge(places)
        return carry

    lax.fori_loop(1, 6, inside, 0)
    lax.fori_loop(0, MICRO // 2, ends, 0)


def with_halo(own, halo, side):
    return jnp.concatenate([own, halo] if side else [halo, own], axis=0)


COLS = [[slice(D * i + 128 * g, D * i + 128 * g + 128) for i in range(3)] for g in range(4)]


def load_inner(mixed, places, grads=None):
    items = []
    for w, rows in places:
        for g in range(4):
            item = [mixed[rows, c] for c in COLS[g]]
            items.append((w, g, *item, None if grads is None else grads[rows, COLS[g][0]]))
    return items


def load_edge(mixed, low, high, places, grads=None):
    zero = jnp.zeros((16, 128), BF16)
    items = []
    for m, w, rows, side in places:
        halo = high if side else low
        for g in range(4):
            cols = COLS[g]
            q = with_halo(mixed[rows, cols[0]], zero, side)
            k = with_halo(mixed[rows, cols[1]], halo[m, :, cols[0]], side)
            v = with_halo(mixed[rows, cols[2]], halo[m, :, cols[1]], side)
            grad = None if grads is None else with_halo(grads[rows, cols[0]], zero, side)
            items.append((w, g, q, k, v, grad))
    return items


def attend_kernel(mixed, low, high, mask, heads_i, attended_o, probs_o):
    heads = heads_i[...]
    lane_head = iota((32, 128), 1) // 32

    def windows(items):
        scores = [dot(k, head_rows(q, heads), NT) * SCALE for w, g, q, k, v, _ in items]
        probs = []
        for (w, g, *_), score in zip(items, scores):
            score = jnp.where(mask[w] > 0.5, score, -1e30)
            grown = jnp.exp(score - jnp.max(score, axis=0, keepdims=True))
            one = grown * (1.0 / jnp.sum(grown, axis=0, keepdims=True))
            probs_o[w, :, 128 * g : 128 * g + 128] = one
            probs.append(one.astype(BF16))
        full = [dot(one, item[4], TN) for item, one in zip(items, probs)]
        return [own_head(one, lane_head).astype(BF16) for one in full]

    def inner(places):
        outs = windows(load_inner(mixed, places))
        for i, (w, rows) in enumerate(places):
            for g in range(4):
                attended_o[rows, COLS[g][0]] = outs[4 * i + g]

    def edge(places):
        outs = windows(load_edge(mixed, low, high, places))
        for i, (m, w, rows, side) in enumerate(places):
            for g in range(4):
                out = outs[4 * i + g]
                attended_o[rows, COLS[g][0]] = out[:16] if side else out[16:]

    window_loop(edge, inner)


def gelu_parts(x):
    bell = jnp.exp(-0.5 * x * x)
    t = 1.0 / (1.0 + 0.3275911 * 0.5**0.5 * jnp.abs(x))
    poly = 0.127414796 + t * (
        -0.142248368 + t * (0.7107068705 + t * (-0.7265760135 + t * 0.5307027145))
    )
    tail = t * poly * bell
    share = jnp.where(x >= 0, 1.0 - tail, tail)
    return x * share, share + x * bell * 0.3989422804014327


def before_kernel(cot, down_w, g_act_o):
    for f in range(4):
        cols = slice(512 * f, 512 * f + 512)
        g_act_o[:, cols] = dot(cot[...], down_w[cols, :], NT)


def mlp_kernel(
    core, hidden, attended, cot, g_act, out_w, up_w, vecs, up_b,
    middle_o, act_o, gexp_o, n2t_o, send_o, n2_s,
):
    tile = 256
    blocks = [slice(512 * f, 512 * f + 512) for f in range(4)]

    lines = [slice(i * tile, (i + 1) * tile) for i in range(ALL // tile)]
    for rows in lines:
        middle = hidden[rows, :] + dot(attended[rows, :], out_w[...]) + vecs[0:1, :]
        middle_o[rows, :] = middle
        normal, unused = norm_parts(middle)
        n2_s[rows, :] = (normal * vecs[1:2, :] + vecs[2:3, :]).astype(BF16)
    places = [(rows, cols) for rows in lines for cols in blocks]
    ahead = dot(n2_s[lines[0], :], up_w[:, blocks[0]])
    for i, (rows, cols) in enumerate(places):
        expand = ahead + up_b[0:1, cols]
        if i + 1 < len(places):
            ahead = dot(n2_s[places[i + 1][0], :], up_w[:, places[i + 1][1]])
        value, slope = gelu_parts(expand)
        act_o[rows, cols] = value.astype(BF16)
        gexp_o[rows, cols] = (g_act[rows, cols] * slope).astype(BF16)
    n2t_o[...] = jnp.transpose(n2_s[...])
    weight_half(1 - core[0], send_o, act_o, gexp_o, n2t_o, cot)


def weight_half(half, out, act, gexp, n2t, cot):
    for b in range(2):
        cols = pl.ds(pl.multiple_of(half * 1024 + 512 * b, 512), 512)
        rows = slice(512 * b, 512 * b + 512)
        out[rows, :] = dot(act[:, cols], cot[...], TN).astype(BF16)
        rows = slice(1024 + 512 * b, 1536 + 512 * b)
        out[rows, :] = dot(n2t[...], gexp[:, cols]).astype(BF16)


def mlp_keep_kernel(core, act, gexp, n2t, cot, keep_o):
    weight_half(core[0], keep_o, act, gexp, n2t, cot)


def back_kernel(
    middle_i, attended_i, cot_i, act_i, gexp_i, out_i, up_i, down_i, mixed_i, low_i, high_i,
    probs_f, vecs, heads_i,
    output_o, gmid_o, gout_o, sums_o, gmixed_o, low_o, high_o, rim_o,
    middle_s, attended, cot, act, gexp, out_w, up_w, down_w, mixed, low, high, probs_i, gatt, gb_s,
    sems,
):
    copies = fetch(
        [
            (up_i, up_w), (gexp_i, gexp), (down_i, down_w), (act_i, act), (middle_i, middle_s),
            (cot_i, cot), (out_i, out_w), (attended_i, attended), (mixed_i, mixed),
            (low_i, low), (high_i, high), (probs_f, probs_i),
        ],
        sems,
    )
    tile = 256
    sums_o[...] = jnp.zeros((8, D), F32)
    for i in range(ALL // tile):
        rows = slice(i * tile, (i + 1) * tile)
        if i == 0:
            copies[0].wait()
            copies[1].wait()
        grad = dot(gexp[rows, :], up_w[...], NT)
        if i == 0:
            copies[2].wait()
            copies[3].wait()
            copies[4].wait()
        middle = middle_s[rows, :]
        output_o[rows, :] = (middle + vecs[3:4, :] + dot(act[rows, :], down_w[...])).astype(BF16)
        if i == 0:
            copies[5].wait()
            copies[6].wait()
        normal, inverse = norm_parts(middle)
        g_float = cot[rows, :].astype(F32)
        g_mid = g_float + norm_back(grad, normal, inverse, vecs[1:2, :])
        gmid_o[rows, :] = g_mid
        g_low = g_mid.astype(BF16)
        gb_s[rows, :] = g_low
        gatt[rows, :] = dot(g_low, out_w[...], NT).astype(BF16)
        sums_o[0:1, :] += jnp.sum(g_low.astype(F32), axis=0, keepdims=True)
        sums_o[1:2, :] += jnp.sum(grad * normal, axis=0, keepdims=True)
        sums_o[2:3, :] += jnp.sum(grad, axis=0, keepdims=True)
        sums_o[3:4, :] += jnp.sum(g_float, axis=0, keepdims=True)
        for f in range(4):
            part = gexp[rows, 512 * f : 512 * f + 512].astype(F32)
            sums_o[4 + f : 5 + f, :] += jnp.sum(part, axis=0, keepdims=True)
    copies[7].wait()
    gout_o[...] = dot(attended[...], gb_s[...], TN).astype(BF16)
    for copy in copies[8:]:
        copy.wait()
    attend_back(mixed, low, high, probs_i, gatt, heads_i, gmixed_o, low_o, high_o, rim_o)


def attend_back(
    mixed, low, high, probs_i, gatt, heads_i, gmixed_o, low_o, high_o, rim_o
):
    heads = heads_i[...]
    lane_head = iota((32, 128), 1) // 32

    def windows(items):
        q_m = [head_rows(q, heads) for w, g, q, k, v, grad in items]
        g_m = [head_rows(grad, heads) for w, g, q, k, v, grad in items]
        g_probs = [dot(item[4], one, NT) for item, one in zip(items, g_m)]
        low_probs, g_scores = [], []
        for (w, g, *_), g_prob in zip(items, g_probs):
            probs = probs_i[w, :, 128 * g : 128 * g + 128]
            inner = jnp.sum(probs * g_prob, axis=0, keepdims=True)
            g_scores.append((probs * (g_prob - inner)).astype(BF16))
            low_probs.append(probs.astype(BF16))
        d_value = [dot(one, grad) for one, grad in zip(low_probs, g_m)]
        d_key = [dot(one, q) * SCALE for one, q in zip(g_scores, q_m)]
        full = [dot(one, item[3], TN) for item, one in zip(items, g_scores)]
        d_query = [(own_head(one, lane_head) * SCALE).astype(BF16) for one in full]
        return list(zip(d_query, d_key, d_value))

    def inner(places):
        outs = windows(load_inner(mixed, places, gatt))
        for i, (w, rows) in enumerate(places):
            for g in range(4):
                for col, value in zip(COLS[g], outs[4 * i + g]):
                    gmixed_o[rows, col] = value.astype(BF16)

    def edge(places):
        outs = windows(load_edge(mixed, low, high, places, gatt))
        for i, (m, w, rows, side) in enumerate(places):
            out = high_o if side else low_o
            own, far = (slice(0, 16), slice(16, 32)) if side else (slice(16, 32), slice(0, 16))
            for g in range(4):
                cols = COLS[g]
                d_query, d_key, d_value = outs[4 * i + g]
                gmixed_o[rows, cols[0]] = d_query[own]
                rim_o[m, side, :, cols[0]] = d_key[own]
                rim_o[m, side, :, cols[1]] = d_value[own]
                out[m, :, cols[0]] = d_key[far].astype(BF16)
                out[m, :, cols[1]] = d_value[far].astype(BF16)

    window_loop(edge, inner)
    for m in range(MICRO):
        for base in (m * CELLS, m * CELLS + CELLS - 16):
            gmixed_o[base : base + 16, D:] = jnp.zeros((16, 2 * D), BF16)


def leave_kernel(
    core, gmixed_i, low_i, high_i, rim_i, hidden_i, normed_i, filled_i, gmid_i, qkv_i, gout_i,
    seen, vecs, sums, gm_o, gf_o, small_o, send_o,
    from_low, from_high, rim, hidden, normed, filled, gmid, qkv_w, gout, sems,
):
    pairs = [(qkv_i, qkv_w), (low_i, from_low), (high_i, from_high), (rim_i, rim)]
    for m in range(MICRO):
        rows = pl.ds(m * CELLS, CELLS)
        pairs += [(gmixed_i.at[rows], gm_o.at[rows]), (hidden_i.at[rows], hidden.at[rows])]
        pairs.append((gmid_i.at[rows], gmid.at[rows]))
    pairs += [(normed_i, normed), (filled_i, filled), (gout_i, gout)]
    copies = fetch(pairs, sems)
    small = jnp.zeros((1, D), F32)
    gain_sum, shift_sum, mask_sum, embed_sum, query_sum, value_sum = [small] * 6
    for m in range(MICRO):
        base = m * CELLS
        rows = slice(base, base + CELLS)
        for copy in copies[0 if m == 0 else 3 * m + 4 : 3 * m + 7]:
            copy.wait()
        gm_o[base : base + 16, D:] = (rim[m, 0] + from_low[m].astype(F32)).astype(BF16)
        gm_o[base + CELLS - 16 : base + CELLS, D:] = (rim[m, 1] + from_high[m].astype(F32)).astype(
            BF16
        )
        gm = gm_o[rows, :]
        grad = dot(gm, qkv_w[...], NT)
        normal, inverse = norm_parts(hidden[rows, :])
        g_hidden = gmid[rows, :] + norm_back(grad, normal, inverse, vecs[2:3, :])
        there = seen[rows, :] > 0.5
        g_low = g_hidden.astype(BF16)
        gf_o[rows, :] = g_low
        gain_sum += jnp.sum(grad * normal, axis=0, keepdims=True)
        shift_sum += jnp.sum(grad, axis=0, keepdims=True)
        mask_sum += jnp.sum(jnp.where(there, 0.0, g_hidden), axis=0, keepdims=True)
        embed_sum += jnp.sum(jnp.where(there, g_low.astype(F32), 0.0), axis=0, keepdims=True)
        query_sum += jnp.sum(gm[:, :D].astype(F32), axis=0, keepdims=True)
        value_sum += jnp.sum(gm[:, 2 * D :].astype(F32), axis=0, keepdims=True)
    small_o[...] = jnp.concatenate(
        [
            embed_sum, mask_sum, gain_sum, shift_sum, query_sum, value_sum,
            small, small, sums[...],
        ],
        axis=0,
    )
    for copy in copies[3 * MICRO + 4 :]:
        copy.wait()
    one_half(core[0] != 0, send_o, normed, filled, gm_o, gf_o, gout, small_o)


def one_half(first, out, normed, filled, gm, gf, gout, small):
    @pl.when(first)
    def _():
        turned = jnp.transpose(normed[...])
        for b in range(3):
            cols = slice(512 * b, 512 * b + 512)
            out[cols, :] = dot(turned, gm[:, cols]).astype(BF16)

    @pl.when(jnp.logical_not(first))
    def _():
        out[0:512, :] = gout[...]
        out[512:1280, :] = dot(jnp.transpose(filled[...]), gf[...]).astype(BF16)
        out[1280:1296, :] = small[...].astype(BF16)
        out[1296:1536, :] = jnp.zeros((240, D), BF16)


def leave_keep_kernel(core, gm, gf, small, normed, filled, gout, cell, keep_o, ret_o):
    one_half(core[0] == 0, keep_o, normed, filled, gm, gf, gout, small)
    ret_o[...] = dot(one_hot(iota((GOT, ALL), 1) == cell[...]), gf[...]).astype(BF16)


def return_kernel(dest, came, embed_w, out):
    for m in range(MICRO):
        select = one_hot(iota((dest.shape[1], GOT), 1) == dest[m])
        g_proj = dot(select, came[...]).astype(BF16)
        out[m] = dot(g_proj, embed_w[...], NT).astype(BF16)


def unpack_one_kernel(down_i, up_i, down_o, up_o):
    down_o[...] = down_i[...].reshape(512, D).astype(F32)
    up_o[...] = up_i[...].reshape(512, D).astype(F32)


def unpack_one(gathered):
    block = (16, 1, 32, D)
    return pl.pallas_call(
        unpack_one_kernel,
        name="unpack_one",
        grid=(4,),
        out_shape=[jax.ShapeDtypeStruct((FF, D), F32), jax.ShapeDtypeStruct((D, FF), F32)],
        in_specs=[
            pl.BlockSpec(block, lambda i: (i % 2, i // 2, 0, 0)),
            pl.BlockSpec(block, lambda i: (2 + i % 2, i // 2, 0, 0)),
        ],
        out_specs=[
            pl.BlockSpec((512, D), lambda i: (i, 0)),
            pl.BlockSpec((512, D), lambda i: (0, i)),
        ],
        compiler_params=pltpu.CompilerParams(vmem_limit_bytes=16 * 2**20),
        cost_estimate=pl.CostEstimate(flops=0, bytes_accessed=12 * 2**20, transcendentals=0),
    )(gathered, gathered)


def unpack_two_kernel(core, mine, other, qkv_o, embed_o, out_o, small_o):
    def write(first, second):
        for b in range(3):
            qkv_o[:, 512 * b : 512 * b + 512] = first[512 * b : 512 * b + 512, :].astype(F32)
        out_o[...] = second[0:512, :].astype(F32)
        embed_o[...] = second[512:1280, :].astype(F32)
        small_o[...] = second[1280:1296, :].astype(F32)

    @pl.when(core[0] == 0)
    def _():
        write(mine, other)

    @pl.when(core[0] != 0)
    def _():
        write(other, mine)


def clip_ident(lengths, rows):
    first = lengths[:, 0:1]
    second = first + lengths[:, 1:2]
    ident = (rows[None, :] >= first).astype(jnp.int32) + (rows[None, :] >= second).astype(jnp.int32)
    start = jnp.where(ident >= 1, first, 0) + jnp.where(ident >= 2, lengths[:, 1:2], 0)
    inside = (rows >= 0) & (rows < LONG)
    return (jnp.where(inside[None, :], ident, -1), rows[None, :] - start)


def position_tables(row_in_clip, width):
    quarter = width // 4
    omega = 1.0 / 10000.0 ** (jnp.arange(quarter, dtype=jnp.float32) / quarter)
    row_angle = row_in_clip.astype(jnp.float32)[..., None] * omega
    freq_angle = jnp.arange(FREQ, dtype=jnp.float32)[:, None] * omega
    row_part = jnp.concatenate([jnp.sin(row_angle), jnp.cos(row_angle)], -1)
    freq_part = jnp.concatenate([jnp.sin(freq_angle), jnp.cos(freq_angle)], -1)
    return row_part.reshape(-1, width // 2), freq_part


def window_mask(ident):
    cells = jnp.repeat(ident.reshape(MICRO * 7, 4), FREQ, axis=1)
    freq = np.tile((np.arange(FREQ) + 2) % 8 // 4, 4)
    same = (cells[:, :, None] == cells[:, None, :]) & (cells[:, :, None] >= 0)
    same = same & jnp.asarray(freq[:, None] == freq[None, :])[None]
    return jnp.tile(same.astype(F32), (1, 1, 4))


def on_device(
    encoded, visible_pos, clip_len, cotangent, embed_weight, embed_bias, mask_token, attn_gain,
    attn_shift, qkv_weight, query_bias, value_bias, out_weight, out_bias, mlp_gain, mlp_shift,
    up_weight, up_bias, down_weight, down_bias,
):
    both = ("clip", "band")
    groups = lax.axis_size("clip")
    bands = lax.axis_size("band")
    band = lax.axis_index("band")
    side = band % 2
    core = side.astype(jnp.int32).reshape(1)
    halves = [
        [c * bands + 2 * x + k for c in range(groups) for x in range(bands // 2)] for k in range(2)
    ]
    swap = [(i, i ^ 1) for i in range(bands)]
    forward = [(i, i + 1) for i in range(bands - 1)]
    backward = [(b, a) for a, b in forward]
    chips = groups * bands // 2

    def to_all(block):
        return lax.all_to_all(
            block, both, split_axis=0, concat_axis=0, tiled=True, axis_index_groups=halves
        )

    def chip_sum(keep, other):
        mine = (keep.astype(F32) + other.astype(F32)).astype(BF16)
        return mine.reshape(chips, -1, D)

    def total(parts):
        return jnp.sum(parts.astype(F32), 0).astype(BF16)

    def spread(chunk):
        return jnp.broadcast_to(chunk[None], (chips,) + chunk.shape)

    vis = visible_pos.shape[1]
    packed, dest = call(
        pack_kernel, "pack", [((GOT, ENC), BF16), ((MICRO, vis, 1), jnp.int32)],
        (band.astype(jnp.int32).reshape(1), visible_pos, encoded), smem=1,
        flops=GOT * MICRO * vis * ENC * 2,
    )
    cot = cotangent.reshape(ALL, D)
    (g_act,) = call(
        before_kernel, "before", [((ALL, FF), F32)], (cot, down_weight), flops=2 * ALL * D * FF,
    )
    got = lax.all_to_all(
        packed.reshape(SRC, BLK, ENC), "clip", split_axis=0, concat_axis=0, tiled=True
    ).reshape(GOT, ENC)

    place = np.arange(GOT)
    within = place % BLK
    index = np.zeros((8, GOT), np.int32)
    index[0], index[1], index[2] = place // BLK, within, np.where(within < 36, within // CAP, 99)
    heads = jnp.asarray(np.arange(128)[None, :] // 32 == np.arange(16)[:, None] % 4, BF16)

    unused, row_in_clip = clip_ident(clip_len[:, 0], band * ROWS + jnp.arange(ROWS))
    row_table, freq_table = position_tables(row_in_clip, D)
    ident_ext, unused = clip_ident(clip_len[:, 0], band * ROWS - 2 + jnp.arange(ROWS + 4))
    mask = window_mask(ident_ext)
    zero = jnp.zeros((D,), BF16)
    vecs_one = jnp.stack([embed_bias, mask_token, attn_gain, attn_shift] * 2).astype(F32)
    vecs_two = jnp.stack([out_bias, mlp_gain, mlp_shift, down_bias] * 2).astype(F32)
    qkv_b = jnp.concatenate([query_bias, zero, value_bias]).astype(F32)[None]
    up_b = up_bias.astype(F32)[None]

    hidden, normed, mixed, filled, seen, cell, low, high = call(
        enter_kernel, "enter",
        [
            ((ALL, D), F32), ((ALL, D), BF16), ((ALL, 3 * D), BF16), ((ALL, ENC), BF16),
            ((ALL, 1), F32), ((GOT, 1), jnp.int32),
            ((MICRO, 16, 2 * D), BF16), ((MICRO, 16, 2 * D), BF16),
        ],
        (
            jnp.asarray(index), jnp.asarray(np.ascontiguousarray(index.T)), got, row_table,
            freq_table, embed_weight, qkv_weight, vecs_one, qkv_b,
        ),
        scratch=[
            pltpu.VMEM((GOT, ENC), BF16), pltpu.VMEM((ENC, D), BF16), pltpu.VMEM((D, 3 * D), BF16),
            pltpu.SemaphoreType.DMA((3,)),
        ],
        far=(2, 5, 6),
        flops=2 * ALL * (GOT * ENC + ENC * D + 3 * D * D),
    )
    from_low = lax.ppermute(high, "band", forward)
    from_high = lax.ppermute(low, "band", backward)
    attended, probs = call(
        attend_kernel, "attend",
        [((ALL, D), BF16), ((MICRO * 7, 32, D), F32)],
        (mixed, from_low, from_high, mask, heads),
        flops=MICRO * 7 * 4 * 2**20,
    )
    middle, act, gexp, n2t, send = call(
        mlp_kernel, "mlp",
        [
            ((ALL, D), F32), ((ALL, FF), BF16), ((ALL, FF), BF16), ((D, ALL), BF16),
            ((FF, D), BF16),
        ],
        (core, hidden, attended, cot, g_act, out_weight, up_weight, vecs_two, up_b),
        scratch=[pltpu.VMEM((ALL, D), BF16)],
        smem=1, flops=2 * ALL * (2 * D * FF + D * D), vmem=24,
    )
    (keep,) = call(
        mlp_keep_kernel, "mlp_keep", [((FF, D), BF16)], (core, act, gexp, n2t, cot),
        smem=1, flops=2 * ALL * D * FF,
    )
    chip_one = chip_sum(keep, lax.ppermute(send, "band", swap))
    act, chip_one = lax.optimization_barrier((act, chip_one))
    parts_one = to_all(chip_one)
    inputs = (
        middle, attended, cot, act, gexp, out_weight, up_weight, down_weight, mixed, from_low,
        from_high, probs,
    )
    output, gmid, gout, sums, gmixed, low, high, rim = call(
        back_kernel, "back",
        [
            ((ALL, D), BF16), ((ALL, D), F32), ((D, D), BF16), ((8, D), F32),
            ((ALL, 3 * D), BF16), ((MICRO, 16, 2 * D), BF16), ((MICRO, 16, 2 * D), BF16),
            ((MICRO, 2, 16, 2 * D), F32),
        ],
        inputs + (vecs_two, heads),
        scratch=[pltpu.VMEM(x.shape, x.dtype) for x in inputs]
        + [pltpu.VMEM((ALL, D), BF16)] * 2
        + [pltpu.SemaphoreType.DMA((len(inputs),))],
        flops=2 * ALL * (2 * D * FF + 2 * D * D) + MICRO * 7 * 4 * 2**22,
        far=range(len(inputs)), vmem=52,
    )
    from_low = lax.ppermute(high, "band", forward)
    from_high = lax.ppermute(low, "band", backward)
    total_one = total(parts_one)
    total_one, from_low, from_high = lax.optimization_barrier((total_one, from_low, from_high))
    kept = (from_low, from_high, rim, hidden, normed, filled, gmid, qkv_weight, gout)
    fetched = (gmixed,) + kept
    gm, gf, small, send = call(
        leave_kernel, "leave",
        [((ALL, 3 * D), BF16), ((ALL, D), BF16), ((16, D), F32), ((3 * D, D), BF16)],
        (core,) + fetched + (seen, vecs_one, sums),
        scratch=[pltpu.VMEM(x.shape, x.dtype) for x in kept]
        + [pltpu.SemaphoreType.DMA((3 * MICRO + 7,))],
        smem=1, flops=2 * ALL * 5 * D * D, far=range(1, 1 + len(fetched)), vmem=50,
    )
    other = lax.ppermute(send, "band", swap)
    total_one = lax.all_gather(total_one, both, axis=0).reshape(chips, 2, -1, D)
    keep, returned = call(
        leave_keep_kernel, "leave_keep", [((3 * D, D), BF16), ((GOT, D), BF16)],
        (core, gm, gf, small, normed, filled, gout, cell),
        smem=1, flops=2 * ALL * (2 * D * D + GOT * D),
    )
    mine = to_all(spread(total(to_all(chip_sum(keep, other))))).reshape(-1, D)
    mine, returned = lax.optimization_barrier((mine, returned))
    qkv, g_embed, g_out, small = call(
        unpack_two_kernel, "unpack_two",
        [((D, 3 * D), F32), ((ENC, D), F32), ((D, D), F32), ((16, D), F32)],
        (core, mine, lax.ppermute(mine, "band", swap)), smem=1,
    )
    came = lax.all_to_all(
        returned.reshape(SRC, BLK, D), "clip", split_axis=0, concat_axis=0, tiled=True
    ).reshape(GOT, D)
    down, up = unpack_one(total_one)
    lines = tuple(small[i] for i in (0, 1, 2, 3, 4, 5, 8, 9, 10, 11))
    lines += (small[12:16].reshape(FF),)
    came, down, lines = lax.optimization_barrier((came, down, lines))
    (grad_enc,) = call(
        return_kernel, "return", [((MICRO, vis, ENC), BF16)], (dest, came, embed_weight),
        flops=2 * MICRO * vis * D * (GOT + ENC),
    )
    return (
        output.reshape(cotangent.shape), grad_enc, g_embed, *lines[:4], qkv, *lines[4:6], g_out,
        *lines[6:9], up, lines[10], down, lines[9],
    )


def solution(mesh):
    whole = P()
    return jax.shard_map(
        on_device,
        mesh=mesh,
        in_specs=(
            P(None, ("clip", "band"), None),
            P(None, ("clip", "band")),
            P(None, "clip", None),
            P(None, "clip", "band", None, None),
        )
        + (whole,) * 16,
        out_specs=(P(None, "clip", "band", None, None), P(None, ("clip", "band"), None))
        + (whole,) * 16,
        check_vma=False,
    )
```

```python
import jax
import jax.numpy as jnp
import numpy as np
from jax import lax
from jax.experimental import pallas as pl
from jax.experimental.pallas import tpu as pltpu
from jax.sharding import PartitionSpec as P

HEADS = 16
FREQ = 8
LONG = 192
MICRO = 4
ROWS = 24
CELLS = ROWS * FREQ
ALL = MICRO * CELLS
CAP = 9
BLK = 40
SRC = 16
GOT = SRC * BLK
D = 512
FF = 2048
ENC = 768
EPS = 1e-06
SCALE = (D // HEADS) ** (-0.5)
F32 = jnp.float32
BF16 = jnp.bfloat16

NN = (((1,), (0,)), ((), ()))
NT = (((1,), (1,)), ((), ()))
TN = (((0,), (0,)), ((), ()))


def dot(left, right, dims=NN):
    return lax.dot_general(left, right, dims, preferred_element_type=F32)


def iota(shape, dim):
    return lax.broadcasted_iota(jnp.int32, shape, dim)


def one_hot(hit):
    return jnp.where(hit, 1.0, 0.0).astype(BF16)


def call(kernel, name, out_shape, args, scratch=(), smem=0, flops=0, vmem=16, far=()):
    spaces = [pltpu.SMEM] * smem + [pltpu.VMEM] * (len(args) - smem)
    for i in far:
        spaces[i] = pltpu.HBM
    outs = [jax.ShapeDtypeStruct(shape, dtype) for shape, dtype in out_shape]
    size = sum(a.size * a.dtype.itemsize for a in args) + sum(
        o.size * o.dtype.itemsize for o in outs
    )
    return pl.pallas_call(
        kernel,
        name=name,
        out_shape=outs,
        in_specs=[pl.BlockSpec(memory_space=space) for space in spaces],
        out_specs=[pl.BlockSpec(memory_space=pltpu.VMEM)] * len(outs),
        scratch_shapes=list(scratch),
        compiler_params=pltpu.CompilerParams(vmem_limit_bytes=vmem * 2**20),
        cost_estimate=pl.CostEstimate(flops=flops, bytes_accessed=size, transcendentals=0),
    )(*args)


def pack_kernel(band, pos, enc, out, dest):
    count = pos.shape[1]
    low = iota((count, count), 0)
    high = iota((count, count), 1)
    packed = jnp.zeros((GOT, ENC), F32)
    places = jnp.zeros((SRC, 128), F32)
    for m in range(MICRO):
        cell_r = pos[m : m + 1, :]
        cell_c = jnp.sum(jnp.where(low == high, cell_r, 0), axis=1, keepdims=True)
        slot = LONG * FREQ
        dev_r = jnp.sum(
            jnp.where(cell_r >= slot * iota((SRC, count), 0) + slot, 1, 0), axis=0, keepdims=True
        )
        dev_c = jnp.sum(
            jnp.where(cell_c >= slot * iota((count, SRC), 1) + slot, 1, 0), axis=1, keepdims=True
        )
        same = dev_c == dev_r
        rank_r = jnp.sum(jnp.where(same & (low < high), 1, 0), axis=0, keepdims=True)
        rank_c = jnp.sum(jnp.where(same & (high < low), 1, 0), axis=1, keepdims=True)
        dest[m] = dev_c * BLK + m * CAP + rank_c
        select = one_hot(iota((GOT, count), 0) == dev_r * BLK + m * CAP + rank_r)
        packed = packed + dot(select, enc[m])
        number = cell_r - dev_r * slot - band[0] * CELLS + 1
        to_dev = jnp.where(iota((SRC, count), 0) == dev_r, number.astype(F32), 0.0).astype(BF16)
        to_lane = one_hot(iota((count, 128), 1) == m * CAP + rank_c)
        places = places + dot(to_dev, to_lane)
    spread = one_hot(iota((GOT, SRC), 0) == iota((GOT, SRC), 1) * BLK + (BLK - 4))
    out[:, :128] = (packed[:, :128] + dot(spread, places.astype(BF16))).astype(BF16)
    out[:, 128:] = packed[:, 128:].astype(BF16)


def norm_parts(values):
    center = values - jnp.mean(values, -1, keepdims=True)
    inverse = lax.rsqrt(jnp.mean(center * center, -1, keepdims=True) + EPS)
    return center * inverse, inverse


def norm_back(grad, normal, inverse, gain):
    scaled = grad * gain
    return inverse * (
        scaled
        - jnp.mean(scaled, -1, keepdims=True)
        - normal * jnp.mean(scaled * normal, -1, keepdims=True)
    )


def fetch(pairs, sems):
    copies = [pltpu.make_async_copy(far, near, sems.at[i]) for i, (far, near) in enumerate(pairs)]
    for copy in copies:
        copy.start()
    return copies


def enter_kernel(
    idx_r, idx_c, got_i, row_table, freq_table, embed_i, qkv_i, vecs, qkv_b,
    hidden_o, normed_o, mixed_o, filled_o, seen_o, cell_o, low_o, high_o,
    got, embed_w, qkv_w, sems,
):
    copies = fetch([(got_i, got), (embed_i, embed_w), (qkv_i, qkv_w)], sems)
    copies[0].wait()
    hit = one_hot(iota((SRC, GOT), 1) == iota((SRC, GOT), 0) * BLK + (BLK - 4))
    numbers = dot(hit, got[:, :128]).astype(BF16)
    spread_r = dot(numbers, one_hot(iota((SRC, GOT), 0) == idx_r[0:1, :]), TN)
    value_r = jnp.sum(
        jnp.where(iota((128, GOT), 0) == idx_r[1:2, :], spread_r, 0.0), axis=0, keepdims=True
    )
    cell_r = jnp.where(
        value_r > 0.5, idx_r[2:3, :] * CELLS + value_r.astype(jnp.int32) - 1, -1
    )
    spread_c = dot(one_hot(iota((GOT, SRC), 1) == idx_c[:, 0:1]), numbers)
    value_c = jnp.sum(
        jnp.where(iota((GOT, 128), 1) == idx_c[:, 1:2], spread_c, 0.0), axis=1, keepdims=True
    )
    cell_o[...] = jnp.where(
        value_c > 0.5, idx_c[:, 2:3] * CELLS + value_c.astype(jnp.int32) - 1, -1
    )
    for m in range(MICRO):
        rows = slice(m * CELLS, (m + 1) * CELLS)
        match = jnp.where(iota((CELLS, GOT), 0) + m * CELLS == cell_r, 1.0, 0.0)
        seen = jnp.sum(match, axis=1, keepdims=True)
        filled = dot(match.astype(BF16), got[...]).astype(BF16)
        filled_o[rows, :] = filled
        seen_o[rows, :] = seen
    copies[1].wait()
    copies[2].wait()
    freq = jnp.broadcast_to(freq_table[...][None], (ROWS, FREQ, D // 2)).reshape(CELLS, D // 2)
    for m in range(MICRO):
        rows = slice(m * CELLS, (m + 1) * CELLS)
        seen = seen_o[rows, :]
        proj = (dot(filled_o[rows, :], embed_w[...]) + vecs[0:1, :]).astype(BF16).astype(F32)
        line = row_table[m * ROWS : (m + 1) * ROWS, :]
        line = jnp.broadcast_to(line[:, None, :], (ROWS, FREQ, D // 2)).reshape(CELLS, D // 2)
        table = jnp.concatenate([line, freq], axis=1)
        hidden = jnp.where(seen > 0.5, proj, vecs[1:2, :]) + table
        hidden_o[rows, :] = hidden
        normal, unused = norm_parts(hidden)
        normed = (normal * vecs[2:3, :] + vecs[3:4, :]).astype(BF16)
        normed_o[rows, :] = normed
        mixed = (dot(normed, qkv_w[...]) + qkv_b[...]).astype(BF16)
        mixed_o[rows, :] = mixed
        low_o[m] = mixed[:16, D:]
        high_o[m] = mixed[CELLS - 16 :, D:]


def head_rows(block, heads):
    return jnp.concatenate([block * heads[h : h + 1, :] for h in range(4)], axis=0)


def own_head(full, lane_head):
    out = full[0:32, :]
    for h in range(1, 4):
        out = jnp.where(lane_head == h, full[32 * h : 32 * h + 32, :], out)
    return out


def window_loop(edge, inner):
    def inside(p, carry):
        places = []
        for m in range(MICRO):
            base = pl.multiple_of(m * CELLS + 32 * p - 16, 16)
            places.append((m * 7 + p, pl.ds(base, 32)))
        inner(places)
        return carry

    def ends(i, carry):
        places = []
        for j in range(2):
            m = 2 * i + j
            first = pl.multiple_of(m * CELLS, 16)
            last = pl.multiple_of(m * CELLS + CELLS - 16, 16)
            places.append((m, m * 7, pl.ds(first, 16), 0))
            places.append((m, m * 7 + 6, pl.ds(last, 16), 1))
        edge(places)
        return carry

    lax.fori_loop(1, 6, inside, 0)
    lax.fori_loop(0, MICRO // 2, ends, 0)


def with_halo(own, halo, side):
    return jnp.concatenate([own, halo] if side else [halo, own], axis=0)


COLS = [[slice(D * i + 128 * g, D * i + 128 * g + 128) for i in range(3)] for g in range(4)]


def load_inner(mixed, places, grads=None):
    items = []
    for w, rows in places:
        for g in range(4):
            item = [mixed[rows, c] for c in COLS[g]]
            items.append((w, g, *item, None if grads is None else grads[rows, COLS[g][0]]))
    return items


def load_edge(mixed, low, high, places, grads=None):
    zero = jnp.zeros((16, 128), BF16)
    items = []
    for m, w, rows, side in places:
        halo = high if side else low
        for g in range(4):
            cols = COLS[g]
            q = with_halo(mixed[rows, cols[0]], zero, side)
            k = with_halo(mixed[rows, cols[1]], halo[m, :, cols[0]], side)
            v = with_halo(mixed[rows, cols[2]], halo[m, :, cols[1]], side)
            grad = None if grads is None else with_halo(grads[rows, cols[0]], zero, side)
            items.append((w, g, q, k, v, grad))
    return items


def attend_kernel(mixed, low, high, mask, heads_i, attended_o, probs_o):
    heads = heads_i[...]
    lane_head = iota((32, 128), 1) // 32

    def windows(items):
        scores = [dot(k, head_rows(q, heads), NT) * SCALE for w, g, q, k, v, _ in items]
        probs = []
        for (w, g, *_), score in zip(items, scores):
            score = jnp.where(mask[w] > 0.5, score, -1e30)
            grown = jnp.exp(score - jnp.max(score, axis=0, keepdims=True))
            one = grown * (1.0 / jnp.sum(grown, axis=0, keepdims=True))
            probs_o[w, :, 128 * g : 128 * g + 128] = one
            probs.append(one.astype(BF16))
        full = [dot(one, item[4], TN) for item, one in zip(items, probs)]
        return [own_head(one, lane_head).astype(BF16) for one in full]

    def inner(places):
        outs = windows(load_inner(mixed, places))
        for i, (w, rows) in enumerate(places):
            for g in range(4):
                attended_o[rows, COLS[g][0]] = outs[4 * i + g]

    def edge(places):
        outs = windows(load_edge(mixed, low, high, places))
        for i, (m, w, rows, side) in enumerate(places):
            for g in range(4):
                out = outs[4 * i + g]
                attended_o[rows, COLS[g][0]] = out[:16] if side else out[16:]

    window_loop(edge, inner)


def gelu_parts(x):
    bell = jnp.exp(-0.5 * x * x)
    t = 1.0 / (1.0 + 0.3275911 * 0.5**0.5 * jnp.abs(x))
    poly = 0.127414796 + t * (
        -0.142248368 + t * (0.7107068705 + t * (-0.7265760135 + t * 0.5307027145))
    )
    tail = t * poly * bell
    share = jnp.where(x >= 0, 1.0 - tail, tail)
    return x * share, share + x * bell * 0.3989422804014327


def before_kernel(cot, down_w, g_act_o):
    for f in range(4):
        cols = slice(512 * f, 512 * f + 512)
        g_act_o[:, cols] = dot(cot[...], down_w[cols, :], NT)


def mlp_kernel(
    core, hidden, attended, cot, g_act, out_w, up_w, vecs, up_b,
    middle_o, act_o, gexp_o, n2t_o, send_o, n2_s,
):
    tile = 256
    blocks = [slice(512 * f, 512 * f + 512) for f in range(4)]

    lines = [slice(i * tile, (i + 1) * tile) for i in range(ALL // tile)]
    for rows in lines:
        middle = hidden[rows, :] + dot(attended[rows, :], out_w[...]) + vecs[0:1, :]
        middle_o[rows, :] = middle
        normal, unused = norm_parts(middle)
        n2_s[rows, :] = (normal * vecs[1:2, :] + vecs[2:3, :]).astype(BF16)
    places = [(rows, cols) for rows in lines for cols in blocks]
    ahead = dot(n2_s[lines[0], :], up_w[:, blocks[0]])
    for i, (rows, cols) in enumerate(places):
        expand = ahead + up_b[0:1, cols]
        if i + 1 < len(places):
            ahead = dot(n2_s[places[i + 1][0], :], up_w[:, places[i + 1][1]])
        value, slope = gelu_parts(expand)
        act_o[rows, cols] = value.astype(BF16)
        gexp_o[rows, cols] = (g_act[rows, cols] * slope).astype(BF16)
    n2t_o[...] = jnp.transpose(n2_s[...])
    weight_half(1 - core[0], send_o, act_o, gexp_o, n2t_o, cot)


def weight_half(half, out, act, gexp, n2t, cot):
    for b in range(2):
        cols = pl.ds(pl.multiple_of(half * 1024 + 512 * b, 512), 512)
        rows = slice(512 * b, 512 * b + 512)
        out[rows, :] = dot(act[:, cols], cot[...], TN).astype(BF16)
        rows = slice(1024 + 512 * b, 1536 + 512 * b)
        out[rows, :] = dot(n2t[...], gexp[:, cols]).astype(BF16)


def mlp_keep_kernel(core, act, gexp, n2t, cot, keep_o):
    weight_half(core[0], keep_o, act, gexp, n2t, cot)


def back_kernel(
    middle_i, attended_i, cot_i, act_i, gexp_i, out_i, up_i, down_i, mixed_i, low_i, high_i,
    probs_f, vecs, heads_i,
    output_o, gmid_o, gout_o, sums_o, gmixed_o, low_o, high_o, rim_o,
    middle_s, attended, cot, act, gexp, out_w, up_w, down_w, mixed, low, high, probs_i, gatt, gb_s,
    sems,
):
    copies = fetch(
        [
            (up_i, up_w), (gexp_i, gexp), (down_i, down_w), (act_i, act), (middle_i, middle_s),
            (cot_i, cot), (out_i, out_w), (attended_i, attended), (mixed_i, mixed),
            (low_i, low), (high_i, high), (probs_f, probs_i),
        ],
        sems,
    )
    tile = 256
    sums_o[...] = jnp.zeros((8, D), F32)
    for i in range(ALL // tile):
        rows = slice(i * tile, (i + 1) * tile)
        if i == 0:
            copies[0].wait()
            copies[1].wait()
        grad = dot(gexp[rows, :], up_w[...], NT)
        if i == 0:
            copies[2].wait()
            copies[3].wait()
            copies[4].wait()
        middle = middle_s[rows, :]
        output_o[rows, :] = (middle + vecs[3:4, :] + dot(act[rows, :], down_w[...])).astype(BF16)
        if i == 0:
            copies[5].wait()
            copies[6].wait()
        normal, inverse = norm_parts(middle)
        g_float = cot[rows, :].astype(F32)
        g_mid = g_float + norm_back(grad, normal, inverse, vecs[1:2, :])
        gmid_o[rows, :] = g_mid
        g_low = g_mid.astype(BF16)
        gb_s[rows, :] = g_low
        gatt[rows, :] = dot(g_low, out_w[...], NT).astype(BF16)
        sums_o[0:1, :] += jnp.sum(g_low.astype(F32), axis=0, keepdims=True)
        sums_o[1:2, :] += jnp.sum(grad * normal, axis=0, keepdims=True)
        sums_o[2:3, :] += jnp.sum(grad, axis=0, keepdims=True)
        sums_o[3:4, :] += jnp.sum(g_float, axis=0, keepdims=True)
        for f in range(4):
            part = gexp[rows, 512 * f : 512 * f + 512].astype(F32)
            sums_o[4 + f : 5 + f, :] += jnp.sum(part, axis=0, keepdims=True)
    copies[7].wait()
    gout_o[...] = dot(attended[...], gb_s[...], TN).astype(BF16)
    for copy in copies[8:]:
        copy.wait()
    attend_back(mixed, low, high, probs_i, gatt, heads_i, gmixed_o, low_o, high_o, rim_o)


def attend_back(
    mixed, low, high, probs_i, gatt, heads_i, gmixed_o, low_o, high_o, rim_o
):
    heads = heads_i[...]
    lane_head = iota((32, 128), 1) // 32

    def windows(items):
        q_m = [head_rows(q, heads) for w, g, q, k, v, grad in items]
        g_m = [head_rows(grad, heads) for w, g, q, k, v, grad in items]
        g_probs = [dot(item[4], one, NT) for item, one in zip(items, g_m)]
        low_probs, g_scores = [], []
        for (w, g, *_), g_prob in zip(items, g_probs):
            probs = probs_i[w, :, 128 * g : 128 * g + 128]
            inner = jnp.sum(probs * g_prob, axis=0, keepdims=True)
            g_scores.append((probs * (g_prob - inner)).astype(BF16))
            low_probs.append(probs.astype(BF16))
        d_value = [dot(one, grad) for one, grad in zip(low_probs, g_m)]
        d_key = [dot(one, q) * SCALE for one, q in zip(g_scores, q_m)]
        full = [dot(one, item[3], TN) for item, one in zip(items, g_scores)]
        d_query = [(own_head(one, lane_head) * SCALE).astype(BF16) for one in full]
        return list(zip(d_query, d_key, d_value))

    def inner(places):
        outs = windows(load_inner(mixed, places, gatt))
        for i, (w, rows) in enumerate(places):
            for g in range(4):
                for col, value in zip(COLS[g], outs[4 * i + g]):
                    gmixed_o[rows, col] = value.astype(BF16)

    def edge(places):
        outs = windows(load_edge(mixed, low, high, places, gatt))
        for i, (m, w, rows, side) in enumerate(places):
            out = high_o if side else low_o
            own, far = (slice(0, 16), slice(16, 32)) if side else (slice(16, 32), slice(0, 16))
            for g in range(4):
                cols = COLS[g]
                d_query, d_key, d_value = outs[4 * i + g]
                gmixed_o[rows, cols[0]] = d_query[own]
                rim_o[m, side, :, cols[0]] = d_key[own]
                rim_o[m, side, :, cols[1]] = d_value[own]
                out[m, :, cols[0]] = d_key[far].astype(BF16)
                out[m, :, cols[1]] = d_value[far].astype(BF16)

    window_loop(edge, inner)
    for m in range(MICRO):
        for base in (m * CELLS, m * CELLS + CELLS - 16):
            gmixed_o[base : base + 16, D:] = jnp.zeros((16, 2 * D), BF16)


def leave_kernel(
    core, gmixed_i, low_i, high_i, rim_i, hidden_i, normed_i, filled_i, gmid_i, qkv_i, gout_i,
    seen, vecs, sums, gm_o, gf_o, small_o, send_o,
    from_low, from_high, rim, hidden, normed, filled, gmid, qkv_w, gout, sems,
):
    pairs = [(qkv_i, qkv_w), (low_i, from_low), (high_i, from_high), (rim_i, rim)]
    for m in range(MICRO):
        rows = pl.ds(m * CELLS, CELLS)
        pairs += [(gmixed_i.at[rows], gm_o.at[rows]), (hidden_i.at[rows], hidden.at[rows])]
        pairs.append((gmid_i.at[rows], gmid.at[rows]))
    pairs += [(normed_i, normed), (filled_i, filled), (gout_i, gout)]
    copies = fetch(pairs, sems)
    small = jnp.zeros((1, D), F32)
    gain_sum, shift_sum, mask_sum, embed_sum, query_sum, value_sum = [small] * 6
    for m in range(MICRO):
        base = m * CELLS
        rows = slice(base, base + CELLS)
        for copy in copies[0 if m == 0 else 3 * m + 4 : 3 * m + 7]:
            copy.wait()
        gm_o[base : base + 16, D:] = (rim[m, 0] + from_low[m].astype(F32)).astype(BF16)
        gm_o[base + CELLS - 16 : base + CELLS, D:] = (rim[m, 1] + from_high[m].astype(F32)).astype(
            BF16
        )
        gm = gm_o[rows, :]
        grad = dot(gm, qkv_w[...], NT)
        normal, inverse = norm_parts(hidden[rows, :])
        g_hidden = gmid[rows, :] + norm_back(grad, normal, inverse, vecs[2:3, :])
        there = seen[rows, :] > 0.5
        g_low = g_hidden.astype(BF16)
        gf_o[rows, :] = g_low
        gain_sum += jnp.sum(grad * normal, axis=0, keepdims=True)
        shift_sum += jnp.sum(grad, axis=0, keepdims=True)
        mask_sum += jnp.sum(jnp.where(there, 0.0, g_hidden), axis=0, keepdims=True)
        embed_sum += jnp.sum(jnp.where(there, g_low.astype(F32), 0.0), axis=0, keepdims=True)
        query_sum += jnp.sum(gm[:, :D].astype(F32), axis=0, keepdims=True)
        value_sum += jnp.sum(gm[:, 2 * D :].astype(F32), axis=0, keepdims=True)
    small_o[...] = jnp.concatenate(
        [
            embed_sum, mask_sum, gain_sum, shift_sum, query_sum, value_sum,
            small, small, sums[...],
        ],
        axis=0,
    )
    for copy in copies[3 * MICRO + 4 :]:
        copy.wait()
    one_half(core[0] != 0, send_o, normed, filled, gm_o, gf_o, gout, small_o)


def one_half(first, out, normed, filled, gm, gf, gout, small):
    @pl.when(first)
    def _():
        turned = jnp.transpose(normed[...])
        for b in range(3):
            cols = slice(512 * b, 512 * b + 512)
            out[cols, :] = dot(turned, gm[:, cols]).astype(BF16)

    @pl.when(jnp.logical_not(first))
    def _():
        out[0:512, :] = gout[...]
        out[512:1280, :] = dot(jnp.transpose(filled[...]), gf[...]).astype(BF16)
        out[1280:1296, :] = small[...].astype(BF16)
        out[1296:1536, :] = jnp.zeros((240, D), BF16)


def leave_keep_kernel(
    core, gm_i, gf, small, normed, filled, gout, cell, keep_o, ret_o, gm, sems
):
    copies = fetch([(gm_i, gm)], sems)
    ret_o[...] = dot(one_hot(iota((GOT, ALL), 1) == cell[...]), gf[...]).astype(BF16)
    copies[0].wait()
    one_half(core[0] == 0, keep_o, normed, filled, gm, gf, gout, small)


def return_kernel(dest, came, embed_w, out):
    for m in range(MICRO):
        select = one_hot(iota((dest.shape[1], GOT), 1) == dest[m])
        g_proj = dot(select, came[...]).astype(BF16)
        out[m] = dot(g_proj, embed_w[...], NT).astype(BF16)


def unpack_one_kernel(down_i, up_i, down_o, up_o):
    down_o[...] = down_i[...].reshape(512, D).astype(F32)
    up_o[...] = up_i[...].reshape(512, D).astype(F32)


def unpack_one(gathered):
    block = (16, 1, 32, D)
    return pl.pallas_call(
        unpack_one_kernel,
        name="unpack_one",
        grid=(4,),
        out_shape=[jax.ShapeDtypeStruct((FF, D), F32), jax.ShapeDtypeStruct((D, FF), F32)],
        in_specs=[
            pl.BlockSpec(block, lambda i: (i % 2, i // 2, 0, 0)),
            pl.BlockSpec(block, lambda i: (2 + i % 2, i // 2, 0, 0)),
        ],
        out_specs=[
            pl.BlockSpec((512, D), lambda i: (i, 0)),
            pl.BlockSpec((512, D), lambda i: (0, i)),
        ],
        compiler_params=pltpu.CompilerParams(vmem_limit_bytes=16 * 2**20),
        cost_estimate=pl.CostEstimate(flops=0, bytes_accessed=12 * 2**20, transcendentals=0),
    )(gathered, gathered)


def unpack_two_kernel(core, mine, other, qkv_o, embed_o, out_o, small_o):
    def write(first, second):
        for b in range(3):
            qkv_o[:, 512 * b : 512 * b + 512] = first[512 * b : 512 * b + 512, :].astype(F32)
        out_o[...] = second[0:512, :].astype(F32)
        embed_o[...] = second[512:1280, :].astype(F32)
        small_o[...] = second[1280:1296, :].astype(F32)

    @pl.when(core[0] == 0)
    def _():
        write(mine, other)

    @pl.when(core[0] != 0)
    def _():
        write(other, mine)


def clip_ident(lengths, rows):
    first = lengths[:, 0:1]
    second = first + lengths[:, 1:2]
    ident = (rows[None, :] >= first).astype(jnp.int32) + (rows[None, :] >= second).astype(jnp.int32)
    start = jnp.where(ident >= 1, first, 0) + jnp.where(ident >= 2, lengths[:, 1:2], 0)
    inside = (rows >= 0) & (rows < LONG)
    return (jnp.where(inside[None, :], ident, -1), rows[None, :] - start)


def position_tables(row_in_clip, width):
    quarter = width // 4
    omega = 1.0 / 10000.0 ** (jnp.arange(quarter, dtype=jnp.float32) / quarter)
    row_angle = row_in_clip.astype(jnp.float32)[..., None] * omega
    freq_angle = jnp.arange(FREQ, dtype=jnp.float32)[:, None] * omega
    row_part = jnp.concatenate([jnp.sin(row_angle), jnp.cos(row_angle)], -1)
    freq_part = jnp.concatenate([jnp.sin(freq_angle), jnp.cos(freq_angle)], -1)
    return row_part.reshape(-1, width // 2), freq_part


def window_mask(ident):
    cells = jnp.repeat(ident.reshape(MICRO * 7, 4), FREQ, axis=1)
    freq = np.tile((np.arange(FREQ) + 2) % 8 // 4, 4)
    same = (cells[:, :, None] == cells[:, None, :]) & (cells[:, :, None] >= 0)
    same = same & jnp.asarray(freq[:, None] == freq[None, :])[None]
    return jnp.tile(same.astype(F32), (1, 1, 4))


def on_device(
    encoded, visible_pos, clip_len, cotangent, embed_weight, embed_bias, mask_token, attn_gain,
    attn_shift, qkv_weight, query_bias, value_bias, out_weight, out_bias, mlp_gain, mlp_shift,
    up_weight, up_bias, down_weight, down_bias,
):
    both = ("clip", "band")
    groups = lax.axis_size("clip")
    bands = lax.axis_size("band")
    band = lax.axis_index("band")
    side = band % 2
    core = side.astype(jnp.int32).reshape(1)
    halves = [
        [c * bands + 2 * x + k for c in range(groups) for x in range(bands // 2)] for k in range(2)
    ]
    swap = [(i, i ^ 1) for i in range(bands)]
    forward = [(i, i + 1) for i in range(bands - 1)]
    backward = [(b, a) for a, b in forward]
    chips = groups * bands // 2

    def to_all(block):
        return lax.all_to_all(
            block, both, split_axis=0, concat_axis=0, tiled=True, axis_index_groups=halves
        )

    def chip_sum(keep, other):
        mine = (keep.astype(F32) + other.astype(F32)).astype(BF16)
        return mine.reshape(chips, -1, D)

    def total(parts):
        return jnp.sum(parts.astype(F32), 0).astype(BF16)

    def spread(chunk):
        return jnp.broadcast_to(chunk[None], (chips,) + chunk.shape)

    vis = visible_pos.shape[1]
    packed, dest = call(
        pack_kernel, "pack", [((GOT, ENC), BF16), ((MICRO, vis, 1), jnp.int32)],
        (band.astype(jnp.int32).reshape(1), visible_pos, encoded), smem=1,
        flops=GOT * MICRO * vis * ENC * 2,
    )
    cot = cotangent.reshape(ALL, D)
    (g_act,) = call(
        before_kernel, "before", [((ALL, FF), F32)], (cot, down_weight), flops=2 * ALL * D * FF,
    )
    got = lax.all_to_all(
        packed.reshape(SRC, BLK, ENC), "clip", split_axis=0, concat_axis=0, tiled=True
    ).reshape(GOT, ENC)

    place = np.arange(GOT)
    within = place % BLK
    index = np.zeros((8, GOT), np.int32)
    index[0], index[1], index[2] = place // BLK, within, np.where(within < 36, within // CAP, 99)
    heads = jnp.asarray(np.arange(128)[None, :] // 32 == np.arange(16)[:, None] % 4, BF16)

    unused, row_in_clip = clip_ident(clip_len[:, 0], band * ROWS + jnp.arange(ROWS))
    row_table, freq_table = position_tables(row_in_clip, D)
    ident_ext, unused = clip_ident(clip_len[:, 0], band * ROWS - 2 + jnp.arange(ROWS + 4))
    mask = window_mask(ident_ext)
    zero = jnp.zeros((D,), BF16)
    vecs_one = jnp.stack([embed_bias, mask_token, attn_gain, attn_shift] * 2).astype(F32)
    vecs_two = jnp.stack([out_bias, mlp_gain, mlp_shift, down_bias] * 2).astype(F32)
    qkv_b = jnp.concatenate([query_bias, zero, value_bias]).astype(F32)[None]
    up_b = up_bias.astype(F32)[None]

    hidden, normed, mixed, filled, seen, cell, low, high = call(
        enter_kernel, "enter",
        [
            ((ALL, D), F32), ((ALL, D), BF16), ((ALL, 3 * D), BF16), ((ALL, ENC), BF16),
            ((ALL, 1), F32), ((GOT, 1), jnp.int32),
            ((MICRO, 16, 2 * D), BF16), ((MICRO, 16, 2 * D), BF16),
        ],
        (
            jnp.asarray(index), jnp.asarray(np.ascontiguousarray(index.T)), got, row_table,
            freq_table, embed_weight, qkv_weight, vecs_one, qkv_b,
        ),
        scratch=[
            pltpu.VMEM((GOT, ENC), BF16), pltpu.VMEM((ENC, D), BF16), pltpu.VMEM((D, 3 * D), BF16),
            pltpu.SemaphoreType.DMA((3,)),
        ],
        far=(2, 5, 6),
        flops=2 * ALL * (GOT * ENC + ENC * D + 3 * D * D),
    )
    from_low = lax.ppermute(high, "band", forward)
    from_high = lax.ppermute(low, "band", backward)
    attended, probs = call(
        attend_kernel, "attend",
        [((ALL, D), BF16), ((MICRO * 7, 32, D), F32)],
        (mixed, from_low, from_high, mask, heads),
        flops=MICRO * 7 * 4 * 2**20,
    )
    middle, act, gexp, n2t, send = call(
        mlp_kernel, "mlp",
        [
            ((ALL, D), F32), ((ALL, FF), BF16), ((ALL, FF), BF16), ((D, ALL), BF16),
            ((FF, D), BF16),
        ],
        (core, hidden, attended, cot, g_act, out_weight, up_weight, vecs_two, up_b),
        scratch=[pltpu.VMEM((ALL, D), BF16)],
        smem=1, flops=2 * ALL * (2 * D * FF + D * D), vmem=24,
    )
    (keep,) = call(
        mlp_keep_kernel, "mlp_keep", [((FF, D), BF16)], (core, act, gexp, n2t, cot),
        smem=1, flops=2 * ALL * D * FF,
    )
    chip_one = chip_sum(keep, lax.ppermute(send, "band", swap))
    act, chip_one = lax.optimization_barrier((act, chip_one))
    parts_one = to_all(chip_one)
    inputs = (
        middle, attended, cot, act, gexp, out_weight, up_weight, down_weight, mixed, from_low,
        from_high, probs,
    )
    output, gmid, gout, sums, gmixed, low, high, rim = call(
        back_kernel, "back",
        [
            ((ALL, D), BF16), ((ALL, D), F32), ((D, D), BF16), ((8, D), F32),
            ((ALL, 3 * D), BF16), ((MICRO, 16, 2 * D), BF16), ((MICRO, 16, 2 * D), BF16),
            ((MICRO, 2, 16, 2 * D), F32),
        ],
        inputs + (vecs_two, heads),
        scratch=[pltpu.VMEM(x.shape, x.dtype) for x in inputs]
        + [pltpu.VMEM((ALL, D), BF16)] * 2
        + [pltpu.SemaphoreType.DMA((len(inputs),))],
        flops=2 * ALL * (2 * D * FF + 2 * D * D) + MICRO * 7 * 4 * 2**22,
        far=range(len(inputs)), vmem=52,
    )
    from_low = lax.ppermute(high, "band", forward)
    from_high = lax.ppermute(low, "band", backward)
    total_one = total(parts_one)
    total_one, from_low, from_high = lax.optimization_barrier((total_one, from_low, from_high))
    kept = (from_low, from_high, rim, hidden, normed, filled, gmid, qkv_weight, gout)
    fetched = (gmixed,) + kept
    gm, gf, small, send = call(
        leave_kernel, "leave",
        [((ALL, 3 * D), BF16), ((ALL, D), BF16), ((16, D), F32), ((3 * D, D), BF16)],
        (core,) + fetched + (seen, vecs_one, sums),
        scratch=[pltpu.VMEM(x.shape, x.dtype) for x in kept]
        + [pltpu.SemaphoreType.DMA((3 * MICRO + 7,))],
        smem=1, flops=2 * ALL * 5 * D * D, far=range(1, 1 + len(fetched)), vmem=50,
    )
    other = lax.ppermute(send, "band", swap)
    total_one = lax.all_gather(total_one, both, axis=0).reshape(chips, 2, -1, D)
    keep, returned = call(
        leave_keep_kernel, "leave_keep", [((3 * D, D), BF16), ((GOT, D), BF16)],
        (core, gm, gf, small, normed, filled, gout, cell),
        scratch=[pltpu.VMEM(gm.shape, gm.dtype), pltpu.SemaphoreType.DMA((1,))],
        far=(1,), vmem=54, smem=1, flops=2 * ALL * (2 * D * D + GOT * D),
    )
    mine = to_all(spread(total(to_all(chip_sum(keep, other))))).reshape(-1, D)
    mine, returned = lax.optimization_barrier((mine, returned))
    qkv, g_embed, g_out, small = call(
        unpack_two_kernel, "unpack_two",
        [((D, 3 * D), F32), ((ENC, D), F32), ((D, D), F32), ((16, D), F32)],
        (core, mine, lax.ppermute(mine, "band", swap)), smem=1,
    )
    came = lax.all_to_all(
        returned.reshape(SRC, BLK, D), "clip", split_axis=0, concat_axis=0, tiled=True
    ).reshape(GOT, D)
    down, up = unpack_one(total_one)
    lines = tuple(small[i] for i in (0, 1, 2, 3, 4, 5, 8, 9, 10, 11))
    lines += (small[12:16].reshape(FF),)
    came, down, lines = lax.optimization_barrier((came, down, lines))
    (grad_enc,) = call(
        return_kernel, "return", [((MICRO, vis, ENC), BF16)], (dest, came, embed_weight),
        flops=2 * MICRO * vis * D * (GOT + ENC),
    )
    return (
        output.reshape(cotangent.shape), grad_enc, g_embed, *lines[:4], qkv, *lines[4:6], g_out,
        *lines[6:9], up, lines[10], down, lines[9],
    )


def solution(mesh):
    whole = P()
    return jax.shard_map(
        on_device,
        mesh=mesh,
        in_specs=(
            P(None, ("clip", "band"), None),
            P(None, ("clip", "band")),
            P(None, "clip", None),
            P(None, "clip", "band", None, None),
        )
        + (whole,) * 16,
        out_specs=(P(None, "clip", "band", None, None), P(None, ("clip", "band"), None))
        + (whole,) * 16,
        check_vma=False,
    )
```
